32 devices in a mesh: dp: 8 (over z, y), seq: 4 (over x, core).
Axes of the slice: x: 2, y: 2, z: 4, core: 2. Of those that a mesh axis runs over, the one named last changes fastest.
Arguments:
- tokens: bfloat16 [16, 2048, 768], P('dp', 'seq'), may hold values from -6 to 6
- cotangent: bfloat16 [16, 2048, 768], P('dp', 'seq'), may hold values from -6 to 6
- lengths: int32 [16], P('dp'), may hold values from 256 to 2048, as said below
- patch_mask: int32 [16, 2048], P('dp'), may hold values 0 or 1
- owners: int32 [48], replicated, may hold values from 0 to 7, as said below
- master: float32 [48, 384, 384], P('dp'), may hold values from -1 to 1
- moment_one: float32 [48, 384, 384], P('dp'), may hold values from -64 to 64
- moment_two: float32 [48, 384, 384], P('dp'), may hold values from 8.192 to 32.768
- left_stats: float32 [48, 384, 384], P('dp'), may hold values from -32768 to 12582912, as said below
- right_stats: float32 [48, 384, 384], P('dp'), may hold values from -32768 to 12582912, as said below
- left_basis: float32 [48, 384, 384], P('dp'), may hold values from -1 to 1, as said below
- right_basis: float32 [48, 384, 384], P('dp'), may hold values from -1 to 1, as said below
- vec_params: float32 [12, 768], replicated, may hold values from -2 to 2
- vec_one: float32 [12, 768], replicated, may hold values from -64 to 64
- vec_two: float32 [12, 768], replicated, may hold values from 8.192 to 32.768
Outputs:
- output: bfloat16 [16, 2048, 768], P('dp', 'seq')
- d_tokens: bfloat16 [16, 2048, 768], P('dp', 'seq')
- grad_blocks: float32 [48, 384, 384], P('dp')
- master_new: float32 [48, 384, 384], P('dp')
- moment_one_new: float32 [48, 384, 384], P('dp')
- moment_two_new: float32 [48, 384, 384], P('dp')
- left_new: float32 [48, 384, 384], P('dp')
- right_new: float32 [48, 384, 384], P('dp')
- left_basis_new: float32 [48, 384, 384], P('dp')
- right_basis_new: float32 [48, 384, 384], P('dp')
- vec_one_new: float32 [12, 768], replicated
- vec_two_new: float32 [12, 768], replicated
- vec_new: float32 [12, 768], replicated
The draws below stay inside these ranges and needn't reach their ends.
Inputs may be any that keep to these rules, and one draw needn't show every extreme that they name: `lengths`: in each group of 2 sequences of one index of dp, one has length 2048. `owners`: at most 6 blocks share an owner, and some owner has exactly 6. `left_stats`: symmetric positive definite. `right_stats`: symmetric positive definite. `left_basis`: each block orthogonal. `right_basis`: each block orthogonal.
All inputs are finite; a program needn't handle non-finite values. No bound on the sum of `patch_mask` on one device may be relied on, other than what follows from the above.
Results may differ from the reference program's by a relative error of at most 0.014.
The reference program's roundings to bfloat16 on the way count: a program that leaves them out, or rounds other values in their place, can miss the bound.
Values may be sent and summed in bfloat16 or wider, within the bound.
No kernel may reach another device: no remote copies, remote signals or barrier semaphores. Data moves between devices by JAX's collectives and lax.ppermute only.
A program may use at most 320 MiB of HBM per device.

```python
import math
import jax
import jax.numpy as jnp
from jax import lax

D = 768
NH = 12
HD = 64
FF = 3072
BLK = 384
LEN = 2048
SEQ_GRP = 2
STEP = 10
SEQS = 16
TOK_ALL = 32768
NBLK = 48
SLOTS = 6
POS = 48
VROWS = 12
N_DP = 8


def owner_list(key):
    total_places = N_DP * SLOTS
    order_key, pick_key, shuffle_key = jax.random.split(key, 3)
    order = jax.random.permutation(order_key, total_places)
    chosen = jax.random.randint(pick_key, (), 0, N_DP)
    ranked = jnp.arange(total_places)
    scores = jnp.where(order // SLOTS == chosen, ranked - total_places, ranked)
    lined = order[jnp.argsort(scores)]
    picked = lined[:NBLK][jax.random.permutation(shuffle_key, NBLK)]
    return (picked // SLOTS).astype(jnp.int32)


def draw_owners(key, part):
    return owner_list(key)


def draw_master(key, part):
    owner_ids = owner_list(key)
    key = jax.random.fold_in(key, 12)
    block_ids = jnp.arange(NBLK)
    earlier = (owner_ids[:, None] == owner_ids[None, :]) & (block_ids[None, :] < block_ids[:, None])
    places = owner_ids * SLOTS + jnp.sum(earlier.astype(jnp.int32), axis=1)
    across = D // BLK
    end_qkv = across * 3 * across
    end_out = end_qkv + across * across
    end_up = end_out + across * (FF // BLK)
    scales = jnp.where(block_ids < end_qkv, 1.4 / math.sqrt(D), jnp.where(block_ids < end_out, 3.0 / math.sqrt(D), jnp.where(block_ids < end_up, 1.0 / math.sqrt(D), 1.0 / math.sqrt(FF))))
    spread = jnp.full((POS,), 1.0 / math.sqrt(D), jnp.float32).at[places].set(scales.astype(jnp.float32))
    return jnp.clip(jax.random.normal(key, (POS, BLK, BLK), jnp.float32) * spread[:, None, None], -1.0, 1.0)


def draw_lengths(key, part):
    key = jax.random.fold_in(key, 13)
    length_key, which_key = jax.random.split(key)
    drawn = jax.random.randint(length_key, (N_DP, SEQ_GRP), LEN // 8, LEN + 1)
    which = jax.random.randint(which_key, (N_DP, 1), 0, SEQ_GRP)
    return jnp.where(jnp.arange(SEQ_GRP)[None, :] == which, LEN, drawn).reshape(-1).astype(jnp.int32)


def statistics(diag_key, noise):
    base_level = 0.013 * BLK * TOK_ALL
    diagonal = base_level * jnp.exp(jax.random.uniform(diag_key, (POS, BLK), jnp.float32, 0.0, math.log(4.0)))
    symmetric = 0.5 * (noise + jnp.transpose(noise, (0, 2, 1)))
    identity = jnp.eye(BLK, dtype=jnp.float32)
    return symmetric * (0.25 * base_level / BLK) * (1.0 - identity) + diagonal[:, None, :] * identity


def draw_left_stats(key, part):
    key = jax.random.fold_in(key, 14)
    diag_key, noise_key = jax.random.split(key)
    noise = jax.random.uniform(noise_key, (POS, BLK, BLK), jnp.float32, -1.0, 1.0)
    return statistics(diag_key, noise)


def draw_right_stats(key, part):
    key = jax.random.fold_in(key, 15)
    diag_key, noise_key = jax.random.split(key)
    noise = jax.random.uniform(noise_key, (POS, BLK, BLK), jnp.float32, -1.0, 1.0)
    return statistics(diag_key, noise)


def orthogonal(key):
    freqs = jnp.arange(BLK, dtype=jnp.float32)
    table = math.sqrt(2.0 / BLK) * jnp.cos(math.pi * (freqs[None, :] + 0.5) * freqs[:, None] / BLK)
    table = table * jnp.where(freqs == 0.0, math.sqrt(0.5), 1.0)[:, None]
    place_keys = jax.random.split(key, POS)

    def one_place(place_key):
        row_key, col_key, sign_key = jax.random.split(place_key, 3)
        row_order = jax.random.permutation(row_key, BLK)
        col_order = jax.random.permutation(col_key, BLK)
        signs = jnp.where(jax.random.bernoulli(sign_key, 0.5, (BLK,)), 1.0, -1.0)
        return table[row_order][:, col_order] * signs[None, :]
    return jax.vmap(one_place)(place_keys)


def draw_left_basis(key, part):
    key = jax.random.fold_in(key, 16)
    return orthogonal(key)


def draw_right_basis(key, part):
    key = jax.random.fold_in(key, 17)
    return orthogonal(key)


def draw_vec_params(key, part):
    key = jax.random.fold_in(key, 18)
    raw_values = jnp.clip(jax.random.normal(key, (VROWS, D), jnp.float32), -3.0, 3.0)
    row_ids = jnp.arange(VROWS)
    gain_rows = (row_ids == 0) | (row_ids == 2)
    return jnp.where(gain_rows[:, None], 1.0 + 0.15 * raw_values, 0.2 * raw_values)


def with_ends(entries, key, low, high):
    shape = entries.shape
    index_at = [jax.random.randint(jax.random.fold_in(key, axis), (), 0, shape[axis]) for axis in range(len(shape))]
    entries = entries.at[tuple(index_at)].set(low)
    longest = shape.index(max(shape))
    index_at[longest] = (index_at[longest] + 1) % shape[longest]
    return entries.at[tuple(index_at)].set(high)


def block_levels(stream_key, extent, shards, smallest, high):
    factor_of, own = 1.0, jax.random.fold_in(stream_key, 6)
    for dim, shards_of in shards:
        draws = jnp.exp(jax.random.uniform(jax.random.fold_in(own, dim), (shards_of,), jnp.float32, smallest / len(shards), high / len(shards)))
        factor_of = factor_of * jnp.repeat(draws, extent[dim] // shards_of).reshape([-1 if axis == dim else 1 for axis in range(len(extent))])
    return factor_of


def bell_draw(key, dims, deviation, limit, cuts=(), kind=jnp.bfloat16):
    gain = block_levels(key, dims, cuts, -0.22, 0.18) if cuts else 1.0
    values = jax.random.normal(key, dims, jnp.float32) * deviation * gain
    return jnp.minimum(jnp.maximum(values, -limit), limit).astype(kind)


def setup_inputs(seed: int = 0) -> dict:
    seeds = jax.random.split(jax.random.key(seed), 16)
    return {
        "tokens": bell_draw(seeds[0], (SEQS, LEN, D), 1.0, 6.0, ((0, 8), (1, 4))),
        "cotangent": bell_draw(seeds[1], (SEQS, LEN, D), 1.0, 6.0, ((0, 8), (1, 4))),
        "lengths": draw_lengths(jax.random.fold_in(seeds[15], 71), 0),
        "patch_mask": with_ends((jax.random.randint(seeds[3], (SEQS, LEN), 0, 4) < 3).astype(jnp.int32), jax.random.fold_in(seeds[3], 1), 0, 1),
        "owners": draw_owners(jax.random.fold_in(seeds[15], 71), 0),
        "master": draw_master(jax.random.fold_in(seeds[15], 71), 0),
        "moment_one": bell_draw(seeds[6], (POS, BLK, BLK), (0.056 * TOK_ALL ** 0.5), 64.0, ((0, 8),), jnp.float32),
        "moment_two": jnp.clip(jnp.exp(math.log(32.768) - 1.3862944 * jax.random.uniform(seeds[7], (POS, BLK, BLK), jnp.float32) ** block_levels(seeds[7], (POS, BLK, BLK), ((0, 8),), -0.2, 0.2)), 8.192, 32.768),
        "left_stats": draw_left_stats(jax.random.fold_in(seeds[15], 71), 0),
        "right_stats": draw_right_stats(jax.random.fold_in(seeds[15], 71), 0),
        "left_basis": draw_left_basis(jax.random.fold_in(seeds[15], 71), 0),
        "right_basis": draw_right_basis(jax.random.fold_in(seeds[15], 71), 0),
        "vec_params": draw_vec_params(jax.random.fold_in(seeds[15], 71), 0),
        "vec_one": bell_draw(seeds[13], (VROWS, D), (0.056 * TOK_ALL ** 0.5), 64.0, (), jnp.float32),
        "vec_two": jnp.clip(jnp.exp(jax.random.uniform(seeds[14], (VROWS, D), jnp.float32, math.log(8.192), math.log(32.768))), 8.192, 32.768),
    }


@jax.custom_vjp
def low(v):
    return lax.optimization_barrier(v.astype(jnp.bfloat16)).astype(jnp.float32)

@jax.custom_vjp
def low_back(v):
    return v

def low_keep(v):
    return (low(v), None)

def low_pass(kept, grad):
    return (grad,)

def back_keep(v):
    return (v, None)

def back_low(kept, grad):
    return (low(grad),)
low.defvjp(low_keep, low_pass)
low_back.defvjp(back_keep, back_low)
PRECISE = lax.Precision.HIGHEST
NORM_EPS = 1e-06
NEG_FILL = -1000000000.0
BETA_ONE = 0.9
BETA_TWO = 0.999
BETA_STAT = 0.95
RATE_MATRIX = 0.1
RATE_VECTOR = 0.3
DECAY_RATE = 0.01
ADAM_EPS = 1e-08

def layer_norm(inputs, norm_gain, norm_shift):
    center = inputs - lax.optimization_barrier(jnp.mean(inputs, axis=-1, keepdims=True))
    spread = lax.optimization_barrier(jnp.mean(center * center, axis=-1, keepdims=True))
    return center * lax.rsqrt(spread + NORM_EPS) * norm_gain + norm_shift

def block_layout(owners, owner_count, slot_count):
    block_count = owners.shape[0]
    block_ids = jnp.arange(block_count, dtype=jnp.int32)
    earlier = (owners[:, None] == owners[None, :]) & (block_ids[None, :] < block_ids[:, None])
    slot_ids = lax.optimization_barrier(jnp.sum(earlier.astype(jnp.int32), axis=1)).astype(jnp.int32)
    places = (owners * slot_count + slot_ids).astype(jnp.int32)
    place_ids = jnp.arange(owner_count * slot_count, dtype=jnp.int32)
    matched = places[None, :] == place_ids[:, None]
    missing = 1 - jnp.any(matched, axis=1).astype(jnp.int32)
    sources = lax.optimization_barrier(jnp.sum(jnp.where(matched, block_ids[None, :], 0), axis=1)) + block_count * missing
    return (places, sources.astype(jnp.int32))

def tile_matrix(tiles, row_tiles, col_tiles):
    return tiles.reshape(row_tiles, col_tiles, BLK, BLK).transpose(0, 2, 1, 3).reshape(row_tiles * BLK, col_tiles * BLK)

def assemble(blocks):
    across = D // BLK
    wide = FF // BLK
    end_qkv = across * 3 * across
    end_out = end_qkv + across * across
    end_up = end_out + across * wide
    return (tile_matrix(blocks[:end_qkv], across, 3 * across), tile_matrix(blocks[end_qkv:end_out], across, across), tile_matrix(blocks[end_out:end_up], across, wide), tile_matrix(blocks[end_up:], wide, across))

def split_blocks(matrices):
    pieces = []
    for matrix in matrices:
        row_tiles = matrix.shape[0] // BLK
        col_tiles = matrix.shape[1] // BLK
        pieces.append(matrix.reshape(row_tiles, BLK, col_tiles, BLK).transpose(0, 2, 1, 3).reshape(row_tiles * col_tiles, BLK, BLK))
    return jnp.concatenate(pieces, axis=0)

def key_valid(lengths, patch_mask):
    positions = jnp.arange(patch_mask.shape[-1], dtype=jnp.int32)
    return (positions[None, :] < lengths[:, None]) & ((patch_mask == 1) | (positions[None, :] == 0))

def orthonormal(matrix):
    gram_matrix = jnp.matmul(matrix.T, matrix, precision=PRECISE)
    factor = jnp.linalg.cholesky(gram_matrix)
    return lax.linalg.triangular_solve(factor, matrix, left_side=False, lower=True, transpose_a=True)

def soap_update(packed):
    gradient, weight, first_mom, second_mom, left_mat, right_mat, left_rot, right_rot = packed
    rotated = jnp.matmul(jnp.matmul(left_rot.T, gradient, precision=PRECISE), right_rot, precision=PRECISE)
    first_mom = BETA_ONE * first_mom + (1.0 - BETA_ONE) * rotated
    second_mom = BETA_TWO * second_mom + (1.0 - BETA_TWO) * rotated * rotated
    scaled = first_mom / (1.0 - BETA_ONE ** STEP) / (jnp.sqrt(second_mom / (1.0 - BETA_TWO ** STEP)) + ADAM_EPS)
    back_rotated = jnp.matmul(jnp.matmul(left_rot, scaled, precision=PRECISE), right_rot.T, precision=PRECISE)
    weight = weight - RATE_MATRIX * (back_rotated + DECAY_RATE * weight)
    left_mat = BETA_STAT * left_mat + (1.0 - BETA_STAT) * jnp.matmul(gradient, gradient.T, precision=PRECISE)
    right_mat = BETA_STAT * right_mat + (1.0 - BETA_STAT) * jnp.matmul(gradient.T, gradient, precision=PRECISE)
    left_rot = orthonormal(jnp.matmul(left_mat, left_rot, precision=PRECISE))
    right_rot = orthonormal(jnp.matmul(right_mat, right_rot, precision=PRECISE))
    return (weight, first_mom, second_mom, left_mat, right_mat, left_rot, right_rot)

def adam_vectors(gradient, params, first_mom, second_mom):
    first_mom = BETA_ONE * first_mom + (1.0 - BETA_ONE) * gradient
    second_mom = BETA_TWO * second_mom + (1.0 - BETA_TWO) * gradient * gradient
    step_size = first_mom / (1.0 - BETA_ONE ** STEP) / (jnp.sqrt(second_mom / (1.0 - BETA_TWO ** STEP)) + ADAM_EPS)
    return (first_mom, second_mom, params - RATE_VECTOR * step_size)

def sequence_forward(matrices, vectors, inputs, live_keys):
    w_qkv, w_out, w_up, w_down = matrices
    normed_one = layer_norm(inputs, vectors[0], vectors[1])
    bias_qkv = jnp.concatenate([vectors[4], jnp.zeros_like(vectors[4]), vectors[5]])
    qkv_all = low_back(low(jnp.dot(low(normed_one), w_qkv, precision=PRECISE) + bias_qkv))
    heads = qkv_all.reshape(LEN, 3, NH, HD).transpose(1, 2, 0, 3)
    query, keys_all, values_all = (heads[0], heads[1], heads[2])
    block_rows = min(512, LEN)
    block_count = LEN // block_rows
    query_blocks = query.reshape(NH, block_count, block_rows, HD).transpose(1, 0, 2, 3)

    @jax.checkpoint
    def attend(query_blk):
        logits = low_back(jnp.einsum('hqd,hkd->hqk', query_blk, keys_all, precision=PRECISE) * HD ** (-0.5))
        logits = jnp.where(live_keys[None, None, :], logits, NEG_FILL)
        probs = jax.nn.softmax(logits, axis=-1)
        return jnp.einsum('hqk,hkd->hqd', low(probs), values_all, precision=PRECISE)
    attended = lax.map(attend, query_blocks)
    attn_out = low_back(low(attended.transpose(0, 2, 1, 3).reshape(LEN, D)))
    middle = inputs + low_back(jnp.dot(attn_out, w_out, precision=PRECISE) + vectors[6])
    normed_two = layer_norm(middle, vectors[2], vectors[3])
    hidden = low_back(jnp.dot(low(normed_two), w_up, precision=PRECISE) + vectors[8:].reshape(FF))
    activated = low(jax.nn.gelu(hidden, approximate=False))
    return middle + jnp.dot(activated, w_down, precision=PRECISE) + vectors[7]

def reference(tokens, cotangent, lengths, patch_mask, owners, master, moment_one, moment_two, left_stats, right_stats, left_basis, right_basis, vec_params, vec_one, vec_two):
    places, sources = block_layout(owners, N_DP, SLOTS)
    matrices = assemble(jnp.take(low(master), places, axis=0))
    live_all = key_valid(lengths, patch_mask)

    def whole_layer(mats, vectors, inputs):

        def one_step(carry, packed):
            return (carry, jax.checkpoint(sequence_forward)(mats, vectors, packed[0], packed[1]))
        _, outputs = lax.scan(one_step, jnp.zeros((), jnp.float32), (inputs, live_all))
        return outputs
    outputs, pull_back = jax.vjp(whole_layer, matrices, vec_params, tokens.astype(jnp.float32))
    d_mats, d_vectors, d_inputs = pull_back(cotangent.astype(jnp.float32))
    grad_tiles = jnp.concatenate([split_blocks(d_mats), jnp.zeros((1, BLK, BLK), jnp.float32)], axis=0)
    grad_blocks = jnp.take(grad_tiles, sources, axis=0)
    updates = lax.map(soap_update, (grad_blocks, master, moment_one, moment_two, left_stats, right_stats, left_basis, right_basis))
    vec_first, vec_second, vec_next = adam_vectors(d_vectors, vec_params, vec_one, vec_two)
    return (outputs.astype(jnp.bfloat16), d_inputs.astype(jnp.bfloat16), grad_blocks, updates[0], updates[1], updates[2], updates[3], updates[4], updates[5], updates[6], vec_first, vec_second, vec_next)
```

```python
import functools

import jax
import jax.numpy as jnp
from jax import lax
from jax.experimental import pallas as pl
from jax.experimental.pallas import tpu as pltpu
from jax.sharding import PartitionSpec as P

D = 768
FF = 3072
BLK = 384
STEP = 10

HIGHEST = lax.Precision.HIGHEST
NORM_EPS = 1e-06
NEG_FILL = -1000000000.0
BETA_ONE = 0.9
BETA_TWO = 0.999
BETA_STAT = 0.95
RATE_MATRIX = 0.1
RATE_VECTOR = 0.3
DECAY_RATE = 0.01
ADAM_EPS = 1e-08

LOW = jnp.bfloat16
F32 = jnp.float32
AXES = ("dp", "seq")
MIB = 2**20

TAIL_P = 0.24
TAIL_C = (
    0.09575380798443668,
    0.09552183543465394,
    0.09284136585084933,
    0.06338567653857548,
    0.11841694922211018,
    -0.06574016740998187,
    0.15281935057715396,
    -0.052998628523732765,
)


def dot(a, b, ca, cb, precision=None):
    return lax.dot_general(
        a, b, (((ca,), (cb,)), ((), ())), precision=precision, preferred_element_type=F32
    )


def lanes(shape):
    return lax.broadcasted_iota(jnp.int32, shape, len(shape) - 1)


def gelu_pair(x):
    u = jnp.abs(x)
    t = 1.0 / (1.0 + TAIL_P * u)
    poly = TAIL_C[-1]
    for coeff in TAIL_C[-2::-1]:
        poly = poly * t + coeff
    expo = jnp.exp(-0.5 * u * u)
    tail = poly * t * expo
    cdf = jnp.where(x < 0, tail, 1.0 - tail)
    return x * cdf, cdf + x * (expo * 0.3989422804014327)


def norm_parts(rows):
    center = rows - jnp.mean(rows, axis=-1, keepdims=True)
    rstd = lax.rsqrt(jnp.mean(center * center, axis=-1, keepdims=True) + NORM_EPS)
    return center * rstd, rstd


def norm_back(grad, hat, rstd):
    return rstd * (
        grad
        - jnp.mean(grad, axis=-1, keepdims=True)
        - hat * jnp.mean(grad * hat, axis=-1, keepdims=True)
    )


def params(limit):
    return pltpu.CompilerParams(vmem_limit_bytes=limit * MIB)


def tile_spec(block_of):
    return pl.BlockSpec(
        (1, 4, 1, BLK // 4, BLK),
        lambda i, own, slot: (own[block_of(i)], 0, slot[block_of(i)], 0, 0),
    )


def tile(ref):
    return ref[...].reshape(BLK, BLK)


def full_spec(shape):
    return pl.BlockSpec(shape, lambda i, own, slot: (0,) * len(shape))


def put_tile(ref, i, value):
    rows = BLK // 4
    low = value.astype(LOW)
    for quarter in range(4):
        ref[quarter % 2, quarter // 2, i, 0] = low[quarter * rows : quarter * rows + rows]


def qkv_kernel(own, slot, x_ref, vec_ref, bias_ref, t0, t1, qkv_ref, a_ref):
    @pl.when(pl.program_id(0) == 0)
    def _():
        hat, _ = norm_parts(x_ref[...].astype(F32))
        a_ref[...] = (hat * vec_ref[0:1, :] + vec_ref[1:2, :]).astype(LOW)

    total = dot(a_ref[:, :BLK], tile(t0), 1, 0) + dot(a_ref[:, BLK:], tile(t1), 1, 0)
    qkv_ref[...] = (total + bias_ref[...]).astype(LOW)


def qkv_forward(own, slot, x, vec, bias, gathered):
    rows = x.shape[0]
    return pl.pallas_call(
        qkv_kernel,
        grid_spec=pltpu.PrefetchScalarGridSpec(
            num_scalar_prefetch=2,
            grid=(6,),
            in_specs=[
                full_spec((rows, D)),
                full_spec(vec.shape),
                pl.BlockSpec((1, BLK), lambda i, own, slot: (0, i)),
                tile_spec(lambda i: i),
                tile_spec(lambda i: 6 + i),
            ],
            out_specs=[
                pl.BlockSpec((rows, BLK), lambda i, own, slot: (0, i)),
                full_spec((rows, D)),
            ],
        ),
        out_shape=[
            jax.ShapeDtypeStruct((rows, 3 * D), LOW),
            jax.ShapeDtypeStruct((rows, D), LOW),
        ],
        compiler_params=params(48),
        name="qkv",
    )(own, slot, x, vec, bias, gathered, gathered)


def attn_fwd_kernel(q_ref, k1, v1, k2, v2, bias_ref, o_ref, lse_ref, ka, kb, va, vb):
    rows = k1.shape[0]

    @pl.when(pl.program_id(1) == 0)
    def _():
        ln = lanes((rows, 128))
        for i, (k, v) in enumerate(((k1, v1), (k2, v2))):
            r = slice(i * rows, i * rows + rows)
            keys, values, bias = k[...], v[...], bias_ref[r, :]
            one = jnp.ones_like(values)
            ka[r, :] = jnp.where(ln == 64, bias, keys)
            kb[r, :] = jnp.where(ln == 0, bias, keys)
            va[r, :] = jnp.where(ln < 64, values, one)
            vb[r, :] = jnp.where(ln < 64, one, values)

    q = q_ref[...] * jnp.asarray(0.125, LOW)
    ln = lanes(q.shape)
    one, zero = jnp.ones_like(q), jnp.zeros_like(q)
    qa = jnp.where(ln < 64, q, jnp.where(ln == 64, one, zero))
    qb = jnp.where(ln < 64, jnp.where(ln == 0, one, zero), q)
    outs, tops = [], []
    for query, keys, values in ((qa, ka, va), (qb, kb, vb)):
        logits = dot(query, keys[...], 1, 1)
        top = jnp.max(logits, axis=1, keepdims=True)
        expo = jnp.exp(logits - top).astype(LOW)
        outs.append(dot(expo, values[...], 1, 0))
        tops.append(top)
    total = jnp.where(ln < 64, outs[1], outs[0])
    attended = jnp.where(ln < 64, outs[0], outs[1])
    o_ref[...] = (attended / pltpu.roll(total, 64, 1)).astype(LOW)
    lse_ref[...] = jnp.where(ln < 64, tops[1], tops[0]) + jnp.log(total)


def attn_forward(qkv, other, bias, q_rows=256):
    rows, pairs = qkv.shape[0], D // 128
    keys = 2 * rows
    q_spec = pl.BlockSpec((q_rows, 128), lambda p, i: (i, p))
    return pl.pallas_call(
        attn_fwd_kernel,
        grid=(pairs, rows // q_rows),
        in_specs=[
            q_spec,
            pl.BlockSpec((rows, 128), lambda p, i: (0, pairs + p)),
            pl.BlockSpec((rows, 128), lambda p, i: (0, 2 * pairs + p)),
            pl.BlockSpec((rows, 128), lambda p, i: (0, p)),
            pl.BlockSpec((rows, 128), lambda p, i: (0, pairs + p)),
            pl.BlockSpec((keys, 128), lambda p, i: (0, 0)),
        ],
        out_specs=[q_spec, q_spec],
        out_shape=[
            jax.ShapeDtypeStruct((rows, D), LOW),
            jax.ShapeDtypeStruct((rows, D), F32),
        ],
        scratch_shapes=[pltpu.VMEM((keys, 128), LOW)] * 4,
        compiler_params=params(48),
        name="attn_fwd",
    )(qkv, qkv, qkv, other, other, bias)


def three_parts(x):
    high = x.astype(LOW).astype(F32)
    rest = x - high
    mid = rest.astype(LOW).astype(F32)
    return high, mid, rest - mid


def with_spare(x, spare, value, one, first):
    ln = lanes(x.shape)
    high, mid, low = three_parts(value)
    filled = jnp.where(ln == first + 3, one, 0.0)
    for i, part in enumerate((high, mid, low)):
        filled = jnp.where(ln == first + i, part, filled)
    return jnp.where(spare, filled, x).astype(LOW)


def attn_bwd_kernel(
    q_ref, k1, v1, k2, v2, bias_ref, o_ref, lse_ref, do_ref,
    dq_ref, dk1, dv1, dk2, dv2, ka, kb, va, vb, kt, dk, dv, *, chunk,
):
    rows = k1.shape[0]

    @pl.when(pl.program_id(1) == 0)
    def _():
        ln = lanes((rows, 128))
        for i, (k, v) in enumerate(((k1, v1), (k2, v2))):
            r = slice(i * rows, i * rows + rows)
            keys, values, bias = k[...], v[...], bias_ref[r, :]
            one, zero = jnp.ones_like(values), jnp.zeros_like(values)
            ka[r, :] = jnp.where(ln < 64, keys, jnp.where(ln < 67, one, jnp.where(ln == 67, bias, zero)))
            kb[r, :] = jnp.where(ln >= 64, keys, jnp.where(ln < 3, one, jnp.where(ln == 3, bias, zero)))
            va[r, :] = jnp.where(ln < 64, values, jnp.where(ln < 67, one, zero))
            vb[r, :] = jnp.where(ln >= 64, values, jnp.where(ln < 3, one, zero))
            kt[:, r] = keys.T
        dk[...] = jnp.zeros_like(dk)
        dv[...] = jnp.zeros_like(dv)

    q = q_ref[...].astype(F32) * 0.125
    left = lanes(q.shape) < 64
    grad = do_ref[...].astype(F32)
    prod = grad * o_ref[...].astype(F32)
    sum_a = jnp.sum(jnp.where(left, prod, 0.0), axis=1, keepdims=True)
    sum_b = jnp.sum(jnp.where(left, 0.0, prod), axis=1, keepdims=True)
    delta = jnp.where(left, sum_b, sum_a)
    lse = lse_ref[...]
    zero = jnp.zeros_like(q)
    heads = (
        (
            with_spare(q, ~left, -lse, 1.0, 64), with_spare(grad, ~left, -delta, 0.0, 64), ka, va,
            jnp.where(left, q, zero).astype(LOW), jnp.where(left, grad, zero).astype(LOW),
        ),
        (
            with_spare(q, left, -lse, 1.0, 0), with_spare(grad, left, -delta, 0.0, 0), kb, vb,
            jnp.where(left, zero, q).astype(LOW), jnp.where(left, zero, grad).astype(LOW),
        ),
    )
    d_query = [jnp.zeros((64, q.shape[0]), F32)] * 2
    for c in range(2 * rows // chunk):
        r = slice(c * chunk, c * chunk + chunk)
        dv_c, dk_c = dv[r, :], dk[r, :]
        for h, (q_aug, g_aug, keys, values, q_only, g_only) in enumerate(heads):
            probs = jnp.exp(dot(keys[r, :], q_aug, 1, 1))
            d_logits = (probs * dot(values[r, :], g_aug, 1, 1)).astype(LOW)
            dv_c = dv_c + dot(probs.astype(LOW), g_only, 1, 0)
            dk_c = dk_c + dot(d_logits, q_only, 1, 0)
            d_query[h] = d_query[h] + dot(kt[64 * h : 64 * h + 64, r], d_logits, 1, 0)
        dv[r, :] = dv_c
        dk[r, :] = dk_c
    dq_ref[...] = (jnp.concatenate(d_query, axis=0) * 0.125).T.astype(LOW)

    @pl.when(pl.program_id(1) == pl.num_programs(1) - 1)
    def _():
        dk1[...] = dk[:rows, :].astype(LOW)
        dk2[...] = dk[rows:, :].astype(LOW)
        dv1[...] = dv[:rows, :].astype(LOW)
        dv2[...] = dv[rows:, :].astype(LOW)


def attn_backward(qkv, other, bias, attn, lse, d_attn, q_rows=512, chunk=1024):
    rows, pairs = qkv.shape[0], D // 128
    keys = 2 * rows
    q_spec = pl.BlockSpec((q_rows, 128), lambda p, i: (i, p))
    k_spec = pl.BlockSpec((rows, 128), lambda p, i: (0, p))
    return pl.pallas_call(
        functools.partial(attn_bwd_kernel, chunk=chunk),
        grid=(pairs, rows // q_rows),
        in_specs=[
            q_spec,
            pl.BlockSpec((rows, 128), lambda p, i: (0, pairs + p)),
            pl.BlockSpec((rows, 128), lambda p, i: (0, 2 * pairs + p)),
            k_spec,
            pl.BlockSpec((rows, 128), lambda p, i: (0, pairs + p)),
            pl.BlockSpec((keys, 128), lambda p, i: (0, 0)),
            q_spec,
            q_spec,
            q_spec,
        ],
        out_specs=[q_spec, k_spec, k_spec, k_spec, k_spec],
        out_shape=[jax.ShapeDtypeStruct((rows, D), LOW)] * 5,
        scratch_shapes=[pltpu.VMEM((keys, 128), LOW)] * 4
        + [pltpu.VMEM((128, keys), LOW)]
        + [pltpu.VMEM((keys, 128), F32)] * 2,
        compiler_params=params(56),
        name="attn_bwd",
    )(qkv, qkv, qkv, other, other, bias, attn, lse, d_attn)


def mid_kernel(
    own, slot, x_ref, attn_ref, dy_ref, vec_ref, b1_ref, o00, o01, o10, o11, u0, u1, w0, w1,
    res_ref, dmid_ref, dattn_ref, g_up, g_down, g_out, sums_ref, gb1_ref,
    mid, a2, acc, da2, *, chunk,
):
    step = pl.program_id(0)
    last = pl.num_programs(0) - 1

    @pl.when(step == 0)
    def _():
        left, right = attn_ref[:, :BLK], attn_ref[:, BLK:]
        for j, (top, bottom) in enumerate(((o00, o10), (o01, o11))):
            c = slice(j * BLK, j * BLK + BLK)
            mid[:, c] = (
                x_ref[:, c].astype(F32)
                + (dot(left, tile(top), 1, 0) + dot(right, tile(bottom), 1, 0))
                + vec_ref[6:7, c]
            )
        hat, _ = norm_parts(mid[...])
        a2[...] = (hat * vec_ref[2:3, :] + vec_ref[3:4, :]).astype(LOW)
        acc[...] = jnp.zeros_like(acc)
        da2[...] = jnp.zeros_like(da2)

    @pl.when((step > 0) & (step < last))
    def _():
        rows = a2.shape[0]
        up0, up1, down0, down1 = tile(u0), tile(u1), tile(w0), tile(w1)
        bias_grad = jnp.zeros((1, BLK), F32)
        acts, d_hids = [], []
        for c in range(rows // chunk):
            r = slice(c * chunk, c * chunk + chunk)
            hidden = dot(a2[r, :BLK], up0, 1, 0) + dot(a2[r, BLK:], up1, 1, 0) + b1_ref[...]
            act, slope = gelu_pair(hidden)
            act = act.astype(LOW)
            back = dot(dy_ref[r, :BLK], down0, 1, 1) + dot(dy_ref[r, BLK:], down1, 1, 1)
            d_hid = (back * slope).astype(LOW)
            acc[r, :BLK] += dot(act, down0, 1, 0)
            acc[r, BLK:] += dot(act, down1, 1, 0)
            da2[r, :BLK] += dot(d_hid, up0, 1, 1)
            da2[r, BLK:] += dot(d_hid, up1, 1, 1)
            bias_grad = bias_grad + jnp.sum(d_hid.astype(F32), axis=0, keepdims=True)
            acts.append(act)
            d_hids.append(d_hid)
        gb1_ref[...] = bias_grad
        act = jnp.concatenate(acts, axis=0)
        d_hid = jnp.concatenate(d_hids, axis=0)
        for j in range(2):
            c = slice(j * BLK, j * BLK + BLK)
            put_tile(g_up, j, dot(a2[:, c], d_hid, 0, 0))
            rows_q = BLK // 4
            low = dot(act, dy_ref[:, c], 0, 0).astype(LOW)
            for quarter in range(4):
                g_down[quarter % 2, quarter // 2, 0, j] = low[quarter * rows_q : quarter * rows_q + rows_q]

    @pl.when(step == last)
    def _():
        res_ref[...] = (mid[...] + acc[...] + vec_ref[7:8, :]).astype(LOW)
        hat, rstd = norm_parts(mid[...])
        grad = da2[...]
        dy = dy_ref[...].astype(F32)
        sums_ref[0:1, :] = jnp.sum(hat * grad, axis=0, keepdims=True)
        sums_ref[1:2, :] = jnp.sum(grad, axis=0, keepdims=True)
        d_mid = dy + norm_back(grad * vec_ref[2:3, :], hat, rstd)
        dmid_ref[...] = d_mid
        d_proj = d_mid.astype(LOW)
        sums_ref[2:3, :] = jnp.sum(d_proj.astype(F32), axis=0, keepdims=True)
        sums_ref[3:4, :] = jnp.sum(dy, axis=0, keepdims=True)
        sums_ref[4:8, :] = jnp.zeros((4, D), F32)
        for i, (first, second) in enumerate(((o00, o01), (o10, o11))):
            c = slice(i * BLK, i * BLK + BLK)
            dattn_ref[:, c] = (
                dot(d_proj[:, :BLK], tile(first), 1, 1) + dot(d_proj[:, BLK:], tile(second), 1, 1)
            ).astype(LOW)
            for j in range(2):
                rows_q = BLK // 4
                low = dot(attn_ref[:, c], d_proj[:, j * BLK : j * BLK + BLK], 0, 0).astype(LOW)
                for quarter in range(4):
                    g_out[quarter % 2, quarter // 2, i, j] = low[quarter * rows_q : quarter * rows_q + rows_q]


def mid_layer(own, slot, x, attn, dy, vec, b1, gathered, chunk=256):
    rows = x.shape[0]
    wide = FF // BLK
    quarter = BLK // 4

    def part(i):
        return jnp.clip(i - 1, 0, wide - 1)

    row_spec = full_spec((rows, D))
    return pl.pallas_call(
        functools.partial(mid_kernel, chunk=chunk),
        grid_spec=pltpu.PrefetchScalarGridSpec(
            num_scalar_prefetch=2,
            grid=(wide + 2,),
            in_specs=[
                row_spec,
                row_spec,
                row_spec,
                full_spec(vec.shape),
                pl.BlockSpec((1, BLK), lambda i, own, slot: (0, part(i))),
                tile_spec(lambda i: 12),
                tile_spec(lambda i: 13),
                tile_spec(lambda i: 14),
                tile_spec(lambda i: 15),
                tile_spec(lambda i: 16 + part(i)),
                tile_spec(lambda i: 24 + part(i)),
                tile_spec(lambda i: 32 + 2 * part(i)),
                tile_spec(lambda i: 33 + 2 * part(i)),
            ],
            out_specs=[
                row_spec,
                row_spec,
                row_spec,
                pl.BlockSpec((2, 2, 2, 1, quarter, BLK), lambda i, own, slot: (0, 0, 0, part(i), 0, 0)),
                pl.BlockSpec((2, 2, 1, 2, quarter, BLK), lambda i, own, slot: (0, 0, part(i), 0, 0, 0)),
                full_spec((2, 2, 2, 2, quarter, BLK)),
                full_spec((8, D)),
                pl.BlockSpec((1, BLK), lambda i, own, slot: (0, part(i))),
            ],
            scratch_shapes=[
                pltpu.VMEM((rows, D), F32),
                pltpu.VMEM((rows, D), LOW),
                pltpu.VMEM((rows, D), F32),
                pltpu.VMEM((rows, D), F32),
            ],
        ),
        out_shape=[
            jax.ShapeDtypeStruct((rows, D), LOW),
            jax.ShapeDtypeStruct((rows, D), F32),
            jax.ShapeDtypeStruct((rows, D), LOW),
            jax.ShapeDtypeStruct((2, 2, 2, wide, quarter, BLK), LOW),
            jax.ShapeDtypeStruct((2, 2, wide, 2, quarter, BLK), LOW),
            jax.ShapeDtypeStruct((2, 2, 2, 2, quarter, BLK), LOW),
            jax.ShapeDtypeStruct((8, D), F32),
            jax.ShapeDtypeStruct((1, FF), F32),
        ],
        compiler_params=params(58),
        name="mid",
    )(own, slot, x, attn, dy, vec, b1, *([gathered] * 8))


def qkv_bwd_kernel(
    own, slot, x_ref, a_ref, dmid_ref, vec_ref, dq, dk, rk, dv, rv, t0, t1,
    dx_ref, g_qkv, sums_ref, cols_ref, acc,
):
    step = pl.program_id(0)

    @pl.when(step == 0)
    def _():
        acc[...] = jnp.zeros_like(acc)

    def work(d_cols):
        acc[:, :BLK] += dot(d_cols, tile(t0), 1, 1)
        acc[:, BLK:] += dot(d_cols, tile(t1), 1, 1)
        put_tile(g_qkv, 0, dot(a_ref[:, :BLK], d_cols, 0, 0))
        put_tile(g_qkv, 1, dot(a_ref[:, BLK:], d_cols, 0, 0))
        cols_ref[...] = jnp.sum(d_cols.astype(F32), axis=0, keepdims=True)

    @pl.when(step < 2)
    def _():
        work(dq[...])

    @pl.when((step >= 2) & (step < 4))
    def _():
        work((dk[...].astype(F32) + rk[...].astype(F32)).astype(LOW))

    @pl.when(step >= 4)
    def _():
        work((dv[...].astype(F32) + rv[...].astype(F32)).astype(LOW))

    @pl.when(step == 5)
    def _():
        hat, rstd = norm_parts(x_ref[...].astype(F32))
        grad = acc[...]
        sums_ref[0:1, :] = jnp.sum(hat * grad, axis=0, keepdims=True)
        sums_ref[1:2, :] = jnp.sum(grad, axis=0, keepdims=True)
        sums_ref[2:8, :] = jnp.zeros((6, D), F32)
        dx_ref[...] = (dmid_ref[...] + norm_back(grad * vec_ref[0:1, :], hat, rstd)).astype(LOW)


def qkv_backward(own, slot, x, normed, d_mid, vec, dq, dk, rk, dv, rv, gathered):
    rows = x.shape[0]
    quarter = BLK // 4
    row_spec = full_spec((rows, D))

    def cols(first):
        return pl.BlockSpec((rows, BLK), lambda i, own, slot: (0, jnp.clip(i - first, 0, 1)))

    return pl.pallas_call(
        qkv_bwd_kernel,
        grid_spec=pltpu.PrefetchScalarGridSpec(
            num_scalar_prefetch=2,
            grid=(6,),
            in_specs=[
                row_spec, row_spec, row_spec, full_spec(vec.shape),
                cols(0), cols(2), cols(2), cols(4), cols(4),
                tile_spec(lambda i: i), tile_spec(lambda i: 6 + i),
            ],
            out_specs=[
                row_spec,
                pl.BlockSpec((2, 2, 2, 1, quarter, BLK), lambda i, own, slot: (0, 0, 0, i, 0, 0)),
                full_spec((8, D)),
                pl.BlockSpec((1, BLK), lambda i, own, slot: (0, i)),
            ],
            scratch_shapes=[pltpu.VMEM((rows, D), F32)],
        ),
        out_shape=[
            jax.ShapeDtypeStruct((rows, D), LOW),
            jax.ShapeDtypeStruct((2, 2, 2, 6, quarter, BLK), LOW),
            jax.ShapeDtypeStruct((8, D), F32),
            jax.ShapeDtypeStruct((1, 3 * D), F32),
        ],
        compiler_params=params(58),
        name="qkv_bwd",
    )(own, slot, x, normed, d_mid, vec, dq, dk, rk, dv, rv, gathered, gathered)


def eliminate(y_ref):
    count, size = y_ref.shape[0], y_ref.shape[1]
    lane = lanes((1, 8, size))
    sub = lax.broadcasted_iota(jnp.int32, (1, 8, size), 1)
    wide_lane = lanes((size, size))
    shape = (count, 8, size)

    def group(g, carry):
        base = pl.multiple_of(8 * g, 8)
        slab = y_ref[:, pl.ds(base, 8), :]
        rolled = jnp.stack([pltpu.roll(slab[b], size - base, 1) for b in range(count)], axis=0)
        columns = [jnp.broadcast_to(rolled[:, :, k : k + 1], shape) for k in range(8)]
        inside = (lane >= base) & (lane < base + 8)
        rows = jnp.where(inside, jnp.where(lane - base == sub, 1.0, 0.0), slab)
        scale = jnp.zeros(shape, F32)
        for j in range(8):
            inv_root = lax.rsqrt(jnp.broadcast_to(columns[j][:, j : j + 1, :], shape))
            scale = jnp.where(sub == j, inv_root, scale)
            factor = jnp.where(sub > j, columns[j] * (inv_root * inv_root), 0.0)
            rows = rows - factor * jnp.broadcast_to(rows[:, j : j + 1, :], shape)
            for k in range(j + 1, 8):
                columns[k] = columns[k] - factor * jnp.broadcast_to(columns[k][:, j : j + 1, :], shape)
        rows = rows * scale
        below = jnp.where(lane >= base + 8, rows, 0.0)
        passed = (wide_lane >= base) & (wide_lane < base + 8)
        for b in range(count):
            high, mid, low = three_parts(rows[b])
            b_high, b_mid, b_low = three_parts(below[b])
            first = jnp.concatenate([b_high, b_high, b_mid, b_high, b_low, b_mid], axis=0)
            second = jnp.concatenate([high, mid, high, low, high, mid], axis=0)
            update = dot(first.astype(LOW), second.astype(LOW), 0, 0)
            y_ref[b] = jnp.where(passed, 0.0, y_ref[b]) - update
            y_ref[b, pl.ds(base, 8), :] = rows[b]
        return carry

    lax.fori_loop(0, size // 8, group, 0)


def soap_kernel(
    seq_ref, g0, g1, g2, g3, w_ref, one_ref, two_ref, ls_ref, rs_ref, lb_ref, rb_ref,
    grad_ref, w_out, one_out, two_out, ls_out, rs_out, lb_out, rb_out,
    grad_s, gram, work, inv,
):
    step = pl.program_id(0)
    slots = pl.num_programs(0)
    count = lb_out.shape[0]
    quarter = BLK // 4
    for piece, flip in ((g0, 0), (g1, 2), (g2, 1), (g3, 3)):
        start = pl.multiple_of((seq_ref[0] ^ flip) * quarter, quarter)
        grad_s[pl.ds(start, quarter), :] = piece[0].astype(F32)
    grad_ref[0] = grad_s[...]
    grad = grad_s[...].astype(LOW)
    left, right = lb_ref[0], rb_ref[0]
    left_low, right_low = left.astype(LOW), right.astype(LOW)
    rotated = dot(dot(left_low, grad, 0, 0).astype(LOW), right_low, 1, 0)
    one = BETA_ONE * one_ref[0] + (1.0 - BETA_ONE) * rotated
    two = BETA_TWO * two_ref[0] + (1.0 - BETA_TWO) * rotated * rotated
    one_out[0] = one
    two_out[0] = two
    scaled = (one / (1.0 - BETA_ONE**STEP)) / (jnp.sqrt(two / (1.0 - BETA_TWO**STEP)) + ADAM_EPS)
    back = dot(dot(left_low, scaled.astype(LOW), 1, 0).astype(LOW), right_low, 1, 1)
    w_out[0] = w_ref[0] - RATE_MATRIX * (back + DECAY_RATE * w_ref[0])
    left_new = BETA_STAT * ls_ref[0] + (1.0 - BETA_STAT) * dot(grad, grad, 1, 1)
    right_new = BETA_STAT * rs_ref[0] + (1.0 - BETA_STAT) * dot(grad, grad, 0, 0)
    ls_out[0] = left_new
    rs_out[0] = right_new
    for side, (stats, basis) in enumerate(((left_new, left), (right_new, right))):
        product = dot(stats, basis, 1, 0, HIGHEST)
        at = side * count + step
        work[at] = product
        gram[at] = dot(product, product, 0, 0, HIGHEST)

    @pl.when(step == slots - 1)
    def _():
        for p in range(BLK // 128):
            c = slice(128 * p, 128 * p + 128)
            rest = slice(128 * p + 128, BLK)
            inv[...] = gram[:, c, c]
            eliminate(inv)

            def solve(b, carry, out):
                at = b + (count if out is rb_out else 0)
                factor = inv[at]
                solved = dot(work[at, :, c], factor, 1, 1, HIGHEST)
                out[b, :, c] = solved
                if p < BLK // 128 - 1:
                    upper = dot(factor, gram[at, c, rest], 1, 0, HIGHEST)
                    work[at, :, rest] = work[at, :, rest] - dot(solved, upper, 1, 0, HIGHEST)
                    gram[at, rest, rest] = gram[at, rest, rest] - dot(upper, upper, 0, 0, HIGHEST)
                return carry

            lax.fori_loop(0, count, functools.partial(solve, out=lb_out), 0)
            lax.fori_loop(0, count, functools.partial(solve, out=rb_out), 0)


def soap_update(seq_id, pieces, master, one, two, left_stats, right_stats, left_basis, right_basis):
    count = master.shape[0]
    piece_spec = pl.BlockSpec((1, BLK // 4, BLK), lambda i, s: (i, 0, 0))
    block_spec = pl.BlockSpec((1, BLK, BLK), lambda i, s: (i, 0, 0))
    whole_spec = pl.BlockSpec((count, BLK, BLK), lambda i, s: (0, 0, 0))
    shape = jax.ShapeDtypeStruct((count, BLK, BLK), F32)
    return pl.pallas_call(
        soap_kernel,
        grid_spec=pltpu.PrefetchScalarGridSpec(
            num_scalar_prefetch=1,
            grid=(count,),
            in_specs=[piece_spec] * 4 + [block_spec] * 7,
            out_specs=[block_spec] * 6 + [whole_spec] * 2,
            scratch_shapes=[
                pltpu.VMEM((BLK, BLK), F32),
                pltpu.VMEM((2 * count, BLK, BLK), F32),
                pltpu.VMEM((2 * count, BLK, BLK), F32),
                pltpu.VMEM((2 * count, 128, 128), F32),
            ],
        ),
        out_shape=[shape] * 8,
        compiler_params=params(60),
        name="soap",
    )(seq_id, *pieces, master, one, two, left_stats, right_stats, left_basis, right_basis)


def swap(x, axis, bit):
    size = lax.axis_size(axis)
    return lax.ppermute(x, axis, [(i, i ^ bit) for i in range(size)])


def add_low(a, b):
    return (a.astype(F32) + b.astype(F32)).astype(LOW)


def halve(x, dim, axis, bit, mine):
    kept = lax.dynamic_index_in_dim(x, mine, dim, keepdims=False)
    sent = lax.dynamic_index_in_dim(x, 1 - mine, dim, keepdims=False)
    return add_low(kept, swap(sent, axis, bit))


def block_places(owners, owner_count, slot_count):
    block_count = owners.shape[0]
    ids = jnp.arange(block_count, dtype=jnp.int32)
    earlier = (owners[:, None] == owners[None, :]) & (ids[None, :] < ids[:, None])
    slots = jnp.sum(earlier.astype(jnp.int32), axis=1)
    places = owners * slot_count + slots
    matched = places[None, :] == jnp.arange(owner_count * slot_count, dtype=jnp.int32)[:, None]
    missing = 1 - jnp.any(matched, axis=1).astype(jnp.int32)
    sources = jnp.sum(jnp.where(matched, ids[None, :], 0), axis=1) + block_count * missing
    return slots, sources


def adam_vectors(gradient, vec, first_mom, second_mom):
    first_mom = BETA_ONE * first_mom + (1.0 - BETA_ONE) * gradient
    second_mom = BETA_TWO * second_mom + (1.0 - BETA_TWO) * gradient * gradient
    step_size = (first_mom / (1.0 - BETA_ONE**STEP)) / (
        jnp.sqrt(second_mom / (1.0 - BETA_TWO**STEP)) + ADAM_EPS
    )
    return first_mom, second_mom, vec - RATE_VECTOR * step_size


def on_device(
    tokens, cotangent, lengths, patch_mask, owners, master, moment_one, moment_two,
    left_stats, right_stats, left_basis, right_basis, vec, vec_one, vec_two,
):
    owner_count = lax.axis_size("dp")
    slot_count = master.shape[0]
    quarter = BLK // 4
    seq_id = lax.axis_index("seq").astype(jnp.int32)
    dp_id = lax.axis_index("dp").astype(jnp.int32)
    core, chip = seq_id % 2, seq_id // 2
    part_len = tokens.shape[1]
    slots, sources = block_places(owners, owner_count, slot_count)

    mine = lax.dynamic_index_in_dim(
        master.reshape(slot_count, 4, quarter, BLK), seq_id, 1, keepdims=False
    ).astype(LOW)
    gathered = lax.all_gather(mine, AXES, axis=0, tiled=False).reshape(
        owner_count, 4, slot_count, quarter, BLK
    )

    def to_sequence(pair):
        kept = lax.dynamic_index_in_dim(pair, chip, 0, keepdims=False)
        sent = lax.dynamic_index_in_dim(pair, 1 - chip, 0, keepdims=False)
        return jnp.concatenate([kept, swap(sent, "seq", 2)], axis=0)

    def to_positions(rows):
        other = swap(rows[part_len:], "seq", 2)
        mine = rows[:part_len]
        return jnp.where(chip == 0, jnp.stack([mine, other]), jnp.stack([other, mine]))

    x = to_sequence(tokens)
    dy = to_sequence(cotangent)

    positions = jnp.arange(patch_mask.shape[-1], dtype=jnp.int32)
    live = (positions[None, :] < lengths[:, None]) & ((patch_mask == 1) | (positions[None, :] == 0))
    live = lax.dynamic_index_in_dim(live, chip, 0, keepdims=False).reshape(4, part_len)
    order = seq_id ^ jnp.array([0, 2, 1, 3], jnp.int32)
    fill = jnp.where(jnp.take(live, order, axis=0).reshape(-1), 0.0, NEG_FILL).astype(LOW)
    fill = jnp.broadcast_to(fill[:, None], (fill.shape[0], 128))

    bias = jnp.concatenate([vec[4], jnp.zeros_like(vec[4]), vec[5]])[None, :]
    qkv, normed = qkv_forward(owners, slots, x, vec, bias, gathered)
    other = swap(qkv[:, D:], "seq", 1)
    attn, lse = attn_forward(qkv, other, fill)
    b1 = vec[8:].reshape(1, FF)
    result, d_mid, d_attn, g_up, g_down, g_out, sums_two, bias_grad = mid_layer(
        owners, slots, x, attn, dy, vec, b1, gathered
    )
    output = to_positions(result)
    early = jnp.concatenate(
        [g.reshape(2, 2, -1, quarter, BLK) for g in (g_out, g_up, g_down)], axis=2
    )
    early = halve(early, 0, "seq", 1, core)
    early = halve(early, 0, "seq", 2, chip)
    dq, dk, dv, sent_k, sent_v = attn_backward_order(qkv, other, fill, attn, lse, d_attn)
    got_k, got_v = swap(sent_k, "seq", 1), swap(sent_v, "seq", 1)
    d_x, g_qkv, sums_one, cols = qkv_backward(
        owners, slots, x, normed, d_mid, vec, dq, dk, got_k, dv, got_v, gathered
    )
    d_tokens = to_positions(d_x)
    late = g_qkv.reshape(2, 2, -1, quarter, BLK)
    late = halve(late, 0, "seq", 1, core)
    late = halve(late, 0, "seq", 2, chip)

    tiles = jnp.concatenate([late, early, jnp.zeros((1, quarter, BLK), LOW)], axis=0)
    owned = jnp.take(tiles, sources, axis=0).reshape(owner_count, slot_count, quarter, BLK)
    bit = 1
    while bit < owner_count:
        rest = owned.shape[0] // 2
        owned = halve(owned.reshape((rest, 2) + owned.shape[1:]), 1, "dp", bit, (dp_id // bit) % 2)
        bit *= 2
    owned = owned[0]

    across = swap(owned, "seq", 2)
    beside = swap(jnp.stack([owned, across]), "seq", 1)
    updates = soap_update(
        seq_id.reshape(1), (owned, across, beside[0], beside[1]), master, moment_one, moment_two,
        left_stats, right_stats, left_basis, right_basis,
    )

    vec_grad = jnp.concatenate(
        [
            sums_one[0:2],
            sums_two[0:2],
            cols[:, :D],
            cols[:, 2 * D :],
            sums_two[2:4],
            bias_grad.reshape(-1, D),
        ],
        axis=0,
    )
    vec_total = lax.psum(vec_grad, AXES)
    vec_first, vec_second, vec_next = adam_vectors(vec_total, vec, vec_one, vec_two)
    grad_blocks, w_new, one_new, two_new, ls_new, rs_new, lb_new, rb_new = updates
    return (
        output, d_tokens, grad_blocks, w_new, one_new, two_new, ls_new, rs_new, lb_new, rb_new,
        vec_first, vec_second, vec_next,
    )


def attn_backward_order(qkv, other, fill, attn, lse, d_attn):
    dq, dk1, dv1, dk2, dv2 = attn_backward(qkv, other, fill, attn, lse, d_attn)
    return dq, dk1, dv1, dk2, dv2


def solution(mesh):
    rows, blocks, whole = P("dp", "seq", None), P("dp", None, None), P()
    return jax.shard_map(
        on_device,
        mesh=mesh,
        in_specs=(rows, rows, P("dp"), P("dp", None), whole) + (blocks,) * 7 + (whole,) * 3,
        out_specs=(rows, rows) + (blocks,) * 8 + (whole,) * 3,
        check_vma=False,
    )
```

```python
import functools

import jax
import jax.numpy as jnp
from jax import lax
from jax.experimental import pallas as pl
from jax.experimental.pallas import tpu as pltpu
from jax.sharding import PartitionSpec as P

D = 768
FF = 3072
BLK = 384
STEP = 10

HIGHEST = lax.Precision.HIGHEST
NORM_EPS = 1e-06
NEG_FILL = -1000000000.0
BETA_ONE = 0.9
BETA_TWO = 0.999
BETA_STAT = 0.95
RATE_MATRIX = 0.1
RATE_VECTOR = 0.3
DECAY_RATE = 0.01
ADAM_EPS = 1e-08

LOW = jnp.bfloat16
F32 = jnp.float32
AXES = ("dp", "seq")
MIB = 2**20

TAIL_P = 0.24
TAIL_C = (
    0.09575380798443668,
    0.09552183543465394,
    0.09284136585084933,
    0.06338567653857548,
    0.11841694922211018,
    -0.06574016740998187,
    0.15281935057715396,
    -0.052998628523732765,
)


def dot(a, b, ca, cb, precision=None):
    return lax.dot_general(
        a, b, (((ca,), (cb,)), ((), ())), precision=precision, preferred_element_type=F32
    )


def lanes(shape):
    return lax.broadcasted_iota(jnp.int32, shape, len(shape) - 1)


def gelu_pair(x):
    u = jnp.abs(x)
    t = 1.0 / (1.0 + TAIL_P * u)
    poly = TAIL_C[-1]
    for coeff in TAIL_C[-2::-1]:
        poly = poly * t + coeff
    expo = jnp.exp(-0.5 * u * u)
    tail = poly * t * expo
    cdf = jnp.where(x < 0, tail, 1.0 - tail)
    return x * cdf, cdf + x * (expo * 0.3989422804014327)


def norm_parts(rows):
    center = rows - jnp.mean(rows, axis=-1, keepdims=True)
    rstd = lax.rsqrt(jnp.mean(center * center, axis=-1, keepdims=True) + NORM_EPS)
    return center * rstd, rstd


def norm_back(grad, hat, rstd):
    return rstd * (
        grad
        - jnp.mean(grad, axis=-1, keepdims=True)
        - hat * jnp.mean(grad * hat, axis=-1, keepdims=True)
    )


def params(limit):
    return pltpu.CompilerParams(vmem_limit_bytes=limit * MIB)


def tile_spec(block_of):
    return pl.BlockSpec(
        (1, 4, 1, BLK // 4, BLK),
        lambda i, own, slot: (own[block_of(i)], 0, slot[block_of(i)], 0, 0),
    )


def tile(ref):
    return ref[...].reshape(BLK, BLK)


def full_spec(shape):
    return pl.BlockSpec(shape, lambda i, own, slot: (0,) * len(shape))


def put_tile(ref, i, value):
    rows = BLK // 4
    low = value.astype(LOW)
    for quarter in range(4):
        ref[quarter % 2, quarter // 2, i, 0] = low[quarter * rows : quarter * rows + rows]


def qkv_kernel(own, slot, x_ref, vec_ref, bias_ref, t0, t1, qkv_ref, a_ref):
    @pl.when(pl.program_id(0) == 0)
    def _():
        hat, _ = norm_parts(x_ref[...].astype(F32))
        a_ref[...] = (hat * vec_ref[0:1, :] + vec_ref[1:2, :]).astype(LOW)

    total = dot(a_ref[:, :BLK], tile(t0), 1, 0) + dot(a_ref[:, BLK:], tile(t1), 1, 0)
    qkv_ref[...] = (total + bias_ref[...]).astype(LOW)


def qkv_forward(own, slot, x, vec, bias, gathered):
    rows = x.shape[0]
    return pl.pallas_call(
        qkv_kernel,
        grid_spec=pltpu.PrefetchScalarGridSpec(
            num_scalar_prefetch=2,
            grid=(6,),
            in_specs=[
                full_spec((rows, D)),
                full_spec(vec.shape),
                pl.BlockSpec((1, BLK), lambda i, own, slot: (0, i)),
                tile_spec(lambda i: i),
                tile_spec(lambda i: 6 + i),
            ],
            out_specs=[
                pl.BlockSpec((rows, BLK), lambda i, own, slot: (0, i)),
                full_spec((rows, D)),
            ],
        ),
        out_shape=[
            jax.ShapeDtypeStruct((rows, 3 * D), LOW),
            jax.ShapeDtypeStruct((rows, D), LOW),
        ],
        compiler_params=params(48),
        name="qkv",
    )(own, slot, x, vec, bias, gathered, gathered)


def attn_fwd_kernel(q_ref, k1, v1, k2, v2, bias_ref, o_ref, lse_ref, ka, kb, va, vb):
    rows = k1.shape[0]

    @pl.when(pl.program_id(1) == 0)
    def _():
        ln = lanes((rows, 128))
        for i, (k, v) in enumerate(((k1, v1), (k2, v2))):
            r = slice(i * rows, i * rows + rows)
            keys, values, bias = k[...], v[...], bias_ref[r, :]
            one = jnp.ones_like(values)
            ka[r, :] = jnp.where(ln == 64, bias, keys)
            kb[r, :] = jnp.where(ln == 0, bias, keys)
            va[r, :] = jnp.where(ln < 64, values, one)
            vb[r, :] = jnp.where(ln < 64, one, values)

    q = q_ref[...] * jnp.asarray(0.125, LOW)
    ln = lanes(q.shape)
    one, zero = jnp.ones_like(q), jnp.zeros_like(q)
    qa = jnp.where(ln < 64, q, jnp.where(ln == 64, one, zero))
    qb = jnp.where(ln < 64, jnp.where(ln == 0, one, zero), q)
    outs, tops = [], []
    for query, keys, values in ((qa, ka, va), (qb, kb, vb)):
        logits = dot(query, keys[...], 1, 1)
        top = jnp.max(logits, axis=1, keepdims=True)
        expo = jnp.exp(logits - top).astype(LOW)
        outs.append(dot(expo, values[...], 1, 0))
        tops.append(top)
    total = jnp.where(ln < 64, outs[1], outs[0])
    attended = jnp.where(ln < 64, outs[0], outs[1])
    o_ref[...] = (attended / pltpu.roll(total, 64, 1)).astype(LOW)
    lse_ref[...] = jnp.where(ln < 64, tops[1], tops[0]) + jnp.log(total)


def attn_forward(qkv, other, bias, q_rows=256):
    rows, pairs = qkv.shape[0], D // 128
    keys = 2 * rows
    q_spec = pl.BlockSpec((q_rows, 128), lambda p, i: (i, p))
    return pl.pallas_call(
        attn_fwd_kernel,
        grid=(pairs, rows // q_rows),
        in_specs=[
            q_spec,
            pl.BlockSpec((rows, 128), lambda p, i: (0, pairs + p)),
            pl.BlockSpec((rows, 128), lambda p, i: (0, 2 * pairs + p)),
            pl.BlockSpec((rows, 128), lambda p, i: (0, p)),
            pl.BlockSpec((rows, 128), lambda p, i: (0, pairs + p)),
            pl.BlockSpec((keys, 128), lambda p, i: (0, 0)),
        ],
        out_specs=[q_spec, q_spec],
        out_shape=[
            jax.ShapeDtypeStruct((rows, D), LOW),
            jax.ShapeDtypeStruct((rows, D), F32),
        ],
        scratch_shapes=[pltpu.VMEM((keys, 128), LOW)] * 4,
        compiler_params=params(48),
        name="attn_fwd",
    )(qkv, qkv, qkv, other, other, bias)


def three_parts(x):
    high = x.astype(LOW).astype(F32)
    rest = x - high
    mid = rest.astype(LOW).astype(F32)
    return high, mid, rest - mid


def with_spare(x, spare, value, one, first):
    ln = lanes(x.shape)
    high, mid, low = three_parts(value)
    filled = jnp.where(ln == first + 3, one, 0.0)
    for i, part in enumerate((high, mid, low)):
        filled = jnp.where(ln == first + i, part, filled)
    return jnp.where(spare, filled, x).astype(LOW)


def attn_bwd_kernel(
    q_ref, k1, v1, k2, v2, bias_ref, o_ref, lse_ref, do_ref,
    dq_ref, dk1, dv1, dk2, dv2, ka, kb, va, vb, kt, dk, dv, *, chunk,
):
    rows = k1.shape[0]

    @pl.when(pl.program_id(1) == 0)
    def _():
        ln = lanes((rows, 128))
        for i, (k, v) in enumerate(((k1, v1), (k2, v2))):
            r = slice(i * rows, i * rows + rows)
            keys, values, bias = k[...], v[...], bias_ref[r, :]
            one, zero = jnp.ones_like(values), jnp.zeros_like(values)
            ka[r, :] = jnp.where(ln < 64, keys, jnp.where(ln < 67, one, jnp.where(ln == 67, bias, zero)))
            kb[r, :] = jnp.where(ln >= 64, keys, jnp.where(ln < 3, one, jnp.where(ln == 3, bias, zero)))
            va[r, :] = jnp.where(ln < 64, values, jnp.where(ln < 67, one, zero))
            vb[r, :] = jnp.where(ln >= 64, values, jnp.where(ln < 3, one, zero))
            kt[:, r] = keys.T
        dk[...] = jnp.zeros_like(dk)
        dv[...] = jnp.zeros_like(dv)

    q = q_ref[...].astype(F32) * 0.125
    left = lanes(q.shape) < 64
    grad = do_ref[...].astype(F32)
    prod = grad * o_ref[...].astype(F32)
    sum_a = jnp.sum(jnp.where(left, prod, 0.0), axis=1, keepdims=True)
    sum_b = jnp.sum(jnp.where(left, 0.0, prod), axis=1, keepdims=True)
    delta = jnp.where(left, sum_b, sum_a)
    lse = lse_ref[...]
    zero = jnp.zeros_like(q)
    heads = (
        (
            with_spare(q, ~left, -lse, 1.0, 64), with_spare(grad, ~left, -delta, 0.0, 64), ka, va,
            jnp.where(left, q, zero).astype(LOW), jnp.where(left, grad, zero).astype(LOW),
        ),
        (
            with_spare(q, left, -lse, 1.0, 0), with_spare(grad, left, -delta, 0.0, 0), kb, vb,
            jnp.where(left, zero, q).astype(LOW), jnp.where(left, zero, grad).astype(LOW),
        ),
    )
    d_query = [jnp.zeros((64, q.shape[0]), F32)] * 2
    for c in range(2 * rows // chunk):
        r = slice(c * chunk, c * chunk + chunk)
        dv_c, dk_c = dv[r, :], dk[r, :]
        for h, (q_aug, g_aug, keys, values, q_only, g_only) in enumerate(heads):
            probs = jnp.exp(dot(keys[r, :], q_aug, 1, 1))
            d_logits = (probs * dot(values[r, :], g_aug, 1, 1)).astype(LOW)
            dv_c = dv_c + dot(probs.astype(LOW), g_only, 1, 0)
            dk_c = dk_c + dot(d_logits, q_only, 1, 0)
            d_query[h] = d_query[h] + dot(kt[64 * h : 64 * h + 64, r], d_logits, 1, 0)
        dv[r, :] = dv_c
        dk[r, :] = dk_c
    dq_ref[...] = (jnp.concatenate(d_query, axis=0) * 0.125).T.astype(LOW)

    @pl.when(pl.program_id(1) == pl.num_programs(1) - 1)
    def _():
        dk1[...] = dk[:rows, :].astype(LOW)
        dk2[...] = dk[rows:, :].astype(LOW)
        dv1[...] = dv[:rows, :].astype(LOW)
        dv2[...] = dv[rows:, :].astype(LOW)


def attn_backward(qkv, other, bias, attn, lse, d_attn, first, place, total, before, after, q_rows=512, chunk=1024):
    rows, pairs = qkv.shape[0], D // 128
    keys = 2 * rows
    out_spec = pl.BlockSpec((q_rows, 128), lambda p, i: (i, place))
    k_out = pl.BlockSpec((rows, 128), lambda p, i: (0, place))
    anywhere = pl.BlockSpec(memory_space=pl.ANY)
    q_spec = pl.BlockSpec((q_rows, 128), lambda p, i: (i, first))
    extra = list(before) + list(after)

    def kernel(*refs):
        attn_bwd_kernel(*refs[:9], *refs[9 + len(extra) :], chunk=chunk)

    return pl.pallas_call(
        kernel,
        grid=(1, rows // q_rows),
        in_specs=[
            q_spec,
            pl.BlockSpec((rows, 128), lambda p, i: (0, pairs + first)),
            pl.BlockSpec((rows, 128), lambda p, i: (0, 2 * pairs + first)),
            pl.BlockSpec((rows, 128), lambda p, i: (0, first)),
            pl.BlockSpec((rows, 128), lambda p, i: (0, pairs + first)),
            pl.BlockSpec((keys, 128), lambda p, i: (0, 0)),
            q_spec,
            q_spec,
            q_spec,
        ]
        + [anywhere] * len(extra),
        out_specs=[out_spec, k_out, k_out, k_out, k_out],
        out_shape=[jax.ShapeDtypeStruct((rows, total * 128), LOW)] * 5,
        scratch_shapes=[pltpu.VMEM((keys, 128), LOW)] * 4
        + [pltpu.VMEM((128, keys), LOW)]
        + [pltpu.VMEM((keys, 128), F32)] * 2,
        input_output_aliases={9 + i: i for i in range(len(before))},
        compiler_params=params(56),
        name="attn_bwd",
    )(qkv, qkv, qkv, other, other, bias, attn, lse, d_attn, *extra)


def mid_kernel(
    own, slot, x_ref, attn_ref, dy_ref, vec_ref, b1_ref, o00, o01, o10, o11, u0, u1, w0, w1,
    res_ref, dmid_ref, dattn_ref, g_up, g_down, g_out, sums_ref, gb1_ref,
    mid, a2, acc, da2, *, chunk,
):
    step = pl.program_id(0)
    last = pl.num_programs(0) - 1

    @pl.when(step == 0)
    def _():
        left, right = attn_ref[:, :BLK], attn_ref[:, BLK:]
        for j, (top, bottom) in enumerate(((o00, o10), (o01, o11))):
            c = slice(j * BLK, j * BLK + BLK)
            mid[:, c] = (
                x_ref[:, c].astype(F32)
                + (dot(left, tile(top), 1, 0) + dot(right, tile(bottom), 1, 0))
                + vec_ref[6:7, c]
            )
        hat, _ = norm_parts(mid[...])
        a2[...] = (hat * vec_ref[2:3, :] + vec_ref[3:4, :]).astype(LOW)
        acc[...] = jnp.zeros_like(acc)
        da2[...] = jnp.zeros_like(da2)

    @pl.when((step > 0) & (step < last))
    def _():
        rows = a2.shape[0]
        up0, up1, down0, down1 = tile(u0), tile(u1), tile(w0), tile(w1)
        bias_grad = jnp.zeros((1, BLK), F32)
        acts, d_hids = [], []
        for c in range(rows // chunk):
            r = slice(c * chunk, c * chunk + chunk)
            hidden = dot(a2[r, :BLK], up0, 1, 0) + dot(a2[r, BLK:], up1, 1, 0) + b1_ref[...]
            act, slope = gelu_pair(hidden)
            act = act.astype(LOW)
            back = dot(dy_ref[r, :BLK], down0, 1, 1) + dot(dy_ref[r, BLK:], down1, 1, 1)
            d_hid = (back * slope).astype(LOW)
            acc[r, :BLK] += dot(act, down0, 1, 0)
            acc[r, BLK:] += dot(act, down1, 1, 0)
            da2[r, :BLK] += dot(d_hid, up0, 1, 1)
            da2[r, BLK:] += dot(d_hid, up1, 1, 1)
            bias_grad = bias_grad + jnp.sum(d_hid.astype(F32), axis=0, keepdims=True)
            acts.append(act)
            d_hids.append(d_hid)
        gb1_ref[...] = bias_grad
        act = jnp.concatenate(acts, axis=0)
        d_hid = jnp.concatenate(d_hids, axis=0)
        for j in range(2):
            c = slice(j * BLK, j * BLK + BLK)
            put_tile(g_up, j, dot(a2[:, c], d_hid, 0, 0))
            rows_q = BLK // 4
            low = dot(act, dy_ref[:, c], 0, 0).astype(LOW)
            for quarter in range(4):
                g_down[quarter % 2, quarter // 2, 0, j] = low[quarter * rows_q : quarter * rows_q + rows_q]

    @pl.when(step == last)
    def _():
        res_ref[...] = (mid[...] + acc[...] + vec_ref[7:8, :]).astype(LOW)
        hat, rstd = norm_parts(mid[...])
        grad = da2[...]
        dy = dy_ref[...].astype(F32)
        sums_ref[0:1, :] = jnp.sum(hat * grad, axis=0, keepdims=True)
        sums_ref[1:2, :] = jnp.sum(grad, axis=0, keepdims=True)
        d_mid = dy + norm_back(grad * vec_ref[2:3, :], hat, rstd)
        dmid_ref[...] = d_mid
        d_proj = d_mid.astype(LOW)
        sums_ref[2:3, :] = jnp.sum(d_proj.astype(F32), axis=0, keepdims=True)
        sums_ref[3:4, :] = jnp.sum(dy, axis=0, keepdims=True)
        sums_ref[4:8, :] = jnp.zeros((4, D), F32)
        for i, (first, second) in enumerate(((o00, o01), (o10, o11))):
            c = slice(i * BLK, i * BLK + BLK)
            dattn_ref[:, c] = (
                dot(d_proj[:, :BLK], tile(first), 1, 1) + dot(d_proj[:, BLK:], tile(second), 1, 1)
            ).astype(LOW)
            for j in range(2):
                rows_q = BLK // 4
                low = dot(attn_ref[:, c], d_proj[:, j * BLK : j * BLK + BLK], 0, 0).astype(LOW)
                for quarter in range(4):
                    g_out[quarter % 2, quarter // 2, i, j] = low[quarter * rows_q : quarter * rows_q + rows_q]


def mid_layer(own, slot, x, attn, dy, vec, b1, gathered, chunk=256):
    rows = x.shape[0]
    wide = FF // BLK
    quarter = BLK // 4

    def part(i):
        return jnp.clip(i - 1, 0, wide - 1)

    row_spec = full_spec((rows, D))
    return pl.pallas_call(
        functools.partial(mid_kernel, chunk=chunk),
        grid_spec=pltpu.PrefetchScalarGridSpec(
            num_scalar_prefetch=2,
            grid=(wide + 2,),
            in_specs=[
                row_spec,
                row_spec,
                row_spec,
                full_spec(vec.shape),
                pl.BlockSpec((1, BLK), lambda i, own, slot: (0, part(i))),
                tile_spec(lambda i: 12),
                tile_spec(lambda i: 13),
                tile_spec(lambda i: 14),
                tile_spec(lambda i: 15),
                tile_spec(lambda i: 16 + part(i)),
                tile_spec(lambda i: 24 + part(i)),
                tile_spec(lambda i: 32 + 2 * part(i)),
                tile_spec(lambda i: 33 + 2 * part(i)),
            ],
            out_specs=[
                row_spec,
                row_spec,
                row_spec,
                pl.BlockSpec((2, 2, 2, 1, quarter, BLK), lambda i, own, slot: (0, 0, 0, part(i), 0, 0)),
                pl.BlockSpec((2, 2, 1, 2, quarter, BLK), lambda i, own, slot: (0, 0, part(i), 0, 0, 0)),
                full_spec((2, 2, 2, 2, quarter, BLK)),
                full_spec((8, D)),
                pl.BlockSpec((1, BLK), lambda i, own, slot: (0, part(i))),
            ],
            scratch_shapes=[
                pltpu.VMEM((rows, D), F32),
                pltpu.VMEM((rows, D), LOW),
                pltpu.VMEM((rows, D), F32),
                pltpu.VMEM((rows, D), F32),
            ],
        ),
        out_shape=[
            jax.ShapeDtypeStruct((rows, D), LOW),
            jax.ShapeDtypeStruct((rows, D), F32),
            jax.ShapeDtypeStruct((rows, D), LOW),
            jax.ShapeDtypeStruct((2, 2, 2, wide, quarter, BLK), LOW),
            jax.ShapeDtypeStruct((2, 2, wide, 2, quarter, BLK), LOW),
            jax.ShapeDtypeStruct((2, 2, 2, 2, quarter, BLK), LOW),
            jax.ShapeDtypeStruct((8, D), F32),
            jax.ShapeDtypeStruct((1, FF), F32),
        ],
        compiler_params=params(58),
        name="mid",
    )(own, slot, x, attn, dy, vec, b1, *([gathered] * 8))


def qkv_bwd_kernel(own, slot, x_ref, a_ref, dmid_ref, vec_ref, *refs):
    grads, (t0, t1, dx_ref, g_qkv, sums_ref, cols_ref, acc) = refs[:10], refs[10:]
    step = pl.program_id(0)

    @pl.when(step == 0)
    def _():
        acc[...] = jnp.zeros_like(acc)

    def work(d_cols):
        acc[:, :BLK] += dot(d_cols, tile(t0), 1, 1)
        acc[:, BLK:] += dot(d_cols, tile(t1), 1, 1)
        put_tile(g_qkv, 0, dot(a_ref[:, :BLK], d_cols, 0, 0))
        put_tile(g_qkv, 1, dot(a_ref[:, BLK:], d_cols, 0, 0))
        cols_ref[...] = jnp.sum(d_cols.astype(F32), axis=0, keepdims=True)

    for half in range(2):
        dq, dk, rk, dv, rv = grads[5 * half : 5 * half + 5]

        @pl.when(step == half)
        def _():
            work(dq[...])

        @pl.when(step == 2 + half)
        def _():
            work((dk[...].astype(F32) + rk[...].astype(F32)).astype(LOW))

        @pl.when(step == 4 + half)
        def _():
            work((dv[...].astype(F32) + rv[...].astype(F32)).astype(LOW))

    @pl.when(step == 5)
    def _():
        hat, rstd = norm_parts(x_ref[...].astype(F32))
        grad = acc[...]
        sums_ref[0:1, :] = jnp.sum(hat * grad, axis=0, keepdims=True)
        sums_ref[1:2, :] = jnp.sum(grad, axis=0, keepdims=True)
        sums_ref[2:8, :] = jnp.zeros((6, D), F32)
        dx_ref[...] = (dmid_ref[...] + norm_back(grad * vec_ref[0:1, :], hat, rstd)).astype(LOW)


def qkv_backward(own, slot, x, normed, d_mid, vec, halves, gathered):
    rows = x.shape[0]
    quarter = BLK // 4
    row_spec = full_spec((rows, D))
    return pl.pallas_call(
        qkv_bwd_kernel,
        grid_spec=pltpu.PrefetchScalarGridSpec(
            num_scalar_prefetch=2,
            grid=(6,),
            in_specs=[row_spec, row_spec, row_spec, full_spec(vec.shape)]
            + [full_spec((rows, BLK))] * 10
            + [tile_spec(lambda i: i), tile_spec(lambda i: 6 + i)],
            out_specs=[
                row_spec,
                pl.BlockSpec((2, 2, 2, 1, quarter, BLK), lambda i, own, slot: (0, 0, 0, i, 0, 0)),
                full_spec((8, D)),
                pl.BlockSpec((1, BLK), lambda i, own, slot: (0, i)),
            ],
            scratch_shapes=[pltpu.VMEM((rows, D), F32)],
        ),
        out_shape=[
            jax.ShapeDtypeStruct((rows, D), LOW),
            jax.ShapeDtypeStruct((2, 2, 2, 6, quarter, BLK), LOW),
            jax.ShapeDtypeStruct((8, D), F32),
            jax.ShapeDtypeStruct((1, 3 * D), F32),
        ],
        compiler_params=params(60),
        name="qkv_bwd",
    )(own, slot, x, normed, d_mid, vec, *halves[0], *halves[1], gathered, gathered)


def eliminate(y_ref):
    count, size = y_ref.shape[0], y_ref.shape[1]
    lane = lanes((1, 8, size))
    sub = lax.broadcasted_iota(jnp.int32, (1, 8, size), 1)
    wide_lane = lanes((size, size))
    shape = (count, 8, size)

    def group(g, carry):
        base = pl.multiple_of(8 * g, 8)
        slab = y_ref[:, pl.ds(base, 8), :]
        rolled = jnp.stack([pltpu.roll(slab[b], size - base, 1) for b in range(count)], axis=0)
        columns = [jnp.broadcast_to(rolled[:, :, k : k + 1], shape) for k in range(8)]
        inside = (lane >= base) & (lane < base + 8)
        rows = jnp.where(inside, jnp.where(lane - base == sub, 1.0, 0.0), slab)
        scale = jnp.zeros(shape, F32)
        for j in range(8):
            inv_root = lax.rsqrt(jnp.broadcast_to(columns[j][:, j : j + 1, :], shape))
            scale = jnp.where(sub == j, inv_root, scale)
            factor = jnp.where(sub > j, columns[j] * (inv_root * inv_root), 0.0)
            rows = rows - factor * jnp.broadcast_to(rows[:, j : j + 1, :], shape)
            for k in range(j + 1, 8):
                columns[k] = columns[k] - factor * jnp.broadcast_to(columns[k][:, j : j + 1, :], shape)
        rows = rows * scale
        below = jnp.where(lane >= base + 8, rows, 0.0)
        passed = (wide_lane >= base) & (wide_lane < base + 8)
        for b in range(count):
            high, mid, low = three_parts(rows[b])
            b_high, b_mid, b_low = three_parts(below[b])
            first = jnp.concatenate([b_high, b_high, b_mid, b_high, b_low, b_mid], axis=0)
            second = jnp.concatenate([high, mid, high, low, high, mid], axis=0)
            update = dot(first.astype(LOW), second.astype(LOW), 0, 0)
            y_ref[b] = jnp.where(passed, 0.0, y_ref[b]) - update
            y_ref[b, pl.ds(base, 8), :] = rows[b]
        return carry

    lax.fori_loop(0, size // 8, group, 0)


def soap_kernel(
    seq_ref, g0, g1, g2, g3, w_ref, one_ref, two_ref, ls_ref, rs_ref, lb_ref, rb_ref,
    *refs,
):
    (
        grad_ref, w_out, one_out, two_out, ls_out, rs_out, lb_out, rb_out,
        grad_s, gram, work, inv,
    ) = refs[-12:]
    step = pl.program_id(0)
    slots = pl.num_programs(0)
    count = lb_out.shape[0]
    quarter = BLK // 4
    for piece, flip in ((g0, 0), (g1, 2), (g2, 1), (g3, 3)):
        start = pl.multiple_of((seq_ref[0] ^ flip) * quarter, quarter)
        grad_s[pl.ds(start, quarter), :] = piece[0].astype(F32)
    grad_ref[0] = grad_s[...]
    grad = grad_s[...].astype(LOW)
    left, right = lb_ref[0], rb_ref[0]
    left_low, right_low = left.astype(LOW), right.astype(LOW)
    rotated = dot(dot(left_low, grad, 0, 0).astype(LOW), right_low, 1, 0)
    one = BETA_ONE * one_ref[0] + (1.0 - BETA_ONE) * rotated
    two = BETA_TWO * two_ref[0] + (1.0 - BETA_TWO) * rotated * rotated
    one_out[0] = one
    two_out[0] = two
    scaled = (one / (1.0 - BETA_ONE**STEP)) / (jnp.sqrt(two / (1.0 - BETA_TWO**STEP)) + ADAM_EPS)
    back = dot(dot(left_low, scaled.astype(LOW), 1, 0).astype(LOW), right_low, 1, 1)
    w_out[0] = w_ref[0] - RATE_MATRIX * (back + DECAY_RATE * w_ref[0])
    left_new = BETA_STAT * ls_ref[0] + (1.0 - BETA_STAT) * dot(grad, grad, 1, 1)
    right_new = BETA_STAT * rs_ref[0] + (1.0 - BETA_STAT) * dot(grad, grad, 0, 0)
    ls_out[0] = left_new
    rs_out[0] = right_new
    for side, (stats, basis) in enumerate(((left_new, left), (right_new, right))):
        product = dot(stats, basis, 1, 0, HIGHEST)
        at = side * count + step
        work[at] = product
        gram[at] = dot(product, product, 0, 0, HIGHEST)

    @pl.when(step == slots - 1)
    def _():
        for p in range(BLK // 128):
            c = slice(128 * p, 128 * p + 128)
            rest = slice(128 * p + 128, BLK)
            inv[...] = gram[:, c, c]
            eliminate(inv)

            def solve(b, carry, out):
                at = b + (count if out is rb_out else 0)
                factor = inv[at]
                solved = dot(work[at, :, c], factor, 1, 1, HIGHEST)
                out[b, :, c] = solved
                if p < BLK // 128 - 1:
                    upper = dot(factor, gram[at, c, rest], 1, 0, HIGHEST)
                    work[at, :, rest] = work[at, :, rest] - dot(solved, upper, 1, 0, HIGHEST)
                    gram[at, rest, rest] = gram[at, rest, rest] - dot(upper, upper, 0, 0, HIGHEST)
                return carry

            lax.fori_loop(0, count, functools.partial(solve, out=lb_out), 0)
            lax.fori_loop(0, count, functools.partial(solve, out=rb_out), 0)


def soap_update(seq_id, pieces, state, first, count, before):
    slots = state[0].shape[0]
    piece_spec = pl.BlockSpec((1, BLK // 4, BLK), lambda i, s: (i, 0, 0))
    block_spec = pl.BlockSpec((1, BLK, BLK), lambda i, s: (first + i, 0, 0))
    whole_spec = pl.BlockSpec((count, BLK, BLK), lambda i, s: (first // count, 0, 0))
    shape = jax.ShapeDtypeStruct((slots, BLK, BLK), F32)
    return pl.pallas_call(
        soap_kernel,
        grid_spec=pltpu.PrefetchScalarGridSpec(
            num_scalar_prefetch=1,
            grid=(count,),
            in_specs=[piece_spec] * 4
            + [block_spec] * 7
            + [pl.BlockSpec(memory_space=pl.ANY)] * len(before),
            out_specs=[block_spec] * 6 + [whole_spec] * 2,
            scratch_shapes=[
                pltpu.VMEM((BLK, BLK), F32),
                pltpu.VMEM((2 * count, BLK, BLK), F32),
                pltpu.VMEM((2 * count, BLK, BLK), F32),
                pltpu.VMEM((2 * count, 128, 128), F32),
            ],
        ),
        out_shape=[shape] * 8,
        input_output_aliases={12 + i: i for i in range(len(before))},
        compiler_params=params(60),
        name="soap",
    )(seq_id, *pieces, *state, *before)


def swap(x, axis, bit):
    size = lax.axis_size(axis)
    return lax.ppermute(x, axis, [(i, i ^ bit) for i in range(size)])


def add_low(a, b):
    return (a.astype(F32) + b.astype(F32)).astype(LOW)


def halve(x, dim, axis, bit, mine):
    kept = lax.dynamic_index_in_dim(x, mine, dim, keepdims=False)
    sent = lax.dynamic_index_in_dim(x, 1 - mine, dim, keepdims=False)
    return add_low(kept, swap(sent, axis, bit))


def quarters(piece):
    across = swap(piece, "seq", 2)
    beside = swap(jnp.stack([piece, across]), "seq", 1)
    return piece, across, beside[0], beside[1]


def block_places(owners, owner_count, slot_count):
    block_count = owners.shape[0]
    ids = jnp.arange(block_count, dtype=jnp.int32)
    earlier = (owners[:, None] == owners[None, :]) & (ids[None, :] < ids[:, None])
    slots = jnp.sum(earlier.astype(jnp.int32), axis=1)
    places = owners * slot_count + slots
    matched = places[None, :] == jnp.arange(owner_count * slot_count, dtype=jnp.int32)[:, None]
    missing = 1 - jnp.any(matched, axis=1).astype(jnp.int32)
    sources = jnp.sum(jnp.where(matched, ids[None, :], 0), axis=1) + block_count * missing
    return slots, sources


def adam_vectors(gradient, vec, first_mom, second_mom):
    first_mom = BETA_ONE * first_mom + (1.0 - BETA_ONE) * gradient
    second_mom = BETA_TWO * second_mom + (1.0 - BETA_TWO) * gradient * gradient
    step_size = (first_mom / (1.0 - BETA_ONE**STEP)) / (
        jnp.sqrt(second_mom / (1.0 - BETA_TWO**STEP)) + ADAM_EPS
    )
    return first_mom, second_mom, vec - RATE_VECTOR * step_size


def on_device(
    tokens, cotangent, lengths, patch_mask, owners, master, moment_one, moment_two,
    left_stats, right_stats, left_basis, right_basis, vec, vec_one, vec_two,
):
    owner_count = lax.axis_size("dp")
    slot_count = master.shape[0]
    quarter = BLK // 4
    seq_id = lax.axis_index("seq").astype(jnp.int32)
    dp_id = lax.axis_index("dp").astype(jnp.int32)
    core, chip = seq_id % 2, seq_id // 2
    part_len = tokens.shape[1]
    slots, sources = block_places(owners, owner_count, slot_count)
    first_blocks = 3 * (D // BLK) ** 2

    mine = lax.dynamic_index_in_dim(
        master.reshape(slot_count, 4, quarter, BLK), seq_id, 1, keepdims=False
    ).astype(LOW)
    gathered = lax.all_gather(mine, AXES, axis=0, tiled=False).reshape(
        owner_count, 4, slot_count, quarter, BLK
    )

    def to_sequence(pair):
        kept = lax.dynamic_index_in_dim(pair, chip, 0, keepdims=False)
        sent = lax.dynamic_index_in_dim(pair, 1 - chip, 0, keepdims=False)
        return jnp.concatenate([kept, swap(sent, "seq", 2)], axis=0)

    def to_positions(rows):
        other = swap(rows[part_len:], "seq", 2)
        mine = rows[:part_len]
        return jnp.where(chip == 0, jnp.stack([mine, other]), jnp.stack([other, mine]))

    x = to_sequence(tokens)
    dy = to_sequence(cotangent)

    positions = jnp.arange(patch_mask.shape[-1], dtype=jnp.int32)
    live = (positions[None, :] < lengths[:, None]) & ((patch_mask == 1) | (positions[None, :] == 0))
    live = lax.dynamic_index_in_dim(live, chip, 0, keepdims=False).reshape(4, part_len)
    order = seq_id ^ jnp.array([0, 2, 1, 3], jnp.int32)
    fill = jnp.where(jnp.take(live, order, axis=0).reshape(-1), 0.0, NEG_FILL).astype(LOW)
    fill = jnp.broadcast_to(fill[:, None], (fill.shape[0], 128))

    bias = jnp.concatenate([vec[4], jnp.zeros_like(vec[4]), vec[5]])[None, :]
    qkv, normed = qkv_forward(owners, slots, x, vec, bias, gathered)
    other = swap(qkv[:, D:], "seq", 1)
    attn, lse = attn_forward(qkv, other, fill)
    b1 = vec[8:].reshape(1, FF)
    result, d_mid, d_attn, g_up, g_down, g_out, sums_two, bias_grad = mid_layer(
        owners, slots, x, attn, dy, vec, b1, gathered
    )
    output = to_positions(result)
    early = jnp.concatenate(
        [g.reshape(2, 2, -1, quarter, BLK) for g in (g_out, g_up, g_down)], axis=2
    )
    early = halve(early, 0, "seq", 1, core)

    bits = owner_count.bit_length() - 1
    dims = ["x"] + list(range(bits))[::-1]
    if slot_count % 3 == 0 and bits == 3:
        plans = [["x", 0, 1, 2], [0, 1, "x", 2], [1, "x", 0, 2]]
    else:
        plans = [["x"] + list(range(bits))]
    per = slot_count // len(plans)
    early = jnp.concatenate([early, jnp.zeros((2, 1, quarter, BLK), LOW)], axis=1)
    early_at = jnp.where(sources >= first_blocks, sources - first_blocks, sources.shape[0])
    early_at = jnp.minimum(early_at, early.shape[1] - 1).reshape(owner_count, slot_count)
    groups = [
        jnp.take(early, early_at[:, per * g : per * g + per].reshape(-1), axis=1).reshape(
            (2,) * len(dims) + (per, quarter, BLK)
        )
        for g in range(len(plans))
    ]
    left = [list(dims) for _ in plans]

    def advance(step):
        for g, plan in enumerate(plans):
            name = plan[step]
            at = left[g].index(name)
            left[g].pop(at)
            if name == "x":
                groups[g] = halve(groups[g], at, "seq", 2, chip)
            else:
                groups[g] = halve(groups[g], at, "dp", 2**name, (dp_id // 2**name) % 2)

    halves = []
    pairs = D // 128 // 2
    call = taken = 0
    for half in range(2):
        before = []
        for place in range(pairs):
            after = list(groups) if call else []
            if call > 1 and taken < len(dims) - 1:
                advance(taken)
                taken += 1
                after = list(groups)
            before = attn_backward(
                qkv, other, fill, attn, lse, d_attn, pairs * half + place, place, pairs, before, after
            )
            call += 1
        dq, dk, dv, sent_k, sent_v = before
        halves.append((dq, dk, swap(sent_k, "seq", 1), dv, swap(sent_v, "seq", 1)))
    for step in range(taken, len(dims)):
        advance(step)
    early = jnp.concatenate(groups, axis=0)
    early_pieces = quarters(early)

    d_x, g_qkv, sums_one, cols = qkv_backward(owners, slots, x, normed, d_mid, vec, halves, gathered)
    d_tokens = to_positions(d_x)
    late = g_qkv.reshape(2, 2, -1, quarter, BLK)
    late = halve(late, 0, "seq", 1, core)
    late = halve(late, 0, "seq", 2, chip)
    late = jnp.concatenate([late, jnp.zeros((1, quarter, BLK), LOW)], axis=0)
    late_at = jnp.minimum(sources, first_blocks).reshape(owner_count, slot_count)
    state = (master, moment_one, moment_two, left_stats, right_stats, left_basis, right_basis)

    def finish(count, late, early_pieces, state):
        sent = jnp.take(late, late_at[:, :count].reshape(-1), axis=0)
        got = lax.all_to_all(
            sent.reshape(owner_count, count, quarter, BLK), "dp", split_axis=0, concat_axis=0, tiled=True
        )
        total = jnp.sum(got.astype(F32), axis=0) + early_pieces[0][:count].astype(F32)
        pieces = quarters(total.astype(LOW))
        done = []
        if count < slot_count:
            rest = [piece[count:] for piece in early_pieces]
            done = soap_update(seq_id.reshape(1), rest, state, count, slot_count - count, done)
        return soap_update(seq_id.reshape(1), pieces, state, 0, count, done)

    counts = [3, 4, 6] if slot_count == 6 else [slot_count]
    most = jnp.max(jnp.sum((owners[:first_blocks, None] == jnp.arange(owner_count)[None, :]).astype(jnp.int32), axis=0))
    if len(counts) == 1:
        updates = finish(counts[0], late, early_pieces, state)
    else:
        which = sum((most > count).astype(jnp.int32) for count in counts[:-1])
        updates = lax.switch(which, [functools.partial(finish, count) for count in counts], late, early_pieces, state)

    vec_grad = jnp.concatenate(
        [
            sums_one[0:2],
            sums_two[0:2],
            cols[:, :D],
            cols[:, 2 * D :],
            sums_two[2:4],
            bias_grad.reshape(-1, D),
        ],
        axis=0,
    )
    vec_total = jnp.sum(lax.all_gather(vec_grad, AXES, axis=0, tiled=False), axis=0)
    vec_first, vec_second, vec_next = adam_vectors(vec_total, vec, vec_one, vec_two)
    grad_blocks, w_new, one_new, two_new, ls_new, rs_new, lb_new, rb_new = updates
    return (
        output, d_tokens, grad_blocks, w_new, one_new, two_new, ls_new, rs_new, lb_new, rb_new,
        vec_first, vec_second, vec_next,
    )


def solution(mesh):
    rows, blocks, whole = P("dp", "seq", None), P("dp", None, None), P()
    return jax.shard_map(
        on_device,
        mesh=mesh,
        in_specs=(rows, rows, P("dp"), P("dp", None), whole) + (blocks,) * 7 + (whole,) * 3,
        out_specs=(rows, rows) + (blocks,) * 8 + (whole,) * 3,
        check_vma=False,
    )
```

```python
import functools

import jax
import jax.numpy as jnp
from jax import lax
from jax.experimental import pallas as pl
from jax.experimental.pallas import tpu as pltpu
from jax.sharding import PartitionSpec as P

D = 768
FF = 3072
BLK = 384
STEP = 10

HIGHEST = lax.Precision.HIGHEST
NORM_EPS = 1e-06
NEG_FILL = -1000000000.0
BETA_ONE = 0.9
BETA_TWO = 0.999
BETA_STAT = 0.95
RATE_MATRIX = 0.1
RATE_VECTOR = 0.3
DECAY_RATE = 0.01
ADAM_EPS = 1e-08

LOW = jnp.bfloat16
F32 = jnp.float32
AXES = ("dp", "seq")
MIB = 2**20

TAIL_P = 0.24
TAIL_C = (
    0.09575380798443668,
    0.09552183543465394,
    0.09284136585084933,
    0.06338567653857548,
    0.11841694922211018,
    -0.06574016740998187,
    0.15281935057715396,
    -0.052998628523732765,
)


def dot(a, b, ca, cb, precision=None):
    return lax.dot_general(
        a, b, (((ca,), (cb,)), ((), ())), precision=precision, preferred_element_type=F32
    )


def lanes(shape):
    return lax.broadcasted_iota(jnp.int32, shape, len(shape) - 1)


def gelu_pair(x):
    u = jnp.abs(x)
    t = 1.0 / (1.0 + TAIL_P * u)
    poly = TAIL_C[-1]
    for coeff in TAIL_C[-2::-1]:
        poly = poly * t + coeff
    expo = jnp.exp(-0.5 * u * u)
    tail = poly * t * expo
    cdf = jnp.where(x < 0, tail, 1.0 - tail)
    return x * cdf, cdf + x * (expo * 0.3989422804014327)


def norm_parts(rows):
    center = rows - jnp.mean(rows, axis=-1, keepdims=True)
    rstd = lax.rsqrt(jnp.mean(center * center, axis=-1, keepdims=True) + NORM_EPS)
    return center * rstd, rstd


def norm_back(grad, hat, rstd):
    return rstd * (
        grad
        - jnp.mean(grad, axis=-1, keepdims=True)
        - hat * jnp.mean(grad * hat, axis=-1, keepdims=True)
    )


def params(limit):
    return pltpu.CompilerParams(vmem_limit_bytes=limit * MIB)


def tile_spec(block_of):
    return pl.BlockSpec(
        (1, 4, 1, BLK // 4, BLK),
        lambda i, own, slot: (own[block_of(i)], 0, slot[block_of(i)], 0, 0),
    )


def tile(ref):
    return ref[...].reshape(BLK, BLK)


def full_spec(shape):
    return pl.BlockSpec(shape, lambda i, own, slot: (0,) * len(shape))


def quarter_at(seq, rel_core, rel_x):
    return seq ^ (2 * rel_x + rel_core)


def qkv_kernel(own, slot, x_ref, vec_ref, bias_ref, t0, t1, q_ref, kv_ref, a_ref):
    @pl.when(pl.program_id(0) == 0)
    def _():
        hat, _ = norm_parts(x_ref[...].astype(F32))
        a_ref[...] = (hat * vec_ref[0:1, :] + vec_ref[1:2, :]).astype(LOW)

    total = dot(a_ref[:, :BLK], tile(t0), 1, 0) + dot(a_ref[:, BLK:], tile(t1), 1, 0)
    low = (total + bias_ref[...]).astype(LOW)

    @pl.when(pl.program_id(0) < 2)
    def _():
        q_ref[...] = low

    @pl.when(pl.program_id(0) >= 2)
    def _():
        kv_ref[...] = low


def qkv_forward(own, slot, x, vec, bias, gathered):
    rows = x.shape[0]
    return pl.pallas_call(
        qkv_kernel,
        grid_spec=pltpu.PrefetchScalarGridSpec(
            num_scalar_prefetch=2,
            grid=(6,),
            in_specs=[
                full_spec((rows, D)),
                full_spec(vec.shape),
                pl.BlockSpec((1, BLK), lambda i, own, slot: (0, i)),
                tile_spec(lambda i: i),
                tile_spec(lambda i: 6 + i),
            ],
            out_specs=[
                pl.BlockSpec((rows, BLK), lambda i, own, slot: (0, jnp.minimum(i, 1))),
                pl.BlockSpec((rows, BLK), lambda i, own, slot: (0, jnp.maximum(i - 2, 0))),
                full_spec((rows, D)),
            ],
        ),
        out_shape=[
            jax.ShapeDtypeStruct((rows, D), LOW),
            jax.ShapeDtypeStruct((rows, 2 * D), LOW),
            jax.ShapeDtypeStruct((rows, D), LOW),
        ],
        compiler_params=params(48),
        name="qkv",
    )(own, slot, x, vec, bias, gathered, gathered)


def attn_fwd_kernel(q_ref, k1, v1, k2, v2, bias_ref, o_ref, lse_ref, ka, kb, va, vb):
    rows = k1.shape[0]

    @pl.when(pl.program_id(1) == 0)
    def _():
        ln = lanes((rows, 128))
        for i, (k, v) in enumerate(((k1, v1), (k2, v2))):
            r = slice(i * rows, i * rows + rows)
            keys, values, bias = k[...], v[...], bias_ref[r, :]
            one = jnp.ones_like(values)
            ka[r, :] = jnp.where(ln == 64, bias, keys)
            kb[r, :] = jnp.where(ln == 0, bias, keys)
            va[r, :] = jnp.where(ln < 64, values, one)
            vb[r, :] = jnp.where(ln < 64, one, values)

    q = q_ref[...] * jnp.asarray(0.125, LOW)
    ln = lanes(q.shape)
    one, zero = jnp.ones_like(q), jnp.zeros_like(q)
    qa = jnp.where(ln < 64, q, jnp.where(ln == 64, one, zero))
    qb = jnp.where(ln < 64, jnp.where(ln == 0, one, zero), q)
    outs, tops = [], []
    for query, keys, values in ((qa, ka, va), (qb, kb, vb)):
        logits = dot(query, keys[...], 1, 1)
        top = jnp.max(logits, axis=1, keepdims=True)
        expo = jnp.exp(logits - top).astype(LOW)
        outs.append(dot(expo, values[...], 1, 0))
        tops.append(top)
    total = jnp.where(ln < 64, outs[1], outs[0])
    attended = jnp.where(ln < 64, outs[0], outs[1])
    o_ref[...] = (attended / pltpu.roll(total, 64, 1)).astype(LOW)
    lse_ref[...] = jnp.where(ln < 64, tops[1], tops[0]) + jnp.log(total)


def attn_forward(q, kv, other, bias, q_rows=256):
    rows, pairs = q.shape[0], D // 128
    keys = 2 * rows
    q_spec = pl.BlockSpec((q_rows, 128), lambda p, i: (i, p))
    return pl.pallas_call(
        attn_fwd_kernel,
        grid=(pairs, rows // q_rows),
        in_specs=[
            q_spec,
            pl.BlockSpec((rows, 128), lambda p, i: (0, p)),
            pl.BlockSpec((rows, 128), lambda p, i: (0, pairs + p)),
            pl.BlockSpec((rows, 128), lambda p, i: (0, p)),
            pl.BlockSpec((rows, 128), lambda p, i: (0, pairs + p)),
            pl.BlockSpec((keys, 128), lambda p, i: (0, 0)),
        ],
        out_specs=[q_spec, q_spec],
        out_shape=[
            jax.ShapeDtypeStruct((rows, D), LOW),
            jax.ShapeDtypeStruct((rows, D), F32),
        ],
        scratch_shapes=[pltpu.VMEM((keys, 128), LOW)] * 4,
        compiler_params=params(48),
        name="attn_fwd",
    )(q, kv, kv, other, other, bias)


def three_parts(x):
    high = x.astype(LOW).astype(F32)
    rest = x - high
    mid = rest.astype(LOW).astype(F32)
    return high, mid, rest - mid


def with_spare(x, spare, value, one, first):
    ln = lanes(x.shape)
    high, mid, low = three_parts(value)
    filled = jnp.where(ln == first + 3, one, 0.0)
    for i, part in enumerate((high, mid, low)):
        filled = jnp.where(ln == first + i, part, filled)
    return jnp.where(spare, filled, x).astype(LOW)


def attn_bwd_kernel(
    q_ref, k1, v1, k2, v2, bias_ref, o_ref, lse_ref, do_ref,
    dq_ref, dk1, dv1, dk2, dv2, ka, kb, va, vb, kt, dk, dv, *, chunk,
):
    rows = k1.shape[0]

    @pl.when(pl.program_id(1) == 0)
    def _():
        ln = lanes((rows, 128))
        for i, (k, v) in enumerate(((k1, v1), (k2, v2))):
            r = slice(i * rows, i * rows + rows)
            keys, values, bias = k[...], v[...], bias_ref[r, :]
            one, zero = jnp.ones_like(values), jnp.zeros_like(values)
            ka[r, :] = jnp.where(ln < 64, keys, jnp.where(ln < 67, one, jnp.where(ln == 67, bias, zero)))
            kb[r, :] = jnp.where(ln >= 64, keys, jnp.where(ln < 3, one, jnp.where(ln == 3, bias, zero)))
            va[r, :] = jnp.where(ln < 64, values, jnp.where(ln < 67, one, zero))
            vb[r, :] = jnp.where(ln >= 64, values, jnp.where(ln < 3, one, zero))
            kt[:, r] = keys.T
        dk[...] = jnp.zeros_like(dk)
        dv[...] = jnp.zeros_like(dv)

    q = q_ref[...].astype(F32) * 0.125
    left = lanes(q.shape) < 64
    grad = do_ref[...].astype(F32)
    prod = grad * o_ref[...].astype(F32)
    sum_a = jnp.sum(jnp.where(left, prod, 0.0), axis=1, keepdims=True)
    sum_b = jnp.sum(jnp.where(left, 0.0, prod), axis=1, keepdims=True)
    delta = jnp.where(left, sum_b, sum_a)
    lse = lse_ref[...]
    zero = jnp.zeros_like(q)
    heads = (
        (
            with_spare(q, ~left, -lse, 1.0, 64), with_spare(grad, ~left, -delta, 0.0, 64), ka, va,
            jnp.where(left, q, zero).astype(LOW), jnp.where(left, grad, zero).astype(LOW),
        ),
        (
            with_spare(q, left, -lse, 1.0, 0), with_spare(grad, left, -delta, 0.0, 0), kb, vb,
            jnp.where(left, zero, q).astype(LOW), jnp.where(left, zero, grad).astype(LOW),
        ),
    )
    d_query = [jnp.zeros((64, q.shape[0]), F32)] * 2
    for c in range(2 * rows // chunk):
        r = slice(c * chunk, c * chunk + chunk)
        dv_c, dk_c = dv[r, :], dk[r, :]
        for h, (q_aug, g_aug, keys, values, q_only, g_only) in enumerate(heads):
            probs = jnp.exp(dot(keys[r, :], q_aug, 1, 1))
            d_logits = (probs * dot(values[r, :], g_aug, 1, 1)).astype(LOW)
            dv_c = dv_c + dot(probs.astype(LOW), g_only, 1, 0)
            dk_c = dk_c + dot(d_logits, q_only, 1, 0)
            d_query[h] = d_query[h] + dot(kt[64 * h : 64 * h + 64, r], d_logits, 1, 0)
        dv[r, :] = dv_c
        dk[r, :] = dk_c
    dq_ref[...] = (jnp.concatenate(d_query, axis=0) * 0.125).T.astype(LOW)

    @pl.when(pl.program_id(1) == pl.num_programs(1) - 1)
    def _():
        dk1[...] = dk[:rows, :].astype(LOW)
        dk2[...] = dk[rows:, :].astype(LOW)
        dv1[...] = dv[:rows, :].astype(LOW)
        dv2[...] = dv[rows:, :].astype(LOW)


def attn_backward(q, kv, other, bias, attn, lse, d_attn, first, count, place, total, before, q_rows=512, chunk=1024):
    rows, pairs = q.shape[0], D // 128
    keys = 2 * rows
    out_spec = pl.BlockSpec((q_rows, 128), lambda p, i: (i, place + p))
    k_out = pl.BlockSpec((rows, 128), lambda p, i: (0, place + p))
    q_spec = pl.BlockSpec((q_rows, 128), lambda p, i: (i, first + p))
    k_spec = pl.BlockSpec((rows, 128), lambda p, i: (0, first + p))
    v_spec = pl.BlockSpec((rows, 128), lambda p, i: (0, pairs + first + p))

    def kernel(*refs):
        attn_bwd_kernel(*refs[:9], *refs[9 + len(before) :], chunk=chunk)

    return pl.pallas_call(
        kernel,
        grid=(count, rows // q_rows),
        in_specs=[
            q_spec, k_spec, v_spec, k_spec, v_spec, pl.BlockSpec((keys, 128), lambda p, i: (0, 0)),
            q_spec, q_spec, q_spec,
        ]
        + [pl.BlockSpec(memory_space=pl.ANY)] * len(before),
        out_specs=[out_spec, k_out, k_out, k_out, k_out],
        out_shape=[jax.ShapeDtypeStruct((rows, total * 128), LOW)] * 5,
        scratch_shapes=[pltpu.VMEM((keys, 128), LOW)] * 4
        + [pltpu.VMEM((128, keys), LOW)]
        + [pltpu.VMEM((keys, 128), F32)] * 2,
        input_output_aliases={9 + i: i for i in range(len(before))},
        compiler_params=params(56),
        name="attn_bwd",
    )(q, kv, kv, other, other, bias, attn, lse, d_attn, *before)


def mid_kernel(
    own, slot, rel, seq, x_ref, attn_ref, dy_ref, vec_ref, b1_ref, o00, o01, o10, o11, u0, u1, w0, w1,
    res_ref, dmid_ref, dattn_ref, keep, send, sums_ref, gb1_ref,
    mid, a2, acc, da2, stage, sems, *, chunk,
):
    step = pl.program_id(0)
    last = pl.num_programs(0) - 1
    quarter = BLK // 4

    def copies(buf, i, block):
        found = []
        for rel_core, out in enumerate((keep, send)):
            for rel_x in range(2):
                found.append(
                    pltpu.make_async_copy(
                        stage.at[buf, i, quarter_at(seq[0], rel_core, rel_x)],
                        out.at[rel_x, rel[block], slot[block]],
                        sems.at[buf, i, 2 * rel_core + rel_x],
                    )
                )
        return found

    def put(buf, i, block, value):
        low = value.astype(LOW)
        for part in range(4):
            stage[buf, i, part] = low[part * quarter : part * quarter + quarter]
        for copy in copies(buf, i, block):
            copy.start()

    def settle(buf):
        for i in range(4):
            for copy in copies(buf, i, 0):
                copy.wait()

    @pl.when(step == 0)
    def _():
        left, right = attn_ref[:, :BLK], attn_ref[:, BLK:]
        for j, (top, bottom) in enumerate(((o00, o10), (o01, o11))):
            c = slice(j * BLK, j * BLK + BLK)
            mid[:, c] = (
                x_ref[:, c].astype(F32)
                + (dot(left, tile(top), 1, 0) + dot(right, tile(bottom), 1, 0))
                + vec_ref[6:7, c]
            )
        hat, _ = norm_parts(mid[...])
        a2[...] = (hat * vec_ref[2:3, :] + vec_ref[3:4, :]).astype(LOW)
        acc[...] = jnp.zeros_like(acc)
        da2[...] = jnp.zeros_like(da2)

    @pl.when((step > 0) & (step < last))
    def _():
        rows = a2.shape[0]
        up0, up1, down0, down1 = tile(u0), tile(u1), tile(w0), tile(w1)
        bias_grad = jnp.zeros((1, BLK), F32)
        acts, d_hids = [], []
        for c in range(rows // chunk):
            r = slice(c * chunk, c * chunk + chunk)
            hidden = dot(a2[r, :BLK], up0, 1, 0) + dot(a2[r, BLK:], up1, 1, 0) + b1_ref[...]
            act, slope = gelu_pair(hidden)
            act = act.astype(LOW)
            back = dot(dy_ref[r, :BLK], down0, 1, 1) + dot(dy_ref[r, BLK:], down1, 1, 1)
            d_hid = (back * slope).astype(LOW)
            acc[r, :BLK] += dot(act, down0, 1, 0)
            acc[r, BLK:] += dot(act, down1, 1, 0)
            da2[r, :BLK] += dot(d_hid, up0, 1, 1)
            da2[r, BLK:] += dot(d_hid, up1, 1, 1)
            bias_grad = bias_grad + jnp.sum(d_hid.astype(F32), axis=0, keepdims=True)
            acts.append(act)
            d_hids.append(d_hid)
        gb1_ref[...] = bias_grad
        act = jnp.concatenate(acts, axis=0)
        d_hid = jnp.concatenate(d_hids, axis=0)
        buf = step % 2

        @pl.when(step > 2)
        def _():
            settle(buf)

        for j in range(2):
            c = slice(j * BLK, j * BLK + BLK)
            put(buf, j, 16 + 8 * j + step - 1, dot(a2[:, c], d_hid, 0, 0))
            put(buf, 2 + j, 32 + 2 * (step - 1) + j, dot(act, dy_ref[:, c], 0, 0))

    @pl.when(step == last)
    def _():
        res_ref[...] = (mid[...] + acc[...] + vec_ref[7:8, :]).astype(LOW)
        hat, rstd = norm_parts(mid[...])
        grad = da2[...]
        dy = dy_ref[...].astype(F32)
        sums_ref[0:1, :] = jnp.sum(hat * grad, axis=0, keepdims=True)
        sums_ref[1:2, :] = jnp.sum(grad, axis=0, keepdims=True)
        d_mid = dy + norm_back(grad * vec_ref[2:3, :], hat, rstd)
        dmid_ref[...] = d_mid
        d_proj = d_mid.astype(LOW)
        sums_ref[2:3, :] = jnp.sum(d_proj.astype(F32), axis=0, keepdims=True)
        sums_ref[3:4, :] = jnp.sum(dy, axis=0, keepdims=True)
        sums_ref[4:8, :] = jnp.zeros((4, D), F32)
        for i, (first, second) in enumerate(((o00, o01), (o10, o11))):
            c = slice(i * BLK, i * BLK + BLK)
            dattn_ref[:, c] = (
                dot(d_proj[:, :BLK], tile(first), 1, 1) + dot(d_proj[:, BLK:], tile(second), 1, 1)
            ).astype(LOW)
        settle(0)
        for i in range(2):
            for j in range(2):
                c, k = slice(i * BLK, i * BLK + BLK), slice(j * BLK, j * BLK + BLK)
                put(0, 2 * i + j, 12 + 2 * i + j, dot(attn_ref[:, c], d_proj[:, k], 0, 0))
        settle(1)
        settle(0)


def mid_layer(own, slot, rel, seq, x, attn, dy, vec, b1, gathered, chunk=256):
    rows = x.shape[0]
    wide = FF // BLK
    quarter = BLK // 4
    owners, slots = gathered.shape[0], gathered.shape[2]

    def part(i):
        return jnp.clip(i - 1, 0, wide - 1)

    def full(shape):
        return pl.BlockSpec(shape, lambda i, own, slot, rel, seq: (0,) * len(shape))

    def tile_at(block_of):
        return pl.BlockSpec(
            (1, 4, 1, quarter, BLK),
            lambda i, own, slot, rel, seq: (own[block_of(i)], 0, slot[block_of(i)], 0, 0),
        )

    row_spec = full((rows, D))
    strip = pl.BlockSpec((1, BLK), lambda i, own, slot, rel, seq: (0, part(i)))
    anywhere = pl.BlockSpec(memory_space=pl.ANY)
    place_shape = jax.ShapeDtypeStruct((2, owners, slots, quarter, BLK), LOW)
    return pl.pallas_call(
        functools.partial(mid_kernel, chunk=chunk),
        grid_spec=pltpu.PrefetchScalarGridSpec(
            num_scalar_prefetch=4,
            grid=(wide + 2,),
            in_specs=[row_spec, row_spec, row_spec, full(vec.shape), strip]
            + [tile_at(lambda i, b=b: b) for b in (12, 13, 14, 15)]
            + [
                tile_at(lambda i: 16 + part(i)),
                tile_at(lambda i: 24 + part(i)),
                tile_at(lambda i: 32 + 2 * part(i)),
                tile_at(lambda i: 33 + 2 * part(i)),
            ],
            out_specs=[row_spec, row_spec, row_spec, anywhere, anywhere, full((8, D)), strip],
            scratch_shapes=[
                pltpu.VMEM((rows, D), F32),
                pltpu.VMEM((rows, D), LOW),
                pltpu.VMEM((rows, D), F32),
                pltpu.VMEM((rows, D), F32),
                pltpu.VMEM((2, 4, 4, quarter, BLK), LOW),
                pltpu.SemaphoreType.DMA((2, 4, 4)),
            ],
        ),
        out_shape=[
            jax.ShapeDtypeStruct((rows, D), LOW),
            jax.ShapeDtypeStruct((rows, D), F32),
            jax.ShapeDtypeStruct((rows, D), LOW),
            place_shape,
            place_shape,
            jax.ShapeDtypeStruct((8, D), F32),
            jax.ShapeDtypeStruct((1, FF), F32),
        ],
        compiler_params=params(60),
        name="mid",
    )(own, slot, rel, seq, x, attn, dy, vec, b1, *([gathered] * 8))


def d_columns(step, grads, work):
    for half in range(2):
        dq, dk, rk, dv, rv = grads[5 * half : 5 * half + 5]

        @pl.when(step == half)
        def _():
            work(dq[...])

        @pl.when(step == 2 + half)
        def _():
            work((dk[...].astype(F32) + rk[...].astype(F32)).astype(LOW))

        @pl.when(step == 4 + half)
        def _():
            work((dv[...].astype(F32) + rv[...].astype(F32)).astype(LOW))


def qkv_grad_kernel(seq, a_ref, *refs):
    grads, (keep, send, cols_ref, stage) = refs[:10], refs[10:]
    quarter = BLK // 4

    def work(d_cols):
        cols_ref[...] = jnp.sum(d_cols.astype(F32), axis=0, keepdims=True)
        for i in range(2):
            stage[...] = dot(a_ref[:, i * BLK : i * BLK + BLK], d_cols, 0, 0).astype(LOW)
            for rel_core, out in enumerate((keep, send)):
                for rel_x in range(2):
                    start = pl.multiple_of(quarter_at(seq[0], rel_core, rel_x) * quarter, quarter)
                    out[rel_x, i, 0] = stage[pl.ds(start, quarter), :]

    d_columns(pl.program_id(0), grads, work)


def qkv_grad(seq, normed, halves):
    rows = normed.shape[0]
    quarter = BLK // 4
    tile_out = pl.BlockSpec((2, 2, 1, quarter, BLK), lambda i, seq: (0, 0, i, 0, 0))
    shape = jax.ShapeDtypeStruct((2, 2, 6, quarter, BLK), LOW)
    return pl.pallas_call(
        qkv_grad_kernel,
        grid_spec=pltpu.PrefetchScalarGridSpec(
            num_scalar_prefetch=1,
            grid=(6,),
            in_specs=[pl.BlockSpec((rows, D), lambda i, seq: (0, 0))]
            + [pl.BlockSpec((rows, BLK), lambda i, seq: (0, 0))] * 10,
            out_specs=[tile_out, tile_out, pl.BlockSpec((1, BLK), lambda i, seq: (0, i))],
            scratch_shapes=[pltpu.VMEM((BLK, BLK), LOW)],
        ),
        out_shape=[shape, shape, jax.ShapeDtypeStruct((1, 3 * D), F32)],
        compiler_params=params(48),
        name="qkv_grad",
    )(seq, normed, *halves[0], *halves[1])


def qkv_bwd_kernel(own, slot, x_ref, dmid_ref, vec_ref, *refs):
    grads, (t0, t1, dx_ref, sums_ref, acc) = refs[:10], refs[10:]
    step = pl.program_id(0)

    @pl.when(step == 0)
    def _():
        acc[...] = jnp.zeros_like(acc)

    def work(d_cols):
        acc[:, :BLK] += dot(d_cols, tile(t0), 1, 1)
        acc[:, BLK:] += dot(d_cols, tile(t1), 1, 1)

    d_columns(step, grads, work)

    @pl.when(step == 5)
    def _():
        hat, rstd = norm_parts(x_ref[...].astype(F32))
        grad = acc[...]
        sums_ref[0:1, :] = jnp.sum(hat * grad, axis=0, keepdims=True)
        sums_ref[1:2, :] = jnp.sum(grad, axis=0, keepdims=True)
        sums_ref[2:8, :] = jnp.zeros((6, D), F32)
        dx_ref[...] = (dmid_ref[...] + norm_back(grad * vec_ref[0:1, :], hat, rstd)).astype(LOW)


def qkv_backward(own, slot, x, d_mid, vec, halves, gathered):
    rows = x.shape[0]
    row_spec = full_spec((rows, D))
    return pl.pallas_call(
        qkv_bwd_kernel,
        grid_spec=pltpu.PrefetchScalarGridSpec(
            num_scalar_prefetch=2,
            grid=(6,),
            in_specs=[row_spec, row_spec, full_spec(vec.shape)]
            + [full_spec((rows, BLK))] * 10
            + [tile_spec(lambda i: i), tile_spec(lambda i: 6 + i)],
            out_specs=[row_spec, full_spec((8, D))],
            scratch_shapes=[pltpu.VMEM((rows, D), F32)],
        ),
        out_shape=[jax.ShapeDtypeStruct((rows, D), LOW), jax.ShapeDtypeStruct((8, D), F32)],
        compiler_params=params(60),
        name="qkv_bwd",
    )(own, slot, x, d_mid, vec, *halves[0], *halves[1], gathered, gathered)


def eliminate(y_ref):
    count, size = y_ref.shape[0], y_ref.shape[1]
    lane = lanes((1, 8, size))
    sub = lax.broadcasted_iota(jnp.int32, (1, 8, size), 1)
    wide_lane = lanes((size, size))
    shape = (count, 8, size)

    def group(g, carry):
        base = pl.multiple_of(8 * g, 8)
        slab = y_ref[:, pl.ds(base, 8), :]
        rolled = jnp.stack([pltpu.roll(slab[b], size - base, 1) for b in range(count)], axis=0)
        columns = [jnp.broadcast_to(rolled[:, :, k : k + 1], shape) for k in range(8)]
        inside = (lane >= base) & (lane < base + 8)
        rows = jnp.where(inside, jnp.where(lane - base == sub, 1.0, 0.0), slab)
        scale = jnp.zeros(shape, F32)
        for j in range(8):
            inv_root = lax.rsqrt(jnp.broadcast_to(columns[j][:, j : j + 1, :], shape))
            scale = jnp.where(sub == j, inv_root, scale)
            factor = jnp.where(sub > j, columns[j] * (inv_root * inv_root), 0.0)
            rows = rows - factor * jnp.broadcast_to(rows[:, j : j + 1, :], shape)
            for k in range(j + 1, 8):
                columns[k] = columns[k] - factor * jnp.broadcast_to(columns[k][:, j : j + 1, :], shape)
        rows = rows * scale
        below = jnp.where(lane >= base + 8, rows, 0.0)
        passed = (wide_lane >= base) & (wide_lane < base + 8)
        for b in range(count):
            high, mid, low = three_parts(rows[b])
            b_high, b_mid, b_low = three_parts(below[b])
            first = jnp.concatenate([b_high, b_high, b_mid, b_high, b_low, b_mid], axis=0)
            second = jnp.concatenate([high, mid, high, low, high, mid], axis=0)
            update = dot(first.astype(LOW), second.astype(LOW), 0, 0)
            y_ref[b] = jnp.where(passed, 0.0, y_ref[b]) - update
            y_ref[b, pl.ds(base, 8), :] = rows[b]
        return carry

    lax.fori_loop(0, size // 8, group, 0)


def soap_kernel(
    seq_ref, g0, g1, g2, g3, w_ref, one_ref, two_ref, ls_ref, rs_ref, lb_ref, rb_ref,
    *refs,
):
    (
        grad_ref, w_out, one_out, two_out, ls_out, rs_out, lb_out, rb_out,
        grad_s, gram, work, inv,
    ) = refs[-12:]
    step = pl.program_id(0)
    slots = pl.num_programs(0)
    count = lb_out.shape[0]
    quarter = BLK // 4
    for piece, flip in ((g0, 0), (g1, 2), (g2, 1), (g3, 3)):
        start = pl.multiple_of((seq_ref[0] ^ flip) * quarter, quarter)
        grad_s[pl.ds(start, quarter), :] = piece[0].astype(F32)
    grad_ref[0] = grad_s[...]
    grad = grad_s[...].astype(LOW)
    left, right = lb_ref[0], rb_ref[0]
    left_low, right_low = left.astype(LOW), right.astype(LOW)
    rotated = dot(dot(left_low, grad, 0, 0).astype(LOW), right_low, 1, 0)
    one = BETA_ONE * one_ref[0] + (1.0 - BETA_ONE) * rotated
    two = BETA_TWO * two_ref[0] + (1.0 - BETA_TWO) * rotated * rotated
    one_out[0] = one
    two_out[0] = two
    scaled = (one / (1.0 - BETA_ONE**STEP)) / (jnp.sqrt(two / (1.0 - BETA_TWO**STEP)) + ADAM_EPS)
    back = dot(dot(left_low, scaled.astype(LOW), 1, 0).astype(LOW), right_low, 1, 1)
    w_out[0] = w_ref[0] - RATE_MATRIX * (back + DECAY_RATE * w_ref[0])
    left_new = BETA_STAT * ls_ref[0] + (1.0 - BETA_STAT) * dot(grad, grad, 1, 1)
    right_new = BETA_STAT * rs_ref[0] + (1.0 - BETA_STAT) * dot(grad, grad, 0, 0)
    ls_out[0] = left_new
    rs_out[0] = right_new
    for side, (stats, basis) in enumerate(((left_new, left), (right_new, right))):
        product = dot(stats, basis, 1, 0, HIGHEST)
        at = side * count + step
        work[at] = product
        gram[at] = dot(product, product, 0, 0, HIGHEST)

    @pl.when(step == slots - 1)
    def _():
        for p in range(BLK // 128):
            c = slice(128 * p, 128 * p + 128)
            rest = slice(128 * p + 128, BLK)
            inv[...] = gram[:, c, c]
            eliminate(inv)

            def solve(b, carry, out):
                at = b + (count if out is rb_out else 0)
                factor = inv[at]
                solved = dot(work[at, :, c], factor, 1, 1, HIGHEST)
                out[b, :, c] = solved
                if p < BLK // 128 - 1:
                    upper = dot(factor, gram[at, c, rest], 1, 0, HIGHEST)
                    work[at, :, rest] = work[at, :, rest] - dot(solved, upper, 1, 0, HIGHEST)
                    gram[at, rest, rest] = gram[at, rest, rest] - dot(upper, upper, 0, 0, HIGHEST)
                return carry

            lax.fori_loop(0, count, functools.partial(solve, out=lb_out), 0)
            lax.fori_loop(0, count, functools.partial(solve, out=rb_out), 0)


def soap_update(seq, pieces, state):
    count = state[0].shape[0]
    piece_spec = pl.BlockSpec((1, BLK // 4, BLK), lambda i, s: (i, 0, 0))
    block_spec = pl.BlockSpec((1, BLK, BLK), lambda i, s: (i, 0, 0))
    whole_spec = pl.BlockSpec((count, BLK, BLK), lambda i, s: (0, 0, 0))
    shape = jax.ShapeDtypeStruct((count, BLK, BLK), F32)
    return pl.pallas_call(
        soap_kernel,
        grid_spec=pltpu.PrefetchScalarGridSpec(
            num_scalar_prefetch=1,
            grid=(count,),
            in_specs=[piece_spec] * 4 + [block_spec] * 7,
            out_specs=[block_spec] * 6 + [whole_spec] * 2,
            scratch_shapes=[
                pltpu.VMEM((BLK, BLK), F32),
                pltpu.VMEM((2 * count, BLK, BLK), F32),
                pltpu.VMEM((2 * count, BLK, BLK), F32),
                pltpu.VMEM((2 * count, 128, 128), F32),
            ],
        ),
        out_shape=[shape] * 8,
        compiler_params=params(60),
        name="soap",
    )(seq, *pieces, *state)


def split_kernel(dp, a_ref, b_ref, *outs):
    for k, out in enumerate(outs):
        out[...] = (a_ref[dp[0] ^ k].astype(F32) + b_ref[dp[0] ^ k].astype(F32)).astype(LOW)


def split_sum(dp, a, b):
    parts = a.shape[0]
    shape = a.shape[1:]
    return pl.pallas_call(
        split_kernel,
        grid_spec=pltpu.PrefetchScalarGridSpec(
            num_scalar_prefetch=1,
            grid=(1,),
            in_specs=[pl.BlockSpec(a.shape, lambda i, dp: (0,) * a.ndim)] * 2,
            out_specs=[pl.BlockSpec(shape, lambda i, dp: (0,) * len(shape))] * parts,
        ),
        out_shape=[jax.ShapeDtypeStruct(shape, LOW)] * parts,
        compiler_params=params(32),
        name="split_sum",
    )(dp, a, b)


def choose_kernel(dp, source, *refs):
    parts, early, out, held = refs[:-3], refs[-3], refs[-2], refs[-1]
    per, half = held.shape[1], held.shape[2]
    for k, part in enumerate(parts):
        held[k] = part[...]
    slots = out.shape[0]
    units = len(parts) * per

    def one(i, carry):
        block = source[i]

        @pl.when(2 * block >= units)
        def _():
            out[i] = early[i]

        @pl.when(2 * block < units)
        def _():
            for h in range(2):
                unit = 2 * block + h
                out[i, h * half : h * half + half] = held[lax.div(unit, per) ^ dp[0], lax.rem(unit, per)]

        return carry

    lax.fori_loop(0, slots, one, 0)


def choose(dp, source, parts, early):
    return pl.pallas_call(
        choose_kernel,
        grid_spec=pltpu.PrefetchScalarGridSpec(
            num_scalar_prefetch=2,
            grid=(1,),
            in_specs=[pl.BlockSpec(parts[0].shape, lambda i, dp, src: (0, 0, 0))] * len(parts)
            + [pl.BlockSpec(early.shape, lambda i, dp, src: (0, 0, 0))],
            out_specs=pl.BlockSpec(early.shape, lambda i, dp, src: (0, 0, 0)),
            scratch_shapes=[pltpu.VMEM((len(parts),) + parts[0].shape, LOW)],
        ),
        out_shape=jax.ShapeDtypeStruct(early.shape, LOW),
        compiler_params=params(32),
        name="choose",
    )(dp, source, *parts, early)


def swap(x, axis, bit):
    size = lax.axis_size(axis)
    return lax.ppermute(x, axis, [(i, i ^ bit) for i in range(size)])


def add_low(a, b):
    return (a.astype(F32) + b.astype(F32)).astype(LOW)


class Halving:
    def __init__(self, kept, got, names):
        self.kept, self.got, self.names = kept, got, list(names)

    def take(self, name, index):
        at = (slice(None),) * self.names.index(name) + (index,)
        return add_low(self.kept[at], self.got[at])

    def send(self, name):
        sent, kept = self.take(name, 1), self.take(name, 0)
        self.names.remove(name)
        self.kept = kept
        self.sent, self.name = sent, name
        return sent

    def receive(self, sent):
        axis, bit = ("seq", 2) if self.name == "x" else ("dp", 2**self.name)
        self.got = swap(sent, axis, bit)

    def total(self):
        return add_low(self.kept, self.got)


def quarters(piece):
    across = swap(piece, "seq", 2)
    beside = swap(jnp.stack([piece, across]), "seq", 1)
    return piece, across, beside[0], beside[1]


def block_places(owners, owner_count, slot_count):
    block_count = owners.shape[0]
    ids = jnp.arange(block_count, dtype=jnp.int32)
    earlier = (owners[:, None] == owners[None, :]) & (ids[None, :] < ids[:, None])
    slots = jnp.sum(earlier.astype(jnp.int32), axis=1)
    places = owners * slot_count + slots
    matched = places[None, :] == jnp.arange(owner_count * slot_count, dtype=jnp.int32)[:, None]
    missing = 1 - jnp.any(matched, axis=1).astype(jnp.int32)
    sources = jnp.sum(jnp.where(matched, ids[None, :], 0), axis=1) + block_count * missing
    return slots, sources


def adam_vectors(gradient, vec, first_mom, second_mom):
    first_mom = BETA_ONE * first_mom + (1.0 - BETA_ONE) * gradient
    second_mom = BETA_TWO * second_mom + (1.0 - BETA_TWO) * gradient * gradient
    step_size = (first_mom / (1.0 - BETA_ONE**STEP)) / (
        jnp.sqrt(second_mom / (1.0 - BETA_TWO**STEP)) + ADAM_EPS
    )
    return first_mom, second_mom, vec - RATE_VECTOR * step_size


def on_device(
    tokens, cotangent, lengths, patch_mask, owners, master, moment_one, moment_two,
    left_stats, right_stats, left_basis, right_basis, vec, vec_one, vec_two,
):
    owner_count = lax.axis_size("dp")
    slot_count = master.shape[0]
    quarter = BLK // 4
    seq_id = lax.axis_index("seq").astype(jnp.int32)
    dp_id = lax.axis_index("dp").astype(jnp.int32)
    core, chip = seq_id % 2, seq_id // 2
    part_len = tokens.shape[1]
    slots, sources = block_places(owners, owner_count, slot_count)
    first_blocks = 3 * (D // BLK) ** 2

    mine = lax.dynamic_index_in_dim(
        master.reshape(slot_count, 4, quarter, BLK), seq_id, 1, keepdims=False
    ).astype(LOW)
    gathered = lax.all_gather(mine, AXES, axis=0, tiled=False).reshape(
        owner_count, 4, slot_count, quarter, BLK
    )

    pair = jnp.stack([tokens, cotangent])
    kept = lax.dynamic_index_in_dim(pair, chip, 1, keepdims=False)
    got = swap(lax.dynamic_index_in_dim(pair, 1 - chip, 1, keepdims=False), "seq", 2)
    x = jnp.concatenate([kept[0], got[0]], axis=0)
    dy = jnp.concatenate([kept[1], got[1]], axis=0)

    def to_positions(rows):
        other = swap(rows[part_len:], "seq", 2)
        mine = rows[:part_len]
        return jnp.where(chip == 0, jnp.stack([mine, other]), jnp.stack([other, mine]))

    positions = jnp.arange(patch_mask.shape[-1], dtype=jnp.int32)
    live = (positions[None, :] < lengths[:, None]) & ((patch_mask == 1) | (positions[None, :] == 0))
    live = lax.dynamic_index_in_dim(live, chip, 0, keepdims=False).reshape(4, part_len)
    order = seq_id ^ jnp.array([0, 2, 1, 3], jnp.int32)
    fill = jnp.where(jnp.take(live, order, axis=0).reshape(-1), 0.0, NEG_FILL).astype(LOW)
    fill = jnp.broadcast_to(fill[:, None], (fill.shape[0], 128))

    bias = jnp.concatenate([vec[4], jnp.zeros_like(vec[4]), vec[5]])[None, :]
    q, kv, normed = qkv_forward(owners, slots, x, vec, bias, gathered)
    other = swap(kv, "seq", 1)
    attn, lse = attn_forward(q, kv, other, fill)
    b1 = vec[8:].reshape(1, FF)
    seq_of, dp_of = seq_id.reshape(1), dp_id.reshape(1)
    result, d_mid, d_attn, keep, send, sums_two, bias_grad = mid_layer(
        owners, slots, owners ^ dp_id, seq_of, x, attn, dy, vec, b1, gathered
    )
    output = to_positions(result)

    bits = owner_count.bit_length() - 1
    if slot_count % 3 == 0 and bits == 3:
        plans = [["x", 0, 1, 2], [0, 1, "x", 2], [1, "x", 0, 2]]
    else:
        plans = [["x"] + list(range(bits))]
    per = slot_count // len(plans)
    names = ["x"] + list(range(bits))[::-1]
    shape = (2,) * (1 + bits) + keep.shape[2:]
    keep, got = keep.reshape(shape), swap(send, "seq", 1).reshape(shape)
    groups = [
        Halving(keep[..., per * g : per * g + per, :, :], got, names) for g in range(len(plans))
    ]
    guard = fill

    def advance(step, guard):
        if step == 0:
            for g, group in enumerate(groups):
                group.got = group.got[..., per * g : per * g + per, :, :]
        sent = [group.send(plan[step]) for group, plan in zip(groups, plans, strict=True)]
        *sent, guard = lax.optimization_barrier((*sent, guard))
        for group, array in zip(groups, sent, strict=True):
            group.receive(array)
        return guard

    halves = []
    half_pairs = D // 128 // 2
    taken = 0
    for half in range(2):
        before, first = [], half * half_pairs
        for place, count in ((0, 2), (2, 1)):
            if (half or place) and (half, place) != (1, 0):
                guard = advance(taken, guard)
                taken += 1
            before = attn_backward(
                q, kv, other, guard, attn, lse, d_attn, first + place, count, place, half_pairs, before
            )
            got, before = lax.optimization_barrier(([group.got for group in groups], before))
            for group, array in zip(groups, got, strict=True):
                group.got = array
        dq, dk, dv, sent_k, sent_v = before
        halves.append((dq, dk, swap(sent_k, "seq", 1), dv, swap(sent_v, "seq", 1)))
    late_keep, late_send, cols = qkv_grad(seq_of, normed, halves)
    late_shape = (2, -1, quarter, BLK)
    late_got = swap(late_send.reshape(late_shape), "seq", 1)
    d_x, sums_one = qkv_backward(owners, slots, x, d_mid, vec, halves, gathered)
    d_tokens = to_positions(d_x)
    while taken < len(names):
        advance(taken, guard)
        taken += 1
    early = jnp.concatenate([group.total() for group in groups], axis=0)

    late = Halving(late_keep.reshape(late_shape), late_got, ["x"])
    late.receive(late.send("x"))
    mine_from = lax.dynamic_slice_in_dim(sources, dp_id * slot_count, slot_count)
    if 2 * first_blocks % owner_count == 0:
        unit = (owner_count, 2 * first_blocks // owner_count, quarter // 2, BLK)
        parts = split_sum(dp_of, late.kept.reshape(unit), late.got.reshape(unit))
        parts = [parts[0]] + [swap(part, "dp", k) for k, part in enumerate(parts) if k]
        total = sum(part.astype(F32) for part in parts).astype(LOW)
        parts = [total] + [swap(total, "dp", k) for k in range(1, owner_count)]
        piece = choose(dp_of, mine_from, parts, early)
    else:
        tiles = jnp.concatenate([late.total(), jnp.zeros((1, quarter, BLK), LOW)], axis=0)
        at = sources.reshape(owner_count, slot_count)[dp_id ^ jnp.arange(owner_count)]
        tiles = jnp.take(tiles, jnp.minimum(at, first_blocks).reshape(-1), axis=0)
        tiles = tiles.reshape((2,) * bits + (slot_count, quarter, BLK))
        owned = Halving(tiles, jnp.zeros_like(tiles), names[1:])
        for bit in range(bits):
            owned.receive(owned.send(bit))
        piece = jnp.where((mine_from < first_blocks)[:, None, None], owned.total(), early)
    state = (master, moment_one, moment_two, left_stats, right_stats, left_basis, right_basis)
    piece = jnp.where((mine_from < owners.shape[0])[:, None, None], piece, jnp.zeros_like(piece))
    updates = soap_update(seq_of, quarters(piece), state)

    vec_grad = jnp.concatenate(
        [
            sums_one[0:2],
            sums_two[0:2],
            cols[:, :D],
            cols[:, 2 * D :],
            sums_two[2:4],
            bias_grad.reshape(-1, D),
        ],
        axis=0,
    )
    vec_total = jnp.sum(lax.all_gather(vec_grad, AXES, axis=0, tiled=False), axis=0)
    vec_first, vec_second, vec_next = adam_vectors(vec_total, vec, vec_one, vec_two)
    grad_blocks, w_new, one_new, two_new, ls_new, rs_new, lb_new, rb_new = updates
    return (
        output, d_tokens, grad_blocks, w_new, one_new, two_new, ls_new, rs_new, lb_new, rb_new,
        vec_first, vec_second, vec_next,
    )


def solution(mesh):
    rows, blocks, whole = P("dp", "seq", None), P("dp", None, None), P()
    return jax.shard_map(
        on_device,
        mesh=mesh,
        in_specs=(rows, rows, P("dp"), P("dp", None), whole) + (blocks,) * 7 + (whole,) * 3,
        out_specs=(rows, rows) + (blocks,) * 8 + (whole,) * 3,
        check_vma=False,
    )
```

```python
import functools

import jax
import jax.numpy as jnp
from jax import lax
from jax.experimental import pallas as pl
from jax.experimental.pallas import tpu as pltpu
from jax.sharding import PartitionSpec as P

D = 768
FF = 3072
BLK = 384
STEP = 10

NORM_EPS = 1e-06
NEG_FILL = -1000000000.0
BETA_ONE = 0.9
BETA_TWO = 0.999
BETA_STAT = 0.95
RATE_MATRIX = 0.1
RATE_VECTOR = 0.3
DECAY_RATE = 0.01
ADAM_EPS = 1e-08

LOW = jnp.bfloat16
F32 = jnp.float32
AXES = ("dp", "seq")
MIB = 2**20

TAIL_P = 0.24
TAIL_C = (
    0.09575380798443668,
    0.09552183543465394,
    0.09284136585084933,
    0.06338567653857548,
    0.11841694922211018,
    -0.06574016740998187,
    0.15281935057715396,
    -0.052998628523732765,
)


def dot(a, b, ca, cb):
    return lax.dot_general(a, b, (((ca,), (cb,)), ((), ())), preferred_element_type=F32)


def lanes(shape):
    return lax.broadcasted_iota(jnp.int32, shape, len(shape) - 1)


def gelu_pair(x):
    u = jnp.abs(x)
    t = 1.0 / (1.0 + TAIL_P * u)
    poly = TAIL_C[-1]
    for coeff in TAIL_C[-2::-1]:
        poly = poly * t + coeff
    expo = jnp.exp(-0.5 * u * u)
    tail = poly * t * expo
    cdf = jnp.where(x < 0, tail, 1.0 - tail)
    return x * cdf, cdf + x * (expo * 0.3989422804014327)


def norm_parts(rows):
    center = rows - jnp.mean(rows, axis=-1, keepdims=True)
    rstd = lax.rsqrt(jnp.mean(center * center, axis=-1, keepdims=True) + NORM_EPS)
    return center * rstd, rstd


def norm_back(grad, hat, rstd):
    return rstd * (
        grad
        - jnp.mean(grad, axis=-1, keepdims=True)
        - hat * jnp.mean(grad * hat, axis=-1, keepdims=True)
    )


def params(limit):
    return pltpu.CompilerParams(vmem_limit_bytes=limit * MIB)


def tile_spec(block_of):
    return pl.BlockSpec(
        (1, 4, 1, BLK // 4, BLK),
        lambda i, own, slot: (own[block_of(i)], 0, slot[block_of(i)], 0, 0),
    )


def tile(ref):
    return ref[...].reshape(BLK, BLK)


def full_spec(shape):
    return pl.BlockSpec(shape, lambda i, own, slot: (0,) * len(shape))


def quarter_at(seq, rel_core, rel_x):
    return seq ^ (2 * rel_x + rel_core)


def square(tiles, held):
    for i in range(2):
        for j in range(2):
            held[i * BLK : i * BLK + BLK, j * BLK : j * BLK + BLK] = tile(tiles[2 * i + j])
    return held[...]


def qkv_kernel(own, slot, x_ref, vec_ref, bias_ref, t00, t01, t10, t11, q_ref, kv_ref, a_ref, held):
    @pl.when(pl.program_id(0) == 0)
    def _():
        hat, _ = norm_parts(x_ref[...].astype(F32))
        a_ref[...] = (hat * vec_ref[0:1, :] + vec_ref[1:2, :]).astype(LOW)

    low = (dot(a_ref[...], square((t00, t01, t10, t11), held), 1, 0) + bias_ref[...]).astype(LOW)

    @pl.when(pl.program_id(0) == 0)
    def _():
        q_ref[...] = low

    @pl.when(pl.program_id(0) > 0)
    def _():
        kv_ref[...] = low


def qkv_tiles():
    return [tile_spec(lambda i, n=n: 6 * (n // 2) + 2 * i + n % 2) for n in range(4)]


def qkv_forward(own, slot, x, vec, bias, gathered):
    rows = x.shape[0]
    return pl.pallas_call(
        qkv_kernel,
        grid_spec=pltpu.PrefetchScalarGridSpec(
            num_scalar_prefetch=2,
            grid=(3,),
            in_specs=[
                full_spec((rows, D)),
                full_spec(vec.shape),
                pl.BlockSpec((1, D), lambda i, own, slot: (0, i)),
            ]
            + qkv_tiles(),
            out_specs=[
                full_spec((rows, D)),
                pl.BlockSpec((rows, D), lambda i, own, slot: (0, jnp.maximum(i - 1, 0))),
                full_spec((rows, D)),
            ],
            scratch_shapes=[pltpu.VMEM((D, D), LOW)],
        ),
        out_shape=[
            jax.ShapeDtypeStruct((rows, D), LOW),
            jax.ShapeDtypeStruct((rows, 2 * D), LOW),
            jax.ShapeDtypeStruct((rows, D), LOW),
        ],
        compiler_params=params(48),
        name="qkv",
    )(own, slot, x, vec, bias, *([gathered] * 4))


def attn_fwd_kernel(q_ref, k1, v1, k2, v2, bias_ref, o_ref, lse_ref, ka, kb, va, vb):
    rows = k1.shape[0]

    @pl.when(pl.program_id(1) == 0)
    def _():
        ln = lanes((rows, 128))
        for i, (k, v) in enumerate(((k1, v1), (k2, v2))):
            r = slice(i * rows, i * rows + rows)
            keys, values, bias = k[...], v[...], bias_ref[r, :]
            one = jnp.ones_like(values)
            ka[r, :] = jnp.where(ln == 64, bias, keys)
            kb[r, :] = jnp.where(ln == 0, bias, keys)
            va[r, :] = jnp.where(ln < 64, values, one)
            vb[r, :] = jnp.where(ln < 64, one, values)

    q = q_ref[...] * jnp.asarray(0.125, LOW)
    ln = lanes(q.shape)
    one, zero = jnp.ones_like(q), jnp.zeros_like(q)
    qa = jnp.where(ln < 64, q, jnp.where(ln == 64, one, zero))
    qb = jnp.where(ln < 64, jnp.where(ln == 0, one, zero), q)
    outs, tops = [], []
    for query, keys, values in ((qa, ka, va), (qb, kb, vb)):
        logits = dot(query, keys[...], 1, 1)
        top = jnp.max(logits, axis=1, keepdims=True)
        expo = jnp.exp(logits - top).astype(LOW)
        outs.append(dot(expo, values[...], 1, 0))
        tops.append(top)
    total = jnp.where(ln < 64, outs[1], outs[0])
    attended = jnp.where(ln < 64, outs[0], outs[1])
    o_ref[...] = (attended / pltpu.roll(total, 64, 1)).astype(LOW)
    lse_ref[...] = jnp.where(ln < 64, tops[1], tops[0]) + jnp.log(total)


def attn_forward(q, kv, other, bias, q_rows=256):
    rows, pairs = q.shape[0], D // 128
    keys = 2 * rows
    q_spec = pl.BlockSpec((q_rows, 128), lambda p, i: (i, p))
    return pl.pallas_call(
        attn_fwd_kernel,
        grid=(pairs, rows // q_rows),
        in_specs=[
            q_spec,
            pl.BlockSpec((rows, 128), lambda p, i: (0, p)),
            pl.BlockSpec((rows, 128), lambda p, i: (0, pairs + p)),
            pl.BlockSpec((rows, 128), lambda p, i: (0, p)),
            pl.BlockSpec((rows, 128), lambda p, i: (0, pairs + p)),
            pl.BlockSpec((keys, 128), lambda p, i: (0, 0)),
        ],
        out_specs=[q_spec, q_spec],
        out_shape=[
            jax.ShapeDtypeStruct((rows, D), LOW),
            jax.ShapeDtypeStruct((rows, D), F32),
        ],
        scratch_shapes=[pltpu.VMEM((keys, 128), LOW)] * 4,
        compiler_params=params(48),
        name="attn_fwd",
    )(q, kv, kv, other, other, bias)


def three_parts(x):
    high = x.astype(LOW).astype(F32)
    rest = x - high
    mid = rest.astype(LOW).astype(F32)
    return high, mid, rest - mid


def low_parts(x, count):
    found = []
    for _ in range(count):
        part = x.astype(LOW)
        found.append(part)
        x = x - part.astype(F32)
    return found


def dot_parts(a, b, ca, cb, order):
    pairs = [(i, j) for i in range(len(a)) for j in range(len(b)) if i + j < order]
    a = jnp.concatenate([a[i] for i, _ in pairs], axis=ca)
    b = jnp.concatenate([b[j] for _, j in pairs], axis=cb)
    return dot(a, b, ca, cb)


def with_spare(x, spare, value, one, first):
    ln = lanes(x.shape)
    high, mid, low = three_parts(value)
    filled = jnp.where(ln == first + 3, one, 0.0)
    for i, part in enumerate((high, mid, low)):
        filled = jnp.where(ln == first + i, part, filled)
    return jnp.where(spare, filled, x).astype(LOW)


def attn_bwd_kernel(
    q_ref, k1, v1, k2, v2, bias_ref, o_ref, lse_ref, do_ref,
    dq_ref, dk1, dv1, dk2, dv2, ka, kb, va, vb, kt, dk, dv, *, chunk,
):
    rows = k1.shape[0]

    @pl.when(pl.program_id(1) == 0)
    def _():
        ln = lanes((rows, 128))
        for i, (k, v) in enumerate(((k1, v1), (k2, v2))):
            r = slice(i * rows, i * rows + rows)
            keys, values, bias = k[...], v[...], bias_ref[r, :]
            one, zero = jnp.ones_like(values), jnp.zeros_like(values)
            ka[r, :] = jnp.where(ln < 64, keys, jnp.where(ln < 67, one, jnp.where(ln == 67, bias, zero)))
            kb[r, :] = jnp.where(ln >= 64, keys, jnp.where(ln < 3, one, jnp.where(ln == 3, bias, zero)))
            va[r, :] = jnp.where(ln < 64, values, jnp.where(ln < 67, one, zero))
            vb[r, :] = jnp.where(ln >= 64, values, jnp.where(ln < 3, one, zero))
            kt[:, r] = keys.T
        dk[...] = jnp.zeros_like(dk)
        dv[...] = jnp.zeros_like(dv)

    q = q_ref[...].astype(F32) * 0.125
    left = lanes(q.shape) < 64
    grad = do_ref[...].astype(F32)
    prod = grad * o_ref[...].astype(F32)
    sum_a = jnp.sum(jnp.where(left, prod, 0.0), axis=1, keepdims=True)
    sum_b = jnp.sum(jnp.where(left, 0.0, prod), axis=1, keepdims=True)
    delta = jnp.where(left, sum_b, sum_a)
    lse = lse_ref[...]
    zero = jnp.zeros_like(q)
    heads = (
        (
            with_spare(q, ~left, -lse, 1.0, 64), with_spare(grad, ~left, -delta, 0.0, 64), ka, va,
            jnp.where(left, q, zero).astype(LOW), jnp.where(left, grad, zero).astype(LOW),
        ),
        (
            with_spare(q, left, -lse, 1.0, 0), with_spare(grad, left, -delta, 0.0, 0), kb, vb,
            jnp.where(left, zero, q).astype(LOW), jnp.where(left, zero, grad).astype(LOW),
        ),
    )
    d_query = [jnp.zeros((64, q.shape[0]), F32)] * 2
    for c in range(2 * rows // chunk):
        r = slice(c * chunk, c * chunk + chunk)
        dv_c, dk_c = dv[r, :], dk[r, :]
        for h, (q_aug, g_aug, keys, values, q_only, g_only) in enumerate(heads):
            probs = jnp.exp(dot(keys[r, :], q_aug, 1, 1))
            d_logits = (probs * dot(values[r, :], g_aug, 1, 1)).astype(LOW)
            dv_c = dv_c + dot(probs.astype(LOW), g_only, 1, 0)
            dk_c = dk_c + dot(d_logits, q_only, 1, 0)
            d_query[h] = d_query[h] + dot(kt[64 * h : 64 * h + 64, r], d_logits, 1, 0)
        dv[r, :] = dv_c
        dk[r, :] = dk_c
    dq_ref[...] = (jnp.concatenate(d_query, axis=0) * 0.125).T.astype(LOW)

    @pl.when(pl.program_id(1) == pl.num_programs(1) - 1)
    def _():
        dk1[...] = dk[:rows, :].astype(LOW)
        dk2[...] = dk[rows:, :].astype(LOW)
        dv1[...] = dv[:rows, :].astype(LOW)
        dv2[...] = dv[rows:, :].astype(LOW)


def attn_backward(q, kv, other, bias, attn, lse, d_attn, first, count, place, total, before, q_rows=512, chunk=1024):
    rows, pairs = q.shape[0], D // 128
    keys = 2 * rows
    out_spec = pl.BlockSpec((q_rows, 128), lambda p, i: (i, place + p))
    k_out = pl.BlockSpec((rows, 128), lambda p, i: (0, place + p))
    q_spec = pl.BlockSpec((q_rows, 128), lambda p, i: (i, first + p))
    k_spec = pl.BlockSpec((rows, 128), lambda p, i: (0, first + p))
    v_spec = pl.BlockSpec((rows, 128), lambda p, i: (0, pairs + first + p))

    def kernel(*refs):
        attn_bwd_kernel(*refs[:9], *refs[9 + len(before) :], chunk=chunk)

    return pl.pallas_call(
        kernel,
        grid=(count, rows // q_rows),
        in_specs=[
            q_spec, k_spec, v_spec, k_spec, v_spec, pl.BlockSpec((keys, 128), lambda p, i: (0, 0)),
            q_spec, q_spec, q_spec,
        ]
        + [pl.BlockSpec(memory_space=pl.ANY)] * len(before),
        out_specs=[out_spec, k_out, k_out, k_out, k_out],
        out_shape=[jax.ShapeDtypeStruct((rows, total * 128), LOW)] * 5,
        scratch_shapes=[pltpu.VMEM((keys, 128), LOW)] * 4
        + [pltpu.VMEM((128, keys), LOW)]
        + [pltpu.VMEM((keys, 128), F32)] * 2,
        input_output_aliases={9 + i: i for i in range(len(before))},
        compiler_params=params(56),
        name="attn_bwd",
    )(q, kv, kv, other, other, bias, attn, lse, d_attn, *before)


def mid_kernel(
    own, slot, rel, seq, x_ref, attn_ref, dy_ref, vec_ref, b1_ref, o00, o01, o10, o11, *refs, chunk):
    ups, downs = refs[:4], refs[4:8]
    (
        res_ref, dmid_ref, dattn_ref, keep, send, sums_ref, gb1_ref,
        mid, a2, acc, da2, up_s, down_s, stage, sems,
    ) = refs[8:]
    step = pl.program_id(0)
    last = pl.num_programs(0) - 1
    quarter = BLK // 4

    def copies(buf, i, block):
        found = []
        for rel_core, out in enumerate((keep, send)):
            for rel_x in range(2):
                found.append(
                    pltpu.make_async_copy(
                        stage.at[buf, i, quarter_at(seq[0], rel_core, rel_x)],
                        out.at[rel_x, rel[block], slot[block]],
                        sems.at[buf, i, 2 * rel_core + rel_x],
                    )
                )
        return found

    def put(buf, i, block, value):
        low = value.astype(LOW)
        for part in range(4):
            stage[buf, i, part] = low[part * quarter : part * quarter + quarter]
        for copy in copies(buf, i, block):
            copy.start()

    def settle(buf, count=8):
        for i in range(count):
            for copy in copies(buf, i, 0):
                copy.wait()

    @pl.when(step == 0)
    def _():
        mid[...] = (
            x_ref[...].astype(F32)
            + dot(attn_ref[...], square((o00, o01, o10, o11), up_s), 1, 0)
            + vec_ref[6:7, :]
        )
        hat, _ = norm_parts(mid[...])
        a2[...] = (hat * vec_ref[2:3, :] + vec_ref[3:4, :]).astype(LOW)
        acc[...] = jnp.zeros_like(acc)
        da2[...] = jnp.zeros_like(da2)

    @pl.when((step > 0) & (step < last))
    def _():
        rows = a2.shape[0]
        up, down = square(ups, up_s), square(downs, down_s)
        bias_grad = jnp.zeros((1, D), F32)
        acts, d_hids = [], []
        for c in range(rows // chunk):
            r = slice(c * chunk, c * chunk + chunk)
            act, slope = gelu_pair(dot(a2[r, :], up, 1, 0) + b1_ref[...])
            act = act.astype(LOW)
            d_hid = (dot(dy_ref[r, :], down, 1, 1) * slope).astype(LOW)
            acc[r, :] += dot(act, down, 1, 0)
            da2[r, :] += dot(d_hid, up, 1, 1)
            bias_grad = bias_grad + jnp.sum(d_hid.astype(F32), axis=0, keepdims=True)
            acts.append(act)
            d_hids.append(d_hid)
        gb1_ref[...] = bias_grad
        act = jnp.concatenate(acts, axis=0)
        d_hid = jnp.concatenate(d_hids, axis=0)
        buf = step % 2

        @pl.when(step > 2)
        def _():
            settle(buf)

        for i in range(2):
            c = slice(i * BLK, i * BLK + BLK)
            up_grad = dot(a2[:, c], d_hid, 0, 0)
            down_grad = dot(act[:, c], dy_ref[...], 0, 0)
            for j in range(2):
                k = slice(j * BLK, j * BLK + BLK)
                put(buf, 2 * i + j, 16 + 8 * i + 2 * (step - 1) + j, up_grad[:, k])
                put(buf, 4 + 2 * i + j, 32 + 4 * (step - 1) + 2 * i + j, down_grad[:, k])

    @pl.when(step == last)
    def _():
        res_ref[...] = (mid[...] + acc[...] + vec_ref[7:8, :]).astype(LOW)
        hat, rstd = norm_parts(mid[...])
        grad = da2[...]
        dy = dy_ref[...].astype(F32)
        sums_ref[0:1, :] = jnp.sum(hat * grad, axis=0, keepdims=True)
        sums_ref[1:2, :] = jnp.sum(grad, axis=0, keepdims=True)
        d_mid = dy + norm_back(grad * vec_ref[2:3, :], hat, rstd)
        dmid_ref[...] = d_mid
        d_proj = d_mid.astype(LOW)
        sums_ref[2:3, :] = jnp.sum(d_proj.astype(F32), axis=0, keepdims=True)
        sums_ref[3:4, :] = jnp.sum(dy, axis=0, keepdims=True)
        sums_ref[4:8, :] = jnp.zeros((4, D), F32)
        dattn_ref[...] = dot(d_proj, square((o00, o01, o10, o11), up_s), 1, 1).astype(LOW)
        settle(0)
        for i in range(2):
            out_grad = dot(attn_ref[:, i * BLK : i * BLK + BLK], d_proj, 0, 0)
            for j in range(2):
                put(0, 2 * i + j, 12 + 2 * i + j, out_grad[:, j * BLK : j * BLK + BLK])
        settle(1)
        settle(0, 4)


def mid_layer(own, slot, rel, seq, x, attn, dy, vec, b1, gathered, chunk=512):
    rows = x.shape[0]
    wide = FF // D
    quarter = BLK // 4
    owners, slots = gathered.shape[0], gathered.shape[2]

    def part(i):
        return jnp.clip(i - 1, 0, wide - 1)

    def full(shape):
        return pl.BlockSpec(shape, lambda i, own, slot, rel, seq: (0,) * len(shape))

    def tile_at(block_of):
        return pl.BlockSpec(
            (1, 4, 1, quarter, BLK),
            lambda i, own, slot, rel, seq: (own[block_of(i)], 0, slot[block_of(i)], 0, 0),
        )

    row_spec = full((rows, D))
    strip = pl.BlockSpec((1, D), lambda i, own, slot, rel, seq: (0, part(i)))
    anywhere = pl.BlockSpec(memory_space=pl.ANY)
    place_shape = jax.ShapeDtypeStruct((2, owners, slots, quarter, BLK), LOW)
    return pl.pallas_call(
        functools.partial(mid_kernel, chunk=chunk),
        grid_spec=pltpu.PrefetchScalarGridSpec(
            num_scalar_prefetch=4,
            grid=(wide + 2,),
            in_specs=[row_spec, row_spec, row_spec, full(vec.shape), strip]
            + [tile_at(lambda i, b=b: b) for b in (12, 13, 14, 15)]
            + [tile_at(lambda i, n=n: 16 + 8 * (n // 2) + 2 * part(i) + n % 2) for n in range(4)]
            + [tile_at(lambda i, n=n: 32 + 4 * part(i) + n) for n in range(4)],
            out_specs=[row_spec, row_spec, row_spec, anywhere, anywhere, full((8, D)), strip],
            scratch_shapes=[
                pltpu.VMEM((rows, D), F32),
                pltpu.VMEM((rows, D), LOW),
                pltpu.VMEM((rows, D), F32),
                pltpu.VMEM((rows, D), F32),
                pltpu.VMEM((D, D), LOW),
                pltpu.VMEM((D, D), LOW),
                pltpu.VMEM((2, 8, 4, quarter, BLK), LOW),
                pltpu.SemaphoreType.DMA((2, 8, 4)),
            ],
        ),
        out_shape=[
            jax.ShapeDtypeStruct((rows, D), LOW),
            jax.ShapeDtypeStruct((rows, D), F32),
            jax.ShapeDtypeStruct((rows, D), LOW),
            place_shape,
            place_shape,
            jax.ShapeDtypeStruct((8, D), F32),
            jax.ShapeDtypeStruct((1, FF), F32),
        ],
        compiler_params=params(60),
        name="mid",
    )(own, slot, rel, seq, x, attn, dy, vec, b1, *([gathered] * 12))


def d_columns(step, grads, work):
    def both(n):
        return jnp.concatenate([grads[n][...], grads[5 + n][...]], axis=1)

    @pl.when(step == 0)
    def _():
        work(both(0))

    for n in (1, 3):

        @pl.when(step == (n + 1) // 2)
        def _():
            work((both(n).astype(F32) + both(n + 1).astype(F32)).astype(LOW))


def qkv_grad_kernel(seq, a_ref, *refs):
    grads, (keep, send, cols_ref, stage) = refs[:10], refs[10:]
    quarter = BLK // 4

    def work(d_cols):
        cols_ref[...] = jnp.sum(d_cols.astype(F32), axis=0, keepdims=True)
        for i in range(2):
            stage[...] = dot(a_ref[:, i * BLK : i * BLK + BLK], d_cols, 0, 0).astype(LOW)
            for rel_core, out in enumerate((keep, send)):
                for rel_x in range(2):
                    start = pl.multiple_of(quarter_at(seq[0], rel_core, rel_x) * quarter, quarter)
                    for j in range(2):
                        out[rel_x, i, j] = stage[pl.ds(start, quarter), j * BLK : j * BLK + BLK]

    d_columns(pl.program_id(0), grads, work)


def qkv_grad(seq, normed, halves):
    rows = normed.shape[0]
    quarter = BLK // 4
    tile_out = pl.BlockSpec((2, 2, 2, quarter, BLK), lambda i, seq: (0, 0, i, 0, 0))
    shape = jax.ShapeDtypeStruct((2, 2, 6, quarter, BLK), LOW)
    return pl.pallas_call(
        qkv_grad_kernel,
        grid_spec=pltpu.PrefetchScalarGridSpec(
            num_scalar_prefetch=1,
            grid=(3,),
            in_specs=[pl.BlockSpec((rows, D), lambda i, seq: (0, 0))]
            + [pl.BlockSpec((rows, BLK), lambda i, seq: (0, 0))] * 10,
            out_specs=[tile_out, tile_out, pl.BlockSpec((1, D), lambda i, seq: (0, i))],
            scratch_shapes=[pltpu.VMEM((BLK, D), LOW)],
        ),
        out_shape=[shape, shape, jax.ShapeDtypeStruct((1, 3 * D), F32)],
        compiler_params=params(48),
        name="qkv_grad",
    )(seq, normed, *halves[0], *halves[1])


def qkv_bwd_kernel(own, slot, x_ref, dmid_ref, vec_ref, *refs):
    grads, tiles, (dx_ref, sums_ref, acc, held) = refs[:10], refs[10:14], refs[14:]
    step = pl.program_id(0)

    @pl.when(step == 0)
    def _():
        acc[...] = jnp.zeros_like(acc)

    def work(d_cols):
        acc[...] += dot(d_cols, square(tiles, held), 1, 1)

    d_columns(step, grads, work)

    @pl.when(step == 2)
    def _():
        hat, rstd = norm_parts(x_ref[...].astype(F32))
        grad = acc[...]
        sums_ref[0:1, :] = jnp.sum(hat * grad, axis=0, keepdims=True)
        sums_ref[1:2, :] = jnp.sum(grad, axis=0, keepdims=True)
        sums_ref[2:8, :] = jnp.zeros((6, D), F32)
        dx_ref[...] = (dmid_ref[...] + norm_back(grad * vec_ref[0:1, :], hat, rstd)).astype(LOW)


def qkv_backward(own, slot, x, d_mid, vec, halves, gathered):
    rows = x.shape[0]
    row_spec = full_spec((rows, D))
    return pl.pallas_call(
        qkv_bwd_kernel,
        grid_spec=pltpu.PrefetchScalarGridSpec(
            num_scalar_prefetch=2,
            grid=(3,),
            in_specs=[row_spec, row_spec, full_spec(vec.shape)]
            + [full_spec((rows, BLK))] * 10
            + qkv_tiles(),
            out_specs=[row_spec, full_spec((8, D))],
            scratch_shapes=[pltpu.VMEM((rows, D), F32), pltpu.VMEM((D, D), LOW)],
        ),
        out_shape=[jax.ShapeDtypeStruct((rows, D), LOW), jax.ShapeDtypeStruct((8, D), F32)],
        compiler_params=params(60),
        name="qkv_bwd",
    )(own, slot, x, d_mid, vec, *halves[0], *halves[1], *([gathered] * 4))


def eliminate(blocks):
    count, size = len(blocks), blocks[0].shape[0]
    batch = min(count, 6)
    lane = lanes((1, 8, size))
    sub = lax.broadcasted_iota(jnp.int32, (1, 8, size), 1)
    wide_lane = lanes((size, size))
    shape = (batch, 8, size)

    def group(g, carry):
        base = pl.multiple_of(8 * g, 8)
        for at in range(0, count, batch):
            some = blocks[at : at + batch]
            slab = jnp.stack([y[pl.ds(base, 8), :] for y in some], axis=0)
            rolled = jnp.stack([pltpu.roll(slab[b], size - base, 1) for b in range(batch)], axis=0)
            columns = [jnp.broadcast_to(rolled[:, :, k : k + 1], shape) for k in range(8)]
            inside = (lane >= base) & (lane < base + 8)
            rows = jnp.where(inside, jnp.where(lane - base == sub, 1.0, 0.0), slab)
            scale = jnp.zeros(shape, F32)
            for j in range(8):
                inv_root = lax.rsqrt(jnp.broadcast_to(columns[j][:, j : j + 1, :], shape))
                scale = jnp.where(sub == j, inv_root, scale)
                factor = jnp.where(sub > j, columns[j] * (inv_root * inv_root), 0.0)
                rows = rows - factor * jnp.broadcast_to(rows[:, j : j + 1, :], shape)
                for k in range(j + 1, 8):
                    columns[k] = columns[k] - factor * jnp.broadcast_to(columns[k][:, j : j + 1, :], shape)
            rows = rows * scale
            passed = (wide_lane >= base) & (wide_lane < base + 8)
            for b, y in enumerate(some):
                high, mid, low = three_parts(rows[b])
                first = jnp.concatenate([high, high, mid, high, low, mid], axis=0)
                first = jnp.where(jnp.broadcast_to(lane[0, :1] >= base + 8, first.shape), first, 0.0)
                second = jnp.concatenate([high, mid, high, low, high, mid], axis=0)
                update = dot(first.astype(LOW), second.astype(LOW), 0, 0)
                y[...] = jnp.where(passed, 0.0, y[...]) - update
                y[pl.ds(base, 8), :] = rows[b]
        return carry

    lax.fori_loop(0, size // 8, group, 0)


def stats_kernel(ls_ref, rs_ref, lb_ref, rb_ref, left, right):
    for stats, basis, out in ((ls_ref, lb_ref, left), (rs_ref, rb_ref, right)):
        out[0] = BETA_STAT * dot_parts(low_parts(stats[0], 3), low_parts(basis[0], 3), 1, 0, 3)


def stats_product(left_stats, right_stats, left_basis, right_basis):
    count = left_stats.shape[0]
    block_spec = pl.BlockSpec((1, BLK, BLK), lambda i: (i, 0, 0))
    return pl.pallas_call(
        stats_kernel,
        grid=(count,),
        in_specs=[block_spec] * 4,
        out_specs=[block_spec] * 2,
        out_shape=[jax.ShapeDtypeStruct((count, BLK, BLK), F32)] * 2,
        compiler_params=params(32),
        name="stats",
    )(left_stats, right_stats, left_basis, right_basis)


def soap_kernel(
    seq_ref, g0, g1, g2, g3, w_ref, one_ref, two_ref, ls_ref, rs_ref, lb_ref, rb_ref, lp_ref, rp_ref,
    grad_ref, w_out, one_out, two_out, ls_out, rs_out, lb_out, rb_out,
    grad_s, gram, work, *inv,
):
    step = pl.program_id(0)
    slots = pl.num_programs(0)
    count = lb_out.shape[0]
    quarter = BLK // 4
    for piece, flip in ((g0, 0), (g1, 2), (g2, 1), (g3, 3)):
        start = pl.multiple_of((seq_ref[0] ^ flip) * quarter, quarter)
        grad_s[pl.ds(start, quarter), :] = piece[0]
    grad = grad_s[...]
    grad_ref[0] = grad.astype(F32)
    left, right = low_parts(lb_ref[0], 2), low_parts(rb_ref[0], 2)
    left_grad = dot_parts(left, [grad], 0, 0, 2)
    grad_right = dot_parts([grad], right, 1, 0, 2)
    rotated = dot(left_grad.astype(LOW), right[0], 1, 0)
    one = BETA_ONE * one_ref[0] + (1.0 - BETA_ONE) * rotated
    two = BETA_TWO * two_ref[0] + (1.0 - BETA_TWO) * rotated * rotated
    one_out[0] = one
    two_out[0] = two
    scaled = (one / (1.0 - BETA_ONE**STEP)) / (jnp.sqrt(two / (1.0 - BETA_TWO**STEP)) + ADAM_EPS)
    back = dot(dot(left[0], scaled.astype(LOW), 1, 0).astype(LOW), right[0], 1, 1)
    w_out[0] = w_ref[0] - RATE_MATRIX * (back + DECAY_RATE * w_ref[0])
    ls_out[0] = BETA_STAT * ls_ref[0] + (1.0 - BETA_STAT) * dot(grad, grad, 1, 1)
    rs_out[0] = BETA_STAT * rs_ref[0] + (1.0 - BETA_STAT) * dot(grad, grad, 0, 0)
    left_new = lp_ref[0] + (1.0 - BETA_STAT) * dot_parts([grad], low_parts(left_grad, 2), 1, 1, 2)
    right_new = rp_ref[0] + (1.0 - BETA_STAT) * dot_parts([grad], low_parts(grad_right, 2), 0, 0, 2)
    for side, product in enumerate((left_new, right_new)):
        at = side * count + step
        work[at] = product
        parts = low_parts(product, 3)
        for p in range(BLK // 128):
            c, on = slice(128 * p, 128 * p + 128), slice(128 * p, BLK)
            gram[at, c, on] = dot_parts([part[:, c] for part in parts], [part[:, on] for part in parts], 0, 0, 3)

    @pl.when(step == slots - 1)
    def _():
        for p in range(BLK // 128):
            c = slice(128 * p, 128 * p + 128)
            rest = slice(128 * p + 128, BLK)
            for b, block in enumerate(inv):
                block[...] = gram[b, c, c]
            eliminate(inv)
            for b, block in enumerate(inv):
                gram[b, c, c] = block[...]

            def solve(b, carry, out):
                at = b + (count if out is rb_out else 0)
                factor = low_parts(gram[at, c, c], 3)
                solved = dot_parts(low_parts(work[at, :, c], 2), factor, 1, 1, 2)
                out[b, :, c] = solved
                if p < BLK // 128 - 1:
                    upper = low_parts(dot_parts(factor, low_parts(gram[at, c, rest], 3), 1, 0, 3), 3)
                    work[at, :, rest] = work[at, :, rest] - dot_parts(low_parts(solved, 2), upper, 1, 0, 2)
                    gram[at, rest, rest] = gram[at, rest, rest] - dot_parts(upper, upper, 0, 0, 3)
                return carry

            lax.fori_loop(0, count, functools.partial(solve, out=lb_out), 0)
            lax.fori_loop(0, count, functools.partial(solve, out=rb_out), 0)


def soap_update(seq, pieces, state, products):
    count = state[0].shape[0]
    piece_spec = pl.BlockSpec((1, BLK // 4, BLK), lambda i, s: (i, 0, 0))
    block_spec = pl.BlockSpec((1, BLK, BLK), lambda i, s: (i, 0, 0))
    whole_spec = pl.BlockSpec((count, BLK, BLK), lambda i, s: (0, 0, 0))
    shape = jax.ShapeDtypeStruct((count, BLK, BLK), F32)
    return pl.pallas_call(
        soap_kernel,
        grid_spec=pltpu.PrefetchScalarGridSpec(
            num_scalar_prefetch=1,
            grid=(count,),
            in_specs=[piece_spec] * 4 + [block_spec] * 9,
            out_specs=[block_spec] * 6 + [whole_spec] * 2,
            scratch_shapes=[
                pltpu.VMEM((BLK, BLK), LOW),
                pltpu.VMEM((2 * count, BLK, BLK), F32),
                pltpu.VMEM((2 * count, BLK, BLK), F32),
            ]
            + [pltpu.VMEM((128, 128), F32)] * (2 * count),
        ),
        out_shape=[shape] * 8,
        compiler_params=params(60),
        name="soap",
    )(seq, *pieces, *state, *products)


def split_kernel(dp, a_ref, b_ref, *outs):
    for k, out in enumerate(outs):
        out[...] = (a_ref[dp[0] ^ k].astype(F32) + b_ref[dp[0] ^ k].astype(F32)).astype(LOW)


def split_sum(dp, a, b):
    parts = a.shape[0]
    shape = a.shape[1:]
    return pl.pallas_call(
        split_kernel,
        grid_spec=pltpu.PrefetchScalarGridSpec(
            num_scalar_prefetch=1,
            grid=(1,),
            in_specs=[pl.BlockSpec(a.shape, lambda i, dp: (0,) * a.ndim)] * 2,
            out_specs=[pl.BlockSpec(shape, lambda i, dp: (0,) * len(shape))] * parts,
        ),
        out_shape=[jax.ShapeDtypeStruct(shape, LOW)] * parts,
        compiler_params=params(32),
        name="split_sum",
    )(dp, a, b)


def choose_kernel(dp, source, *refs):
    parts, early, out, held = refs[:-3], refs[-3], refs[-2], refs[-1]
    per, half = held.shape[1], held.shape[2]
    for k, part in enumerate(parts):
        held[k] = part[...]
    slots = out.shape[0]
    units = len(parts) * per

    def one(i, carry):
        block = source[i]

        @pl.when(2 * block >= units)
        def _():
            out[i] = early[i]

        @pl.when(2 * block < units)
        def _():
            for h in range(2):
                unit = 2 * block + h
                out[i, h * half : h * half + half] = held[lax.div(unit, per) ^ dp[0], lax.rem(unit, per)]

        return carry

    lax.fori_loop(0, slots, one, 0)


def choose(dp, source, parts, early):
    return pl.pallas_call(
        choose_kernel,
        grid_spec=pltpu.PrefetchScalarGridSpec(
            num_scalar_prefetch=2,
            grid=(1,),
            in_specs=[pl.BlockSpec(parts[0].shape, lambda i, dp, src: (0, 0, 0))] * len(parts)
            + [pl.BlockSpec(early.shape, lambda i, dp, src: (0, 0, 0))],
            out_specs=pl.BlockSpec(early.shape, lambda i, dp, src: (0, 0, 0)),
            scratch_shapes=[pltpu.VMEM((len(parts),) + parts[0].shape, LOW)],
        ),
        out_shape=jax.ShapeDtypeStruct(early.shape, LOW),
        compiler_params=params(32),
        name="choose",
    )(dp, source, *parts, early)


def swap(x, axis, bit):
    size = lax.axis_size(axis)
    return lax.ppermute(x, axis, [(i, i ^ bit) for i in range(size)])


def add_low(a, b):
    return (a.astype(F32) + b.astype(F32)).astype(LOW)


class Halving:
    def __init__(self, kept, got, names):
        self.kept, self.got, self.names = kept, got, list(names)

    def take(self, name, index):
        at = (slice(None),) * self.names.index(name) + (index,)
        return add_low(self.kept[at], self.got[at])

    def send(self, name):
        sent, kept = self.take(name, 1), self.take(name, 0)
        self.names.remove(name)
        self.kept = kept
        self.sent, self.name = sent, name
        return sent

    def receive(self, sent):
        axis, bit = ("seq", 2) if self.name == "x" else ("dp", 2**self.name)
        self.got = swap(sent, axis, bit)

    def total(self):
        return add_low(self.kept, self.got)


def quarters(piece):
    across = swap(piece, "seq", 2)
    beside = swap(jnp.stack([piece, across]), "seq", 1)
    return piece, across, beside[0], beside[1]


def block_places(owners, owner_count, slot_count):
    block_count = owners.shape[0]
    ids = jnp.arange(block_count, dtype=jnp.int32)
    earlier = (owners[:, None] == owners[None, :]) & (ids[None, :] < ids[:, None])
    slots = jnp.sum(earlier.astype(jnp.int32), axis=1)
    places = owners * slot_count + slots
    matched = places[None, :] == jnp.arange(owner_count * slot_count, dtype=jnp.int32)[:, None]
    missing = 1 - jnp.any(matched, axis=1).astype(jnp.int32)
    sources = jnp.sum(jnp.where(matched, ids[None, :], 0), axis=1) + block_count * missing
    return slots, sources


def adam_vectors(gradient, vec, first_mom, second_mom):
    first_mom = BETA_ONE * first_mom + (1.0 - BETA_ONE) * gradient
    second_mom = BETA_TWO * second_mom + (1.0 - BETA_TWO) * gradient * gradient
    step_size = (first_mom / (1.0 - BETA_ONE**STEP)) / (
        jnp.sqrt(second_mom / (1.0 - BETA_TWO**STEP)) + ADAM_EPS
    )
    return first_mom, second_mom, vec - RATE_VECTOR * step_size


def on_device(
    tokens, cotangent, lengths, patch_mask, owners, master, moment_one, moment_two,
    left_stats, right_stats, left_basis, right_basis, vec, vec_one, vec_two,
):
    owner_count = lax.axis_size("dp")
    slot_count = master.shape[0]
    quarter = BLK // 4
    seq_id = lax.axis_index("seq").astype(jnp.int32)
    dp_id = lax.axis_index("dp").astype(jnp.int32)
    core, chip = seq_id % 2, seq_id // 2
    part_len = tokens.shape[1]
    slots, sources = block_places(owners, owner_count, slot_count)
    first_blocks = 3 * (D // BLK) ** 2

    mine = lax.dynamic_index_in_dim(
        master.reshape(slot_count, 4, quarter, BLK), seq_id, 1, keepdims=False
    ).astype(LOW)
    gathered = lax.all_gather(mine, AXES, axis=0, tiled=False).reshape(
        owner_count, 4, slot_count, quarter, BLK
    )

    products = stats_product(left_stats, right_stats, left_basis, right_basis)

    pair = jnp.stack([tokens, cotangent])
    kept = lax.dynamic_index_in_dim(pair, chip, 1, keepdims=False)
    got = swap(lax.dynamic_index_in_dim(pair, 1 - chip, 1, keepdims=False), "seq", 2)
    x = jnp.concatenate([kept[0], got[0]], axis=0)
    dy = jnp.concatenate([kept[1], got[1]], axis=0)

    def to_positions(mine, other):
        return jnp.where(chip == 0, jnp.stack([mine, other]), jnp.stack([other, mine]))

    positions = jnp.arange(patch_mask.shape[-1], dtype=jnp.int32)
    live = (positions[None, :] < lengths[:, None]) & ((patch_mask == 1) | (positions[None, :] == 0))
    live = lax.dynamic_index_in_dim(live, chip, 0, keepdims=False).reshape(4, part_len)
    order = seq_id ^ jnp.array([0, 2, 1, 3], jnp.int32)
    fill = jnp.where(jnp.take(live, order, axis=0).reshape(-1), 0.0, NEG_FILL).astype(LOW)
    fill = jnp.broadcast_to(fill[:, None], (fill.shape[0], 128))

    bias = jnp.concatenate([vec[4], jnp.zeros_like(vec[4]), vec[5]])[None, :]
    gathered, products = lax.optimization_barrier((gathered, products))
    q, kv, normed = qkv_forward(owners, slots, x, vec, bias, gathered)
    other = swap(kv, "seq", 1)
    attn, lse = attn_forward(q, kv, other, fill)
    b1 = vec[8:].reshape(1, FF)
    seq_of, dp_of = seq_id.reshape(1), dp_id.reshape(1)
    result, d_mid, d_attn, keep, send, sums_two, bias_grad = mid_layer(
        owners, slots, owners ^ dp_id, seq_of, x, attn, dy, vec, b1, gathered
    )
    result_other = swap(result[part_len:], "seq", 2)

    bits = owner_count.bit_length() - 1
    if slot_count % 3 == 0 and bits == 3:
        plans = [["x", 0, 1, 2], [0, 1, "x", 2], [1, "x", 0, 2]]
    else:
        plans = [["x"] + list(range(bits))]
    per = slot_count // len(plans)
    names = ["x"] + list(range(bits))[::-1]
    shape = (2,) * (1 + bits) + keep.shape[2:]
    keep, got = keep.reshape(shape), swap(send, "seq", 1).reshape(shape)
    groups = [
        Halving(keep[..., per * g : per * g + per, :, :], got, names) for g in range(len(plans))
    ]
    guard = fill

    def advance(step, guard):
        if step == 0:
            for g, group in enumerate(groups):
                group.got = group.got[..., per * g : per * g + per, :, :]
        sent = [group.send(plan[step]) for group, plan in zip(groups, plans, strict=True)]
        *sent, guard = lax.optimization_barrier((*sent, guard))
        for group, array in zip(groups, sent, strict=True):
            group.receive(array)
        return guard

    halves = []
    half_pairs = D // 128 // 2
    taken = 0
    for half in range(2):
        before, first = [], half * half_pairs
        for place, count in ((0, 2), (2, 1)):
            if (half or place) and (half, place) != (1, 0):
                guard = advance(taken, guard)
                taken += 1
            before = attn_backward(
                q, kv, other, guard, attn, lse, d_attn, first + place, count, place, half_pairs, before
            )
            got, before, result_other = lax.optimization_barrier(
                ([group.got for group in groups], before, result_other)
            )
            for group, array in zip(groups, got, strict=True):
                group.got = array
        dq, dk, dv, sent_k, sent_v = before
        halves.append((dq, dk, swap(sent_k, "seq", 1), dv, swap(sent_v, "seq", 1)))
    normed = advance(taken, normed)
    taken += 1
    late_keep, late_send, cols = qkv_grad(seq_of, normed, halves)
    late_shape = (2, -1, quarter, BLK)
    late = Halving(late_keep.reshape(late_shape), swap(late_send.reshape(late_shape), "seq", 1), ["x"])
    late.receive(late.send("x"))
    d_x, sums_one = qkv_backward(owners, slots, x, d_mid, vec, halves, gathered)
    got, late.got, d_x = lax.optimization_barrier(([group.got for group in groups], late.got, d_x))
    for group, array in zip(groups, got, strict=True):
        group.got = array
    d_x_other = swap(d_x[part_len:], "seq", 2)
    while taken < len(names):
        advance(taken, fill)
        taken += 1
    early = jnp.concatenate([group.total() for group in groups], axis=0)

    mine_from = lax.dynamic_slice_in_dim(sources, dp_id * slot_count, slot_count)
    if 2 * first_blocks % owner_count == 0:
        unit = (owner_count, 2 * first_blocks // owner_count, quarter // 2, BLK)
        parts = split_sum(dp_of, late.kept.reshape(unit), late.got.reshape(unit))
        parts = [parts[0]] + [swap(part, "dp", k) for k, part in enumerate(parts) if k]
        total = sum(part.astype(F32) for part in parts).astype(LOW)
        parts = [total] + [swap(total, "dp", k) for k in range(1, owner_count)]
        piece = choose(dp_of, mine_from, parts, early)
    else:
        tiles = jnp.concatenate([late.total(), jnp.zeros((1, quarter, BLK), LOW)], axis=0)
        at = sources.reshape(owner_count, slot_count)[dp_id ^ jnp.arange(owner_count)]
        tiles = jnp.take(tiles, jnp.minimum(at, first_blocks).reshape(-1), axis=0)
        tiles = tiles.reshape((2,) * bits + (slot_count, quarter, BLK))
        owned = Halving(tiles, jnp.zeros_like(tiles), names[1:])
        for bit in range(bits):
            owned.receive(owned.send(bit))
        piece = jnp.where((mine_from < first_blocks)[:, None, None], owned.total(), early)
    state = (master, moment_one, moment_two, left_stats, right_stats, left_basis, right_basis)
    piece = jnp.where((mine_from < owners.shape[0])[:, None, None], piece, jnp.zeros_like(piece))
    updates = soap_update(seq_of, quarters(piece), state, products)

    vec_grad = jnp.concatenate(
        [
            sums_one[0:2],
            sums_two[0:2],
            cols[:, :D],
            cols[:, 2 * D :],
            sums_two[2:4],
            bias_grad.reshape(-1, D),
        ],
        axis=0,
    )
    vec_parts = lax.all_gather(vec_grad, AXES, axis=0, tiled=False)
    updates, vec_parts, d_x, d_x_other, result, result_other = lax.optimization_barrier(
        (updates, vec_parts, d_x, d_x_other, result, result_other)
    )
    output = to_positions(result[:part_len], result_other)
    d_tokens = to_positions(d_x[:part_len], d_x_other)
    vec_total = jnp.sum(vec_parts, axis=0)
    vec_first, vec_second, vec_next = adam_vectors(vec_total, vec, vec_one, vec_two)
    grad_blocks, w_new, one_new, two_new, ls_new, rs_new, lb_new, rb_new = updates
    return (
        output, d_tokens, grad_blocks, w_new, one_new, two_new, ls_new, rs_new, lb_new, rb_new,
        vec_first, vec_second, vec_next,
    )


def solution(mesh):
    rows, blocks, whole = P("dp", "seq", None), P("dp", None, None), P()
    return jax.shard_map(
        on_device,
        mesh=mesh,
        in_specs=(rows, rows, P("dp"), P("dp", None), whole) + (blocks,) * 7 + (whole,) * 3,
        out_specs=(rows, rows) + (blocks,) * 8 + (whole,) * 3,
        check_vma=False,
    )
```

```python
import functools

import jax
import jax.numpy as jnp
from jax import lax
from jax.experimental import pallas as pl
from jax.experimental.pallas import tpu as pltpu
from jax.sharding import PartitionSpec as P

D = 768
FF = 3072
BLK = 384
STEP = 10

NORM_EPS = 1e-06
NEG_FILL = -1000000000.0
BETA_ONE = 0.9
BETA_TWO = 0.999
BETA_STAT = 0.95
RATE_MATRIX = 0.1
RATE_VECTOR = 0.3
DECAY_RATE = 0.01
ADAM_EPS = 1e-08

LOW = jnp.bfloat16
F32 = jnp.float32
AXES = ("dp", "seq")
MIB = 2**20

TAIL_P = 0.24
TAIL_C = (
    0.09575380798443668,
    0.09552183543465394,
    0.09284136585084933,
    0.06338567653857548,
    0.11841694922211018,
    -0.06574016740998187,
    0.15281935057715396,
    -0.052998628523732765,
)


def dot(a, b, ca, cb):
    return lax.dot_general(a, b, (((ca,), (cb,)), ((), ())), preferred_element_type=F32)


def lanes(shape):
    return lax.broadcasted_iota(jnp.int32, shape, len(shape) - 1)


def gelu_pair(x):
    u = jnp.abs(x)
    t = 1.0 / (1.0 + TAIL_P * u)
    poly = TAIL_C[-1]
    for coeff in TAIL_C[-2::-1]:
        poly = poly * t + coeff
    expo = jnp.exp(-0.5 * u * u)
    tail = poly * t * expo
    cdf = jnp.where(x < 0, tail, 1.0 - tail)
    return x * cdf, cdf + x * (expo * 0.3989422804014327)


def norm_parts(rows):
    center = rows - jnp.mean(rows, axis=-1, keepdims=True)
    rstd = lax.rsqrt(jnp.mean(center * center, axis=-1, keepdims=True) + NORM_EPS)
    return center * rstd, rstd


def norm_back(grad, hat, rstd):
    return rstd * (
        grad
        - jnp.mean(grad, axis=-1, keepdims=True)
        - hat * jnp.mean(grad * hat, axis=-1, keepdims=True)
    )


def params(limit):
    return pltpu.CompilerParams(vmem_limit_bytes=limit * MIB)


def tile_spec(block_of):
    return pl.BlockSpec(
        (1, 4, 1, BLK // 4, BLK),
        lambda i, own, slot: (own[block_of(i)], 0, slot[block_of(i)], 0, 0),
    )


def tile(ref):
    return ref[...].reshape(BLK, BLK)


def full_spec(shape):
    return pl.BlockSpec(shape, lambda i, own, slot: (0,) * len(shape))


def quarter_at(seq, rel_core, rel_x):
    return seq ^ (2 * rel_x + rel_core)


def square(tiles, held):
    for i in range(2):
        for j in range(2):
            held[i * BLK : i * BLK + BLK, j * BLK : j * BLK + BLK] = tile(tiles[2 * i + j])
    return held[...]


def qkv_kernel(own, slot, x_ref, vec_ref, bias_ref, t00, t01, t10, t11, q_ref, kv_ref, a_ref, held):
    @pl.when(pl.program_id(0) == 0)
    def _():
        hat, _ = norm_parts(x_ref[...].astype(F32))
        a_ref[...] = (hat * vec_ref[0:1, :] + vec_ref[1:2, :]).astype(LOW)

    low = (dot(a_ref[...], square((t00, t01, t10, t11), held), 1, 0) + bias_ref[...]).astype(LOW)

    @pl.when(pl.program_id(0) == 0)
    def _():
        q_ref[...] = low

    @pl.when(pl.program_id(0) > 0)
    def _():
        kv_ref[...] = low


def qkv_tiles():
    return [tile_spec(lambda i, n=n: 6 * (n // 2) + 2 * i + n % 2) for n in range(4)]


def qkv_forward(own, slot, x, vec, bias, gathered):
    rows = x.shape[0]
    return pl.pallas_call(
        qkv_kernel,
        grid_spec=pltpu.PrefetchScalarGridSpec(
            num_scalar_prefetch=2,
            grid=(3,),
            in_specs=[
                full_spec((rows, D)),
                full_spec(vec.shape),
                pl.BlockSpec((1, D), lambda i, own, slot: (0, i)),
            ]
            + qkv_tiles(),
            out_specs=[
                full_spec((rows, D)),
                pl.BlockSpec((rows, D), lambda i, own, slot: (0, jnp.maximum(i - 1, 0))),
                full_spec((rows, D)),
            ],
            scratch_shapes=[pltpu.VMEM((D, D), LOW)],
        ),
        out_shape=[
            jax.ShapeDtypeStruct((rows, D), LOW),
            jax.ShapeDtypeStruct((rows, 2 * D), LOW),
            jax.ShapeDtypeStruct((rows, D), LOW),
        ],
        compiler_params=params(48),
        name="qkv",
    )(own, slot, x, vec, bias, *([gathered] * 4))


def attn_fwd_kernel(q_ref, k1, v1, k2, v2, bias_ref, o_ref, lse_ref, ka, kb, va, vb):
    rows = k1.shape[0]

    @pl.when(pl.program_id(1) == 0)
    def _():
        ln = lanes((rows, 128))
        for i, (k, v) in enumerate(((k1, v1), (k2, v2))):
            r = slice(i * rows, i * rows + rows)
            keys, values, bias = k[...], v[...], bias_ref[r, :]
            one = jnp.ones_like(values)
            ka[r, :] = jnp.where(ln == 64, bias, keys)
            kb[r, :] = jnp.where(ln == 0, bias, keys)
            va[r, :] = jnp.where(ln < 64, values, one)
            vb[r, :] = jnp.where(ln < 64, one, values)

    q = q_ref[...] * jnp.asarray(0.125, LOW)
    ln = lanes(q.shape)
    one, zero = jnp.ones_like(q), jnp.zeros_like(q)
    qa = jnp.where(ln < 64, q, jnp.where(ln == 64, one, zero))
    qb = jnp.where(ln < 64, jnp.where(ln == 0, one, zero), q)
    outs, tops = [], []
    for query, keys, values in ((qa, ka, va), (qb, kb, vb)):
        logits = dot(query, keys[...], 1, 1)
        top = jnp.max(logits, axis=1, keepdims=True)
        expo = jnp.exp(logits - top).astype(LOW)
        outs.append(dot(expo, values[...], 1, 0))
        tops.append(top)
    total = jnp.where(ln < 64, outs[1], outs[0])
    attended = jnp.where(ln < 64, outs[0], outs[1])
    o_ref[...] = (attended / pltpu.roll(total, 64, 1)).astype(LOW)
    lse_ref[...] = jnp.where(ln < 64, tops[1], tops[0]) + jnp.log(total)


def attn_forward(q, kv, other, bias, q_rows=256):
    rows, pairs = q.shape[0], D // 128
    keys = 2 * rows
    q_spec = pl.BlockSpec((q_rows, 128), lambda p, i: (i, p))
    return pl.pallas_call(
        attn_fwd_kernel,
        grid=(pairs, rows // q_rows),
        in_specs=[
            q_spec,
            pl.BlockSpec((rows, 128), lambda p, i: (0, p)),
            pl.BlockSpec((rows, 128), lambda p, i: (0, pairs + p)),
            pl.BlockSpec((rows, 128), lambda p, i: (0, p)),
            pl.BlockSpec((rows, 128), lambda p, i: (0, pairs + p)),
            pl.BlockSpec((keys, 128), lambda p, i: (0, 0)),
        ],
        out_specs=[q_spec, q_spec],
        out_shape=[
            jax.ShapeDtypeStruct((rows, D), LOW),
            jax.ShapeDtypeStruct((rows, D), F32),
        ],
        scratch_shapes=[pltpu.VMEM((keys, 128), LOW)] * 4,
        compiler_params=params(48),
        name="attn_fwd",
    )(q, kv, kv, other, other, bias)


def three_parts(x):
    high = x.astype(LOW).astype(F32)
    rest = x - high
    mid = rest.astype(LOW).astype(F32)
    return high, mid, rest - mid


def low_parts(x, count):
    found = []
    for _ in range(count):
        part = x.astype(LOW)
        found.append(part)
        x = x - part.astype(F32)
    return found


def dot_parts(a, b, ca, cb, order):
    pairs = [(i, j) for i in range(len(a)) for j in range(len(b)) if i + j < order]
    a = jnp.concatenate([a[i] for i, _ in pairs], axis=ca)
    b = jnp.concatenate([b[j] for _, j in pairs], axis=cb)
    return dot(a, b, ca, cb)


def with_spare(x, spare, value, one, first):
    ln = lanes(x.shape)
    high, mid, low = three_parts(value)
    filled = jnp.where(ln == first + 3, one, 0.0)
    for i, part in enumerate((high, mid, low)):
        filled = jnp.where(ln == first + i, part, filled)
    return jnp.where(spare, filled, x).astype(LOW)


def attn_bwd_kernel(
    q_ref, k1, v1, k2, v2, bias_ref, o_ref, lse_ref, do_ref,
    dq_ref, dk1, dv1, dk2, dv2, ka, kb, va, vb, kt, dk, dv, *, chunk,
):
    rows = k1.shape[0]

    @pl.when(pl.program_id(1) == 0)
    def _():
        ln = lanes((rows, 128))
        for i, (k, v) in enumerate(((k1, v1), (k2, v2))):
            r = slice(i * rows, i * rows + rows)
            keys, values, bias = k[...], v[...], bias_ref[r, :]
            one, zero = jnp.ones_like(values), jnp.zeros_like(values)
            ka[r, :] = jnp.where(ln < 64, keys, jnp.where(ln < 67, one, jnp.where(ln == 67, bias, zero)))
            kb[r, :] = jnp.where(ln >= 64, keys, jnp.where(ln < 3, one, jnp.where(ln == 3, bias, zero)))
            va[r, :] = jnp.where(ln < 64, values, jnp.where(ln < 67, one, zero))
            vb[r, :] = jnp.where(ln >= 64, values, jnp.where(ln < 3, one, zero))
            kt[:, r] = keys.T
        dk[...] = jnp.zeros_like(dk)
        dv[...] = jnp.zeros_like(dv)

    q = q_ref[...].astype(F32) * 0.125
    left = lanes(q.shape) < 64
    grad = do_ref[...].astype(F32)
    prod = grad * o_ref[...].astype(F32)
    sum_a = jnp.sum(jnp.where(left, prod, 0.0), axis=1, keepdims=True)
    sum_b = jnp.sum(jnp.where(left, 0.0, prod), axis=1, keepdims=True)
    delta = jnp.where(left, sum_b, sum_a)
    lse = lse_ref[...]
    zero = jnp.zeros_like(q)
    heads = (
        (
            with_spare(q, ~left, -lse, 1.0, 64), with_spare(grad, ~left, -delta, 0.0, 64), ka, va,
            jnp.where(left, q, zero).astype(LOW), jnp.where(left, grad, zero).astype(LOW),
        ),
        (
            with_spare(q, left, -lse, 1.0, 0), with_spare(grad, left, -delta, 0.0, 0), kb, vb,
            jnp.where(left, zero, q).astype(LOW), jnp.where(left, zero, grad).astype(LOW),
        ),
    )
    d_query = [jnp.zeros((64, q.shape[0]), F32)] * 2
    for c in range(2 * rows // chunk):
        r = slice(c * chunk, c * chunk + chunk)
        dv_c, dk_c = dv[r, :], dk[r, :]
        for h, (q_aug, g_aug, keys, values, q_only, g_only) in enumerate(heads):
            probs = jnp.exp(dot(keys[r, :], q_aug, 1, 1))
            d_logits = (probs * dot(values[r, :], g_aug, 1, 1)).astype(LOW)
            dv_c = dv_c + dot(probs.astype(LOW), g_only, 1, 0)
            dk_c = dk_c + dot(d_logits, q_only, 1, 0)
            d_query[h] = d_query[h] + dot(kt[64 * h : 64 * h + 64, r], d_logits, 1, 0)
        dv[r, :] = dv_c
        dk[r, :] = dk_c
    dq_ref[...] = (jnp.concatenate(d_query, axis=0) * 0.125).T.astype(LOW)

    @pl.when(pl.program_id(1) == pl.num_programs(1) - 1)
    def _():
        dk1[...] = dk[:rows, :].astype(LOW)
        dk2[...] = dk[rows:, :].astype(LOW)
        dv1[...] = dv[:rows, :].astype(LOW)
        dv2[...] = dv[rows:, :].astype(LOW)


def attn_backward(q, kv, other, bias, attn, lse, d_attn, first, count, place, total, before, q_rows=512, chunk=1024):
    rows, pairs = q.shape[0], D // 128
    keys = 2 * rows
    out_spec = pl.BlockSpec((q_rows, 128), lambda p, i: (i, place + p))
    k_out = pl.BlockSpec((rows, 128), lambda p, i: (0, place + p))
    q_spec = pl.BlockSpec((q_rows, 128), lambda p, i: (i, first + p))
    k_spec = pl.BlockSpec((rows, 128), lambda p, i: (0, first + p))
    v_spec = pl.BlockSpec((rows, 128), lambda p, i: (0, pairs + first + p))

    def kernel(*refs):
        attn_bwd_kernel(*refs[:9], *refs[9 + len(before) :], chunk=chunk)

    return pl.pallas_call(
        kernel,
        grid=(count, rows // q_rows),
        in_specs=[
            q_spec, k_spec, v_spec, k_spec, v_spec, pl.BlockSpec((keys, 128), lambda p, i: (0, 0)),
            q_spec, q_spec, q_spec,
        ]
        + [pl.BlockSpec(memory_space=pl.ANY)] * len(before),
        out_specs=[out_spec, k_out, k_out, k_out, k_out],
        out_shape=[jax.ShapeDtypeStruct((rows, total * 128), LOW)] * 5,
        scratch_shapes=[pltpu.VMEM((keys, 128), LOW)] * 4
        + [pltpu.VMEM((128, keys), LOW)]
        + [pltpu.VMEM((keys, 128), F32)] * 2,
        input_output_aliases={9 + i: i for i in range(len(before))},
        compiler_params=params(56),
        name="attn_bwd",
    )(q, kv, kv, other, other, bias, attn, lse, d_attn, *before)


def mid_kernel(
    own, slot, rel, seq, x_ref, attn_ref, dy_ref, vec_ref, b1_ref, o00, o01, o10, o11, *refs, chunk):
    ups, downs = refs[:4], refs[4:8]
    (
        res_ref, dmid_ref, dattn_ref, keep, send, sums_ref, gb1_ref,
        mid, a2, acc, da2, up_s, down_s, stage, sems,
    ) = refs[8:]
    step = pl.program_id(0)
    last = pl.num_programs(0) - 1
    quarter = BLK // 4

    def copies(buf, i, block):
        found = []
        for rel_core, out in enumerate((keep, send)):
            for rel_x in range(2):
                found.append(
                    pltpu.make_async_copy(
                        stage.at[buf, i, quarter_at(seq[0], rel_core, rel_x)],
                        out.at[rel_x, rel[block], slot[block]],
                        sems.at[buf, i, 2 * rel_core + rel_x],
                    )
                )
        return found

    def put(buf, i, block, value):
        low = value.astype(LOW)
        for part in range(4):
            stage[buf, i, part] = low[part * quarter : part * quarter + quarter]
        for copy in copies(buf, i, block):
            copy.start()

    def settle(buf, count=8):
        for i in range(count):
            for copy in copies(buf, i, 0):
                copy.wait()

    @pl.when(step == 0)
    def _():
        mid[...] = (
            x_ref[...].astype(F32)
            + dot(attn_ref[...], square((o00, o01, o10, o11), up_s), 1, 0)
            + vec_ref[6:7, :]
        )
        hat, _ = norm_parts(mid[...])
        a2[...] = (hat * vec_ref[2:3, :] + vec_ref[3:4, :]).astype(LOW)
        acc[...] = jnp.zeros_like(acc)
        da2[...] = jnp.zeros_like(da2)

    @pl.when((step > 0) & (step < last))
    def _():
        rows = a2.shape[0]
        up, down = square(ups, up_s), square(downs, down_s)
        bias_grad = jnp.zeros((1, D), F32)
        acts, d_hids = [], []
        for c in range(rows // chunk):
            r = slice(c * chunk, c * chunk + chunk)
            act, slope = gelu_pair(dot(a2[r, :], up, 1, 0) + b1_ref[...])
            act = act.astype(LOW)
            d_hid = (dot(dy_ref[r, :], down, 1, 1) * slope).astype(LOW)
            acc[r, :] += dot(act, down, 1, 0)
            da2[r, :] += dot(d_hid, up, 1, 1)
            bias_grad = bias_grad + jnp.sum(d_hid.astype(F32), axis=0, keepdims=True)
            acts.append(act)
            d_hids.append(d_hid)
        gb1_ref[...] = bias_grad
        act = jnp.concatenate(acts, axis=0)
        d_hid = jnp.concatenate(d_hids, axis=0)
        buf = step % 2

        @pl.when(step > 2)
        def _():
            settle(buf)

        for i in range(2):
            c = slice(i * BLK, i * BLK + BLK)
            up_grad = dot(a2[:, c], d_hid, 0, 0)
            down_grad = dot(act[:, c], dy_ref[...], 0, 0)
            for j in range(2):
                k = slice(j * BLK, j * BLK + BLK)
                put(buf, 2 * i + j, 16 + 8 * i + 2 * (step - 1) + j, up_grad[:, k])
                put(buf, 4 + 2 * i + j, 32 + 4 * (step - 1) + 2 * i + j, down_grad[:, k])

    @pl.when(step == last)
    def _():
        res_ref[...] = (mid[...] + acc[...] + vec_ref[7:8, :]).astype(LOW)
        hat, rstd = norm_parts(mid[...])
        grad = da2[...]
        dy = dy_ref[...].astype(F32)
        sums_ref[0:1, :] = jnp.sum(hat * grad, axis=0, keepdims=True)
        sums_ref[1:2, :] = jnp.sum(grad, axis=0, keepdims=True)
        d_mid = dy + norm_back(grad * vec_ref[2:3, :], hat, rstd)
        dmid_ref[...] = d_mid
        d_proj = d_mid.astype(LOW)
        sums_ref[2:3, :] = jnp.sum(d_proj.astype(F32), axis=0, keepdims=True)
        sums_ref[3:4, :] = jnp.sum(dy, axis=0, keepdims=True)
        sums_ref[4:8, :] = jnp.zeros((4, D), F32)
        dattn_ref[...] = dot(d_proj, square((o00, o01, o10, o11), up_s), 1, 1).astype(LOW)
        settle(0)
        for i in range(2):
            out_grad = dot(attn_ref[:, i * BLK : i * BLK + BLK], d_proj, 0, 0)
            for j in range(2):
                put(0, 2 * i + j, 12 + 2 * i + j, out_grad[:, j * BLK : j * BLK + BLK])
        settle(1)
        settle(0, 4)


def mid_layer(own, slot, rel, seq, x, attn, dy, vec, b1, gathered, chunk=512):
    rows = x.shape[0]
    wide = FF // D
    quarter = BLK // 4
    owners, slots = gathered.shape[0], gathered.shape[2]

    def part(i):
        return jnp.clip(i - 1, 0, wide - 1)

    def full(shape):
        return pl.BlockSpec(shape, lambda i, own, slot, rel, seq: (0,) * len(shape))

    def tile_at(block_of):
        return pl.BlockSpec(
            (1, 4, 1, quarter, BLK),
            lambda i, own, slot, rel, seq: (own[block_of(i)], 0, slot[block_of(i)], 0, 0),
        )

    row_spec = full((rows, D))
    strip = pl.BlockSpec((1, D), lambda i, own, slot, rel, seq: (0, part(i)))
    anywhere = pl.BlockSpec(memory_space=pl.ANY)
    place_shape = jax.ShapeDtypeStruct((2, owners, slots, quarter, BLK), LOW)
    return pl.pallas_call(
        functools.partial(mid_kernel, chunk=chunk),
        grid_spec=pltpu.PrefetchScalarGridSpec(
            num_scalar_prefetch=4,
            grid=(wide + 2,),
            in_specs=[row_spec, row_spec, row_spec, full(vec.shape), strip]
            + [tile_at(lambda i, b=b: b) for b in (12, 13, 14, 15)]
            + [tile_at(lambda i, n=n: 16 + 8 * (n // 2) + 2 * part(i) + n % 2) for n in range(4)]
            + [tile_at(lambda i, n=n: 32 + 4 * part(i) + n) for n in range(4)],
            out_specs=[row_spec, row_spec, row_spec, anywhere, anywhere, full((8, D)), strip],
            scratch_shapes=[
                pltpu.VMEM((rows, D), F32),
                pltpu.VMEM((rows, D), LOW),
                pltpu.VMEM((rows, D), F32),
                pltpu.VMEM((rows, D), F32),
                pltpu.VMEM((D, D), LOW),
                pltpu.VMEM((D, D), LOW),
                pltpu.VMEM((2, 8, 4, quarter, BLK), LOW),
                pltpu.SemaphoreType.DMA((2, 8, 4)),
            ],
        ),
        out_shape=[
            jax.ShapeDtypeStruct((rows, D), LOW),
            jax.ShapeDtypeStruct((rows, D), F32),
            jax.ShapeDtypeStruct((rows, D), LOW),
            place_shape,
            place_shape,
            jax.ShapeDtypeStruct((8, D), F32),
            jax.ShapeDtypeStruct((1, FF), F32),
        ],
        compiler_params=params(60),
        name="mid",
    )(own, slot, rel, seq, x, attn, dy, vec, b1, *([gathered] * 12))


def d_columns(step, grads, work):
    def both(n):
        return jnp.concatenate([grads[n][...], grads[5 + n][...]], axis=1)

    @pl.when(step == 0)
    def _():
        work(both(0))

    for n in (1, 3):

        @pl.when(step == (n + 1) // 2)
        def _():
            work((both(n).astype(F32) + both(n + 1).astype(F32)).astype(LOW))


def qkv_grad_kernel(seq, a_ref, *refs):
    grads, (keep, send, cols_ref, stage) = refs[:10], refs[10:]
    quarter = BLK // 4

    def work(d_cols):
        cols_ref[...] = jnp.sum(d_cols.astype(F32), axis=0, keepdims=True)
        for i in range(2):
            stage[...] = dot(a_ref[:, i * BLK : i * BLK + BLK], d_cols, 0, 0).astype(LOW)
            for rel_core, out in enumerate((keep, send)):
                for rel_x in range(2):
                    start = pl.multiple_of(quarter_at(seq[0], rel_core, rel_x) * quarter, quarter)
                    for j in range(2):
                        out[rel_x, i, j] = stage[pl.ds(start, quarter), j * BLK : j * BLK + BLK]

    d_columns(pl.program_id(0), grads, work)


def qkv_grad(seq, normed, halves):
    rows = normed.shape[0]
    quarter = BLK // 4
    tile_out = pl.BlockSpec((2, 2, 2, quarter, BLK), lambda i, seq: (0, 0, i, 0, 0))
    shape = jax.ShapeDtypeStruct((2, 2, 6, quarter, BLK), LOW)
    return pl.pallas_call(
        qkv_grad_kernel,
        grid_spec=pltpu.PrefetchScalarGridSpec(
            num_scalar_prefetch=1,
            grid=(3,),
            in_specs=[pl.BlockSpec((rows, D), lambda i, seq: (0, 0))]
            + [pl.BlockSpec((rows, BLK), lambda i, seq: (0, 0))] * 10,
            out_specs=[tile_out, tile_out, pl.BlockSpec((1, D), lambda i, seq: (0, i))],
            scratch_shapes=[pltpu.VMEM((BLK, D), LOW)],
        ),
        out_shape=[shape, shape, jax.ShapeDtypeStruct((1, 3 * D), F32)],
        compiler_params=params(48),
        name="qkv_grad",
    )(seq, normed, *halves[0], *halves[1])


def qkv_bwd_kernel(own, slot, x_ref, dmid_ref, vec_ref, *refs):
    grads, tiles, (dx_ref, sums_ref, acc, held) = refs[:10], refs[10:14], refs[14:]
    step = pl.program_id(0)

    @pl.when(step == 0)
    def _():
        acc[...] = jnp.zeros_like(acc)

    def work(d_cols):
        acc[...] += dot(d_cols, square(tiles, held), 1, 1)

    d_columns(step, grads, work)

    @pl.when(step == 2)
    def _():
        hat, rstd = norm_parts(x_ref[...].astype(F32))
        grad = acc[...]
        sums_ref[0:1, :] = jnp.sum(hat * grad, axis=0, keepdims=True)
        sums_ref[1:2, :] = jnp.sum(grad, axis=0, keepdims=True)
        sums_ref[2:8, :] = jnp.zeros((6, D), F32)
        dx_ref[...] = (dmid_ref[...] + norm_back(grad * vec_ref[0:1, :], hat, rstd)).astype(LOW)


def qkv_backward(own, slot, x, d_mid, vec, halves, gathered):
    rows = x.shape[0]
    row_spec = full_spec((rows, D))
    return pl.pallas_call(
        qkv_bwd_kernel,
        grid_spec=pltpu.PrefetchScalarGridSpec(
            num_scalar_prefetch=2,
            grid=(3,),
            in_specs=[row_spec, row_spec, full_spec(vec.shape)]
            + [full_spec((rows, BLK))] * 10
            + qkv_tiles(),
            out_specs=[row_spec, full_spec((8, D))],
            scratch_shapes=[pltpu.VMEM((rows, D), F32), pltpu.VMEM((D, D), LOW)],
        ),
        out_shape=[jax.ShapeDtypeStruct((rows, D), LOW), jax.ShapeDtypeStruct((8, D), F32)],
        compiler_params=params(60),
        name="qkv_bwd",
    )(own, slot, x, d_mid, vec, *halves[0], *halves[1], *([gathered] * 4))


def eliminate(blocks):
    count, size = len(blocks), blocks[0].shape[0]
    batch = min(count, 6)
    lane = lanes((1, 8, size))
    sub = lax.broadcasted_iota(jnp.int32, (1, 8, size), 1)
    wide_lane = lanes((size, size))
    shape = (batch, 8, size)

    def group(g, carry):
        base = pl.multiple_of(8 * g, 8)
        for at in range(0, count, batch):
            some = blocks[at : at + batch]
            slab = jnp.stack([y[pl.ds(base, 8), :] for y in some], axis=0)
            rolled = jnp.stack([pltpu.roll(slab[b], size - base, 1) for b in range(batch)], axis=0)
            columns = [jnp.broadcast_to(rolled[:, :, k : k + 1], shape) for k in range(8)]
            inside = (lane >= base) & (lane < base + 8)
            rows = jnp.where(inside, jnp.where(lane - base == sub, 1.0, 0.0), slab)
            scale = jnp.zeros(shape, F32)
            for j in range(8):
                inv_root = lax.rsqrt(jnp.broadcast_to(columns[j][:, j : j + 1, :], shape))
                scale = jnp.where(sub == j, inv_root, scale)
                factor = jnp.where(sub > j, columns[j] * (inv_root * inv_root), 0.0)
                rows = rows - factor * jnp.broadcast_to(rows[:, j : j + 1, :], shape)
                for k in range(j + 1, 8):
                    columns[k] = columns[k] - factor * jnp.broadcast_to(columns[k][:, j : j + 1, :], shape)
            rows = rows * scale
            passed = (wide_lane >= base) & (wide_lane < base + 8)
            for b, y in enumerate(some):
                high, mid, low = three_parts(rows[b])
                first = jnp.concatenate([high, high, mid, high, low, mid], axis=0)
                first = jnp.where(jnp.broadcast_to(lane[0, :1] >= base + 8, first.shape), first, 0.0)
                second = jnp.concatenate([high, mid, high, low, high, mid], axis=0)
                update = dot(first.astype(LOW), second.astype(LOW), 0, 0)
                y[...] = jnp.where(passed, 0.0, y[...]) - update
                y[pl.ds(base, 8), :] = rows[b]
        return carry

    lax.fori_loop(0, size // 8, group, 0)


def stats_kernel(ls_ref, rs_ref, lb_ref, rb_ref, left, right):
    for stats, basis, out in ((ls_ref, lb_ref, left), (rs_ref, rb_ref, right)):
        out[0] = BETA_STAT * dot_parts(low_parts(stats[0], 3), low_parts(basis[0], 3), 1, 0, 3)


def stats_product(left_stats, right_stats, left_basis, right_basis):
    count = left_stats.shape[0]
    block_spec = pl.BlockSpec((1, BLK, BLK), lambda i: (i, 0, 0))
    return pl.pallas_call(
        stats_kernel,
        grid=(count,),
        in_specs=[block_spec] * 4,
        out_specs=[block_spec] * 2,
        out_shape=[jax.ShapeDtypeStruct((count, BLK, BLK), F32)] * 2,
        compiler_params=params(32),
        name="stats",
    )(left_stats, right_stats, left_basis, right_basis)


def soap_kernel(
    seq_ref, g0, g1, g2, g3, w_ref, one_ref, two_ref, ls_ref, rs_ref, lb_ref, rb_ref, lp_ref, rp_ref,
    grad_ref, w_out, one_out, two_out, ls_out, rs_out, lb_out, rb_out,
    grad_s, gram, work, *inv,
):
    step = pl.program_id(0)
    slots = pl.num_programs(0)
    count = lb_out.shape[0]
    quarter = BLK // 4
    for piece, flip in ((g0, 0), (g1, 2), (g2, 1), (g3, 3)):
        start = pl.multiple_of((seq_ref[0] ^ flip) * quarter, quarter)
        grad_s[pl.ds(start, quarter), :] = piece[0]
    grad = grad_s[...]
    grad_ref[0] = grad.astype(F32)
    left, right = low_parts(lb_ref[0], 2), low_parts(rb_ref[0], 2)
    left_grad = dot_parts(left, [grad], 0, 0, 2)
    grad_right = dot_parts([grad], right, 1, 0, 2)
    rotated = dot(left_grad.astype(LOW), right[0], 1, 0)
    one = BETA_ONE * one_ref[0] + (1.0 - BETA_ONE) * rotated
    two = BETA_TWO * two_ref[0] + (1.0 - BETA_TWO) * rotated * rotated
    one_out[0] = one
    two_out[0] = two
    scaled = (one / (1.0 - BETA_ONE**STEP)) / (jnp.sqrt(two / (1.0 - BETA_TWO**STEP)) + ADAM_EPS)
    back = dot(dot(left[0], scaled.astype(LOW), 1, 0).astype(LOW), right[0], 1, 1)
    w_out[0] = w_ref[0] - RATE_MATRIX * (back + DECAY_RATE * w_ref[0])
    ls_out[0] = BETA_STAT * ls_ref[0] + (1.0 - BETA_STAT) * dot(grad, grad, 1, 1)
    rs_out[0] = BETA_STAT * rs_ref[0] + (1.0 - BETA_STAT) * dot(grad, grad, 0, 0)
    left_new = lp_ref[0] + (1.0 - BETA_STAT) * dot_parts([grad], low_parts(left_grad, 2), 1, 1, 2)
    right_new = rp_ref[0] + (1.0 - BETA_STAT) * dot_parts([grad], low_parts(grad_right, 2), 0, 0, 2)
    for side, product in enumerate((left_new, right_new)):
        at = side * count + step
        work[at] = product
        parts = low_parts(product, 3)
        for p in range(BLK // 128):
            c, on = slice(128 * p, 128 * p + 128), slice(128 * p, BLK)
            gram[at, c, on] = dot_parts([part[:, c] for part in parts], [part[:, on] for part in parts], 0, 0, 3)

    @pl.when(step == slots - 1)
    def _():
        for p in range(BLK // 128):
            c = slice(128 * p, 128 * p + 128)
            rest = slice(128 * p + 128, BLK)
            for b, block in enumerate(inv):
                block[...] = gram[b, c, c]
            eliminate(inv)
            for b, block in enumerate(inv):
                gram[b, c, c] = block[...]

            def solve(b, carry, out):
                at = b + (count if out is rb_out else 0)
                factor = low_parts(gram[at, c, c], 3)
                solved = dot_parts(low_parts(work[at, :, c], 2), factor, 1, 1, 2)
                out[b, :, c] = solved
                if p < BLK // 128 - 1:
                    upper = low_parts(dot_parts(factor, low_parts(gram[at, c, rest], 3), 1, 0, 3), 3)
                    work[at, :, rest] = work[at, :, rest] - dot_parts(low_parts(solved, 2), upper, 1, 0, 2)
                    gram[at, rest, rest] = gram[at, rest, rest] - dot_parts(upper, upper, 0, 0, 3)
                return carry

            lax.fori_loop(0, count, functools.partial(solve, out=lb_out), 0)
            lax.fori_loop(0, count, functools.partial(solve, out=rb_out), 0)


def soap_update(seq, pieces, state, products):
    count = state[0].shape[0]
    piece_spec = pl.BlockSpec((1, BLK // 4, BLK), lambda i, s: (i, 0, 0))
    block_spec = pl.BlockSpec((1, BLK, BLK), lambda i, s: (i, 0, 0))
    whole_spec = pl.BlockSpec((count, BLK, BLK), lambda i, s: (0, 0, 0))
    shape = jax.ShapeDtypeStruct((count, BLK, BLK), F32)
    return pl.pallas_call(
        soap_kernel,
        grid_spec=pltpu.PrefetchScalarGridSpec(
            num_scalar_prefetch=1,
            grid=(count,),
            in_specs=[piece_spec] * 4 + [block_spec] * 9,
            out_specs=[block_spec] * 6 + [whole_spec] * 2,
            scratch_shapes=[
                pltpu.VMEM((BLK, BLK), LOW),
                pltpu.VMEM((2 * count, BLK, BLK), F32),
                pltpu.VMEM((2 * count, BLK, BLK), F32),
            ]
            + [pltpu.VMEM((128, 128), F32)] * (2 * count),
        ),
        out_shape=[shape] * 8,
        compiler_params=params(60),
        name="soap",
    )(seq, *pieces, *state, *products)


def split_kernel(dp, a_ref, b_ref, *outs):
    for k, out in enumerate(outs):
        out[...] = (a_ref[dp[0] ^ k].astype(F32) + b_ref[dp[0] ^ k].astype(F32)).astype(LOW)


def split_sum(dp, a, b):
    parts = a.shape[0]
    shape = a.shape[1:]
    return pl.pallas_call(
        split_kernel,
        grid_spec=pltpu.PrefetchScalarGridSpec(
            num_scalar_prefetch=1,
            grid=(1,),
            in_specs=[pl.BlockSpec(a.shape, lambda i, dp: (0,) * a.ndim)] * 2,
            out_specs=[pl.BlockSpec(shape, lambda i, dp: (0,) * len(shape))] * parts,
        ),
        out_shape=[jax.ShapeDtypeStruct(shape, LOW)] * parts,
        compiler_params=params(32),
        name="split_sum",
    )(dp, a, b)


def choose_kernel(dp, source, *refs):
    parts, early, out, held = refs[:-3], refs[-3], refs[-2], refs[-1]
    per, half = held.shape[1], held.shape[2]
    for k, part in enumerate(parts):
        held[k] = part[...]
    slots = out.shape[0]
    units = len(parts) * per

    def one(i, carry):
        block = source[i]

        @pl.when(2 * block >= units)
        def _():
            out[i] = early[i]

        @pl.when(2 * block < units)
        def _():
            for h in range(2):
                unit = 2 * block + h
                out[i, h * half : h * half + half] = held[lax.div(unit, per) ^ dp[0], lax.rem(unit, per)]

        return carry

    lax.fori_loop(0, slots, one, 0)


def choose(dp, source, parts, early):
    return pl.pallas_call(
        choose_kernel,
        grid_spec=pltpu.PrefetchScalarGridSpec(
            num_scalar_prefetch=2,
            grid=(1,),
            in_specs=[pl.BlockSpec(parts[0].shape, lambda i, dp, src: (0, 0, 0))] * len(parts)
            + [pl.BlockSpec(early.shape, lambda i, dp, src: (0, 0, 0))],
            out_specs=pl.BlockSpec(early.shape, lambda i, dp, src: (0, 0, 0)),
            scratch_shapes=[pltpu.VMEM((len(parts),) + parts[0].shape, LOW)],
        ),
        out_shape=jax.ShapeDtypeStruct(early.shape, LOW),
        compiler_params=params(32),
        name="choose",
    )(dp, source, *parts, early)


def swap(x, axis, bit):
    size = lax.axis_size(axis)
    return lax.ppermute(x, axis, [(i, i ^ bit) for i in range(size)])


def add_low(a, b):
    return (a.astype(F32) + b.astype(F32)).astype(LOW)


class Halving:
    def __init__(self, kept, got, names, slots=None):
        self.kept, self.got, self.names, self.slots = kept, got, list(names), slots

    def take(self, name, index):
        axis = self.names.index(name)
        found = []
        for array in (self.kept, self.got):
            starts, limits = [0] * array.ndim, list(array.shape)
            starts[axis], limits[axis] = index, index + 1
            if self.slots is not None:
                starts[-3], limits[-3] = self.slots
            part = lax.slice(array, starts, limits)
            found.append(part.reshape(part.shape[:axis] + part.shape[axis + 1 :]))
        return add_low(*found)

    def send(self, name):
        sent, kept = self.take(name, 1), self.take(name, 0)
        self.names.remove(name)
        self.kept, self.slots, self.name = kept, None, name
        return sent

    def receive(self, sent):
        axis, bit = ("seq", 2) if self.name == "x" else ("dp", 2**self.name)
        self.got = swap(sent, axis, bit)

    def total(self):
        return add_low(self.kept, self.got)


def quarters(piece):
    across = swap(piece, "seq", 2)
    beside = swap(jnp.stack([piece, across]), "seq", 1)
    return piece, across, beside[0], beside[1]


def block_places(owners, owner_count, slot_count):
    block_count = owners.shape[0]
    ids = jnp.arange(block_count, dtype=jnp.int32)
    earlier = (owners[:, None] == owners[None, :]) & (ids[None, :] < ids[:, None])
    slots = jnp.sum(earlier.astype(jnp.int32), axis=1)
    places = owners * slot_count + slots
    matched = places[None, :] == jnp.arange(owner_count * slot_count, dtype=jnp.int32)[:, None]
    missing = 1 - jnp.any(matched, axis=1).astype(jnp.int32)
    sources = jnp.sum(jnp.where(matched, ids[None, :], 0), axis=1) + block_count * missing
    return slots, sources


def adam_vectors(gradient, vec, first_mom, second_mom):
    first_mom = BETA_ONE * first_mom + (1.0 - BETA_ONE) * gradient
    second_mom = BETA_TWO * second_mom + (1.0 - BETA_TWO) * gradient * gradient
    step_size = (first_mom / (1.0 - BETA_ONE**STEP)) / (
        jnp.sqrt(second_mom / (1.0 - BETA_TWO**STEP)) + ADAM_EPS
    )
    return first_mom, second_mom, vec - RATE_VECTOR * step_size


def on_device(
    tokens, cotangent, lengths, patch_mask, owners, master, moment_one, moment_two,
    left_stats, right_stats, left_basis, right_basis, vec, vec_one, vec_two,
):
    owner_count = lax.axis_size("dp")
    slot_count = master.shape[0]
    quarter = BLK // 4
    seq_id = lax.axis_index("seq").astype(jnp.int32)
    dp_id = lax.axis_index("dp").astype(jnp.int32)
    core, chip = seq_id % 2, seq_id // 2
    part_len = tokens.shape[1]
    slots, sources = block_places(owners, owner_count, slot_count)
    first_blocks = 3 * (D // BLK) ** 2

    mine = lax.dynamic_index_in_dim(
        master.reshape(slot_count, 4, quarter, BLK), seq_id, 1, keepdims=False
    ).astype(LOW)
    gathered = lax.all_gather(mine, AXES, axis=0, tiled=False).reshape(
        owner_count, 4, slot_count, quarter, BLK
    )

    products = stats_product(left_stats, right_stats, left_basis, right_basis)

    def halves_of(pair):
        kept = lax.dynamic_index_in_dim(pair, chip, 0, keepdims=False)
        return kept, lax.dynamic_index_in_dim(pair, 1 - chip, 0, keepdims=False)

    kept, sent = halves_of(tokens)
    x = jnp.concatenate([kept, swap(sent, "seq", 2)], axis=0)
    dy_kept, dy_sent = halves_of(cotangent)

    def to_positions(mine, other):
        return jnp.where(chip == 0, jnp.stack([mine, other]), jnp.stack([other, mine]))

    positions = jnp.arange(patch_mask.shape[-1], dtype=jnp.int32)
    live = (positions[None, :] < lengths[:, None]) & ((patch_mask == 1) | (positions[None, :] == 0))
    live = lax.dynamic_index_in_dim(live, chip, 0, keepdims=False).reshape(4, part_len)
    order = seq_id ^ jnp.array([0, 2, 1, 3], jnp.int32)
    fill = jnp.where(jnp.take(live, order, axis=0).reshape(-1), 0.0, NEG_FILL).astype(LOW)
    fill = jnp.broadcast_to(fill[:, None], (fill.shape[0], 128))

    bias = jnp.concatenate([vec[4], jnp.zeros_like(vec[4]), vec[5]])[None, :]
    gathered, products, dy_sent = lax.optimization_barrier((gathered, products, dy_sent))
    dy_got = swap(dy_sent, "seq", 2)
    q, kv, normed = qkv_forward(owners, slots, x, vec, bias, gathered)
    other = swap(kv, "seq", 1)
    attn, lse = attn_forward(q, kv, other, fill)
    attn, dy_got = lax.optimization_barrier((attn, dy_got))
    dy = jnp.concatenate([dy_kept, dy_got], axis=0)
    b1 = vec[8:].reshape(1, FF)
    seq_of, dp_of = seq_id.reshape(1), dp_id.reshape(1)
    result, d_mid, d_attn, keep, send, sums_two, bias_grad = mid_layer(
        owners, slots, owners ^ dp_id, seq_of, x, attn, dy, vec, b1, gathered
    )
    result_other = swap(result[part_len:], "seq", 2)

    bits = owner_count.bit_length() - 1
    if slot_count % 3 == 0 and bits == 3:
        plans = [["x", 0, 1, 2], [0, 1, "x", 2], [1, "x", 0, 2]]
    else:
        plans = [["x"] + list(range(bits))]
    per = slot_count // len(plans)
    names = ["x"] + list(range(bits))[::-1]
    shape = (2,) * (1 + bits) + keep.shape[2:]
    keep, got = keep.reshape(shape), swap(send, "seq", 1).reshape(shape)
    groups = [
        Halving(keep, got, names, (per * g, per * g + per)) for g in range(len(plans))
    ]
    guard = fill

    def advance(step, guard):
        sent = [group.send(plan[step]) for group, plan in zip(groups, plans, strict=True)]
        *sent, guard = lax.optimization_barrier((*sent, guard))
        for group, array in zip(groups, sent, strict=True):
            group.receive(array)
        return guard

    halves = []
    half_pairs = D // 128 // 2
    taken = 0
    for half in range(2):
        before, first = [], half * half_pairs
        for place, count in ((0, 2), (2, 1)):
            if (half or place) and (half, place) != (1, 0):
                guard = advance(taken, guard)
                taken += 1
            before = attn_backward(
                q, kv, other, guard, attn, lse, d_attn, first + place, count, place, half_pairs, before
            )
            got, before, result_other = lax.optimization_barrier(
                ([group.got for group in groups], before, result_other)
            )
            for group, array in zip(groups, got, strict=True):
                group.got = array
        dq, dk, dv, sent_k, sent_v = before
        halves.append((dq, dk, swap(sent_k, "seq", 1), dv, swap(sent_v, "seq", 1)))
    normed = advance(taken, normed)
    taken += 1
    late_keep, late_send, cols = qkv_grad(seq_of, normed, halves)
    late_shape = (2, -1, quarter, BLK)
    late = Halving(late_keep.reshape(late_shape), swap(late_send.reshape(late_shape), "seq", 1), ["x"])

    def after(value):
        got, value = lax.optimization_barrier(([group.got for group in groups], value))
        for group, array in zip(groups, got, strict=True):
            group.got = array
        return value

    late.receive(late.send("x"))
    cols = after(cols)
    while taken < len(names):
        advance(taken, fill)
        taken += 1
    d_x, sums_one = qkv_backward(owners, slots, x, d_mid, vec, halves, gathered)
    late.got, d_x = lax.optimization_barrier((late.got, d_x))
    d_x = after(d_x)
    d_x_other = swap(d_x[part_len:], "seq", 2)
    early = jnp.concatenate([group.total() for group in groups], axis=0)
    output = to_positions(result[:part_len], result_other)
    d_tokens = to_positions(d_x[:part_len], d_x_other)
    early, output, d_tokens = lax.optimization_barrier((early, output, d_tokens))

    mine_from = lax.dynamic_slice_in_dim(sources, dp_id * slot_count, slot_count)
    if 2 * first_blocks % owner_count == 0:
        unit = (owner_count, 2 * first_blocks // owner_count, quarter // 2, BLK)
        parts = split_sum(dp_of, late.kept.reshape(unit), late.got.reshape(unit))
        parts = [parts[0]] + [swap(part, "dp", k) for k, part in enumerate(parts) if k]
        total = sum(part.astype(F32) for part in parts).astype(LOW)
        parts = [total] + [swap(total, "dp", k) for k in range(1, owner_count)]
        piece = choose(dp_of, mine_from, parts, early)
    else:
        tiles = jnp.concatenate([late.total(), jnp.zeros((1, quarter, BLK), LOW)], axis=0)
        at = sources.reshape(owner_count, slot_count)[dp_id ^ jnp.arange(owner_count)]
        tiles = jnp.take(tiles, jnp.minimum(at, first_blocks).reshape(-1), axis=0)
        tiles = tiles.reshape((2,) * bits + (slot_count, quarter, BLK))
        owned = Halving(tiles, jnp.zeros_like(tiles), names[1:])
        for bit in range(bits):
            owned.receive(owned.send(bit))
        piece = jnp.where((mine_from < first_blocks)[:, None, None], owned.total(), early)
    state = (master, moment_one, moment_two, left_stats, right_stats, left_basis, right_basis)
    piece = jnp.where((mine_from < owners.shape[0])[:, None, None], piece, jnp.zeros_like(piece))
    piece, sums_one, sums_two, cols, bias_grad = lax.optimization_barrier(
        (piece, sums_one, sums_two, cols, bias_grad)
    )
    updates = soap_update(seq_of, quarters(piece), state, products)

    vec_grad = jnp.concatenate(
        [
            sums_one[0:2],
            sums_two[0:2],
            cols[:, :D],
            cols[:, 2 * D :],
            sums_two[2:4],
            bias_grad.reshape(-1, D),
        ],
        axis=0,
    )
    vec_parts = lax.all_gather(vec_grad, AXES, axis=0, tiled=False)
    updates, vec_parts = lax.optimization_barrier((updates, vec_parts))
    vec_total = jnp.sum(vec_parts, axis=0)
    vec_first, vec_second, vec_next = adam_vectors(vec_total, vec, vec_one, vec_two)
    grad_blocks, w_new, one_new, two_new, ls_new, rs_new, lb_new, rb_new = updates
    return (
        output, d_tokens, grad_blocks, w_new, one_new, two_new, ls_new, rs_new, lb_new, rb_new,
        vec_first, vec_second, vec_next,
    )


def solution(mesh):
    rows, blocks, whole = P("dp", "seq", None), P("dp", None, None), P()
    return jax.shard_map(
        on_device,
        mesh=mesh,
        in_specs=(rows, rows, P("dp"), P("dp", None), whole) + (blocks,) * 7 + (whole,) * 3,
        out_specs=(rows, rows) + (blocks,) * 8 + (whole,) * 3,
        check_vma=False,
    )
```

```python
import functools

import jax
import jax.numpy as jnp
from jax import lax
from jax.experimental import pallas as pl
from jax.experimental.pallas import tpu as pltpu
from jax.sharding import PartitionSpec as P

D = 768
FF = 3072
BLK = 384
STEP = 10

NORM_EPS = 1e-06
NEG_FILL = -1000000000.0
BETA_ONE = 0.9
BETA_TWO = 0.999
BETA_STAT = 0.95
RATE_MATRIX = 0.1
RATE_VECTOR = 0.3
DECAY_RATE = 0.01
ADAM_EPS = 1e-08

LOW = jnp.bfloat16
F32 = jnp.float32
AXES = ("dp", "seq")
MIB = 2**20

TAIL_P = 0.24
TAIL_C = (
    0.09575380798443668,
    0.09552183543465394,
    0.09284136585084933,
    0.06338567653857548,
    0.11841694922211018,
    -0.06574016740998187,
    0.15281935057715396,
    -0.052998628523732765,
)


def dot(a, b, ca, cb):
    return lax.dot_general(a, b, (((ca,), (cb,)), ((), ())), preferred_element_type=F32)


def lanes(shape):
    return lax.broadcasted_iota(jnp.int32, shape, len(shape) - 1)


def gelu_pair(x):
    u = jnp.abs(x)
    t = 1.0 / (1.0 + TAIL_P * u)
    poly = TAIL_C[-1]
    for coeff in TAIL_C[-2::-1]:
        poly = poly * t + coeff
    expo = jnp.exp(-0.5 * u * u)
    tail = poly * t * expo
    cdf = jnp.where(x < 0, tail, 1.0 - tail)
    return x * cdf, cdf + x * (expo * 0.3989422804014327)


def norm_parts(rows):
    center = rows - jnp.mean(rows, axis=-1, keepdims=True)
    rstd = lax.rsqrt(jnp.mean(center * center, axis=-1, keepdims=True) + NORM_EPS)
    return center * rstd, rstd


def norm_back(grad, hat, rstd):
    return rstd * (
        grad
        - jnp.mean(grad, axis=-1, keepdims=True)
        - hat * jnp.mean(grad * hat, axis=-1, keepdims=True)
    )


def params(limit):
    return pltpu.CompilerParams(vmem_limit_bytes=limit * MIB)


def tile_spec(block_of):
    return pl.BlockSpec(
        (1, 4, 1, BLK // 4, BLK),
        lambda i, own, slot: (own[block_of(i)], 0, slot[block_of(i)], 0, 0),
    )


def tile(ref):
    return ref[...].reshape(BLK, BLK)


def full_spec(shape):
    return pl.BlockSpec(shape, lambda i, own, slot: (0,) * len(shape))


def quarter_at(seq, rel_core, rel_x):
    return seq ^ (2 * rel_x + rel_core)


def square(tiles, held):
    for i in range(2):
        for j in range(2):
            held[i * BLK : i * BLK + BLK, j * BLK : j * BLK + BLK] = tile(tiles[2 * i + j])
    return held[...]


def qkv_kernel(own, slot, x_ref, vec_ref, bias_ref, t00, t01, t10, t11, q_ref, kv_ref, a_ref, held):
    @pl.when(pl.program_id(0) == 0)
    def _():
        hat, _ = norm_parts(x_ref[...].astype(F32))
        a_ref[...] = (hat * vec_ref[0:1, :] + vec_ref[1:2, :]).astype(LOW)

    low = (dot(a_ref[...], square((t00, t01, t10, t11), held), 1, 0) + bias_ref[...]).astype(LOW)

    @pl.when(pl.program_id(0) == 0)
    def _():
        q_ref[...] = low

    @pl.when(pl.program_id(0) > 0)
    def _():
        kv_ref[...] = low


def qkv_tiles():
    return [tile_spec(lambda i, n=n: 6 * (n // 2) + 2 * i + n % 2) for n in range(4)]


def qkv_forward(own, slot, x, vec, bias, gathered):
    rows = x.shape[0]
    return pl.pallas_call(
        qkv_kernel,
        grid_spec=pltpu.PrefetchScalarGridSpec(
            num_scalar_prefetch=2,
            grid=(3,),
            in_specs=[
                full_spec((rows, D)),
                full_spec(vec.shape),
                pl.BlockSpec((1, D), lambda i, own, slot: (0, i)),
            ]
            + qkv_tiles(),
            out_specs=[
                full_spec((rows, D)),
                pl.BlockSpec((rows, D), lambda i, own, slot: (0, jnp.maximum(i - 1, 0))),
                full_spec((rows, D)),
            ],
            scratch_shapes=[pltpu.VMEM((D, D), LOW)],
        ),
        out_shape=[
            jax.ShapeDtypeStruct((rows, D), LOW),
            jax.ShapeDtypeStruct((rows, 2 * D), LOW),
            jax.ShapeDtypeStruct((rows, D), LOW),
        ],
        compiler_params=params(48),
        name="qkv",
    )(own, slot, x, vec, bias, *([gathered] * 4))


def attn_fwd_kernel(q_ref, k1, v1, k2, v2, bias_ref, o_ref, lse_ref, ka, kb, va, vb):
    rows = k1.shape[0]

    @pl.when(pl.program_id(1) == 0)
    def _():
        ln = lanes((rows, 128))
        for i, (k, v) in enumerate(((k1, v1), (k2, v2))):
            r = slice(i * rows, i * rows + rows)
            keys, values, bias = k[...], v[...], bias_ref[r, :]
            one = jnp.ones_like(values)
            ka[r, :] = jnp.where(ln == 64, bias, keys)
            kb[r, :] = jnp.where(ln == 0, bias, keys)
            va[r, :] = jnp.where(ln < 64, values, one)
            vb[r, :] = jnp.where(ln < 64, one, values)

    q = q_ref[...] * jnp.asarray(0.125, LOW)
    ln = lanes(q.shape)
    one, zero = jnp.ones_like(q), jnp.zeros_like(q)
    qa = jnp.where(ln < 64, q, jnp.where(ln == 64, one, zero))
    qb = jnp.where(ln < 64, jnp.where(ln == 0, one, zero), q)
    outs, tops = [], []
    for query, keys, values in ((qa, ka, va), (qb, kb, vb)):
        logits = dot(query, keys[...], 1, 1)
        top = jnp.max(logits, axis=1, keepdims=True)
        expo = jnp.exp(logits - top).astype(LOW)
        outs.append(dot(expo, values[...], 1, 0))
        tops.append(top)
    total = jnp.where(ln < 64, outs[1], outs[0])
    attended = jnp.where(ln < 64, outs[0], outs[1])
    o_ref[...] = (attended / pltpu.roll(total, 64, 1)).astype(LOW)
    lse_ref[...] = jnp.where(ln < 64, tops[1], tops[0]) + jnp.log(total)


def attn_forward(q, kv, other, bias, q_rows=256):
    rows, pairs = q.shape[0], D // 128
    keys = 2 * rows
    q_spec = pl.BlockSpec((q_rows, 128), lambda p, i: (i, p))
    return pl.pallas_call(
        attn_fwd_kernel,
        grid=(pairs, rows // q_rows),
        in_specs=[
            q_spec,
            pl.BlockSpec((rows, 128), lambda p, i: (0, p)),
            pl.BlockSpec((rows, 128), lambda p, i: (0, pairs + p)),
            pl.BlockSpec((rows, 128), lambda p, i: (0, p)),
            pl.BlockSpec((rows, 128), lambda p, i: (0, pairs + p)),
            pl.BlockSpec((keys, 128), lambda p, i: (0, 0)),
        ],
        out_specs=[q_spec, q_spec],
        out_shape=[
            jax.ShapeDtypeStruct((rows, D), LOW),
            jax.ShapeDtypeStruct((rows, D), F32),
        ],
        scratch_shapes=[pltpu.VMEM((keys, 128), LOW)] * 4,
        compiler_params=params(48),
        name="attn_fwd",
    )(q, kv, kv, other, other, bias)


def three_parts(x):
    high = x.astype(LOW).astype(F32)
    rest = x - high
    mid = rest.astype(LOW).astype(F32)
    return high, mid, rest - mid


def low_parts(x, count):
    found = []
    for _ in range(count):
        part = x.astype(LOW)
        found.append(part)
        x = x - part.astype(F32)
    return found


def dot_parts(a, b, ca, cb, order):
    pairs = [(i, j) for i in range(len(a)) for j in range(len(b)) if i + j < order]
    a = jnp.concatenate([a[i] for i, _ in pairs], axis=ca)
    b = jnp.concatenate([b[j] for _, j in pairs], axis=cb)
    return dot(a, b, ca, cb)


def with_spare(x, spare, value, one, first):
    ln = lanes(x.shape)
    high, mid, low = three_parts(value)
    filled = jnp.where(ln == first + 3, one, 0.0)
    for i, part in enumerate((high, mid, low)):
        filled = jnp.where(ln == first + i, part, filled)
    return jnp.where(spare, filled, x).astype(LOW)


def attn_bwd_kernel(
    q_ref, k1, v1, k2, v2, bias_ref, o_ref, lse_ref, do_ref,
    dq_ref, dk1, dv1, dk2, dv2, ka, kb, va, vb, kt, dk, dv, *, chunk,
):
    rows = k1.shape[0]

    @pl.when(pl.program_id(1) == 0)
    def _():
        ln = lanes((rows, 128))
        for i, (k, v) in enumerate(((k1, v1), (k2, v2))):
            r = slice(i * rows, i * rows + rows)
            keys, values, bias = k[...], v[...], bias_ref[r, :]
            one, zero = jnp.ones_like(values), jnp.zeros_like(values)
            ka[r, :] = jnp.where(ln < 64, keys, jnp.where(ln < 67, one, jnp.where(ln == 67, bias, zero)))
            kb[r, :] = jnp.where(ln >= 64, keys, jnp.where(ln < 3, one, jnp.where(ln == 3, bias, zero)))
            va[r, :] = jnp.where(ln < 64, values, jnp.where(ln < 67, one, zero))
            vb[r, :] = jnp.where(ln >= 64, values, jnp.where(ln < 3, one, zero))
            kt[:, r] = keys.T
        dk[...] = jnp.zeros_like(dk)
        dv[...] = jnp.zeros_like(dv)

    q = q_ref[...].astype(F32) * 0.125
    left = lanes(q.shape) < 64
    grad = do_ref[...].astype(F32)
    prod = grad * o_ref[...].astype(F32)
    sum_a = jnp.sum(jnp.where(left, prod, 0.0), axis=1, keepdims=True)
    sum_b = jnp.sum(jnp.where(left, 0.0, prod), axis=1, keepdims=True)
    delta = jnp.where(left, sum_b, sum_a)
    lse = lse_ref[...]
    zero = jnp.zeros_like(q)
    heads = (
        (
            with_spare(q, ~left, -lse, 1.0, 64), with_spare(grad, ~left, -delta, 0.0, 64), ka, va,
            jnp.where(left, q, zero).astype(LOW), jnp.where(left, grad, zero).astype(LOW),
        ),
        (
            with_spare(q, left, -lse, 1.0, 0), with_spare(grad, left, -delta, 0.0, 0), kb, vb,
            jnp.where(left, zero, q).astype(LOW), jnp.where(left, zero, grad).astype(LOW),
        ),
    )
    d_query = [jnp.zeros((64, q.shape[0]), F32)] * 2
    for c in range(2 * rows // chunk):
        r = slice(c * chunk, c * chunk + chunk)
        dv_c, dk_c = dv[r, :], dk[r, :]
        for h, (q_aug, g_aug, keys, values, q_only, g_only) in enumerate(heads):
            probs = jnp.exp(dot(keys[r, :], q_aug, 1, 1))
            d_logits = (probs * dot(values[r, :], g_aug, 1, 1)).astype(LOW)
            dv_c = dv_c + dot(probs.astype(LOW), g_only, 1, 0)
            dk_c = dk_c + dot(d_logits, q_only, 1, 0)
            d_query[h] = d_query[h] + dot(kt[64 * h : 64 * h + 64, r], d_logits, 1, 0)
        dv[r, :] = dv_c
        dk[r, :] = dk_c
    dq_ref[...] = (jnp.concatenate(d_query, axis=0) * 0.125).T.astype(LOW)

    @pl.when(pl.program_id(1) == pl.num_programs(1) - 1)
    def _():
        dk1[...] = dk[:rows, :].astype(LOW)
        dk2[...] = dk[rows:, :].astype(LOW)
        dv1[...] = dv[:rows, :].astype(LOW)
        dv2[...] = dv[rows:, :].astype(LOW)


def attn_backward(q, kv, other, bias, attn, lse, d_attn, first, count, q_rows=512, chunk=1024):
    rows, pairs = q.shape[0], D // 128
    keys = 2 * rows
    out_spec = pl.BlockSpec((q_rows, 128), lambda p, i: (i, p))
    k_out = pl.BlockSpec((rows, 128), lambda p, i: (0, p))
    q_spec = pl.BlockSpec((q_rows, 128), lambda p, i: (i, first + p))
    k_spec = pl.BlockSpec((rows, 128), lambda p, i: (0, first + p))
    v_spec = pl.BlockSpec((rows, 128), lambda p, i: (0, pairs + first + p))
    return pl.pallas_call(
        functools.partial(attn_bwd_kernel, chunk=chunk),
        grid=(count, rows // q_rows),
        in_specs=[
            q_spec, k_spec, v_spec, k_spec, v_spec, pl.BlockSpec((keys, 128), lambda p, i: (0, 0)),
            q_spec, q_spec, q_spec,
        ],
        out_specs=[out_spec, k_out, k_out, k_out, k_out],
        out_shape=[jax.ShapeDtypeStruct((rows, count * 128), LOW)] * 5,
        scratch_shapes=[pltpu.VMEM((keys, 128), LOW)] * 4
        + [pltpu.VMEM((128, keys), LOW)]
        + [pltpu.VMEM((keys, 128), F32)] * 2,
        compiler_params=params(56),
        name="attn_bwd",
    )(q, kv, kv, other, other, bias, attn, lse, d_attn)


def mid_kernel(
    own, slot, rel, seq, x_ref, attn_ref, dy_ref, vec_ref, b1_ref, o00, o01, o10, o11, *refs, chunk):
    ups, downs = refs[:4], refs[4:8]
    (
        res_ref, dmid_ref, dattn_ref, keep, send, sums_ref, gb1_ref,
        mid, a2, acc, da2, up_s, down_s, stage, sems,
    ) = refs[8:]
    step = pl.program_id(0)
    last = pl.num_programs(0) - 1
    quarter = BLK // 4

    def copies(buf, i, block):
        found = []
        for rel_core, out in enumerate((keep, send)):
            for rel_x in range(2):
                found.append(
                    pltpu.make_async_copy(
                        stage.at[buf, i, quarter_at(seq[0], rel_core, rel_x)],
                        out.at[rel_x, rel[block], slot[block]],
                        sems.at[buf, i, 2 * rel_core + rel_x],
                    )
                )
        return found

    def put(buf, i, block, value):
        low = value.astype(LOW)
        for part in range(4):
            stage[buf, i, part] = low[part * quarter : part * quarter + quarter]
        for copy in copies(buf, i, block):
            copy.start()

    def settle(buf, count=8):
        for i in range(count):
            for copy in copies(buf, i, 0):
                copy.wait()

    @pl.when(step == 0)
    def _():
        mid[...] = (
            x_ref[...].astype(F32)
            + dot(attn_ref[...], square((o00, o01, o10, o11), up_s), 1, 0)
            + vec_ref[6:7, :]
        )
        hat, _ = norm_parts(mid[...])
        a2[...] = (hat * vec_ref[2:3, :] + vec_ref[3:4, :]).astype(LOW)
        acc[...] = jnp.zeros_like(acc)
        da2[...] = jnp.zeros_like(da2)

    @pl.when((step > 0) & (step < last))
    def _():
        rows = a2.shape[0]
        up, down = square(ups, up_s), square(downs, down_s)
        bias_grad = jnp.zeros((1, D), F32)
        acts, d_hids = [], []
        for c in range(rows // chunk):
            r = slice(c * chunk, c * chunk + chunk)
            act, slope = gelu_pair(dot(a2[r, :], up, 1, 0) + b1_ref[...])
            act = act.astype(LOW)
            d_hid = (dot(dy_ref[r, :], down, 1, 1) * slope).astype(LOW)
            acc[r, :] += dot(act, down, 1, 0)
            da2[r, :] += dot(d_hid, up, 1, 1)
            bias_grad = bias_grad + jnp.sum(d_hid.astype(F32), axis=0, keepdims=True)
            acts.append(act)
            d_hids.append(d_hid)
        gb1_ref[...] = bias_grad
        act = jnp.concatenate(acts, axis=0)
        d_hid = jnp.concatenate(d_hids, axis=0)
        buf = step % 2

        @pl.when(step > 2)
        def _():
            settle(buf)

        for i in range(2):
            c = slice(i * BLK, i * BLK + BLK)
            up_grad = dot(a2[:, c], d_hid, 0, 0)
            down_grad = dot(act[:, c], dy_ref[...], 0, 0)
            for j in range(2):
                k = slice(j * BLK, j * BLK + BLK)
                put(buf, 2 * i + j, 16 + 8 * i + 2 * (step - 1) + j, up_grad[:, k])
                put(buf, 4 + 2 * i + j, 32 + 4 * (step - 1) + 2 * i + j, down_grad[:, k])

    @pl.when(step == last)
    def _():
        res_ref[...] = (mid[...] + acc[...] + vec_ref[7:8, :]).astype(LOW)
        hat, rstd = norm_parts(mid[...])
        grad = da2[...]
        dy = dy_ref[...].astype(F32)
        sums_ref[0:1, :] = jnp.sum(hat * grad, axis=0, keepdims=True)
        sums_ref[1:2, :] = jnp.sum(grad, axis=0, keepdims=True)
        d_mid = dy + norm_back(grad * vec_ref[2:3, :], hat, rstd)
        dmid_ref[...] = d_mid
        d_proj = d_mid.astype(LOW)
        sums_ref[2:3, :] = jnp.sum(d_proj.astype(F32), axis=0, keepdims=True)
        sums_ref[3:4, :] = jnp.sum(dy, axis=0, keepdims=True)
        sums_ref[4:8, :] = jnp.zeros((4, D), F32)
        dattn_ref[...] = dot(d_proj, square((o00, o01, o10, o11), up_s), 1, 1).astype(LOW)
        settle(0)
        for i in range(2):
            out_grad = dot(attn_ref[:, i * BLK : i * BLK + BLK], d_proj, 0, 0)
            for j in range(2):
                put(0, 2 * i + j, 12 + 2 * i + j, out_grad[:, j * BLK : j * BLK + BLK])
        settle(1)
        settle(0, 4)


def mid_layer(own, slot, rel, seq, x, attn, dy, vec, b1, gathered, chunk=512):
    rows = x.shape[0]
    wide = FF // D
    quarter = BLK // 4
    owners, slots = gathered.shape[0], gathered.shape[2]

    def part(i):
        return jnp.clip(i - 1, 0, wide - 1)

    def full(shape):
        return pl.BlockSpec(shape, lambda i, own, slot, rel, seq: (0,) * len(shape))

    def tile_at(block_of):
        return pl.BlockSpec(
            (1, 4, 1, quarter, BLK),
            lambda i, own, slot, rel, seq: (own[block_of(i)], 0, slot[block_of(i)], 0, 0),
        )

    row_spec = full((rows, D))
    strip = pl.BlockSpec((1, D), lambda i, own, slot, rel, seq: (0, part(i)))
    anywhere = pl.BlockSpec(memory_space=pl.ANY)
    place_shape = jax.ShapeDtypeStruct((2, owners, slots, quarter, BLK), LOW)
    return pl.pallas_call(
        functools.partial(mid_kernel, chunk=chunk),
        grid_spec=pltpu.PrefetchScalarGridSpec(
            num_scalar_prefetch=4,
            grid=(wide + 2,),
            in_specs=[row_spec, row_spec, row_spec, full(vec.shape), strip]
            + [tile_at(lambda i, b=b: b) for b in (12, 13, 14, 15)]
            + [tile_at(lambda i, n=n: 16 + 8 * (n // 2) + 2 * part(i) + n % 2) for n in range(4)]
            + [tile_at(lambda i, n=n: 32 + 4 * part(i) + n) for n in range(4)],
            out_specs=[row_spec, row_spec, row_spec, anywhere, anywhere, full((8, D)), strip],
            scratch_shapes=[
                pltpu.VMEM((rows, D), F32),
                pltpu.VMEM((rows, D), LOW),
                pltpu.VMEM((rows, D), F32),
                pltpu.VMEM((rows, D), F32),
                pltpu.VMEM((D, D), LOW),
                pltpu.VMEM((D, D), LOW),
                pltpu.VMEM((2, 8, 4, quarter, BLK), LOW),
                pltpu.SemaphoreType.DMA((2, 8, 4)),
            ],
        ),
        out_shape=[
            jax.ShapeDtypeStruct((rows, D), LOW),
            jax.ShapeDtypeStruct((rows, D), F32),
            jax.ShapeDtypeStruct((rows, D), LOW),
            place_shape,
            place_shape,
            jax.ShapeDtypeStruct((8, D), F32),
            jax.ShapeDtypeStruct((1, FF), F32),
        ],
        compiler_params=params(60),
        name="mid",
    )(own, slot, rel, seq, x, attn, dy, vec, b1, *([gathered] * 12))


def d_columns(step, grads, work):
    def both(n):
        return jnp.concatenate([ref[...] for ref in grads[n::5]], axis=1)

    @pl.when(step == 0)
    def _():
        work(both(0))

    for n in (1, 3):

        @pl.when(step == (n + 1) // 2)
        def _():
            work((both(n).astype(F32) + both(n + 1).astype(F32)).astype(LOW))


def qkv_grad_kernel(seq, a_ref, *refs):
    grads, (keep, send, cols_ref, stage) = refs[:-4], refs[-4:]
    quarter = BLK // 4

    def work(d_cols):
        cols_ref[...] = jnp.sum(d_cols.astype(F32), axis=0, keepdims=True)
        for i in range(2):
            stage[...] = dot(a_ref[:, i * BLK : i * BLK + BLK], d_cols, 0, 0).astype(LOW)
            for rel_core, out in enumerate((keep, send)):
                for rel_x in range(2):
                    start = pl.multiple_of(quarter_at(seq[0], rel_core, rel_x) * quarter, quarter)
                    for j in range(2):
                        out[rel_x, i, j] = stage[pl.ds(start, quarter), j * BLK : j * BLK + BLK]

    d_columns(pl.program_id(0), grads, work)


def qkv_grad(seq, normed, grads):
    rows = normed.shape[0]
    quarter = BLK // 4
    tile_out = pl.BlockSpec((2, 2, 2, quarter, BLK), lambda i, seq: (0, 0, i, 0, 0))
    shape = jax.ShapeDtypeStruct((2, 2, 6, quarter, BLK), LOW)
    return pl.pallas_call(
        qkv_grad_kernel,
        grid_spec=pltpu.PrefetchScalarGridSpec(
            num_scalar_prefetch=1,
            grid=(3,),
            in_specs=[pl.BlockSpec((rows, D), lambda i, seq: (0, 0))]
            + [pl.BlockSpec(grad.shape, lambda i, seq: (0, 0)) for grad in grads],
            out_specs=[tile_out, tile_out, pl.BlockSpec((1, D), lambda i, seq: (0, i))],
            scratch_shapes=[pltpu.VMEM((BLK, D), LOW)],
        ),
        out_shape=[shape, shape, jax.ShapeDtypeStruct((1, 3 * D), F32)],
        compiler_params=params(48),
        name="qkv_grad",
    )(seq, normed, *grads)


def qkv_bwd_kernel(own, slot, x_ref, dmid_ref, vec_ref, *refs):
    grads, tiles, (dx_ref, sums_ref, acc, held) = refs[:-8], refs[-8:-4], refs[-4:]
    step = pl.program_id(0)

    @pl.when(step == 0)
    def _():
        acc[...] = jnp.zeros_like(acc)

    def work(d_cols):
        acc[...] += dot(d_cols, square(tiles, held), 1, 1)

    d_columns(step, grads, work)

    @pl.when(step == 2)
    def _():
        hat, rstd = norm_parts(x_ref[...].astype(F32))
        grad = acc[...]
        sums_ref[0:1, :] = jnp.sum(hat * grad, axis=0, keepdims=True)
        sums_ref[1:2, :] = jnp.sum(grad, axis=0, keepdims=True)
        sums_ref[2:8, :] = jnp.zeros((6, D), F32)
        dx_ref[...] = (dmid_ref[...] + norm_back(grad * vec_ref[0:1, :], hat, rstd)).astype(LOW)


def qkv_backward(own, slot, x, d_mid, vec, grads, gathered):
    rows = x.shape[0]
    row_spec = full_spec((rows, D))
    return pl.pallas_call(
        qkv_bwd_kernel,
        grid_spec=pltpu.PrefetchScalarGridSpec(
            num_scalar_prefetch=2,
            grid=(3,),
            in_specs=[row_spec, row_spec, full_spec(vec.shape)]
            + [full_spec(grad.shape) for grad in grads]
            + qkv_tiles(),
            out_specs=[row_spec, full_spec((8, D))],
            scratch_shapes=[pltpu.VMEM((rows, D), F32), pltpu.VMEM((D, D), LOW)],
        ),
        out_shape=[jax.ShapeDtypeStruct((rows, D), LOW), jax.ShapeDtypeStruct((8, D), F32)],
        compiler_params=params(60),
        name="qkv_bwd",
    )(own, slot, x, d_mid, vec, *grads, *([gathered] * 4))


def eliminate(blocks):
    count, size = len(blocks), blocks[0].shape[0]
    batch = min(count, 6)
    lane = lanes((1, 8, size))
    sub = lax.broadcasted_iota(jnp.int32, (1, 8, size), 1)
    wide_lane = lanes((size, size))
    shape = (batch, 8, size)

    def group(g, carry):
        base = pl.multiple_of(8 * g, 8)
        for at in range(0, count, batch):
            some = blocks[at : at + batch]
            slab = jnp.stack([y[pl.ds(base, 8), :] for y in some], axis=0)
            rolled = jnp.stack([pltpu.roll(slab[b], size - base, 1) for b in range(batch)], axis=0)
            columns = [jnp.broadcast_to(rolled[:, :, k : k + 1], shape) for k in range(8)]
            inside = (lane >= base) & (lane < base + 8)
            rows = jnp.where(inside, jnp.where(lane - base == sub, 1.0, 0.0), slab)
            scale = jnp.zeros(shape, F32)
            for j in range(8):
                inv_root = lax.rsqrt(jnp.broadcast_to(columns[j][:, j : j + 1, :], shape))
                scale = jnp.where(sub == j, inv_root, scale)
                factor = jnp.where(sub > j, columns[j] * (inv_root * inv_root), 0.0)
                rows = rows - factor * jnp.broadcast_to(rows[:, j : j + 1, :], shape)
                for k in range(j + 1, 8):
                    columns[k] = columns[k] - factor * jnp.broadcast_to(columns[k][:, j : j + 1, :], shape)
            rows = rows * scale
            passed = (wide_lane >= base) & (wide_lane < base + 8)
            for b, y in enumerate(some):
                high, mid, low = three_parts(rows[b])
                first = jnp.concatenate([high, high, mid, high, low, mid], axis=0)
                first = jnp.where(jnp.broadcast_to(lane[0, :1] >= base + 8, first.shape), first, 0.0)
                second = jnp.concatenate([high, mid, high, low, high, mid], axis=0)
                update = dot(first.astype(LOW), second.astype(LOW), 0, 0)
                y[...] = jnp.where(passed, 0.0, y[...]) - update
                y[pl.ds(base, 8), :] = rows[b]
        return carry

    lax.fori_loop(0, size // 8, group, 0)


def stats_kernel(ls_ref, rs_ref, lb_ref, rb_ref, left, right):
    for stats, basis, out in ((ls_ref, lb_ref, left), (rs_ref, rb_ref, right)):
        out[0] = BETA_STAT * dot_parts(low_parts(stats[0], 3), low_parts(basis[0], 3), 1, 0, 3)


def stats_product(left_stats, right_stats, left_basis, right_basis):
    count = left_stats.shape[0]
    block_spec = pl.BlockSpec((1, BLK, BLK), lambda i: (i, 0, 0))
    return pl.pallas_call(
        stats_kernel,
        grid=(count,),
        in_specs=[block_spec] * 4,
        out_specs=[block_spec] * 2,
        out_shape=[jax.ShapeDtypeStruct((count, BLK, BLK), F32)] * 2,
        compiler_params=params(32),
        name="stats",
    )(left_stats, right_stats, left_basis, right_basis)


def soap_kernel(
    seq_ref, g0, g1, g2, g3, w_ref, one_ref, two_ref, ls_ref, rs_ref, lb_ref, rb_ref, lp_ref, rp_ref,
    grad_ref, w_out, one_out, two_out, ls_out, rs_out, lb_out, rb_out,
    grad_s, gram, work, *inv,
):
    step = pl.program_id(0)
    slots = pl.num_programs(0)
    count = lb_out.shape[0]
    quarter = BLK // 4
    for piece, flip in ((g0, 0), (g1, 2), (g2, 1), (g3, 3)):
        start = pl.multiple_of((seq_ref[0] ^ flip) * quarter, quarter)
        grad_s[pl.ds(start, quarter), :] = piece[0]
    grad = grad_s[...]
    grad_ref[0] = grad.astype(F32)
    left, right = low_parts(lb_ref[0], 2), low_parts(rb_ref[0], 2)
    left_grad = dot_parts(left, [grad], 0, 0, 2)
    grad_right = dot_parts([grad], right, 1, 0, 2)
    rotated = dot(left_grad.astype(LOW), right[0], 1, 0)
    one = BETA_ONE * one_ref[0] + (1.0 - BETA_ONE) * rotated
    two = BETA_TWO * two_ref[0] + (1.0 - BETA_TWO) * rotated * rotated
    one_out[0] = one
    two_out[0] = two
    scaled = (one / (1.0 - BETA_ONE**STEP)) / (jnp.sqrt(two / (1.0 - BETA_TWO**STEP)) + ADAM_EPS)
    back = dot(dot(left[0], scaled.astype(LOW), 1, 0).astype(LOW), right[0], 1, 1)
    w_out[0] = w_ref[0] - RATE_MATRIX * (back + DECAY_RATE * w_ref[0])
    ls_out[0] = BETA_STAT * ls_ref[0] + (1.0 - BETA_STAT) * dot(grad, grad, 1, 1)
    rs_out[0] = BETA_STAT * rs_ref[0] + (1.0 - BETA_STAT) * dot(grad, grad, 0, 0)
    left_new = lp_ref[0] + (1.0 - BETA_STAT) * dot_parts([grad], low_parts(left_grad, 2), 1, 1, 2)
    right_new = rp_ref[0] + (1.0 - BETA_STAT) * dot_parts([grad], low_parts(grad_right, 2), 0, 0, 2)
    for side, product in enumerate((left_new, right_new)):
        at = side * count + step
        work[at] = product
        parts = low_parts(product, 3)
        for p in range(BLK // 128):
            c, on = slice(128 * p, 128 * p + 128), slice(128 * p, BLK)
            gram[at, c, on] = dot_parts([part[:, c] for part in parts], [part[:, on] for part in parts], 0, 0, 3)

    @pl.when(step == slots - 1)
    def _():
        for p in range(BLK // 128):
            c = slice(128 * p, 128 * p + 128)
            rest = slice(128 * p + 128, BLK)
            for b, block in enumerate(inv):
                block[...] = gram[b, c, c]
            eliminate(inv)
            for b, block in enumerate(inv):
                gram[b, c, c] = block[...]

            def solve(i, carry):
                wide = 2 if count % 2 == 0 else 1
                at = [side * count + wide * i + j for side in range(2) for j in range(wide)]
                factors = [low_parts(gram[b, c, c], 3) for b in at]
                solved = [
                    dot_parts(low_parts(work[b, :, c], 2), factor, 1, 1, 2)
                    for b, factor in zip(at, factors, strict=True)
                ]
                if p < BLK // 128 - 1:
                    uppers = [
                        low_parts(dot_parts(factor, low_parts(gram[b, c, rest], 3), 1, 0, 3), 3)
                        for b, factor in zip(at, factors, strict=True)
                    ]
                    works = [
                        work[b, :, rest] - dot_parts(low_parts(part, 2), upper, 1, 0, 2)
                        for b, part, upper in zip(at, solved, uppers, strict=True)
                    ]
                    grams = [
                        gram[b, rest, rest] - dot_parts(upper, upper, 0, 0, 3)
                        for b, upper in zip(at, uppers, strict=True)
                    ]
                    for b, new_work, new_gram in zip(at, works, grams, strict=True):
                        work[b, :, rest] = new_work
                        gram[b, rest, rest] = new_gram
                for j in range(wide):
                    lb_out[wide * i + j, :, c] = solved[j]
                    rb_out[wide * i + j, :, c] = solved[wide + j]
                return carry

            lax.fori_loop(0, count // (2 if count % 2 == 0 else 1), solve, 0)


def soap_update(seq, pieces, state, products):
    count = state[0].shape[0]
    piece_spec = pl.BlockSpec((1, BLK // 4, BLK), lambda i, s: (i, 0, 0))
    block_spec = pl.BlockSpec((1, BLK, BLK), lambda i, s: (i, 0, 0))
    whole_spec = pl.BlockSpec((count, BLK, BLK), lambda i, s: (0, 0, 0))
    shape = jax.ShapeDtypeStruct((count, BLK, BLK), F32)
    return pl.pallas_call(
        soap_kernel,
        grid_spec=pltpu.PrefetchScalarGridSpec(
            num_scalar_prefetch=1,
            grid=(count,),
            in_specs=[piece_spec] * 4 + [block_spec] * 9,
            out_specs=[block_spec] * 6 + [whole_spec] * 2,
            scratch_shapes=[
                pltpu.VMEM((BLK, BLK), LOW),
                pltpu.VMEM((2 * count, BLK, BLK), F32),
                pltpu.VMEM((2 * count, BLK, BLK), F32),
            ]
            + [pltpu.VMEM((128, 128), F32)] * (2 * count),
        ),
        out_shape=[shape] * 8,
        compiler_params=params(60),
        name="soap",
    )(seq, *pieces, *state, *products)


def split_kernel(dp, a_ref, b_ref, *outs):
    for k, out in enumerate(outs):
        out[...] = (a_ref[dp[0] ^ k].astype(F32) + b_ref[dp[0] ^ k].astype(F32)).astype(LOW)


def split_sum(dp, a, b):
    parts = a.shape[0]
    shape = a.shape[1:]
    return pl.pallas_call(
        split_kernel,
        grid_spec=pltpu.PrefetchScalarGridSpec(
            num_scalar_prefetch=1,
            grid=(1,),
            in_specs=[pl.BlockSpec(a.shape, lambda i, dp: (0,) * a.ndim)] * 2,
            out_specs=[pl.BlockSpec(shape, lambda i, dp: (0,) * len(shape))] * parts,
        ),
        out_shape=[jax.ShapeDtypeStruct(shape, LOW)] * parts,
        compiler_params=params(32),
        name="split_sum",
    )(dp, a, b)


def first_halves_kernel(keep, got, *outs, plans):
    per = keep.shape[4] // len(plans)
    names = ("x", 2, 1, 0)
    for g, plan in enumerate(plans):
        for out, side in zip(outs[2 * g : 2 * g + 2], (1, 0), strict=True):
            for n in range(4):
                where = {plan[0]: side, 2: 0}
                free = [name for name in plan[1:] if name != 2]
                where[free[0]], where[free[1]] = n // 2, n % 2
                at = tuple(where[name] for name in names) + (slice(per * g, per * g + per),)
                to = tuple(where[name] for name in plan[1:])
                out[to] = (keep[at].astype(F32) + got[at].astype(F32)).astype(LOW)


def first_halves(keep, got, plans):
    slots, rows, cols = keep.shape[4:]
    per, cut = slots // len(plans), rows // 3
    whole = pl.BlockSpec((2, 1, 2, 2, slots, cut, cols), lambda i, j: (0, i, 0, 0, 0, j, 0))
    outs = []
    for plan in plans:
        place = plan[1:].index(2)
        block = tuple(1 if n == place else 2 for n in range(3)) + (per, cut, cols)
        outs += [
            pl.BlockSpec(
                block,
                lambda i, j, place=place: tuple(i if n == place else 0 for n in range(3)) + (0, j, 0),
            )
        ] * 2
    shape = jax.ShapeDtypeStruct((2, 2, 2, per, rows, cols), LOW)
    return pl.pallas_call(
        functools.partial(first_halves_kernel, plans=plans),
        grid=(2, 3),
        in_specs=[whole, whole],
        out_specs=outs,
        out_shape=[shape] * len(outs),
        compiler_params=params(60),
        name="first_halves",
    )(keep, got)


def choose_kernel(dp, source, *refs):
    parts, early, out, held = refs[:-3], refs[-3], refs[-2], refs[-1]
    per, half = held.shape[1], held.shape[2]
    for k, part in enumerate(parts):
        held[k] = part[...]
    slots = out.shape[0]
    units = len(parts) * per

    def one(i, carry):
        block = source[i]

        @pl.when(2 * block >= units)
        def _():
            out[i] = early[i]

        @pl.when(2 * block < units)
        def _():
            for h in range(2):
                unit = 2 * block + h
                out[i, h * half : h * half + half] = held[lax.div(unit, per) ^ dp[0], lax.rem(unit, per)]

        return carry

    lax.fori_loop(0, slots, one, 0)


def choose(dp, source, parts, early):
    return pl.pallas_call(
        choose_kernel,
        grid_spec=pltpu.PrefetchScalarGridSpec(
            num_scalar_prefetch=2,
            grid=(1,),
            in_specs=[pl.BlockSpec(parts[0].shape, lambda i, dp, src: (0, 0, 0))] * len(parts)
            + [pl.BlockSpec(early.shape, lambda i, dp, src: (0, 0, 0))],
            out_specs=pl.BlockSpec(early.shape, lambda i, dp, src: (0, 0, 0)),
            scratch_shapes=[pltpu.VMEM((len(parts),) + parts[0].shape, LOW)],
        ),
        out_shape=jax.ShapeDtypeStruct(early.shape, LOW),
        compiler_params=params(32),
        name="choose",
    )(dp, source, *parts, early)


def swap(x, axis, bit):
    size = lax.axis_size(axis)
    return lax.ppermute(x, axis, [(i, i ^ bit) for i in range(size)])


def add_low(a, b):
    return (a.astype(F32) + b.astype(F32)).astype(LOW)


class Halving:
    def __init__(self, kept, got, names, slots=None):
        self.kept, self.got, self.names, self.slots = kept, got, list(names), slots

    def take(self, name, index):
        axis = self.names.index(name)
        found = []
        for array in (self.kept, self.got):
            starts, limits = [0] * array.ndim, list(array.shape)
            starts[axis], limits[axis] = index, index + 1
            if self.slots is not None:
                starts[-3], limits[-3] = self.slots
            part = lax.slice(array, starts, limits)
            found.append(part.reshape(part.shape[:axis] + part.shape[axis + 1 :]))
        return add_low(*found)

    def send(self, name, ready=None):
        sent, kept = ready or (self.take(name, 1), self.take(name, 0))
        self.names.remove(name)
        self.kept, self.slots, self.name = kept, None, name
        return sent

    def receive(self, sent):
        axis, bit = ("seq", 2) if self.name == "x" else ("dp", 2**self.name)
        self.got = swap(sent, axis, bit)

    def total(self):
        return add_low(self.kept, self.got)


def quarters(piece):
    across = swap(piece, "seq", 2)
    beside = swap(jnp.stack([piece, across]), "seq", 1)
    return piece, across, beside[0], beside[1]


def block_places(owners, owner_count, slot_count):
    block_count = owners.shape[0]
    ids = jnp.arange(block_count, dtype=jnp.int32)
    earlier = (owners[:, None] == owners[None, :]) & (ids[None, :] < ids[:, None])
    slots = jnp.sum(earlier.astype(jnp.int32), axis=1)
    places = owners * slot_count + slots
    matched = places[None, :] == jnp.arange(owner_count * slot_count, dtype=jnp.int32)[:, None]
    missing = 1 - jnp.any(matched, axis=1).astype(jnp.int32)
    sources = jnp.sum(jnp.where(matched, ids[None, :], 0), axis=1) + block_count * missing
    return slots, sources


def adam_vectors(gradient, vec, first_mom, second_mom):
    first_mom = BETA_ONE * first_mom + (1.0 - BETA_ONE) * gradient
    second_mom = BETA_TWO * second_mom + (1.0 - BETA_TWO) * gradient * gradient
    step_size = (first_mom / (1.0 - BETA_ONE**STEP)) / (
        jnp.sqrt(second_mom / (1.0 - BETA_TWO**STEP)) + ADAM_EPS
    )
    return first_mom, second_mom, vec - RATE_VECTOR * step_size


def on_device(
    tokens, cotangent, lengths, patch_mask, owners, master, moment_one, moment_two,
    left_stats, right_stats, left_basis, right_basis, vec, vec_one, vec_two,
):
    owner_count = lax.axis_size("dp")
    slot_count = master.shape[0]
    quarter = BLK // 4
    seq_id = lax.axis_index("seq").astype(jnp.int32)
    dp_id = lax.axis_index("dp").astype(jnp.int32)
    core, chip = seq_id % 2, seq_id // 2
    part_len = tokens.shape[1]
    slots, sources = block_places(owners, owner_count, slot_count)
    first_blocks = 3 * (D // BLK) ** 2

    mine = lax.dynamic_index_in_dim(
        master.reshape(slot_count, 4, quarter, BLK), seq_id, 1, keepdims=False
    ).astype(LOW)
    gathered = lax.all_gather(mine, AXES, axis=0, tiled=False).reshape(
        owner_count, 4, slot_count, quarter, BLK
    )

    products = stats_product(left_stats, right_stats, left_basis, right_basis)

    def halves_of(pair):
        kept = lax.dynamic_index_in_dim(pair, chip, 0, keepdims=False)
        return kept, lax.dynamic_index_in_dim(pair, 1 - chip, 0, keepdims=False)

    kept, sent = halves_of(tokens)
    x = jnp.concatenate([kept, swap(sent, "seq", 2)], axis=0)
    dy_kept, dy_sent = halves_of(cotangent)

    def to_positions(mine, other):
        return jnp.where(chip == 0, jnp.stack([mine, other]), jnp.stack([other, mine]))

    positions = jnp.arange(patch_mask.shape[-1], dtype=jnp.int32)
    live = (positions[None, :] < lengths[:, None]) & ((patch_mask == 1) | (positions[None, :] == 0))
    live = lax.dynamic_index_in_dim(live, chip, 0, keepdims=False).reshape(4, part_len)
    order = seq_id ^ jnp.array([0, 2, 1, 3], jnp.int32)
    fill = jnp.where(jnp.take(live, order, axis=0).reshape(-1), 0.0, NEG_FILL).astype(LOW)
    fill = jnp.broadcast_to(fill[:, None], (fill.shape[0], 128))

    bias = jnp.concatenate([vec[4], jnp.zeros_like(vec[4]), vec[5]])[None, :]
    gathered, products, dy_sent = lax.optimization_barrier((gathered, products, dy_sent))
    dy_got = swap(dy_sent, "seq", 2)
    q, kv, normed = qkv_forward(owners, slots, x, vec, bias, gathered)
    other = swap(kv, "seq", 1)
    attn, lse = attn_forward(q, kv, other, fill)
    attn, dy_got = lax.optimization_barrier((attn, dy_got))
    dy = jnp.concatenate([dy_kept, dy_got], axis=0)
    b1 = vec[8:].reshape(1, FF)
    seq_of, dp_of = seq_id.reshape(1), dp_id.reshape(1)
    result, d_mid, d_attn, keep, send, sums_two, bias_grad = mid_layer(
        owners, slots, owners ^ dp_id, seq_of, x, attn, dy, vec, b1, gathered
    )
    result_other = swap(result[part_len:], "seq", 2)

    bits = owner_count.bit_length() - 1
    if slot_count % 3 == 0 and bits == 3:
        plans = [["x", 0, 1, 2], [0, 1, "x", 2], [1, "x", 0, 2]]
    else:
        plans = [["x"] + list(range(bits))]
    per = slot_count // len(plans)
    names = ["x"] + list(range(bits))[::-1]
    shape = (2,) * (1 + bits) + keep.shape[2:]
    keep, got = keep.reshape(shape), swap(send, "seq", 1).reshape(shape)
    groups = [
        Halving(keep, got, names, (per * g, per * g + per)) for g in range(len(plans))
    ]
    guard = fill

    def advance(step, guard):
        ready = [None] * len(plans)
        if step == 0 and len(plans) == 3:
            made = first_halves(keep, groups[0].got, plans)
            ready = [tuple(made[2 * g : 2 * g + 2]) for g in range(3)]
            for group, plan in zip(groups, plans, strict=True):
                group.names = list(plan)
        sent = [group.send(plan[step], own) for group, plan, own in zip(groups, plans, ready, strict=True)]
        *sent, guard = lax.optimization_barrier((*sent, guard))
        for group, array in zip(groups, sent, strict=True):
            group.receive(array)
        return guard

    grads = []
    taken = 0
    for first, count in ((0, 2), (2, 3), (5, 1)):
        if first:
            guard = advance(taken, guard)
            taken += 1
        parts = attn_backward(q, kv, other, guard, attn, lse, d_attn, first, count)
        got, parts, result_other = lax.optimization_barrier(
            ([group.got for group in groups], parts, result_other)
        )
        for group, array in zip(groups, got, strict=True):
            group.got = array
        dq, dk, dv, sent_k, sent_v = parts
        grads += [dq, dk, swap(sent_k, "seq", 1), dv, swap(sent_v, "seq", 1)]
    normed = advance(taken, normed)
    taken += 1
    late_keep, late_send, cols = qkv_grad(seq_of, normed, grads)
    late_shape = (2, -1, quarter, BLK)
    late = Halving(late_keep.reshape(late_shape), swap(late_send.reshape(late_shape), "seq", 1), ["x"])

    def after(value):
        got, value = lax.optimization_barrier(([group.got for group in groups], value))
        for group, array in zip(groups, got, strict=True):
            group.got = array
        return value

    sent_x, d_mid = lax.optimization_barrier((late.send("x"), d_mid))
    late.receive(sent_x)
    cols = after(cols)
    while taken < len(names):
        advance(taken, fill)
        taken += 1
    d_x, sums_one = qkv_backward(owners, slots, x, d_mid, vec, grads, gathered)
    late.got, d_x = lax.optimization_barrier((late.got, d_x))
    d_x = after(d_x)
    d_x_other = swap(d_x[part_len:], "seq", 2)
    early = jnp.concatenate([group.total() for group in groups], axis=0)
    output = to_positions(result[:part_len], result_other)
    d_tokens = to_positions(d_x[:part_len], d_x_other)
    early, output, d_tokens = lax.optimization_barrier((early, output, d_tokens))

    mine_from = lax.dynamic_slice_in_dim(sources, dp_id * slot_count, slot_count)
    if 2 * first_blocks % owner_count == 0:
        unit = (owner_count, 2 * first_blocks // owner_count, quarter // 2, BLK)
        parts = split_sum(dp_of, late.kept.reshape(unit), late.got.reshape(unit))
        parts = [parts[0]] + [swap(part, "dp", k) for k, part in enumerate(parts) if k]
        total = sum(part.astype(F32) for part in parts).astype(LOW)
        parts = [total] + [swap(total, "dp", k) for k in range(1, owner_count)]
        piece = choose(dp_of, mine_from, parts, early)
    else:
        tiles = jnp.concatenate([late.total(), jnp.zeros((1, quarter, BLK), LOW)], axis=0)
        at = sources.reshape(owner_count, slot_count)[dp_id ^ jnp.arange(owner_count)]
        tiles = jnp.take(tiles, jnp.minimum(at, first_blocks).reshape(-1), axis=0)
        tiles = tiles.reshape((2,) * bits + (slot_count, quarter, BLK))
        owned = Halving(tiles, jnp.zeros_like(tiles), names[1:])
        for bit in range(bits):
            owned.receive(owned.send(bit))
        piece = jnp.where((mine_from < first_blocks)[:, None, None], owned.total(), early)
    state = (master, moment_one, moment_two, left_stats, right_stats, left_basis, right_basis)
    piece = jnp.where((mine_from < owners.shape[0])[:, None, None], piece, jnp.zeros_like(piece))
    piece, sums_one, sums_two, cols, bias_grad = lax.optimization_barrier(
        (piece, sums_one, sums_two, cols, bias_grad)
    )
    updates = soap_update(seq_of, quarters(piece), state, products)

    vec_grad = jnp.concatenate(
        [
            sums_one[0:2],
            sums_two[0:2],
            cols[:, :D],
            cols[:, 2 * D :],
            sums_two[2:4],
            bias_grad.reshape(-1, D),
        ],
        axis=0,
    )
    vec_parts = lax.all_gather(vec_grad, AXES, axis=0, tiled=False)
    updates, vec_parts = lax.optimization_barrier((updates, vec_parts))
    vec_total = jnp.sum(vec_parts, axis=0)
    vec_first, vec_second, vec_next = adam_vectors(vec_total, vec, vec_one, vec_two)
    grad_blocks, w_new, one_new, two_new, ls_new, rs_new, lb_new, rb_new = updates
    return (
        output, d_tokens, grad_blocks, w_new, one_new, two_new, ls_new, rs_new, lb_new, rb_new,
        vec_first, vec_second, vec_next,
    )


def solution(mesh):
    rows, blocks, whole = P("dp", "seq", None), P("dp", None, None), P()
    return jax.shard_map(
        on_device,
        mesh=mesh,
        in_specs=(rows, rows, P("dp"), P("dp", None), whole) + (blocks,) * 7 + (whole,) * 3,
        out_specs=(rows, rows) + (blocks,) * 8 + (whole,) * 3,
        check_vma=False,
    )
```

```python
import functools

import jax
import jax.numpy as jnp
from jax import lax
from jax.experimental import pallas as pl
from jax.experimental.pallas import tpu as pltpu
from jax.sharding import PartitionSpec as P

D = 768
FF = 3072
BLK = 384
STEP = 10

NORM_EPS = 1e-06
NEG_FILL = -1000000000.0
BETA_ONE = 0.9
BETA_TWO = 0.999
BETA_STAT = 0.95
RATE_MATRIX = 0.1
RATE_VECTOR = 0.3
DECAY_RATE = 0.01
ADAM_EPS = 1e-08

LOW = jnp.bfloat16
F32 = jnp.float32
AXES = ("dp", "seq")
MIB = 2**20

TAIL_P = 0.24
TAIL_C = (
    0.09575380798443668,
    0.09552183543465394,
    0.09284136585084933,
    0.06338567653857548,
    0.11841694922211018,
    -0.06574016740998187,
    0.15281935057715396,
    -0.052998628523732765,
)


def dot(a, b, ca, cb):
    return lax.dot_general(a, b, (((ca,), (cb,)), ((), ())), preferred_element_type=F32)


def lanes(shape):
    return lax.broadcasted_iota(jnp.int32, shape, len(shape) - 1)


def gelu_pair(x):
    u = jnp.abs(x)
    t = 1.0 / (1.0 + TAIL_P * u)
    poly = TAIL_C[-1]
    for coeff in TAIL_C[-2::-1]:
        poly = poly * t + coeff
    expo = jnp.exp(-0.5 * u * u)
    tail = poly * t * expo
    cdf = jnp.where(x < 0, tail, 1.0 - tail)
    return x * cdf, cdf + x * (expo * 0.3989422804014327)


def norm_parts(rows):
    center = rows - jnp.mean(rows, axis=-1, keepdims=True)
    rstd = lax.rsqrt(jnp.mean(center * center, axis=-1, keepdims=True) + NORM_EPS)
    return center * rstd, rstd


def norm_back(grad, hat, rstd):
    return rstd * (
        grad
        - jnp.mean(grad, axis=-1, keepdims=True)
        - hat * jnp.mean(grad * hat, axis=-1, keepdims=True)
    )


def params(limit):
    return pltpu.CompilerParams(vmem_limit_bytes=limit * MIB)


def tile_spec(block_of):
    return pl.BlockSpec(
        (1, 4, 1, BLK // 4, BLK),
        lambda i, own, slot: (own[block_of(i)], 0, slot[block_of(i)], 0, 0),
    )


def tile(ref):
    return ref[...].reshape(BLK, BLK)


def full_spec(shape):
    return pl.BlockSpec(shape, lambda i, own, slot: (0,) * len(shape))


def quarter_at(seq, rel_core, rel_x):
    return seq ^ (2 * rel_x + rel_core)


def square(tiles, held):
    for i in range(2):
        for j in range(2):
            held[i * BLK : i * BLK + BLK, j * BLK : j * BLK + BLK] = tile(tiles[2 * i + j])
    return held[...]


def qkv_kernel(own, slot, x_ref, vec_ref, bias_ref, t00, t01, t10, t11, q_ref, kv_ref, a_ref, held):
    @pl.when(pl.program_id(0) == 0)
    def _():
        hat, _ = norm_parts(x_ref[...].astype(F32))
        a_ref[...] = (hat * vec_ref[0:1, :] + vec_ref[1:2, :]).astype(LOW)

    low = (dot(a_ref[...], square((t00, t01, t10, t11), held), 1, 0) + bias_ref[...]).astype(LOW)

    @pl.when(pl.program_id(0) == 0)
    def _():
        q_ref[...] = low

    @pl.when(pl.program_id(0) > 0)
    def _():
        kv_ref[...] = low


def qkv_tiles():
    return [tile_spec(lambda i, n=n: 6 * (n // 2) + 2 * i + n % 2) for n in range(4)]


def qkv_forward(own, slot, x, vec, bias, gathered):
    rows = x.shape[0]
    return pl.pallas_call(
        qkv_kernel,
        grid_spec=pltpu.PrefetchScalarGridSpec(
            num_scalar_prefetch=2,
            grid=(3,),
            in_specs=[
                full_spec((rows, D)),
                full_spec(vec.shape),
                pl.BlockSpec((1, D), lambda i, own, slot: (0, i)),
            ]
            + qkv_tiles(),
            out_specs=[
                full_spec((rows, D)),
                pl.BlockSpec((rows, D), lambda i, own, slot: (0, jnp.maximum(i - 1, 0))),
                full_spec((rows, D)),
            ],
            scratch_shapes=[pltpu.VMEM((D, D), LOW)],
        ),
        out_shape=[
            jax.ShapeDtypeStruct((rows, D), LOW),
            jax.ShapeDtypeStruct((rows, 2 * D), LOW),
            jax.ShapeDtypeStruct((rows, D), LOW),
        ],
        compiler_params=params(48),
        name="qkv",
    )(own, slot, x, vec, bias, *([gathered] * 4))


def attn_fwd_kernel(q_ref, k1, v1, k2, v2, bias_ref, o_ref, lse_ref, ka, kb, va, vb):
    rows = k1.shape[0]

    @pl.when(pl.program_id(1) == 0)
    def _():
        ln = lanes((rows, 128))
        for i, (k, v) in enumerate(((k1, v1), (k2, v2))):
            r = slice(i * rows, i * rows + rows)
            keys, values, bias = k[...], v[...], bias_ref[r, :]
            one = jnp.ones_like(values)
            ka[r, :] = jnp.where(ln == 64, bias, keys)
            kb[r, :] = jnp.where(ln == 0, bias, keys)
            va[r, :] = jnp.where(ln < 64, values, one)
            vb[r, :] = jnp.where(ln < 64, one, values)

    q = q_ref[...] * jnp.asarray(0.125, LOW)
    ln = lanes(q.shape)
    one, zero = jnp.ones_like(q), jnp.zeros_like(q)
    qa = jnp.where(ln < 64, q, jnp.where(ln == 64, one, zero))
    qb = jnp.where(ln < 64, jnp.where(ln == 0, one, zero), q)
    outs, tops = [], []
    for query, keys, values in ((qa, ka, va), (qb, kb, vb)):
        logits = dot(query, keys[...], 1, 1)
        top = jnp.max(logits, axis=1, keepdims=True)
        expo = jnp.exp(logits - top).astype(LOW)
        outs.append(dot(expo, values[...], 1, 0))
        tops.append(top)
    total = jnp.where(ln < 64, outs[1], outs[0])
    attended = jnp.where(ln < 64, outs[0], outs[1])
    o_ref[...] = (attended / pltpu.roll(total, 64, 1)).astype(LOW)
    lse_ref[...] = jnp.where(ln < 64, tops[1], tops[0]) + jnp.log(total)


def attn_forward(q, kv, other, bias, q_rows=256):
    rows, pairs = q.shape[0], D // 128
    keys = 2 * rows
    q_spec = pl.BlockSpec((q_rows, 128), lambda p, i: (i, p))
    return pl.pallas_call(
        attn_fwd_kernel,
        grid=(pairs, rows // q_rows),
        in_specs=[
            q_spec,
            pl.BlockSpec((rows, 128), lambda p, i: (0, p)),
            pl.BlockSpec((rows, 128), lambda p, i: (0, pairs + p)),
            pl.BlockSpec((rows, 128), lambda p, i: (0, p)),
            pl.BlockSpec((rows, 128), lambda p, i: (0, pairs + p)),
            pl.BlockSpec((keys, 128), lambda p, i: (0, 0)),
        ],
        out_specs=[q_spec, q_spec],
        out_shape=[
            jax.ShapeDtypeStruct((rows, D), LOW),
            jax.ShapeDtypeStruct((rows, D), F32),
        ],
        scratch_shapes=[pltpu.VMEM((keys, 128), LOW)] * 4,
        compiler_params=params(48),
        name="attn_fwd",
    )(q, kv, kv, other, other, bias)


def three_parts(x):
    high = x.astype(LOW).astype(F32)
    rest = x - high
    mid = rest.astype(LOW).astype(F32)
    return high, mid, rest - mid


def low_parts(x, count):
    found = []
    for _ in range(count):
        part = x.astype(LOW)
        found.append(part)
        x = x - part.astype(F32)
    return found


def dot_parts(a, b, ca, cb, order):
    pairs = [(i, j) for i in range(len(a)) for j in range(len(b)) if i + j < order]
    a = jnp.concatenate([a[i] for i, _ in pairs], axis=ca)
    b = jnp.concatenate([b[j] for _, j in pairs], axis=cb)
    return dot(a, b, ca, cb)


def with_spare(x, spare, value, one, first):
    ln = lanes(x.shape)
    high, mid, low = three_parts(value)
    filled = jnp.where(ln == first + 3, one, 0.0)
    for i, part in enumerate((high, mid, low)):
        filled = jnp.where(ln == first + i, part, filled)
    return jnp.where(spare, filled, x).astype(LOW)


def attn_bwd_kernel(
    q_ref, k1, v1, k2, v2, bias_ref, o_ref, lse_ref, do_ref,
    dq_ref, dk1, dv1, dkv2, ka, kb, va, vb, kt, dk, dv, *, chunk,
):
    rows = k1.shape[0]

    @pl.when(pl.program_id(1) == 0)
    def _():
        ln = lanes((rows, 128))
        for i, (k, v) in enumerate(((k1, v1), (k2, v2))):
            r = slice(i * rows, i * rows + rows)
            keys, values, bias = k[...], v[...], bias_ref[r, :]
            one, zero = jnp.ones_like(values), jnp.zeros_like(values)
            ka[r, :] = jnp.where(ln < 64, keys, jnp.where(ln < 67, one, jnp.where(ln == 67, bias, zero)))
            kb[r, :] = jnp.where(ln >= 64, keys, jnp.where(ln < 3, one, jnp.where(ln == 3, bias, zero)))
            va[r, :] = jnp.where(ln < 64, values, jnp.where(ln < 67, one, zero))
            vb[r, :] = jnp.where(ln >= 64, values, jnp.where(ln < 3, one, zero))
            kt[:, r] = keys.T
        dk[...] = jnp.zeros_like(dk)
        dv[...] = jnp.zeros_like(dv)

    q = q_ref[...].astype(F32) * 0.125
    left = lanes(q.shape) < 64
    grad = do_ref[...].astype(F32)
    prod = grad * o_ref[...].astype(F32)
    sum_a = jnp.sum(jnp.where(left, prod, 0.0), axis=1, keepdims=True)
    sum_b = jnp.sum(jnp.where(left, 0.0, prod), axis=1, keepdims=True)
    delta = jnp.where(left, sum_b, sum_a)
    lse = lse_ref[...]
    zero = jnp.zeros_like(q)
    heads = (
        (
            with_spare(q, ~left, -lse, 1.0, 64), with_spare(grad, ~left, -delta, 0.0, 64), ka, va,
            jnp.where(left, q, zero).astype(LOW), jnp.where(left, grad, zero).astype(LOW),
        ),
        (
            with_spare(q, left, -lse, 1.0, 0), with_spare(grad, left, -delta, 0.0, 0), kb, vb,
            jnp.where(left, zero, q).astype(LOW), jnp.where(left, zero, grad).astype(LOW),
        ),
    )
    d_query = [jnp.zeros((64, q.shape[0]), F32)] * 2
    for c in range(2 * rows // chunk):
        r = slice(c * chunk, c * chunk + chunk)
        dv_c, dk_c = dv[r, :], dk[r, :]
        for h, (q_aug, g_aug, keys, values, q_only, g_only) in enumerate(heads):
            probs = jnp.exp(dot(keys[r, :], q_aug, 1, 1))
            d_logits = (probs * dot(values[r, :], g_aug, 1, 1)).astype(LOW)
            dv_c = dv_c + dot(probs.astype(LOW), g_only, 1, 0)
            dk_c = dk_c + dot(d_logits, q_only, 1, 0)
            d_query[h] = d_query[h] + dot(kt[64 * h : 64 * h + 64, r], d_logits, 1, 0)
        dv[r, :] = dv_c
        dk[r, :] = dk_c
    dq_ref[...] = (jnp.concatenate(d_query, axis=0) * 0.125).T.astype(LOW)

    @pl.when(pl.program_id(1) == pl.num_programs(1) - 1)
    def _():
        dk1[...] = dk[:rows, :].astype(LOW)
        dv1[...] = dv[:rows, :].astype(LOW)
        dkv2[0] = dk[rows:, :].astype(LOW)
        dkv2[1] = dv[rows:, :].astype(LOW)


def attn_backward(q, kv, other, bias, attn, lse, d_attn, first, count, q_rows=512, chunk=1024):
    rows, pairs = q.shape[0], D // 128
    keys = 2 * rows
    out_spec = pl.BlockSpec((q_rows, 128), lambda p, i: (i, p))
    k_out = pl.BlockSpec((rows, 128), lambda p, i: (0, p))
    q_spec = pl.BlockSpec((q_rows, 128), lambda p, i: (i, first + p))
    k_spec = pl.BlockSpec((rows, 128), lambda p, i: (0, first + p))
    v_spec = pl.BlockSpec((rows, 128), lambda p, i: (0, pairs + first + p))
    return pl.pallas_call(
        functools.partial(attn_bwd_kernel, chunk=chunk),
        grid=(count, rows // q_rows),
        in_specs=[
            q_spec, k_spec, v_spec, k_spec, v_spec, pl.BlockSpec((keys, 128), lambda p, i: (0, 0)),
            q_spec, q_spec, q_spec,
        ],
        out_specs=[out_spec, k_out, k_out, pl.BlockSpec((2, rows, 128), lambda p, i: (0, 0, p))],
        out_shape=[jax.ShapeDtypeStruct((rows, count * 128), LOW)] * 3
        + [jax.ShapeDtypeStruct((2, rows, count * 128), LOW)],
        scratch_shapes=[pltpu.VMEM((keys, 128), LOW)] * 4
        + [pltpu.VMEM((128, keys), LOW)]
        + [pltpu.VMEM((keys, 128), F32)] * 2,
        compiler_params=params(56),
        name="attn_bwd",
    )(q, kv, kv, other, other, bias, attn, lse, d_attn)


def mid_kernel(
    own, slot, rel, seq, x_ref, attn_ref, dy_ref, vec_ref, b1_ref, o00, o01, o10, o11, *refs, chunk):
    ups, downs = refs[:4], refs[4:8]
    (
        res_ref, dmid_ref, dattn_ref, keep, send, sums_ref, gb1_ref,
        mid, a2, acc, da2, up_s, down_s, stage, sems,
    ) = refs[8:]
    step = pl.program_id(0)
    last = pl.num_programs(0) - 1
    quarter = BLK // 4

    def copies(buf, i, block):
        found = []
        for rel_core, out in enumerate((keep, send)):
            for rel_x in range(2):
                found.append(
                    pltpu.make_async_copy(
                        stage.at[buf, i, quarter_at(seq[0], rel_core, rel_x)],
                        out.at[rel_x, rel[block], slot[block]],
                        sems.at[buf, i, 2 * rel_core + rel_x],
                    )
                )
        return found

    def put(buf, i, block, value):
        low = value.astype(LOW)
        for part in range(4):
            stage[buf, i, part] = low[part * quarter : part * quarter + quarter]
        for copy in copies(buf, i, block):
            copy.start()

    def settle(buf, count=8):
        for i in range(count):
            for copy in copies(buf, i, 0):
                copy.wait()

    @pl.when(step == 0)
    def _():
        mid[...] = (
            x_ref[...].astype(F32)
            + dot(attn_ref[...], square((o00, o01, o10, o11), up_s), 1, 0)
            + vec_ref[6:7, :]
        )
        hat, _ = norm_parts(mid[...])
        a2[...] = (hat * vec_ref[2:3, :] + vec_ref[3:4, :]).astype(LOW)
        acc[...] = jnp.zeros_like(acc)
        da2[...] = jnp.zeros_like(da2)

    @pl.when((step > 0) & (step < last))
    def _():
        rows = a2.shape[0]
        up, down = square(ups, up_s), square(downs, down_s)
        bias_grad = jnp.zeros((1, D), F32)
        acts, d_hids = [], []
        for c in range(rows // chunk):
            r = slice(c * chunk, c * chunk + chunk)
            act, slope = gelu_pair(dot(a2[r, :], up, 1, 0) + b1_ref[...])
            act = act.astype(LOW)
            d_hid = (dot(dy_ref[r, :], down, 1, 1) * slope).astype(LOW)
            acc[r, :] += dot(act, down, 1, 0)
            da2[r, :] += dot(d_hid, up, 1, 1)
            bias_grad = bias_grad + jnp.sum(d_hid.astype(F32), axis=0, keepdims=True)
            acts.append(act)
            d_hids.append(d_hid)
        gb1_ref[...] = bias_grad
        act = jnp.concatenate(acts, axis=0)
        d_hid = jnp.concatenate(d_hids, axis=0)
        buf = step % 2

        @pl.when(step > 2)
        def _():
            settle(buf)

        for i in range(2):
            c = slice(i * BLK, i * BLK + BLK)
            up_grad = dot(a2[:, c], d_hid, 0, 0)
            down_grad = dot(act[:, c], dy_ref[...], 0, 0)
            for j in range(2):
                k = slice(j * BLK, j * BLK + BLK)
                put(buf, 2 * i + j, 16 + 8 * i + 2 * (step - 1) + j, up_grad[:, k])
                put(buf, 4 + 2 * i + j, 32 + 4 * (step - 1) + 2 * i + j, down_grad[:, k])

    @pl.when(step == last)
    def _():
        res_ref[...] = (mid[...] + acc[...] + vec_ref[7:8, :]).astype(LOW)
        hat, rstd = norm_parts(mid[...])
        grad = da2[...]
        dy = dy_ref[...].astype(F32)
        sums_ref[0:1, :] = jnp.sum(hat * grad, axis=0, keepdims=True)
        sums_ref[1:2, :] = jnp.sum(grad, axis=0, keepdims=True)
        d_mid = dy + norm_back(grad * vec_ref[2:3, :], hat, rstd)
        dmid_ref[...] = d_mid
        d_proj = d_mid.astype(LOW)
        sums_ref[2:3, :] = jnp.sum(d_proj.astype(F32), axis=0, keepdims=True)
        sums_ref[3:4, :] = jnp.sum(dy, axis=0, keepdims=True)
        sums_ref[4:8, :] = jnp.zeros((4, D), F32)
        dattn_ref[...] = dot(d_proj, square((o00, o01, o10, o11), up_s), 1, 1).astype(LOW)
        settle(0)
        for i in range(2):
            out_grad = dot(attn_ref[:, i * BLK : i * BLK + BLK], d_proj, 0, 0)
            for j in range(2):
                put(0, 2 * i + j, 12 + 2 * i + j, out_grad[:, j * BLK : j * BLK + BLK])
        settle(1)
        settle(0, 4)


def mid_layer(own, slot, rel, seq, x, attn, dy, vec, b1, gathered, chunk=512):
    rows = x.shape[0]
    wide = FF // D
    quarter = BLK // 4
    owners, slots = gathered.shape[0], gathered.shape[2]

    def part(i):
        return jnp.clip(i - 1, 0, wide - 1)

    def full(shape):
        return pl.BlockSpec(shape, lambda i, own, slot, rel, seq: (0,) * len(shape))

    def tile_at(block_of):
        return pl.BlockSpec(
            (1, 4, 1, quarter, BLK),
            lambda i, own, slot, rel, seq: (own[block_of(i)], 0, slot[block_of(i)], 0, 0),
        )

    row_spec = full((rows, D))
    strip = pl.BlockSpec((1, D), lambda i, own, slot, rel, seq: (0, part(i)))
    anywhere = pl.BlockSpec(memory_space=pl.ANY)
    place_shape = jax.ShapeDtypeStruct((2, owners, slots, quarter, BLK), LOW)
    return pl.pallas_call(
        functools.partial(mid_kernel, chunk=chunk),
        grid_spec=pltpu.PrefetchScalarGridSpec(
            num_scalar_prefetch=4,
            grid=(wide + 2,),
            in_specs=[row_spec, row_spec, row_spec, full(vec.shape), strip]
            + [tile_at(lambda i, b=b: b) for b in (12, 13, 14, 15)]
            + [tile_at(lambda i, n=n: 16 + 8 * (n // 2) + 2 * part(i) + n % 2) for n in range(4)]
            + [tile_at(lambda i, n=n: 32 + 4 * part(i) + n) for n in range(4)],
            out_specs=[row_spec, row_spec, row_spec, anywhere, anywhere, full((8, D)), strip],
            scratch_shapes=[
                pltpu.VMEM((rows, D), F32),
                pltpu.VMEM((rows, D), LOW),
                pltpu.VMEM((rows, D), F32),
                pltpu.VMEM((rows, D), F32),
                pltpu.VMEM((D, D), LOW),
                pltpu.VMEM((D, D), LOW),
                pltpu.VMEM((2, 8, 4, quarter, BLK), LOW),
                pltpu.SemaphoreType.DMA((2, 8, 4)),
            ],
        ),
        out_shape=[
            jax.ShapeDtypeStruct((rows, D), LOW),
            jax.ShapeDtypeStruct((rows, D), F32),
            jax.ShapeDtypeStruct((rows, D), LOW),
            place_shape,
            place_shape,
            jax.ShapeDtypeStruct((8, D), F32),
            jax.ShapeDtypeStruct((1, FF), F32),
        ],
        compiler_params=params(60),
        name="mid",
    )(own, slot, rel, seq, x, attn, dy, vec, b1, *([gathered] * 12))


def d_columns(step, grads, work):
    def joined(n, *at):
        return jnp.concatenate([ref[at] if at else ref[...] for ref in grads[n::4]], axis=1)

    @pl.when(step == 0)
    def _():
        work(joined(0))

    for n in (1, 2):

        @pl.when(step == n)
        def _():
            work((joined(n).astype(F32) + joined(3, n - 1).astype(F32)).astype(LOW))


def qkv_grad_kernel(seq, a_ref, *refs):
    grads, (keep, send, cols_ref, stage) = refs[:-4], refs[-4:]
    quarter = BLK // 4

    def work(d_cols):
        cols_ref[...] = jnp.sum(d_cols.astype(F32), axis=0, keepdims=True)
        for i in range(2):
            stage[...] = dot(a_ref[:, i * BLK : i * BLK + BLK], d_cols, 0, 0).astype(LOW)
            for rel_core, out in enumerate((keep, send)):
                for rel_x in range(2):
                    start = pl.multiple_of(quarter_at(seq[0], rel_core, rel_x) * quarter, quarter)
                    for j in range(2):
                        out[rel_x, i, j] = stage[pl.ds(start, quarter), j * BLK : j * BLK + BLK]

    d_columns(pl.program_id(0), grads, work)


def qkv_grad(seq, normed, grads):
    rows = normed.shape[0]
    quarter = BLK // 4
    tile_out = pl.BlockSpec((2, 2, 2, quarter, BLK), lambda i, seq: (0, 0, i, 0, 0))
    shape = jax.ShapeDtypeStruct((2, 2, 6, quarter, BLK), LOW)
    return pl.pallas_call(
        qkv_grad_kernel,
        grid_spec=pltpu.PrefetchScalarGridSpec(
            num_scalar_prefetch=1,
            grid=(3,),
            in_specs=[pl.BlockSpec((rows, D), lambda i, seq: (0, 0))]
            + [pl.BlockSpec(grad.shape, lambda i, seq, n=grad.ndim: (0,) * n) for grad in grads],
            out_specs=[tile_out, tile_out, pl.BlockSpec((1, D), lambda i, seq: (0, i))],
            scratch_shapes=[pltpu.VMEM((BLK, D), LOW)],
        ),
        out_shape=[shape, shape, jax.ShapeDtypeStruct((1, 3 * D), F32)],
        compiler_params=params(48),
        name="qkv_grad",
    )(seq, normed, *grads)


def qkv_bwd_kernel(own, slot, x_ref, dmid_ref, vec_ref, *refs):
    grads, tiles, (dx_ref, sums_ref, acc, held) = refs[:-8], refs[-8:-4], refs[-4:]
    step = pl.program_id(0)

    @pl.when(step == 0)
    def _():
        acc[...] = jnp.zeros_like(acc)

    def work(d_cols):
        acc[...] += dot(d_cols, square(tiles, held), 1, 1)

    d_columns(step, grads, work)

    @pl.when(step == 2)
    def _():
        hat, rstd = norm_parts(x_ref[...].astype(F32))
        grad = acc[...]
        sums_ref[0:1, :] = jnp.sum(hat * grad, axis=0, keepdims=True)
        sums_ref[1:2, :] = jnp.sum(grad, axis=0, keepdims=True)
        sums_ref[2:8, :] = jnp.zeros((6, D), F32)
        dx_ref[...] = (dmid_ref[...] + norm_back(grad * vec_ref[0:1, :], hat, rstd)).astype(LOW)


def qkv_backward(own, slot, x, d_mid, vec, grads, gathered):
    rows = x.shape[0]
    row_spec = full_spec((rows, D))
    return pl.pallas_call(
        qkv_bwd_kernel,
        grid_spec=pltpu.PrefetchScalarGridSpec(
            num_scalar_prefetch=2,
            grid=(3,),
            in_specs=[row_spec, row_spec, full_spec(vec.shape)]
            + [full_spec(grad.shape) for grad in grads]
            + qkv_tiles(),
            out_specs=[row_spec, full_spec((8, D))],
            scratch_shapes=[pltpu.VMEM((rows, D), F32), pltpu.VMEM((D, D), LOW)],
        ),
        out_shape=[jax.ShapeDtypeStruct((rows, D), LOW), jax.ShapeDtypeStruct((8, D), F32)],
        compiler_params=params(60),
        name="qkv_bwd",
    )(own, slot, x, d_mid, vec, *grads, *([gathered] * 4))


def eliminate(blocks):
    count, size = len(blocks), blocks[0].shape[0]
    batch = min(count, 6)
    lane = lanes((1, 8, size))
    sub = lax.broadcasted_iota(jnp.int32, (1, 8, size), 1)
    wide_lane = lanes((size, size))
    shape = (batch, 8, size)

    def group(g, carry):
        base = pl.multiple_of(8 * g, 8)
        for at in range(0, count, batch):
            some = blocks[at : at + batch]
            slab = jnp.stack([y[pl.ds(base, 8), :] for y in some], axis=0)
            rolled = jnp.stack([pltpu.roll(slab[b], size - base, 1) for b in range(batch)], axis=0)
            columns = [jnp.broadcast_to(rolled[:, :, k : k + 1], shape) for k in range(8)]
            inside = (lane >= base) & (lane < base + 8)
            rows = jnp.where(inside, jnp.where(lane - base == sub, 1.0, 0.0), slab)
            scale = jnp.zeros(shape, F32)
            for j in range(8):
                inv_root = lax.rsqrt(jnp.broadcast_to(columns[j][:, j : j + 1, :], shape))
                scale = jnp.where(sub == j, inv_root, scale)
                factor = jnp.where(sub > j, columns[j] * (inv_root * inv_root), 0.0)
                rows = rows - factor * jnp.broadcast_to(rows[:, j : j + 1, :], shape)
                for k in range(j + 1, 8):
                    columns[k] = columns[k] - factor * jnp.broadcast_to(columns[k][:, j : j + 1, :], shape)
            rows = rows * scale
            passed = (wide_lane >= base) & (wide_lane < base + 8)
            for b, y in enumerate(some):
                high, mid, low = three_parts(rows[b])
                first = jnp.concatenate([high, high, mid, high, low, mid], axis=0)
                first = jnp.where(jnp.broadcast_to(lane[0, :1] >= base + 8, first.shape), first, 0.0)
                second = jnp.concatenate([high, mid, high, low, high, mid], axis=0)
                update = dot(first.astype(LOW), second.astype(LOW), 0, 0)
                y[...] = jnp.where(passed, 0.0, y[...]) - update
                y[pl.ds(base, 8), :] = rows[b]
        return carry

    lax.fori_loop(0, size // 8, group, 0)


def stats_kernel(ls_ref, rs_ref, lb_ref, rb_ref, left, right):
    for stats, basis, out in ((ls_ref, lb_ref, left), (rs_ref, rb_ref, right)):
        out[0] = BETA_STAT * dot_parts(low_parts(stats[0], 3), low_parts(basis[0], 3), 1, 0, 3)


def stats_product(left_stats, right_stats, left_basis, right_basis):
    count = left_stats.shape[0]
    block_spec = pl.BlockSpec((1, BLK, BLK), lambda i: (i, 0, 0))
    return pl.pallas_call(
        stats_kernel,
        grid=(count,),
        in_specs=[block_spec] * 4,
        out_specs=[block_spec] * 2,
        out_shape=[jax.ShapeDtypeStruct((count, BLK, BLK), F32)] * 2,
        compiler_params=params(32),
        name="stats",
    )(left_stats, right_stats, left_basis, right_basis)


def soap_kernel(
    seq_ref, g0, g1, g2, g3, w_ref, one_ref, two_ref, ls_ref, rs_ref, lb_ref, rb_ref, lp_ref, rp_ref,
    grad_ref, w_out, one_out, two_out, ls_out, rs_out, lb_out, rb_out,
    grad_s, gram, work, *inv,
):
    step = pl.program_id(0)
    slots = pl.num_programs(0)
    count = lb_out.shape[0]
    quarter = BLK // 4
    for piece, flip in ((g0, 0), (g1, 2), (g2, 1), (g3, 3)):
        start = pl.multiple_of((seq_ref[0] ^ flip) * quarter, quarter)
        grad_s[pl.ds(start, quarter), :] = piece[0]
    grad = grad_s[...]
    grad_ref[0] = grad.astype(F32)
    left, right = low_parts(lb_ref[0], 2), low_parts(rb_ref[0], 2)
    left_grad = dot_parts(left, [grad], 0, 0, 2)
    grad_right = dot_parts([grad], right, 1, 0, 2)
    rotated = dot(left_grad.astype(LOW), right[0], 1, 0)
    one = BETA_ONE * one_ref[0] + (1.0 - BETA_ONE) * rotated
    two = BETA_TWO * two_ref[0] + (1.0 - BETA_TWO) * rotated * rotated
    one_out[0] = one
    two_out[0] = two
    scaled = (one / (1.0 - BETA_ONE**STEP)) / (jnp.sqrt(two / (1.0 - BETA_TWO**STEP)) + ADAM_EPS)
    back = dot(dot(left[0], scaled.astype(LOW), 1, 0).astype(LOW), right[0], 1, 1)
    w_out[0] = w_ref[0] - RATE_MATRIX * (back + DECAY_RATE * w_ref[0])
    ls_out[0] = BETA_STAT * ls_ref[0] + (1.0 - BETA_STAT) * dot(grad, grad, 1, 1)
    rs_out[0] = BETA_STAT * rs_ref[0] + (1.0 - BETA_STAT) * dot(grad, grad, 0, 0)
    left_new = lp_ref[0] + (1.0 - BETA_STAT) * dot_parts([grad], low_parts(left_grad, 2), 1, 1, 2)
    right_new = rp_ref[0] + (1.0 - BETA_STAT) * dot_parts([grad], low_parts(grad_right, 2), 0, 0, 2)
    for side, product in enumerate((left_new, right_new)):
        at = side * count + step
        work[at] = product
        parts = low_parts(product, 3)
        for p in range(BLK // 128):
            c, on = slice(128 * p, 128 * p + 128), slice(128 * p, BLK)
            gram[at, c, on] = dot_parts([part[:, c] for part in parts], [part[:, on] for part in parts], 0, 0, 3)

    @pl.when(step == slots - 1)
    def _():
        for p in range(BLK // 128):
            c = slice(128 * p, 128 * p + 128)
            rest = slice(128 * p + 128, BLK)
            for b, block in enumerate(inv):
                block[...] = gram[b, c, c]
            eliminate(inv)
            for b, block in enumerate(inv):
                gram[b, c, c] = block[...]

            def solve(i, carry):
                wide = 2 if count % 2 == 0 else 1
                at = [side * count + wide * i + j for side in range(2) for j in range(wide)]
                factors = [low_parts(gram[b, c, c], 3) for b in at]
                solved = [
                    dot_parts(low_parts(work[b, :, c], 2), factor, 1, 1, 2)
                    for b, factor in zip(at, factors, strict=True)
                ]
                if p < BLK // 128 - 1:
                    uppers = [
                        low_parts(dot_parts(factor, low_parts(gram[b, c, rest], 3), 1, 0, 3), 3)
                        for b, factor in zip(at, factors, strict=True)
                    ]
                    works = [
                        work[b, :, rest] - dot_parts(low_parts(part, 2), upper, 1, 0, 2)
                        for b, part, upper in zip(at, solved, uppers, strict=True)
                    ]
                    grams = [
                        gram[b, rest, rest] - dot_parts(upper, upper, 0, 0, 3)
                        for b, upper in zip(at, uppers, strict=True)
                    ]
                    for b, new_work, new_gram in zip(at, works, grams, strict=True):
                        work[b, :, rest] = new_work
                        gram[b, rest, rest] = new_gram
                for j in range(wide):
                    lb_out[wide * i + j, :, c] = solved[j]
                    rb_out[wide * i + j, :, c] = solved[wide + j]
                return carry

            lax.fori_loop(0, count // (2 if count % 2 == 0 else 1), solve, 0)


def soap_update(seq, pieces, state, products):
    count = state[0].shape[0]
    piece_spec = pl.BlockSpec((1, BLK // 4, BLK), lambda i, s: (i, 0, 0))
    block_spec = pl.BlockSpec((1, BLK, BLK), lambda i, s: (i, 0, 0))
    whole_spec = pl.BlockSpec((count, BLK, BLK), lambda i, s: (0, 0, 0))
    shape = jax.ShapeDtypeStruct((count, BLK, BLK), F32)
    return pl.pallas_call(
        soap_kernel,
        grid_spec=pltpu.PrefetchScalarGridSpec(
            num_scalar_prefetch=1,
            grid=(count,),
            in_specs=[piece_spec] * 4 + [block_spec] * 9,
            out_specs=[block_spec] * 6 + [whole_spec] * 2,
            scratch_shapes=[
                pltpu.VMEM((BLK, BLK), LOW),
                pltpu.VMEM((2 * count, BLK, BLK), F32),
                pltpu.VMEM((2 * count, BLK, BLK), F32),
            ]
            + [pltpu.VMEM((128, 128), F32)] * (2 * count),
        ),
        out_shape=[shape] * 8,
        compiler_params=params(60),
        name="soap",
    )(seq, *pieces, *state, *products)


def split_kernel(dp, a_ref, b_ref, *outs):
    for k, out in enumerate(outs):
        out[...] = (a_ref[dp[0] ^ k].astype(F32) + b_ref[dp[0] ^ k].astype(F32)).astype(LOW)


def split_sum(dp, a, b):
    parts = a.shape[0]
    shape = a.shape[1:]
    return pl.pallas_call(
        split_kernel,
        grid_spec=pltpu.PrefetchScalarGridSpec(
            num_scalar_prefetch=1,
            grid=(1,),
            in_specs=[pl.BlockSpec(a.shape, lambda i, dp: (0,) * a.ndim)] * 2,
            out_specs=[pl.BlockSpec(shape, lambda i, dp: (0,) * len(shape))] * parts,
        ),
        out_shape=[jax.ShapeDtypeStruct(shape, LOW)] * parts,
        compiler_params=params(32),
        name="split_sum",
    )(dp, a, b)


def first_halves_kernel(keep, got, *outs, plans):
    per = keep.shape[4] // len(plans)
    names = ("x", 2, 1, 0)
    for g, plan in enumerate(plans):
        for out, side in zip(outs[2 * g : 2 * g + 2], (1, 0), strict=True):
            for n in range(4):
                where = {plan[0]: side, 2: 0}
                free = [name for name in plan[1:] if name != 2]
                where[free[0]], where[free[1]] = n // 2, n % 2
                at = tuple(where[name] for name in names) + (slice(per * g, per * g + per),)
                to = tuple(where[name] for name in plan[1:])
                out[to] = (keep[at].astype(F32) + got[at].astype(F32)).astype(LOW)


def first_halves(keep, got, plans):
    slots, rows, cols = keep.shape[4:]
    per, cut = slots // len(plans), rows // 3
    whole = pl.BlockSpec((2, 1, 2, 2, slots, cut, cols), lambda i, j: (0, i, 0, 0, 0, j, 0))
    outs = []
    for plan in plans:
        place = plan[1:].index(2)
        block = tuple(1 if n == place else 2 for n in range(3)) + (per, cut, cols)
        outs += [
            pl.BlockSpec(
                block,
                lambda i, j, place=place: tuple(i if n == place else 0 for n in range(3)) + (0, j, 0),
            )
        ] * 2
    shape = jax.ShapeDtypeStruct((2, 2, 2, per, rows, cols), LOW)
    return pl.pallas_call(
        functools.partial(first_halves_kernel, plans=plans),
        grid=(2, 3),
        in_specs=[whole, whole],
        out_specs=outs,
        out_shape=[shape] * len(outs),
        compiler_params=params(60),
        name="first_halves",
    )(keep, got)


def choose_kernel(dp, source, *refs, blocks):
    parts, early, out, held = refs[:-3], refs[-3], refs[-2], refs[-1]
    per, half = held.shape[1], held.shape[2]
    for k, part in enumerate(parts):
        held[k] = part[...]
    slots = out.shape[0]
    units = len(parts) * per

    def one(i, carry):
        block = source[i]

        @pl.when((2 * block >= units) & (block < blocks))
        def _():
            out[i] = early[i]

        @pl.when(block >= blocks)
        def _():
            out[i] = jnp.zeros(out.shape[1:], out.dtype)

        @pl.when(2 * block < units)
        def _():
            for h in range(2):
                unit = 2 * block + h
                out[i, h * half : h * half + half] = held[lax.div(unit, per) ^ dp[0], lax.rem(unit, per)]

        return carry

    lax.fori_loop(0, slots, one, 0)


def choose(dp, source, parts, early, blocks):
    return pl.pallas_call(
        functools.partial(choose_kernel, blocks=blocks),
        grid_spec=pltpu.PrefetchScalarGridSpec(
            num_scalar_prefetch=2,
            grid=(1,),
            in_specs=[pl.BlockSpec(parts[0].shape, lambda i, dp, src: (0, 0, 0))] * len(parts)
            + [pl.BlockSpec(early.shape, lambda i, dp, src: (0, 0, 0))],
            out_specs=pl.BlockSpec(early.shape, lambda i, dp, src: (0, 0, 0)),
            scratch_shapes=[pltpu.VMEM((len(parts),) + parts[0].shape, LOW)],
        ),
        out_shape=jax.ShapeDtypeStruct(early.shape, LOW),
        compiler_params=params(32),
        name="choose",
    )(dp, source, *parts, early)


def swap(x, axis, bit):
    size = lax.axis_size(axis)
    return lax.ppermute(x, axis, [(i, i ^ bit) for i in range(size)])


def add_low(a, b):
    return (a.astype(F32) + b.astype(F32)).astype(LOW)


class Halving:
    def __init__(self, kept, got, names, slots=None):
        self.kept, self.got, self.names, self.slots = kept, got, list(names), slots

    def take(self, name, index):
        axis = self.names.index(name)
        found = []
        for array in (self.kept, self.got):
            starts, limits = [0] * array.ndim, list(array.shape)
            starts[axis], limits[axis] = index, index + 1
            if self.slots is not None:
                starts[-3], limits[-3] = self.slots
            part = lax.slice(array, starts, limits)
            found.append(part.reshape(part.shape[:axis] + part.shape[axis + 1 :]))
        return add_low(*found)

    def send(self, name, ready=None):
        sent, kept = ready or (self.take(name, 1), self.take(name, 0))
        self.names.remove(name)
        self.kept, self.slots, self.name = kept, None, name
        return sent

    def receive(self, sent):
        axis, bit = ("seq", 2) if self.name == "x" else ("dp", 2**self.name)
        self.got = swap(sent, axis, bit)

    def total(self):
        return add_low(self.kept, self.got)


def quarters(piece):
    across = swap(piece, "seq", 2)
    return piece, across, swap(piece, "seq", 1), swap(across, "seq", 1)


def block_places(owners, owner_count, slot_count):
    block_count = owners.shape[0]
    ids = jnp.arange(block_count, dtype=jnp.int32)
    earlier = (owners[:, None] == owners[None, :]) & (ids[None, :] < ids[:, None])
    slots = jnp.sum(earlier.astype(jnp.int32), axis=1)
    places = owners * slot_count + slots
    matched = places[None, :] == jnp.arange(owner_count * slot_count, dtype=jnp.int32)[:, None]
    missing = 1 - jnp.any(matched, axis=1).astype(jnp.int32)
    sources = jnp.sum(jnp.where(matched, ids[None, :], 0), axis=1) + block_count * missing
    return slots, sources


def adam_vectors(gradient, vec, first_mom, second_mom):
    first_mom = BETA_ONE * first_mom + (1.0 - BETA_ONE) * gradient
    second_mom = BETA_TWO * second_mom + (1.0 - BETA_TWO) * gradient * gradient
    step_size = (first_mom / (1.0 - BETA_ONE**STEP)) / (
        jnp.sqrt(second_mom / (1.0 - BETA_TWO**STEP)) + ADAM_EPS
    )
    return first_mom, second_mom, vec - RATE_VECTOR * step_size


def on_device(
    tokens, cotangent, lengths, patch_mask, owners, master, moment_one, moment_two,
    left_stats, right_stats, left_basis, right_basis, vec, vec_one, vec_two,
):
    owner_count = lax.axis_size("dp")
    slot_count = master.shape[0]
    quarter = BLK // 4
    seq_id = lax.axis_index("seq").astype(jnp.int32)
    dp_id = lax.axis_index("dp").astype(jnp.int32)
    core, chip = seq_id % 2, seq_id // 2
    part_len = tokens.shape[1]
    slots, sources = block_places(owners, owner_count, slot_count)
    first_blocks = 3 * (D // BLK) ** 2

    mine = lax.dynamic_index_in_dim(
        master.reshape(slot_count, 4, quarter, BLK), seq_id, 1, keepdims=False
    ).astype(LOW)
    gathered = lax.all_gather(mine, AXES, axis=0, tiled=False).reshape(
        owner_count, 4, slot_count, quarter, BLK
    )

    products = stats_product(left_stats, right_stats, left_basis, right_basis)

    def halves_of(pair):
        kept = lax.dynamic_index_in_dim(pair, chip, 0, keepdims=False)
        return kept, lax.dynamic_index_in_dim(pair, 1 - chip, 0, keepdims=False)

    kept, sent = halves_of(tokens)
    x = jnp.concatenate([kept, swap(sent, "seq", 2)], axis=0)
    dy_kept, dy_sent = halves_of(cotangent)

    def to_positions(mine, other):
        return jnp.where(chip == 0, jnp.stack([mine, other]), jnp.stack([other, mine]))

    positions = jnp.arange(patch_mask.shape[-1], dtype=jnp.int32)
    live = (positions[None, :] < lengths[:, None]) & ((patch_mask == 1) | (positions[None, :] == 0))
    live = lax.dynamic_index_in_dim(live, chip, 0, keepdims=False).reshape(4, part_len)
    order = seq_id ^ jnp.array([0, 2, 1, 3], jnp.int32)
    fill = jnp.where(jnp.take(live, order, axis=0).reshape(-1), 0.0, NEG_FILL).astype(LOW)
    fill = jnp.broadcast_to(fill[:, None], (fill.shape[0], 128))

    bias = jnp.concatenate([vec[4], jnp.zeros_like(vec[4]), vec[5]])[None, :]
    gathered, products, dy_sent = lax.optimization_barrier((gathered, products, dy_sent))
    dy_got = swap(dy_sent, "seq", 2)
    q, kv, normed = qkv_forward(owners, slots, x, vec, bias, gathered)
    other = swap(kv, "seq", 1)
    attn, lse = attn_forward(q, kv, other, fill)
    attn, dy_got = lax.optimization_barrier((attn, dy_got))
    dy = jnp.concatenate([dy_kept, dy_got], axis=0)
    b1 = vec[8:].reshape(1, FF)
    seq_of, dp_of = seq_id.reshape(1), dp_id.reshape(1)
    result, d_mid, d_attn, keep, send, sums_two, bias_grad = mid_layer(
        owners, slots, owners ^ dp_id, seq_of, x, attn, dy, vec, b1, gathered
    )
    result_other = swap(result[part_len:], "seq", 2)

    bits = owner_count.bit_length() - 1
    if slot_count % 3 == 0 and bits == 3:
        plans = [["x", 0, 1, 2], [0, 1, "x", 2], [1, "x", 0, 2]]
    else:
        plans = [["x"] + list(range(bits))]
    per = slot_count // len(plans)
    names = ["x"] + list(range(bits))[::-1]
    shape = (2,) * (1 + bits) + keep.shape[2:]
    keep, got = keep.reshape(shape), swap(send, "seq", 1).reshape(shape)
    groups = [
        Halving(keep, got, names, (per * g, per * g + per)) for g in range(len(plans))
    ]
    guard = fill

    def advance(step, guard):
        if step == len(names) - 1 and len(groups) > 1:
            name = plans[0][step]
            sent = jnp.concatenate([group.take(name, 1) for group in groups], axis=0)
            kept = jnp.concatenate([group.take(name, 0) for group in groups], axis=0)
            groups[:] = [Halving(kept, None, [name])]
            sent, guard = lax.optimization_barrier((groups[0].send(name, (sent, kept)), guard))
            groups[0].receive(sent)
            return guard
        ready = [None] * len(plans)
        if step == 0 and len(plans) == 3:
            made = first_halves(keep, groups[0].got, plans)
            ready = [tuple(made[2 * g : 2 * g + 2]) for g in range(3)]
            for group, plan in zip(groups, plans, strict=True):
                group.names = list(plan)
        sent = [group.send(plan[step], own) for group, plan, own in zip(groups, plans, ready, strict=True)]
        *sent, guard = lax.optimization_barrier((*sent, guard))
        for group, array in zip(groups, sent, strict=True):
            group.receive(array)
        return guard

    grads = []
    taken = 0
    for first, count in ((0, 2), (2, 3), (5, 1)):
        if first:
            guard = advance(taken, guard)
            taken += 1
        parts = attn_backward(q, kv, other, guard, attn, lse, d_attn, first, count)
        got, parts, result_other = lax.optimization_barrier(
            ([group.got for group in groups], parts, result_other)
        )
        for group, array in zip(groups, got, strict=True):
            group.got = array
        dq, dk, dv, sent_kv = parts
        grads += [dq, dk, dv, swap(sent_kv, "seq", 1)]
    normed = advance(taken, normed)
    taken += 1
    late_keep, late_send, cols = qkv_grad(seq_of, normed, grads)
    late_shape = (2, -1, quarter, BLK)
    late = Halving(late_keep.reshape(late_shape), swap(late_send.reshape(late_shape), "seq", 1), ["x"])

    def after(value):
        got, value = lax.optimization_barrier(([group.got for group in groups], value))
        for group, array in zip(groups, got, strict=True):
            group.got = array
        return value

    sent_x, d_mid = lax.optimization_barrier((late.send("x"), d_mid))
    late.receive(sent_x)
    cols = after(cols)
    while taken < len(names):
        advance(taken, fill)
        taken += 1
    d_x, sums_one = qkv_backward(owners, slots, x, d_mid, vec, grads, gathered)
    late.got, d_x = lax.optimization_barrier((late.got, d_x))
    d_x = after(d_x)
    d_x_other = swap(d_x[part_len:], "seq", 2)
    early = groups[0].total()
    output = to_positions(result[:part_len], result_other)
    d_tokens = to_positions(d_x[:part_len], d_x_other)
    early, output, d_tokens = lax.optimization_barrier((early, output, d_tokens))

    mine_from = lax.dynamic_slice_in_dim(sources, dp_id * slot_count, slot_count)
    if 2 * first_blocks % owner_count == 0:
        unit = (owner_count, 2 * first_blocks // owner_count, quarter // 2, BLK)
        parts = split_sum(dp_of, late.kept.reshape(unit), late.got.reshape(unit))
        parts = [parts[0]] + [swap(part, "dp", k) for k, part in enumerate(parts) if k]
        total = sum(part.astype(F32) for part in parts).astype(LOW)
        parts = [total] + [swap(total, "dp", k) for k in range(1, owner_count)]
        piece = choose(dp_of, mine_from, parts, early, owners.shape[0])
    else:
        tiles = jnp.concatenate([late.total(), jnp.zeros((1, quarter, BLK), LOW)], axis=0)
        at = sources.reshape(owner_count, slot_count)[dp_id ^ jnp.arange(owner_count)]
        tiles = jnp.take(tiles, jnp.minimum(at, first_blocks).reshape(-1), axis=0)
        tiles = tiles.reshape((2,) * bits + (slot_count, quarter, BLK))
        owned = Halving(tiles, jnp.zeros_like(tiles), names[1:])
        for bit in range(bits):
            owned.receive(owned.send(bit))
        piece = jnp.where((mine_from < first_blocks)[:, None, None], owned.total(), early)
        piece = jnp.where((mine_from < owners.shape[0])[:, None, None], piece, jnp.zeros_like(piece))
    state = (master, moment_one, moment_two, left_stats, right_stats, left_basis, right_basis)
    piece, sums_one, sums_two, cols, bias_grad = lax.optimization_barrier(
        (piece, sums_one, sums_two, cols, bias_grad)
    )
    updates = soap_update(seq_of, quarters(piece), state, products)

    vec_grad = jnp.concatenate(
        [
            sums_one[0:2],
            sums_two[0:2],
            cols[:, :D],
            cols[:, 2 * D :],
            sums_two[2:4],
            bias_grad.reshape(-1, D),
        ],
        axis=0,
    )
    vec_parts = lax.all_gather(vec_grad, AXES, axis=0, tiled=False)
    updates, vec_parts = lax.optimization_barrier((updates, vec_parts))
    vec_total = jnp.sum(vec_parts, axis=0)
    vec_first, vec_second, vec_next = adam_vectors(vec_total, vec, vec_one, vec_two)
    grad_blocks, w_new, one_new, two_new, ls_new, rs_new, lb_new, rb_new = updates
    return (
        output, d_tokens, grad_blocks, w_new, one_new, two_new, ls_new, rs_new, lb_new, rb_new,
        vec_first, vec_second, vec_next,
    )


def solution(mesh):
    rows, blocks, whole = P("dp", "seq", None), P("dp", None, None), P()
    return jax.shard_map(
        on_device,
        mesh=mesh,
        in_specs=(rows, rows, P("dp"), P("dp", None), whole) + (blocks,) * 7 + (whole,) * 3,
        out_specs=(rows, rows) + (blocks,) * 8 + (whole,) * 3,
        check_vma=False,
    )
```

```python
import functools

import jax
import jax.numpy as jnp
from jax import lax
from jax.experimental import pallas as pl
from jax.experimental.pallas import tpu as pltpu
from jax.sharding import PartitionSpec as P

D = 768
FF = 3072
BLK = 384
STEP = 10

NORM_EPS = 1e-06
NEG_FILL = -1000000000.0
BETA_ONE = 0.9
BETA_TWO = 0.999
BETA_STAT = 0.95
RATE_MATRIX = 0.1
RATE_VECTOR = 0.3
DECAY_RATE = 0.01
ADAM_EPS = 1e-08

LOW = jnp.bfloat16
F32 = jnp.float32
AXES = ("dp", "seq")
MIB = 2**20

TAIL_P = 0.24
TAIL_C = (
    0.09575380798443668,
    0.09552183543465394,
    0.09284136585084933,
    0.06338567653857548,
    0.11841694922211018,
    -0.06574016740998187,
    0.15281935057715396,
    -0.052998628523732765,
)


def dot(a, b, ca, cb):
    return lax.dot_general(a, b, (((ca,), (cb,)), ((), ())), preferred_element_type=F32)


def lanes(shape):
    return lax.broadcasted_iota(jnp.int32, shape, len(shape) - 1)


def gelu_pair(x):
    u = jnp.abs(x)
    t = 1.0 / (1.0 + TAIL_P * u)
    poly = TAIL_C[-1]
    for coeff in TAIL_C[-2::-1]:
        poly = poly * t + coeff
    expo = jnp.exp(-0.5 * u * u)
    tail = poly * t * expo
    cdf = jnp.where(x < 0, tail, 1.0 - tail)
    return x * cdf, cdf + x * (expo * 0.3989422804014327)


def norm_parts(rows):
    center = rows - jnp.mean(rows, axis=-1, keepdims=True)
    rstd = lax.rsqrt(jnp.mean(center * center, axis=-1, keepdims=True) + NORM_EPS)
    return center * rstd, rstd


def norm_back(grad, hat, rstd):
    return rstd * (
        grad
        - jnp.mean(grad, axis=-1, keepdims=True)
        - hat * jnp.mean(grad * hat, axis=-1, keepdims=True)
    )


def params(limit):
    return pltpu.CompilerParams(vmem_limit_bytes=limit * MIB)


def tile_spec(block_of):
    return pl.BlockSpec(
        (1, 4, 1, BLK // 4, BLK),
        lambda i, own, slot: (own[block_of(i)], 0, slot[block_of(i)], 0, 0),
    )


def tile(ref):
    return ref[...].reshape(BLK, BLK)


def full_spec(shape):
    return pl.BlockSpec(shape, lambda i, own, slot: (0,) * len(shape))


def quarter_at(seq, rel_core, rel_x):
    return seq ^ (2 * rel_x + rel_core)


def square(tiles, held):
    for i in range(2):
        for j in range(2):
            held[i * BLK : i * BLK + BLK, j * BLK : j * BLK + BLK] = tile(tiles[2 * i + j])
    return held[...]


def qkv_kernel(own, slot, x_ref, vec_ref, bias_ref, t00, t01, t10, t11, q_ref, kv_ref, a_ref, held):
    @pl.when(pl.program_id(0) == 0)
    def _():
        hat, _ = norm_parts(x_ref[...].astype(F32))
        a_ref[...] = (hat * vec_ref[0:1, :] + vec_ref[1:2, :]).astype(LOW)

    low = (dot(a_ref[...], square((t00, t01, t10, t11), held), 1, 0) + bias_ref[...]).astype(LOW)

    @pl.when(pl.program_id(0) == 0)
    def _():
        q_ref[...] = low

    @pl.when(pl.program_id(0) > 0)
    def _():
        kv_ref[...] = low


def qkv_tiles():
    return [tile_spec(lambda i, n=n: 6 * (n // 2) + 2 * i + n % 2) for n in range(4)]


def qkv_forward(own, slot, x, vec, bias, gathered):
    rows = x.shape[0]
    return pl.pallas_call(
        qkv_kernel,
        grid_spec=pltpu.PrefetchScalarGridSpec(
            num_scalar_prefetch=2,
            grid=(3,),
            in_specs=[
                full_spec((rows, D)),
                full_spec(vec.shape),
                pl.BlockSpec((1, D), lambda i, own, slot: (0, i)),
            ]
            + qkv_tiles(),
            out_specs=[
                full_spec((rows, D)),
                pl.BlockSpec((rows, D), lambda i, own, slot: (0, jnp.maximum(i - 1, 0))),
                full_spec((rows, D)),
            ],
            scratch_shapes=[pltpu.VMEM((D, D), LOW)],
        ),
        out_shape=[
            jax.ShapeDtypeStruct((rows, D), LOW),
            jax.ShapeDtypeStruct((rows, 2 * D), LOW),
            jax.ShapeDtypeStruct((rows, D), LOW),
        ],
        compiler_params=params(48),
        name="qkv",
    )(own, slot, x, vec, bias, *([gathered] * 4))


def attn_fwd_kernel(q_ref, k1, v1, k2, v2, bias_ref, o_ref, lse_ref, ka, kb, va, vb):
    rows = k1.shape[0]

    @pl.when(pl.program_id(1) == 0)
    def _():
        ln = lanes((rows, 128))
        for i, (k, v) in enumerate(((k1, v1), (k2, v2))):
            r = slice(i * rows, i * rows + rows)
            keys, values, bias = k[...], v[...], bias_ref[r, :]
            one = jnp.ones_like(values)
            ka[r, :] = jnp.where(ln == 64, bias, keys)
            kb[r, :] = jnp.where(ln == 0, bias, keys)
            va[r, :] = jnp.where(ln < 64, values, one)
            vb[r, :] = jnp.where(ln < 64, one, values)

    q = q_ref[...] * jnp.asarray(0.125, LOW)
    ln = lanes(q.shape)
    one, zero = jnp.ones_like(q), jnp.zeros_like(q)
    qa = jnp.where(ln < 64, q, jnp.where(ln == 64, one, zero))
    qb = jnp.where(ln < 64, jnp.where(ln == 0, one, zero), q)
    outs, tops = [], []
    for query, keys, values in ((qa, ka, va), (qb, kb, vb)):
        logits = dot(query, keys[...], 1, 1)
        top = jnp.max(logits, axis=1, keepdims=True)
        expo = jnp.exp(logits - top).astype(LOW)
        outs.append(dot(expo, values[...], 1, 0))
        tops.append(top)
    total = jnp.where(ln < 64, outs[1], outs[0])
    attended = jnp.where(ln < 64, outs[0], outs[1])
    o_ref[...] = (attended / pltpu.roll(total, 64, 1)).astype(LOW)
    lse_ref[...] = jnp.where(ln < 64, tops[1], tops[0]) + jnp.log(total)


def attn_forward(q, kv, other, bias, q_rows=256):
    rows, pairs = q.shape[0], D // 128
    keys = 2 * rows
    q_spec = pl.BlockSpec((q_rows, 128), lambda p, i: (i, p))
    return pl.pallas_call(
        attn_fwd_kernel,
        grid=(pairs, rows // q_rows),
        in_specs=[
            q_spec,
            pl.BlockSpec((rows, 128), lambda p, i: (0, p)),
            pl.BlockSpec((rows, 128), lambda p, i: (0, pairs + p)),
            pl.BlockSpec((rows, 128), lambda p, i: (0, p)),
            pl.BlockSpec((rows, 128), lambda p, i: (0, pairs + p)),
            pl.BlockSpec((keys, 128), lambda p, i: (0, 0)),
        ],
        out_specs=[q_spec, q_spec],
        out_shape=[
            jax.ShapeDtypeStruct((rows, D), LOW),
            jax.ShapeDtypeStruct((rows, D), F32),
        ],
        scratch_shapes=[pltpu.VMEM((keys, 128), LOW)] * 4,
        compiler_params=params(48),
        name="attn_fwd",
    )(q, kv, kv, other, other, bias)


def three_parts(x):
    high = x.astype(LOW).astype(F32)
    rest = x - high
    mid = rest.astype(LOW).astype(F32)
    return high, mid, rest - mid


def low_parts(x, count):
    found = []
    for _ in range(count):
        part = x.astype(LOW)
        found.append(part)
        x = x - part.astype(F32)
    return found


def dot_parts(a, b, ca, cb, order):
    pairs = [(i, j) for i in range(len(a)) for j in range(len(b)) if i + j < order]
    a = jnp.concatenate([a[i] for i, _ in pairs], axis=ca)
    b = jnp.concatenate([b[j] for _, j in pairs], axis=cb)
    return dot(a, b, ca, cb)


def with_spare(x, spare, value, one, first):
    ln = lanes(x.shape)
    high, mid, low = three_parts(value)
    filled = jnp.where(ln == first + 3, one, 0.0)
    for i, part in enumerate((high, mid, low)):
        filled = jnp.where(ln == first + i, part, filled)
    return jnp.where(spare, filled, x).astype(LOW)


def attn_bwd_kernel(
    q_ref, k1, v1, k2, v2, bias_ref, o_ref, lse_ref, do_ref,
    dq_ref, dk1, dv1, dkv2, ka, kb, va, vb, kt, dk, dv, *, chunk,
):
    rows = k1.shape[0]

    @pl.when(pl.program_id(1) == 0)
    def _():
        ln = lanes((rows, 128))
        for i, (k, v) in enumerate(((k1, v1), (k2, v2))):
            r = slice(i * rows, i * rows + rows)
            keys, values, bias = k[...], v[...], bias_ref[r, :]
            one, zero = jnp.ones_like(values), jnp.zeros_like(values)
            ka[r, :] = jnp.where(ln < 64, keys, jnp.where(ln < 67, one, jnp.where(ln == 67, bias, zero)))
            kb[r, :] = jnp.where(ln >= 64, keys, jnp.where(ln < 3, one, jnp.where(ln == 3, bias, zero)))
            va[r, :] = jnp.where(ln < 64, values, jnp.where(ln < 67, one, zero))
            vb[r, :] = jnp.where(ln >= 64, values, jnp.where(ln < 3, one, zero))
            kt[:, r] = keys.T
        dk[...] = jnp.zeros_like(dk)
        dv[...] = jnp.zeros_like(dv)

    q = q_ref[...].astype(F32) * 0.125
    left = lanes(q.shape) < 64
    grad = do_ref[...].astype(F32)
    prod = grad * o_ref[...].astype(F32)
    sum_a = jnp.sum(jnp.where(left, prod, 0.0), axis=1, keepdims=True)
    sum_b = jnp.sum(jnp.where(left, 0.0, prod), axis=1, keepdims=True)
    delta = jnp.where(left, sum_b, sum_a)
    lse = lse_ref[...]
    zero = jnp.zeros_like(q)
    heads = (
        (
            with_spare(q, ~left, -lse, 1.0, 64), with_spare(grad, ~left, -delta, 0.0, 64), ka, va,
            jnp.where(left, q, zero).astype(LOW), jnp.where(left, grad, zero).astype(LOW),
        ),
        (
            with_spare(q, left, -lse, 1.0, 0), with_spare(grad, left, -delta, 0.0, 0), kb, vb,
            jnp.where(left, zero, q).astype(LOW), jnp.where(left, zero, grad).astype(LOW),
        ),
    )
    d_query = [jnp.zeros((64, q.shape[0]), F32)] * 2
    for c in range(2 * rows // chunk):
        r = slice(c * chunk, c * chunk + chunk)
        dv_c, dk_c = dv[r, :], dk[r, :]
        for h, (q_aug, g_aug, keys, values, q_only, g_only) in enumerate(heads):
            probs = jnp.exp(dot(keys[r, :], q_aug, 1, 1))
            d_logits = (probs * dot(values[r, :], g_aug, 1, 1)).astype(LOW)
            dv_c = dv_c + dot(probs.astype(LOW), g_only, 1, 0)
            dk_c = dk_c + dot(d_logits, q_only, 1, 0)
            d_query[h] = d_query[h] + dot(kt[64 * h : 64 * h + 64, r], d_logits, 1, 0)
        dv[r, :] = dv_c
        dk[r, :] = dk_c
    dq_ref[...] = (jnp.concatenate(d_query, axis=0) * 0.125).T.astype(LOW)

    @pl.when(pl.program_id(1) == pl.num_programs(1) - 1)
    def _():
        dk1[...] = dk[:rows, :].astype(LOW)
        dv1[...] = dv[:rows, :].astype(LOW)
        dkv2[0] = dk[rows:, :].astype(LOW)
        dkv2[1] = dv[rows:, :].astype(LOW)


def attn_backward(q, kv, other, bias, attn, lse, d_attn, first, count, q_rows=1024, chunk=1024):
    rows, pairs = q.shape[0], D // 128
    keys = 2 * rows
    out_spec = pl.BlockSpec((q_rows, 128), lambda p, i: (i, p))
    k_out = pl.BlockSpec((rows, 128), lambda p, i: (0, p))
    q_spec = pl.BlockSpec((q_rows, 128), lambda p, i: (i, first + p))
    k_spec = pl.BlockSpec((rows, 128), lambda p, i: (0, first + p))
    v_spec = pl.BlockSpec((rows, 128), lambda p, i: (0, pairs + first + p))
    return pl.pallas_call(
        functools.partial(attn_bwd_kernel, chunk=chunk),
        grid=(count, rows // q_rows),
        in_specs=[
            q_spec, k_spec, v_spec, k_spec, v_spec, pl.BlockSpec((keys, 128), lambda p, i: (0, 0)),
            q_spec, q_spec, q_spec,
        ],
        out_specs=[out_spec, k_out, k_out, pl.BlockSpec((2, rows, 128), lambda p, i: (0, 0, p))],
        out_shape=[jax.ShapeDtypeStruct((rows, count * 128), LOW)] * 3
        + [jax.ShapeDtypeStruct((2, rows, count * 128), LOW)],
        scratch_shapes=[pltpu.VMEM((keys, 128), LOW)] * 4
        + [pltpu.VMEM((128, keys), LOW)]
        + [pltpu.VMEM((keys, 128), F32)] * 2,
        compiler_params=params(56),
        name="attn_bwd",
    )(q, kv, kv, other, other, bias, attn, lse, d_attn)


def mid_kernel(
    own, slot, rel, seq, x_ref, attn_ref, dy_ref, vec_ref, b1_ref, o00, o01, o10, o11, *refs, chunk):
    ups, downs = refs[:4], refs[4:8]
    (
        res_ref, dmid_ref, dattn_ref, keep, send, sums_ref, gb1_ref,
        mid, a2, acc, da2, up_s, down_s, stage, sems,
    ) = refs[8:]
    step = pl.program_id(0)
    last = pl.num_programs(0) - 1
    quarter = BLK // 4

    def copies(buf, i, block):
        found = []
        for rel_core, out in enumerate((keep, send)):
            for rel_x in range(2):
                found.append(
                    pltpu.make_async_copy(
                        stage.at[buf, i, quarter_at(seq[0], rel_core, rel_x)],
                        out.at[rel_x, rel[block], slot[block]],
                        sems.at[buf, i, 2 * rel_core + rel_x],
                    )
                )
        return found

    def put(buf, i, block, value):
        low = value.astype(LOW)
        for part in range(4):
            stage[buf, i, part] = low[part * quarter : part * quarter + quarter]
        for copy in copies(buf, i, block):
            copy.start()

    def settle(buf, count=8):
        for i in range(count):
            for copy in copies(buf, i, 0):
                copy.wait()

    @pl.when(step == 0)
    def _():
        mid[...] = (
            x_ref[...].astype(F32)
            + dot(attn_ref[...], square((o00, o01, o10, o11), up_s), 1, 0)
            + vec_ref[6:7, :]
        )
        hat, _ = norm_parts(mid[...])
        a2[...] = (hat * vec_ref[2:3, :] + vec_ref[3:4, :]).astype(LOW)
        acc[...] = jnp.zeros_like(acc)
        da2[...] = jnp.zeros_like(da2)

    @pl.when((step > 0) & (step < last))
    def _():
        rows = a2.shape[0]
        up, down = square(ups, up_s), square(downs, down_s)
        bias_grad = jnp.zeros((1, D), F32)
        acts, d_hids = [], []
        for c in range(rows // chunk):
            r = slice(c * chunk, c * chunk + chunk)
            act, slope = gelu_pair(dot(a2[r, :], up, 1, 0) + b1_ref[...])
            act = act.astype(LOW)
            d_hid = (dot(dy_ref[r, :], down, 1, 1) * slope).astype(LOW)
            acc[r, :] += dot(act, down, 1, 0)
            da2[r, :] += dot(d_hid, up, 1, 1)
            bias_grad = bias_grad + jnp.sum(d_hid.astype(F32), axis=0, keepdims=True)
            acts.append(act)
            d_hids.append(d_hid)
        gb1_ref[...] = bias_grad
        act = jnp.concatenate(acts, axis=0)
        d_hid = jnp.concatenate(d_hids, axis=0)
        buf = step % 2

        @pl.when(step > 2)
        def _():
            settle(buf)

        for i in range(2):
            c = slice(i * BLK, i * BLK + BLK)
            up_grad = dot(a2[:, c], d_hid, 0, 0)
            down_grad = dot(act[:, c], dy_ref[...], 0, 0)
            for j in range(2):
                k = slice(j * BLK, j * BLK + BLK)
                put(buf, 2 * i + j, 16 + 8 * i + 2 * (step - 1) + j, up_grad[:, k])
                put(buf, 4 + 2 * i + j, 32 + 4 * (step - 1) + 2 * i + j, down_grad[:, k])

    @pl.when(step == last)
    def _():
        res_ref[...] = (mid[...] + acc[...] + vec_ref[7:8, :]).astype(LOW)
        hat, rstd = norm_parts(mid[...])
        grad = da2[...]
        dy = dy_ref[...].astype(F32)
        sums_ref[0:1, :] = jnp.sum(hat * grad, axis=0, keepdims=True)
        sums_ref[1:2, :] = jnp.sum(grad, axis=0, keepdims=True)
        d_mid = dy + norm_back(grad * vec_ref[2:3, :], hat, rstd)
        dmid_ref[...] = d_mid
        d_proj = d_mid.astype(LOW)
        sums_ref[2:3, :] = jnp.sum(d_proj.astype(F32), axis=0, keepdims=True)
        sums_ref[3:4, :] = jnp.sum(dy, axis=0, keepdims=True)
        sums_ref[4:8, :] = jnp.zeros((4, D), F32)
        dattn_ref[...] = dot(d_proj, square((o00, o01, o10, o11), up_s), 1, 1).astype(LOW)
        settle(0)
        for i in range(2):
            out_grad = dot(attn_ref[:, i * BLK : i * BLK + BLK], d_proj, 0, 0)
            for j in range(2):
                put(0, 2 * i + j, 12 + 2 * i + j, out_grad[:, j * BLK : j * BLK + BLK])
        settle(1)
        settle(0, 4)


def mid_layer(own, slot, rel, seq, x, attn, dy, vec, b1, gathered, chunk=512):
    rows = x.shape[0]
    wide = FF // D
    quarter = BLK // 4
    owners, slots = gathered.shape[0], gathered.shape[2]

    def part(i):
        return jnp.clip(i - 1, 0, wide - 1)

    def full(shape):
        return pl.BlockSpec(shape, lambda i, own, slot, rel, seq: (0,) * len(shape))

    def tile_at(block_of):
        return pl.BlockSpec(
            (1, 4, 1, quarter, BLK),
            lambda i, own, slot, rel, seq: (own[block_of(i)], 0, slot[block_of(i)], 0, 0),
        )

    row_spec = full((rows, D))
    strip = pl.BlockSpec((1, D), lambda i, own, slot, rel, seq: (0, part(i)))
    anywhere = pl.BlockSpec(memory_space=pl.ANY)
    place_shape = jax.ShapeDtypeStruct((2, owners, slots, quarter, BLK), LOW)
    return pl.pallas_call(
        functools.partial(mid_kernel, chunk=chunk),
        grid_spec=pltpu.PrefetchScalarGridSpec(
            num_scalar_prefetch=4,
            grid=(wide + 2,),
            in_specs=[row_spec, row_spec, row_spec, full(vec.shape), strip]
            + [tile_at(lambda i, b=b: b) for b in (12, 13, 14, 15)]
            + [tile_at(lambda i, n=n: 16 + 8 * (n // 2) + 2 * part(i) + n % 2) for n in range(4)]
            + [tile_at(lambda i, n=n: 32 + 4 * part(i) + n) for n in range(4)],
            out_specs=[row_spec, row_spec, row_spec, anywhere, anywhere, full((8, D)), strip],
            scratch_shapes=[
                pltpu.VMEM((rows, D), F32),
                pltpu.VMEM((rows, D), LOW),
                pltpu.VMEM((rows, D), F32),
                pltpu.VMEM((rows, D), F32),
                pltpu.VMEM((D, D), LOW),
                pltpu.VMEM((D, D), LOW),
                pltpu.VMEM((2, 8, 4, quarter, BLK), LOW),
                pltpu.SemaphoreType.DMA((2, 8, 4)),
            ],
        ),
        out_shape=[
            jax.ShapeDtypeStruct((rows, D), LOW),
            jax.ShapeDtypeStruct((rows, D), F32),
            jax.ShapeDtypeStruct((rows, D), LOW),
            place_shape,
            place_shape,
            jax.ShapeDtypeStruct((8, D), F32),
            jax.ShapeDtypeStruct((1, FF), F32),
        ],
        compiler_params=params(60),
        name="mid",
    )(own, slot, rel, seq, x, attn, dy, vec, b1, *([gathered] * 12))


def d_columns(step, grads, work):
    def joined(n, *at):
        return jnp.concatenate([ref[at] if at else ref[...] for ref in grads[n::4]], axis=1)

    @pl.when(step == 0)
    def _():
        work(joined(0))

    for n in (1, 2):

        @pl.when(step == n)
        def _():
            work((joined(n).astype(F32) + joined(3, n - 1).astype(F32)).astype(LOW))


def qkv_grad_kernel(seq, a_ref, *refs):
    grads, (keep, send, cols_ref, stage) = refs[:-4], refs[-4:]
    quarter = BLK // 4

    def work(d_cols):
        cols_ref[...] = jnp.sum(d_cols.astype(F32), axis=0, keepdims=True)
        for i in range(2):
            stage[...] = dot(a_ref[:, i * BLK : i * BLK + BLK], d_cols, 0, 0).astype(LOW)
            for rel_core, out in enumerate((keep, send)):
                for rel_x in range(2):
                    start = pl.multiple_of(quarter_at(seq[0], rel_core, rel_x) * quarter, quarter)
                    for j in range(2):
                        out[rel_x, i, j] = stage[pl.ds(start, quarter), j * BLK : j * BLK + BLK]

    d_columns(pl.program_id(0), grads, work)


def qkv_grad(seq, normed, grads):
    rows = normed.shape[0]
    quarter = BLK // 4
    tile_out = pl.BlockSpec((2, 2, 2, quarter, BLK), lambda i, seq: (0, 0, i, 0, 0))
    shape = jax.ShapeDtypeStruct((2, 2, 6, quarter, BLK), LOW)
    return pl.pallas_call(
        qkv_grad_kernel,
        grid_spec=pltpu.PrefetchScalarGridSpec(
            num_scalar_prefetch=1,
            grid=(3,),
            in_specs=[pl.BlockSpec((rows, D), lambda i, seq: (0, 0))]
            + [pl.BlockSpec(grad.shape, lambda i, seq, n=grad.ndim: (0,) * n) for grad in grads],
            out_specs=[tile_out, tile_out, pl.BlockSpec((1, D), lambda i, seq: (0, i))],
            scratch_shapes=[pltpu.VMEM((BLK, D), LOW)],
        ),
        out_shape=[shape, shape, jax.ShapeDtypeStruct((1, 3 * D), F32)],
        compiler_params=params(48),
        name="qkv_grad",
    )(seq, normed, *grads)


def qkv_bwd_kernel(own, slot, x_ref, dmid_ref, vec_ref, *refs):
    grads, tiles, (dx_ref, sums_ref, acc, held) = refs[:-8], refs[-8:-4], refs[-4:]
    step = pl.program_id(0)

    @pl.when(step == 0)
    def _():
        acc[...] = jnp.zeros_like(acc)

    def work(d_cols):
        acc[...] += dot(d_cols, square(tiles, held), 1, 1)

    d_columns(step, grads, work)

    @pl.when(step == 2)
    def _():
        hat, rstd = norm_parts(x_ref[...].astype(F32))
        grad = acc[...]
        sums_ref[0:1, :] = jnp.sum(hat * grad, axis=0, keepdims=True)
        sums_ref[1:2, :] = jnp.sum(grad, axis=0, keepdims=True)
        sums_ref[2:8, :] = jnp.zeros((6, D), F32)
        dx_ref[...] = (dmid_ref[...] + norm_back(grad * vec_ref[0:1, :], hat, rstd)).astype(LOW)


def qkv_backward(own, slot, x, d_mid, vec, grads, gathered):
    rows = x.shape[0]
    row_spec = full_spec((rows, D))
    return pl.pallas_call(
        qkv_bwd_kernel,
        grid_spec=pltpu.PrefetchScalarGridSpec(
            num_scalar_prefetch=2,
            grid=(3,),
            in_specs=[row_spec, row_spec, full_spec(vec.shape)]
            + [full_spec(grad.shape) for grad in grads]
            + qkv_tiles(),
            out_specs=[row_spec, full_spec((8, D))],
            scratch_shapes=[pltpu.VMEM((rows, D), F32), pltpu.VMEM((D, D), LOW)],
        ),
        out_shape=[jax.ShapeDtypeStruct((rows, D), LOW), jax.ShapeDtypeStruct((8, D), F32)],
        compiler_params=params(60),
        name="qkv_bwd",
    )(own, slot, x, d_mid, vec, *grads, *([gathered] * 4))


def eliminate(blocks):
    count, size = len(blocks), blocks[0].shape[0]
    batch = min(count, 6)
    lane = lanes((1, 8, size))
    sub = lax.broadcasted_iota(jnp.int32, (1, 8, size), 1)
    wide_lane = lanes((size, size))
    shape = (batch, 8, size)

    def group(g, carry):
        base = pl.multiple_of(8 * g, 8)
        for at in range(0, count, batch):
            some = blocks[at : at + batch]
            slab = jnp.stack([y[pl.ds(base, 8), :] for y in some], axis=0)
            rolled = jnp.stack([pltpu.roll(slab[b], size - base, 1) for b in range(batch)], axis=0)
            columns = [jnp.broadcast_to(rolled[:, :, k : k + 1], shape) for k in range(8)]
            inside = (lane >= base) & (lane < base + 8)
            rows = jnp.where(inside, jnp.where(lane - base == sub, 1.0, 0.0), slab)
            scale = jnp.zeros(shape, F32)
            for j in range(8):
                inv_root = lax.rsqrt(jnp.broadcast_to(columns[j][:, j : j + 1, :], shape))
                scale = jnp.where(sub == j, inv_root, scale)
                factor = jnp.where(sub > j, columns[j] * (inv_root * inv_root), 0.0)
                rows = rows - factor * jnp.broadcast_to(rows[:, j : j + 1, :], shape)
                for k in range(j + 1, 8):
                    columns[k] = columns[k] - factor * jnp.broadcast_to(columns[k][:, j : j + 1, :], shape)
            rows = rows * scale
            passed = (wide_lane >= base) & (wide_lane < base + 8)
            for b, y in enumerate(some):
                high, mid, low = three_parts(rows[b])
                first = jnp.concatenate([high, high, mid, high, low, mid], axis=0)
                first = jnp.where(jnp.broadcast_to(lane[0, :1] >= base + 8, first.shape), first, 0.0)
                second = jnp.concatenate([high, mid, high, low, high, mid], axis=0)
                update = dot(first.astype(LOW), second.astype(LOW), 0, 0)
                y[...] = jnp.where(passed, 0.0, y[...]) - update
                y[pl.ds(base, 8), :] = rows[b]
        return carry

    lax.fori_loop(0, size // 8, group, 0)


def stats_kernel(ls_ref, rs_ref, lb_ref, rb_ref, left, right):
    for stats, basis, out in ((ls_ref, lb_ref, left), (rs_ref, rb_ref, right)):
        out[0] = BETA_STAT * dot_parts(low_parts(stats[0], 3), low_parts(basis[0], 3), 1, 0, 3)


def stats_product(left_stats, right_stats, left_basis, right_basis):
    count = left_stats.shape[0]
    block_spec = pl.BlockSpec((1, BLK, BLK), lambda i: (i, 0, 0))
    return pl.pallas_call(
        stats_kernel,
        grid=(count,),
        in_specs=[block_spec] * 4,
        out_specs=[block_spec] * 2,
        out_shape=[jax.ShapeDtypeStruct((count, BLK, BLK), F32)] * 2,
        compiler_params=params(32),
        name="stats",
    )(left_stats, right_stats, left_basis, right_basis)


def soap_kernel(
    seq_ref, g0, g1, g2, g3, w_ref, one_ref, two_ref, ls_ref, rs_ref, lb_ref, rb_ref, lp_ref, rp_ref,
    grad_ref, w_out, one_out, two_out, ls_out, rs_out, lb_out, rb_out,
    grad_s, gram, work, *inv,
):
    step = pl.program_id(0)
    slots = pl.num_programs(0)
    count = lb_out.shape[0]
    quarter = BLK // 4
    for piece, flip in ((g0, 0), (g1, 2), (g2, 1), (g3, 3)):
        start = pl.multiple_of((seq_ref[0] ^ flip) * quarter, quarter)
        grad_s[pl.ds(start, quarter), :] = piece[0]
    grad = grad_s[...]
    grad_ref[0] = grad.astype(F32)
    left, right = low_parts(lb_ref[0], 2), low_parts(rb_ref[0], 2)
    left_grad = dot_parts(left, [grad], 0, 0, 2)
    grad_right = dot_parts([grad], right, 1, 0, 2)
    rotated = dot(left_grad.astype(LOW), right[0], 1, 0)
    one = BETA_ONE * one_ref[0] + (1.0 - BETA_ONE) * rotated
    two = BETA_TWO * two_ref[0] + (1.0 - BETA_TWO) * rotated * rotated
    one_out[0] = one
    two_out[0] = two
    scaled = (one / (1.0 - BETA_ONE**STEP)) / (jnp.sqrt(two / (1.0 - BETA_TWO**STEP)) + ADAM_EPS)
    back = dot(dot(left[0], scaled.astype(LOW), 1, 0).astype(LOW), right[0], 1, 1)
    w_out[0] = w_ref[0] - RATE_MATRIX * (back + DECAY_RATE * w_ref[0])
    ls_out[0] = BETA_STAT * ls_ref[0] + (1.0 - BETA_STAT) * dot(grad, grad, 1, 1)
    rs_out[0] = BETA_STAT * rs_ref[0] + (1.0 - BETA_STAT) * dot(grad, grad, 0, 0)
    left_new = lp_ref[0] + (1.0 - BETA_STAT) * dot_parts([grad], low_parts(left_grad, 2), 1, 1, 2)
    right_new = rp_ref[0] + (1.0 - BETA_STAT) * dot_parts([grad], low_parts(grad_right, 2), 0, 0, 2)
    for side, product in enumerate((left_new, right_new)):
        at = side * count + step
        work[at] = product
        parts = low_parts(product, 3)
        for p in range(BLK // 128):
            c, on = slice(128 * p, 128 * p + 128), slice(128 * p, BLK)
            gram[at, c, on] = dot_parts([part[:, c] for part in parts], [part[:, on] for part in parts], 0, 0, 3)

    @pl.when(step == slots - 1)
    def _():
        for p in range(BLK // 128):
            c = slice(128 * p, 128 * p + 128)
            rest = slice(128 * p + 128, BLK)
            for b, block in enumerate(inv):
                block[...] = gram[b, c, c]
            eliminate(inv)
            for b, block in enumerate(inv):
                gram[b, c, c] = block[...]

            def solve(i, carry):
                wide = 2 if count % 2 == 0 else 1
                at = [side * count + wide * i + j for side in range(2) for j in range(wide)]
                factors = [low_parts(gram[b, c, c], 3) for b in at]
                solved = [
                    dot_parts(low_parts(work[b, :, c], 2), factor, 1, 1, 2)
                    for b, factor in zip(at, factors, strict=True)
                ]
                if p < BLK // 128 - 1:
                    uppers = [
                        low_parts(dot_parts(factor, low_parts(gram[b, c, rest], 3), 1, 0, 3), 3)
                        for b, factor in zip(at, factors, strict=True)
                    ]
                    works = [
                        work[b, :, rest] - dot_parts(low_parts(part, 2), upper, 1, 0, 2)
                        for b, part, upper in zip(at, solved, uppers, strict=True)
                    ]
                    grams = [
                        gram[b, rest, rest] - dot_parts(upper, upper, 0, 0, 3)
                        for b, upper in zip(at, uppers, strict=True)
                    ]
                    for b, new_work, new_gram in zip(at, works, grams, strict=True):
                        work[b, :, rest] = new_work
                        gram[b, rest, rest] = new_gram
                for j in range(wide):
                    lb_out[wide * i + j, :, c] = solved[j]
                    rb_out[wide * i + j, :, c] = solved[wide + j]
                return carry

            lax.fori_loop(0, count // (2 if count % 2 == 0 else 1), solve, 0)


def soap_update(seq, pieces, state, products):
    count = state[0].shape[0]
    piece_spec = pl.BlockSpec((1, BLK // 4, BLK), lambda i, s: (i, 0, 0))
    block_spec = pl.BlockSpec((1, BLK, BLK), lambda i, s: (i, 0, 0))
    whole_spec = pl.BlockSpec((count, BLK, BLK), lambda i, s: (0, 0, 0))
    shape = jax.ShapeDtypeStruct((count, BLK, BLK), F32)
    return pl.pallas_call(
        soap_kernel,
        grid_spec=pltpu.PrefetchScalarGridSpec(
            num_scalar_prefetch=1,
            grid=(count,),
            in_specs=[piece_spec] * 4 + [block_spec] * 9,
            out_specs=[block_spec] * 6 + [whole_spec] * 2,
            scratch_shapes=[
                pltpu.VMEM((BLK, BLK), LOW),
                pltpu.VMEM((2 * count, BLK, BLK), F32),
                pltpu.VMEM((2 * count, BLK, BLK), F32),
            ]
            + [pltpu.VMEM((128, 128), F32)] * (2 * count),
        ),
        out_shape=[shape] * 8,
        compiler_params=params(60),
        name="soap",
    )(seq, *pieces, *state, *products)


def split_kernel(dp, a_ref, b_ref, *outs):
    for k, out in enumerate(outs):
        out[...] = (a_ref[dp[0] ^ k].astype(F32) + b_ref[dp[0] ^ k].astype(F32)).astype(LOW)


def split_sum(dp, a, b):
    parts = a.shape[0]
    shape = a.shape[1:]
    return pl.pallas_call(
        split_kernel,
        grid_spec=pltpu.PrefetchScalarGridSpec(
            num_scalar_prefetch=1,
            grid=(1,),
            in_specs=[pl.BlockSpec(a.shape, lambda i, dp: (0,) * a.ndim)] * 2,
            out_specs=[pl.BlockSpec(shape, lambda i, dp: (0,) * len(shape))] * parts,
        ),
        out_shape=[jax.ShapeDtypeStruct(shape, LOW)] * parts,
        compiler_params=params(32),
        name="split_sum",
    )(dp, a, b)


def first_halves_kernel(keep, got, *outs, plans):
    per = keep.shape[4] // len(plans)
    names = ("x", 2, 1, 0)
    for g, plan in enumerate(plans):
        for out, side in zip(outs[2 * g : 2 * g + 2], (1, 0), strict=True):
            for n in range(4):
                where = {plan[0]: side, 2: 0}
                free = [name for name in plan[1:] if name != 2]
                where[free[0]], where[free[1]] = n // 2, n % 2
                at = tuple(where[name] for name in names) + (slice(per * g, per * g + per),)
                to = tuple(where[name] for name in plan[1:])
                out[to] = (keep[at].astype(F32) + got[at].astype(F32)).astype(LOW)


def first_halves(keep, got, plans):
    slots, rows, cols = keep.shape[4:]
    per, cut = slots // len(plans), rows // 3
    whole = pl.BlockSpec((2, 1, 2, 2, slots, cut, cols), lambda i, j: (0, i, 0, 0, 0, j, 0))
    outs = []
    for plan in plans:
        place = plan[1:].index(2)
        block = tuple(1 if n == place else 2 for n in range(3)) + (per, cut, cols)
        outs += [
            pl.BlockSpec(
                block,
                lambda i, j, place=place: tuple(i if n == place else 0 for n in range(3)) + (0, j, 0),
            )
        ] * 2
    shape = jax.ShapeDtypeStruct((2, 2, 2, per, rows, cols), LOW)
    return pl.pallas_call(
        functools.partial(first_halves_kernel, plans=plans),
        grid=(2, 3),
        in_specs=[whole, whole],
        out_specs=outs,
        out_shape=[shape] * len(outs),
        compiler_params=params(60),
        name="first_halves",
    )(keep, got)


def choose_kernel(dp, source, *refs, blocks):
    parts, early, out, held = refs[:-3], refs[-3], refs[-2], refs[-1]
    per, half = held.shape[1], held.shape[2]
    for k, part in enumerate(parts):
        held[k] = part[...]
    slots = out.shape[0]
    units = len(parts) * per

    def one(i, carry):
        block = source[i]

        @pl.when((2 * block >= units) & (block < blocks))
        def _():
            out[i] = early[i]

        @pl.when(block >= blocks)
        def _():
            out[i] = jnp.zeros(out.shape[1:], out.dtype)

        @pl.when(2 * block < units)
        def _():
            for h in range(2):
                unit = 2 * block + h
                out[i, h * half : h * half + half] = held[lax.div(unit, per) ^ dp[0], lax.rem(unit, per)]

        return carry

    lax.fori_loop(0, slots, one, 0)


def choose(dp, source, parts, early, blocks):
    return pl.pallas_call(
        functools.partial(choose_kernel, blocks=blocks),
        grid_spec=pltpu.PrefetchScalarGridSpec(
            num_scalar_prefetch=2,
            grid=(1,),
            in_specs=[pl.BlockSpec(parts[0].shape, lambda i, dp, src: (0, 0, 0))] * len(parts)
            + [pl.BlockSpec(early.shape, lambda i, dp, src: (0, 0, 0))],
            out_specs=pl.BlockSpec(early.shape, lambda i, dp, src: (0, 0, 0)),
            scratch_shapes=[pltpu.VMEM((len(parts),) + parts[0].shape, LOW)],
        ),
        out_shape=jax.ShapeDtypeStruct(early.shape, LOW),
        compiler_params=params(32),
        name="choose",
    )(dp, source, *parts, early)


def swap(x, axis, bit):
    size = lax.axis_size(axis)
    return lax.ppermute(x, axis, [(i, i ^ bit) for i in range(size)])


def add_low(a, b):
    return (a.astype(F32) + b.astype(F32)).astype(LOW)


class Halving:
    def __init__(self, kept, got, names, slots=None):
        self.kept, self.got, self.names, self.slots = kept, got, list(names), slots

    def take(self, name, index):
        axis = self.names.index(name)
        found = []
        for array in (self.kept, self.got):
            starts, limits = [0] * array.ndim, list(array.shape)
            starts[axis], limits[axis] = index, index + 1
            if self.slots is not None:
                starts[-3], limits[-3] = self.slots
            part = lax.slice(array, starts, limits)
            found.append(part.reshape(part.shape[:axis] + part.shape[axis + 1 :]))
        return add_low(*found)

    def send(self, name, ready=None):
        sent, kept = ready or (self.take(name, 1), self.take(name, 0))
        self.names.remove(name)
        self.kept, self.slots, self.name = kept, None, name
        return sent

    def receive(self, sent):
        axis, bit = ("seq", 2) if self.name == "x" else ("dp", 2**self.name)
        self.got = swap(sent, axis, bit)

    def total(self):
        return add_low(self.kept, self.got)


def quarters(piece):
    across = swap(piece, "seq", 2)
    return piece, across, swap(piece, "seq", 1), swap(across, "seq", 1)


def block_places(owners, owner_count, slot_count):
    block_count = owners.shape[0]
    ids = jnp.arange(block_count, dtype=jnp.int32)
    earlier = (owners[:, None] == owners[None, :]) & (ids[None, :] < ids[:, None])
    slots = jnp.sum(earlier.astype(jnp.int32), axis=1)
    places = owners * slot_count + slots
    matched = places[None, :] == jnp.arange(owner_count * slot_count, dtype=jnp.int32)[:, None]
    missing = 1 - jnp.any(matched, axis=1).astype(jnp.int32)
    sources = jnp.sum(jnp.where(matched, ids[None, :], 0), axis=1) + block_count * missing
    return slots, sources


def adam_vectors(gradient, vec, first_mom, second_mom):
    first_mom = BETA_ONE * first_mom + (1.0 - BETA_ONE) * gradient
    second_mom = BETA_TWO * second_mom + (1.0 - BETA_TWO) * gradient * gradient
    step_size = (first_mom / (1.0 - BETA_ONE**STEP)) / (
        jnp.sqrt(second_mom / (1.0 - BETA_TWO**STEP)) + ADAM_EPS
    )
    return first_mom, second_mom, vec - RATE_VECTOR * step_size


def on_device(
    tokens, cotangent, lengths, patch_mask, owners, master, moment_one, moment_two,
    left_stats, right_stats, left_basis, right_basis, vec, vec_one, vec_two,
):
    owner_count = lax.axis_size("dp")
    slot_count = master.shape[0]
    quarter = BLK // 4
    seq_id = lax.axis_index("seq").astype(jnp.int32)
    dp_id = lax.axis_index("dp").astype(jnp.int32)
    core, chip = seq_id % 2, seq_id // 2
    part_len = tokens.shape[1]
    slots, sources = block_places(owners, owner_count, slot_count)
    first_blocks = 3 * (D // BLK) ** 2

    mine = lax.dynamic_index_in_dim(
        master.reshape(slot_count, 4, quarter, BLK), seq_id, 1, keepdims=False
    ).astype(LOW)
    gathered = lax.all_gather(mine, AXES, axis=0, tiled=False).reshape(
        owner_count, 4, slot_count, quarter, BLK
    )

    products = stats_product(left_stats, right_stats, left_basis, right_basis)

    def halves_of(pair):
        kept = lax.dynamic_index_in_dim(pair, chip, 0, keepdims=False)
        return kept, lax.dynamic_index_in_dim(pair, 1 - chip, 0, keepdims=False)

    kept, sent = halves_of(tokens)
    x = jnp.concatenate([kept, swap(sent, "seq", 2)], axis=0)
    dy_kept, dy_sent = halves_of(cotangent)

    def to_positions(mine, other):
        return jnp.where(chip == 0, jnp.stack([mine, other]), jnp.stack([other, mine]))

    positions = jnp.arange(patch_mask.shape[-1], dtype=jnp.int32)
    live = (positions[None, :] < lengths[:, None]) & ((patch_mask == 1) | (positions[None, :] == 0))
    live = lax.dynamic_index_in_dim(live, chip, 0, keepdims=False).reshape(4, part_len)
    order = seq_id ^ jnp.array([0, 2, 1, 3], jnp.int32)
    fill = jnp.where(jnp.take(live, order, axis=0).reshape(-1), 0.0, NEG_FILL).astype(LOW)
    fill = jnp.broadcast_to(fill[:, None], (fill.shape[0], 128))

    bias = jnp.concatenate([vec[4], jnp.zeros_like(vec[4]), vec[5]])[None, :]
    gathered, products, dy_sent = lax.optimization_barrier((gathered, products, dy_sent))
    dy_got = swap(dy_sent, "seq", 2)
    q, kv, normed = qkv_forward(owners, slots, x, vec, bias, gathered)
    other = swap(kv, "seq", 1)
    attn, lse = attn_forward(q, kv, other, fill)
    attn, dy_got = lax.optimization_barrier((attn, dy_got))
    dy = jnp.concatenate([dy_kept, dy_got], axis=0)
    b1 = vec[8:].reshape(1, FF)
    seq_of, dp_of = seq_id.reshape(1), dp_id.reshape(1)
    result, d_mid, d_attn, keep, send, sums_two, bias_grad = mid_layer(
        owners, slots, owners ^ dp_id, seq_of, x, attn, dy, vec, b1, gathered
    )
    result_other = swap(result[part_len:], "seq", 2)

    bits = owner_count.bit_length() - 1
    if slot_count % 3 == 0 and bits == 3:
        plans = [["x", 0, 1, 2], [0, 1, "x", 2], [1, "x", 0, 2]]
    else:
        plans = [["x"] + list(range(bits))]
    per = slot_count // len(plans)
    names = ["x"] + list(range(bits))[::-1]
    shape = (2,) * (1 + bits) + keep.shape[2:]
    keep, got = keep.reshape(shape), swap(send, "seq", 1).reshape(shape)
    groups = [
        Halving(keep, got, names, (per * g, per * g + per)) for g in range(len(plans))
    ]
    guard = fill

    def advance(step, guard):
        if step == len(names) - 1 and len(groups) > 1:
            name = plans[0][step]
            sent = jnp.concatenate([group.take(name, 1) for group in groups], axis=0)
            kept = jnp.concatenate([group.take(name, 0) for group in groups], axis=0)
            groups[:] = [Halving(kept, None, [name])]
            sent, guard = lax.optimization_barrier((groups[0].send(name, (sent, kept)), guard))
            groups[0].receive(sent)
            return guard
        ready = [None] * len(plans)
        if step == 0 and len(plans) == 3:
            made = first_halves(keep, groups[0].got, plans)
            ready = [tuple(made[2 * g : 2 * g + 2]) for g in range(3)]
            for group, plan in zip(groups, plans, strict=True):
                group.names = list(plan)
        sent = [group.send(plan[step], own) for group, plan, own in zip(groups, plans, ready, strict=True)]
        *sent, guard = lax.optimization_barrier((*sent, guard))
        for group, array in zip(groups, sent, strict=True):
            group.receive(array)
        return guard

    grads = []
    taken = 0
    for first, count in ((0, 2), (2, 3), (5, 1)):
        if first:
            guard = advance(taken, guard)
            taken += 1
        parts = attn_backward(q, kv, other, guard, attn, lse, d_attn, first, count)
        got, parts, result_other = lax.optimization_barrier(
            ([group.got for group in groups], parts, result_other)
        )
        for group, array in zip(groups, got, strict=True):
            group.got = array
        dq, dk, dv, sent_kv = parts
        grads += [dq, dk, dv, swap(sent_kv, "seq", 1)]
    normed = advance(taken, normed)
    taken += 1
    late_keep, late_send, cols = qkv_grad(seq_of, normed, grads)
    late_shape = (2, -1, quarter, BLK)
    late = Halving(late_keep.reshape(late_shape), swap(late_send.reshape(late_shape), "seq", 1), ["x"])

    def after(value):
        got, value = lax.optimization_barrier(([group.got for group in groups], value))
        for group, array in zip(groups, got, strict=True):
            group.got = array
        return value

    sent_x = late.send("x")
    late.receive(sent_x)
    late.kept, d_mid = after(lax.optimization_barrier((late.kept, d_mid)))
    while taken < len(names):
        advance(taken, fill)
        taken += 1
    d_x, sums_one = qkv_backward(owners, slots, x, d_mid, vec, grads, gathered)
    late.got, d_x = lax.optimization_barrier((late.got, d_x))
    d_x = after(d_x)
    d_x_other = swap(d_x[part_len:], "seq", 2)
    early = groups[0].total()
    output = to_positions(result[:part_len], result_other)
    d_tokens = to_positions(d_x[:part_len], d_x_other)
    early, output, d_tokens = lax.optimization_barrier((early, output, d_tokens))

    mine_from = lax.dynamic_slice_in_dim(sources, dp_id * slot_count, slot_count)
    if 2 * first_blocks % owner_count == 0:
        unit = (owner_count, 2 * first_blocks // owner_count, quarter // 2, BLK)
        parts = split_sum(dp_of, late.kept.reshape(unit), late.got.reshape(unit))
        parts = [parts[0]] + [swap(part, "dp", k) for k, part in enumerate(parts) if k]
        total = sum(part.astype(F32) for part in parts).astype(LOW)
        parts = [total] + [swap(total, "dp", k) for k in range(1, owner_count)]
        piece = choose(dp_of, mine_from, parts, early, owners.shape[0])
    else:
        tiles = jnp.concatenate([late.total(), jnp.zeros((1, quarter, BLK), LOW)], axis=0)
        at = sources.reshape(owner_count, slot_count)[dp_id ^ jnp.arange(owner_count)]
        tiles = jnp.take(tiles, jnp.minimum(at, first_blocks).reshape(-1), axis=0)
        tiles = tiles.reshape((2,) * bits + (slot_count, quarter, BLK))
        owned = Halving(tiles, jnp.zeros_like(tiles), names[1:])
        for bit in range(bits):
            owned.receive(owned.send(bit))
        piece = jnp.where((mine_from < first_blocks)[:, None, None], owned.total(), early)
        piece = jnp.where((mine_from < owners.shape[0])[:, None, None], piece, jnp.zeros_like(piece))
    state = (master, moment_one, moment_two, left_stats, right_stats, left_basis, right_basis)
    piece, sums_one, sums_two, cols, bias_grad = lax.optimization_barrier(
        (piece, sums_one, sums_two, cols, bias_grad)
    )
    updates = soap_update(seq_of, quarters(piece), state, products)

    vec_grad = jnp.concatenate(
        [
            sums_one[0:2],
            sums_two[0:2],
            cols[:, :D],
            cols[:, 2 * D :],
            sums_two[2:4],
            bias_grad.reshape(-1, D),
        ],
        axis=0,
    )
    vec_parts = lax.all_gather(vec_grad, AXES, axis=0, tiled=False)
    updates, vec_parts = lax.optimization_barrier((updates, vec_parts))
    vec_total = jnp.sum(vec_parts, axis=0)
    vec_first, vec_second, vec_next = adam_vectors(vec_total, vec, vec_one, vec_two)
    grad_blocks, w_new, one_new, two_new, ls_new, rs_new, lb_new, rb_new = updates
    return (
        output, d_tokens, grad_blocks, w_new, one_new, two_new, ls_new, rs_new, lb_new, rb_new,
        vec_first, vec_second, vec_next,
    )


def solution(mesh):
    rows, blocks, whole = P("dp", "seq", None), P("dp", None, None), P()
    return jax.shard_map(
        on_device,
        mesh=mesh,
        in_specs=(rows, rows, P("dp"), P("dp", None), whole) + (blocks,) * 7 + (whole,) * 3,
        out_specs=(rows, rows) + (blocks,) * 8 + (whole,) * 3,
        check_vma=False,
    )
```

```python
import functools

import jax
import jax.numpy as jnp
from jax import lax
from jax.experimental import pallas as pl
from jax.experimental.pallas import tpu as pltpu
from jax.sharding import PartitionSpec as P

D = 768
FF = 3072
BLK = 384
STEP = 10

NORM_EPS = 1e-06
NEG_FILL = -1000000000.0
BETA_ONE = 0.9
BETA_TWO = 0.999
BETA_STAT = 0.95
RATE_MATRIX = 0.1
RATE_VECTOR = 0.3
DECAY_RATE = 0.01
ADAM_EPS = 1e-08

LOW = jnp.bfloat16
F32 = jnp.float32
AXES = ("dp", "seq")
MIB = 2**20

TAIL_P = 0.24
TAIL_C = (
    0.09575380798443668,
    0.09552183543465394,
    0.09284136585084933,
    0.06338567653857548,
    0.11841694922211018,
    -0.06574016740998187,
    0.15281935057715396,
    -0.052998628523732765,
)


def dot(a, b, ca, cb):
    return lax.dot_general(a, b, (((ca,), (cb,)), ((), ())), preferred_element_type=F32)


def lanes(shape):
    return lax.broadcasted_iota(jnp.int32, shape, len(shape) - 1)


def gelu_pair(x):
    u = jnp.abs(x)
    t = 1.0 / (1.0 + TAIL_P * u)
    poly = TAIL_C[-1]
    for coeff in TAIL_C[-2::-1]:
        poly = poly * t + coeff
    expo = jnp.exp(-0.5 * u * u)
    tail = poly * t * expo
    cdf = jnp.where(x < 0, tail, 1.0 - tail)
    return x * cdf, cdf + x * (expo * 0.3989422804014327)


def norm_parts(rows):
    center = rows - jnp.mean(rows, axis=-1, keepdims=True)
    rstd = lax.rsqrt(jnp.mean(center * center, axis=-1, keepdims=True) + NORM_EPS)
    return center * rstd, rstd


def norm_back(grad, hat, rstd):
    return rstd * (
        grad
        - jnp.mean(grad, axis=-1, keepdims=True)
        - hat * jnp.mean(grad * hat, axis=-1, keepdims=True)
    )


def params(limit):
    return pltpu.CompilerParams(vmem_limit_bytes=limit * MIB)


def tile_spec(block_of):
    return pl.BlockSpec(
        (1, 4, 1, BLK // 4, BLK),
        lambda i, own, slot: (own[block_of(i)], 0, slot[block_of(i)], 0, 0),
    )


def tile(ref):
    return ref[...].reshape(BLK, BLK)


def full_spec(shape):
    return pl.BlockSpec(shape, lambda i, own, slot: (0,) * len(shape))


def quarter_at(seq, rel_core, rel_x):
    return seq ^ (2 * rel_x + rel_core)


def square(tiles, held):
    for i in range(2):
        for j in range(2):
            held[i * BLK : i * BLK + BLK, j * BLK : j * BLK + BLK] = tile(tiles[2 * i + j])
    return held[...]


def qkv_kernel(own, slot, x_ref, vec_ref, bias_ref, t00, t01, t10, t11, q_ref, kv_ref, a_ref, held):
    @pl.when(pl.program_id(0) == 0)
    def _():
        hat, _ = norm_parts(x_ref[...].astype(F32))
        a_ref[...] = (hat * vec_ref[0:1, :] + vec_ref[1:2, :]).astype(LOW)

    low = (dot(a_ref[...], square((t00, t01, t10, t11), held), 1, 0) + bias_ref[...]).astype(LOW)

    @pl.when(pl.program_id(0) == 0)
    def _():
        q_ref[...] = low

    @pl.when(pl.program_id(0) > 0)
    def _():
        kv_ref[...] = low


def qkv_tiles():
    return [tile_spec(lambda i, n=n: 6 * (n // 2) + 2 * i + n % 2) for n in range(4)]


def qkv_forward(own, slot, x, vec, bias, gathered):
    rows = x.shape[0]
    return pl.pallas_call(
        qkv_kernel,
        grid_spec=pltpu.PrefetchScalarGridSpec(
            num_scalar_prefetch=2,
            grid=(3,),
            in_specs=[
                full_spec((rows, D)),
                full_spec(vec.shape),
                pl.BlockSpec((1, D), lambda i, own, slot: (0, i)),
            ]
            + qkv_tiles(),
            out_specs=[
                full_spec((rows, D)),
                pl.BlockSpec((rows, D), lambda i, own, slot: (0, jnp.maximum(i - 1, 0))),
                full_spec((rows, D)),
            ],
            scratch_shapes=[pltpu.VMEM((D, D), LOW)],
        ),
        out_shape=[
            jax.ShapeDtypeStruct((rows, D), LOW),
            jax.ShapeDtypeStruct((rows, 2 * D), LOW),
            jax.ShapeDtypeStruct((rows, D), LOW),
        ],
        compiler_params=params(48),
        name="qkv",
    )(own, slot, x, vec, bias, *([gathered] * 4))


def attn_fwd_kernel(q_ref, k1, v1, k2, v2, bias_ref, o_ref, lse_ref, ka, kb, va, vb):
    rows = k1.shape[0]

    @pl.when(pl.program_id(1) == 0)
    def _():
        ln = lanes((rows, 128))
        for i, (k, v) in enumerate(((k1, v1), (k2, v2))):
            r = slice(i * rows, i * rows + rows)
            keys, values, bias = k[...], v[...], bias_ref[r, :]
            one = jnp.ones_like(values)
            ka[r, :] = jnp.where(ln == 64, bias, keys)
            kb[r, :] = jnp.where(ln == 0, bias, keys)
            va[r, :] = jnp.where(ln < 64, values, one)
            vb[r, :] = jnp.where(ln < 64, one, values)

    q = q_ref[...] * jnp.asarray(0.125, LOW)
    ln = lanes(q.shape)
    one, zero = jnp.ones_like(q), jnp.zeros_like(q)
    qa = jnp.where(ln < 64, q, jnp.where(ln == 64, one, zero))
    qb = jnp.where(ln < 64, jnp.where(ln == 0, one, zero), q)
    outs, tops = [], []
    for query, keys, values in ((qa, ka, va), (qb, kb, vb)):
        logits = dot(query, keys[...], 1, 1)
        top = jnp.max(logits, axis=1, keepdims=True)
        expo = jnp.exp(logits - top).astype(LOW)
        outs.append(dot(expo, values[...], 1, 0))
        tops.append(top)
    total = jnp.where(ln < 64, outs[1], outs[0])
    attended = jnp.where(ln < 64, outs[0], outs[1])
    o_ref[...] = (attended / pltpu.roll(total, 64, 1)).astype(LOW)
    lse_ref[...] = jnp.where(ln < 64, tops[1], tops[0]) + jnp.log(total)


def attn_forward(q, kv, other, bias, q_rows=256):
    rows, pairs = q.shape[0], D // 128
    keys = 2 * rows
    q_spec = pl.BlockSpec((q_rows, 128), lambda p, i: (i, p))
    return pl.pallas_call(
        attn_fwd_kernel,
        grid=(pairs, rows // q_rows),
        in_specs=[
            q_spec,
            pl.BlockSpec((rows, 128), lambda p, i: (0, p)),
            pl.BlockSpec((rows, 128), lambda p, i: (0, pairs + p)),
            pl.BlockSpec((rows, 128), lambda p, i: (0, p)),
            pl.BlockSpec((rows, 128), lambda p, i: (0, pairs + p)),
            pl.BlockSpec((keys, 128), lambda p, i: (0, 0)),
        ],
        out_specs=[q_spec, q_spec],
        out_shape=[
            jax.ShapeDtypeStruct((rows, D), LOW),
            jax.ShapeDtypeStruct((rows, D), F32),
        ],
        scratch_shapes=[pltpu.VMEM((keys, 128), LOW)] * 4,
        compiler_params=params(48),
        name="attn_fwd",
    )(q, kv, kv, other, other, bias)


def three_parts(x):
    high = x.astype(LOW).astype(F32)
    rest = x - high
    mid = rest.astype(LOW).astype(F32)
    return high, mid, rest - mid


def low_parts(x, count):
    found = []
    for _ in range(count):
        part = x.astype(LOW)
        found.append(part)
        x = x - part.astype(F32)
    return found


def dot_parts(a, b, ca, cb, order):
    pairs = [(i, j) for i in range(len(a)) for j in range(len(b)) if i + j < order]
    a = jnp.concatenate([a[i] for i, _ in pairs], axis=ca)
    b = jnp.concatenate([b[j] for _, j in pairs], axis=cb)
    return dot(a, b, ca, cb)


def with_spare(x, spare, value, one, first):
    ln = lanes(x.shape)
    high, mid, low = three_parts(value)
    filled = jnp.where(ln == first + 3, one, 0.0)
    for i, part in enumerate((high, mid, low)):
        filled = jnp.where(ln == first + i, part, filled)
    return jnp.where(spare, filled, x).astype(LOW)


def attn_bwd_kernel(
    q_ref, k1, v1, k2, v2, bias_ref, o_ref, lse_ref, do_ref,
    dq_ref, dk1, dv1, dkv2, ka, kb, va, vb, kt, dk, dv, *, chunk,
):
    rows = k1.shape[0]

    @pl.when(pl.program_id(1) == 0)
    def _():
        ln = lanes((rows, 128))
        for i, (k, v) in enumerate(((k1, v1), (k2, v2))):
            r = slice(i * rows, i * rows + rows)
            keys, values, bias = k[...], v[...], bias_ref[r, :]
            one, zero = jnp.ones_like(values), jnp.zeros_like(values)
            ka[r, :] = jnp.where(ln < 64, keys, jnp.where(ln < 67, one, jnp.where(ln == 67, bias, zero)))
            kb[r, :] = jnp.where(ln >= 64, keys, jnp.where(ln < 3, one, jnp.where(ln == 3, bias, zero)))
            va[r, :] = jnp.where(ln < 64, values, jnp.where(ln < 67, one, zero))
            vb[r, :] = jnp.where(ln >= 64, values, jnp.where(ln < 3, one, zero))
            kt[:, r] = keys.T
        dk[...] = jnp.zeros_like(dk)
        dv[...] = jnp.zeros_like(dv)

    q = q_ref[...].astype(F32) * 0.125
    left = lanes(q.shape) < 64
    grad = do_ref[...].astype(F32)
    prod = grad * o_ref[...].astype(F32)
    sum_a = jnp.sum(jnp.where(left, prod, 0.0), axis=1, keepdims=True)
    sum_b = jnp.sum(jnp.where(left, 0.0, prod), axis=1, keepdims=True)
    delta = jnp.where(left, sum_b, sum_a)
    lse = lse_ref[...]
    zero = jnp.zeros_like(q)
    heads = (
        (
            with_spare(q, ~left, -lse, 1.0, 64), with_spare(grad, ~left, -delta, 0.0, 64), ka, va,
            jnp.where(left, q, zero).astype(LOW), jnp.where(left, grad, zero).astype(LOW),
        ),
        (
            with_spare(q, left, -lse, 1.0, 0), with_spare(grad, left, -delta, 0.0, 0), kb, vb,
            jnp.where(left, zero, q).astype(LOW), jnp.where(left, zero, grad).astype(LOW),
        ),
    )
    d_query = [jnp.zeros((64, q.shape[0]), F32)] * 2
    for c in range(2 * rows // chunk):
        r = slice(c * chunk, c * chunk + chunk)
        dv_c, dk_c = dv[r, :], dk[r, :]
        for h, (q_aug, g_aug, keys, values, q_only, g_only) in enumerate(heads):
            probs = jnp.exp(dot(keys[r, :], q_aug, 1, 1))
            d_logits = (probs * dot(values[r, :], g_aug, 1, 1)).astype(LOW)
            dv_c = dv_c + dot(probs.astype(LOW), g_only, 1, 0)
            dk_c = dk_c + dot(d_logits, q_only, 1, 0)
            d_query[h] = d_query[h] + dot(kt[64 * h : 64 * h + 64, r], d_logits, 1, 0)
        dv[r, :] = dv_c
        dk[r, :] = dk_c
    dq_ref[...] = (jnp.concatenate(d_query, axis=0) * 0.125).T.astype(LOW)

    @pl.when(pl.program_id(1) == pl.num_programs(1) - 1)
    def _():
        dk1[...] = dk[:rows, :].astype(LOW)
        dv1[...] = dv[:rows, :].astype(LOW)
        dkv2[0] = dk[rows:, :].astype(LOW)
        dkv2[1] = dv[rows:, :].astype(LOW)


def attn_backward(q, kv, other, bias, attn, lse, d_attn, first, count, q_rows=512, chunk=1024):
    rows, pairs = q.shape[0], D // 128
    keys = 2 * rows
    out_spec = pl.BlockSpec((q_rows, 128), lambda p, i: (i, p))
    k_out = pl.BlockSpec((rows, 128), lambda p, i: (0, p))
    q_spec = pl.BlockSpec((q_rows, 128), lambda p, i: (i, first + p))
    k_spec = pl.BlockSpec((rows, 128), lambda p, i: (0, first + p))
    v_spec = pl.BlockSpec((rows, 128), lambda p, i: (0, pairs + first + p))
    return pl.pallas_call(
        functools.partial(attn_bwd_kernel, chunk=chunk),
        grid=(count, rows // q_rows),
        in_specs=[
            q_spec, k_spec, v_spec, k_spec, v_spec, pl.BlockSpec((keys, 128), lambda p, i: (0, 0)),
            q_spec, q_spec, q_spec,
        ],
        out_specs=[out_spec, k_out, k_out, pl.BlockSpec((2, rows, 128), lambda p, i: (0, 0, p))],
        out_shape=[jax.ShapeDtypeStruct((rows, count * 128), LOW)] * 3
        + [jax.ShapeDtypeStruct((2, rows, count * 128), LOW)],
        scratch_shapes=[pltpu.VMEM((keys, 128), LOW)] * 4
        + [pltpu.VMEM((128, keys), LOW)]
        + [pltpu.VMEM((keys, 128), F32)] * 2,
        compiler_params=params(56),
        name="attn_bwd",
    )(q, kv, kv, other, other, bias, attn, lse, d_attn)


def mid_kernel(
    own, slot, rel, seq, x_ref, attn_ref, dy_ref, vec_ref, b1_ref, o00, o01, o10, o11, *refs, chunk):
    ups, downs = refs[:4], refs[4:8]
    (
        res_ref, dmid_ref, dattn_ref, keep, send, sums_ref, gb1_ref,
        mid, a2, acc, da2, up_s, down_s, stage, sems,
    ) = refs[8:]
    step = pl.program_id(0)
    last = pl.num_programs(0) - 1
    quarter = BLK // 4

    def copies(buf, i, block):
        found = []
        for rel_core, out in enumerate((keep, send)):
            for rel_x in range(2):
                found.append(
                    pltpu.make_async_copy(
                        stage.at[buf, i, quarter_at(seq[0], rel_core, rel_x)],
                        out.at[rel_x, rel[block], slot[block]],
                        sems.at[buf, i, 2 * rel_core + rel_x],
                    )
                )
        return found

    def put(buf, i, block, value):
        low = value.astype(LOW)
        for part in range(4):
            stage[buf, i, part] = low[part * quarter : part * quarter + quarter]
        for copy in copies(buf, i, block):
            copy.start()

    def settle(buf, count=8):
        for i in range(count):
            for copy in copies(buf, i, 0):
                copy.wait()

    @pl.when(step == 0)
    def _():
        mid[...] = (
            x_ref[...].astype(F32)
            + dot(attn_ref[...], square((o00, o01, o10, o11), up_s), 1, 0)
            + vec_ref[6:7, :]
        )
        hat, _ = norm_parts(mid[...])
        a2[...] = (hat * vec_ref[2:3, :] + vec_ref[3:4, :]).astype(LOW)
        acc[...] = jnp.zeros_like(acc)
        da2[...] = jnp.zeros_like(da2)

    @pl.when((step > 0) & (step < last))
    def _():
        rows = a2.shape[0]
        up, down = square(ups, up_s), square(downs, down_s)
        bias_grad = jnp.zeros((1, D), F32)
        acts, d_hids = [], []
        for c in range(rows // chunk):
            r = slice(c * chunk, c * chunk + chunk)
            act, slope = gelu_pair(dot(a2[r, :], up, 1, 0) + b1_ref[...])
            act = act.astype(LOW)
            d_hid = (dot(dy_ref[r, :], down, 1, 1) * slope).astype(LOW)
            acc[r, :] += dot(act, down, 1, 0)
            da2[r, :] += dot(d_hid, up, 1, 1)
            bias_grad = bias_grad + jnp.sum(d_hid.astype(F32), axis=0, keepdims=True)
            acts.append(act)
            d_hids.append(d_hid)
        gb1_ref[...] = bias_grad
        act = jnp.concatenate(acts, axis=0)
        d_hid = jnp.concatenate(d_hids, axis=0)
        buf = step % 2

        @pl.when(step > 2)
        def _():
            settle(buf)

        for i in range(2):
            c = slice(i * BLK, i * BLK + BLK)
            up_grad = dot(a2[:, c], d_hid, 0, 0)
            down_grad = dot(act[:, c], dy_ref[...], 0, 0)
            for j in range(2):
                k = slice(j * BLK, j * BLK + BLK)
                put(buf, 2 * i + j, 16 + 8 * i + 2 * (step - 1) + j, up_grad[:, k])
                put(buf, 4 + 2 * i + j, 32 + 4 * (step - 1) + 2 * i + j, down_grad[:, k])

    @pl.when(step == last)
    def _():
        res_ref[...] = (mid[...] + acc[...] + vec_ref[7:8, :]).astype(LOW)
        hat, rstd = norm_parts(mid[...])
        grad = da2[...]
        dy = dy_ref[...].astype(F32)
        sums_ref[0:1, :] = jnp.sum(hat * grad, axis=0, keepdims=True)
        sums_ref[1:2, :] = jnp.sum(grad, axis=0, keepdims=True)
        d_mid = dy + norm_back(grad * vec_ref[2:3, :], hat, rstd)
        dmid_ref[...] = d_mid
        d_proj = d_mid.astype(LOW)
        sums_ref[2:3, :] = jnp.sum(d_proj.astype(F32), axis=0, keepdims=True)
        sums_ref[3:4, :] = jnp.sum(dy, axis=0, keepdims=True)
        sums_ref[4:8, :] = jnp.zeros((4, D), F32)
        dattn_ref[...] = dot(d_proj, square((o00, o01, o10, o11), up_s), 1, 1).astype(LOW)
        settle(0)
        for i in range(2):
            out_grad = dot(attn_ref[:, i * BLK : i * BLK + BLK], d_proj, 0, 0)
            for j in range(2):
                put(0, 2 * i + j, 12 + 2 * i + j, out_grad[:, j * BLK : j * BLK + BLK])
        settle(1)
        settle(0, 4)


def mid_layer(own, slot, rel, seq, x, attn, dy, vec, b1, gathered, chunk=512):
    rows = x.shape[0]
    wide = FF // D
    quarter = BLK // 4
    owners, slots = gathered.shape[0], gathered.shape[2]

    def part(i):
        return jnp.clip(i - 1, 0, wide - 1)

    def full(shape):
        return pl.BlockSpec(shape, lambda i, own, slot, rel, seq: (0,) * len(shape))

    def tile_at(block_of):
        return pl.BlockSpec(
            (1, 4, 1, quarter, BLK),
            lambda i, own, slot, rel, seq: (own[block_of(i)], 0, slot[block_of(i)], 0, 0),
        )

    row_spec = full((rows, D))
    strip = pl.BlockSpec((1, D), lambda i, own, slot, rel, seq: (0, part(i)))
    anywhere = pl.BlockSpec(memory_space=pl.ANY)
    place_shape = jax.ShapeDtypeStruct((2, owners, slots, quarter, BLK), LOW)
    return pl.pallas_call(
        functools.partial(mid_kernel, chunk=chunk),
        grid_spec=pltpu.PrefetchScalarGridSpec(
            num_scalar_prefetch=4,
            grid=(wide + 2,),
            in_specs=[row_spec, row_spec, row_spec, full(vec.shape), strip]
            + [tile_at(lambda i, b=b: b) for b in (12, 13, 14, 15)]
            + [tile_at(lambda i, n=n: 16 + 8 * (n // 2) + 2 * part(i) + n % 2) for n in range(4)]
            + [tile_at(lambda i, n=n: 32 + 4 * part(i) + n) for n in range(4)],
            out_specs=[row_spec, row_spec, row_spec, anywhere, anywhere, full((8, D)), strip],
            scratch_shapes=[
                pltpu.VMEM((rows, D), F32),
                pltpu.VMEM((rows, D), LOW),
                pltpu.VMEM((rows, D), F32),
                pltpu.VMEM((rows, D), F32),
                pltpu.VMEM((D, D), LOW),
                pltpu.VMEM((D, D), LOW),
                pltpu.VMEM((2, 8, 4, quarter, BLK), LOW),
                pltpu.SemaphoreType.DMA((2, 8, 4)),
            ],
        ),
        out_shape=[
            jax.ShapeDtypeStruct((rows, D), LOW),
            jax.ShapeDtypeStruct((rows, D), F32),
            jax.ShapeDtypeStruct((rows, D), LOW),
            place_shape,
            place_shape,
            jax.ShapeDtypeStruct((8, D), F32),
            jax.ShapeDtypeStruct((1, FF), F32),
        ],
        compiler_params=params(60),
        name="mid",
    )(own, slot, rel, seq, x, attn, dy, vec, b1, *([gathered] * 12))


def d_columns(step, grads, work):
    def joined(n, *at):
        return jnp.concatenate([ref[at] if at else ref[...] for ref in grads[n::4]], axis=1)

    @pl.when(step == 0)
    def _():
        work(joined(0))

    for n in (1, 2):

        @pl.when(step == n)
        def _():
            work((joined(n).astype(F32) + joined(3, n - 1).astype(F32)).astype(LOW))


def qkv_grad_kernel(seq, a_ref, *refs):
    grads, (keep, send, cols_ref, stage) = refs[:-4], refs[-4:]
    quarter = BLK // 4

    def work(d_cols):
        cols_ref[...] = jnp.sum(d_cols.astype(F32), axis=0, keepdims=True)
        for i in range(2):
            stage[...] = dot(a_ref[:, i * BLK : i * BLK + BLK], d_cols, 0, 0).astype(LOW)
            for rel_core, out in enumerate((keep, send)):
                for rel_x in range(2):
                    start = pl.multiple_of(quarter_at(seq[0], rel_core, rel_x) * quarter, quarter)
                    for j in range(2):
                        out[rel_x, i, j] = stage[pl.ds(start, quarter), j * BLK : j * BLK + BLK]

    d_columns(pl.program_id(0), grads, work)


def qkv_grad(seq, normed, grads):
    rows = normed.shape[0]
    quarter = BLK // 4
    tile_out = pl.BlockSpec((2, 2, 2, quarter, BLK), lambda i, seq: (0, 0, i, 0, 0))
    shape = jax.ShapeDtypeStruct((2, 2, 6, quarter, BLK), LOW)
    return pl.pallas_call(
        qkv_grad_kernel,
        grid_spec=pltpu.PrefetchScalarGridSpec(
            num_scalar_prefetch=1,
            grid=(3,),
            in_specs=[pl.BlockSpec((rows, D), lambda i, seq: (0, 0))]
            + [pl.BlockSpec(grad.shape, lambda i, seq, n=grad.ndim: (0,) * n) for grad in grads],
            out_specs=[tile_out, tile_out, pl.BlockSpec((1, D), lambda i, seq: (0, i))],
            scratch_shapes=[pltpu.VMEM((BLK, D), LOW)],
        ),
        out_shape=[shape, shape, jax.ShapeDtypeStruct((1, 3 * D), F32)],
        compiler_params=params(48),
        name="qkv_grad",
    )(seq, normed, *grads)


def qkv_bwd_kernel(own, slot, x_ref, dmid_ref, vec_ref, *refs):
    grads, tiles, (dx_ref, sums_ref, acc, held) = refs[:-8], refs[-8:-4], refs[-4:]
    step = pl.program_id(0)

    @pl.when(step == 0)
    def _():
        acc[...] = jnp.zeros_like(acc)

    def work(d_cols):
        acc[...] += dot(d_cols, square(tiles, held), 1, 1)

    d_columns(step, grads, work)

    @pl.when(step == 2)
    def _():
        hat, rstd = norm_parts(x_ref[...].astype(F32))
        grad = acc[...]
        sums_ref[0:1, :] = jnp.sum(hat * grad, axis=0, keepdims=True)
        sums_ref[1:2, :] = jnp.sum(grad, axis=0, keepdims=True)
        sums_ref[2:8, :] = jnp.zeros((6, D), F32)
        dx_ref[...] = (dmid_ref[...] + norm_back(grad * vec_ref[0:1, :], hat, rstd)).astype(LOW)


def qkv_backward(own, slot, x, d_mid, vec, grads, gathered):
    rows = x.shape[0]
    row_spec = full_spec((rows, D))
    return pl.pallas_call(
        qkv_bwd_kernel,
        grid_spec=pltpu.PrefetchScalarGridSpec(
            num_scalar_prefetch=2,
            grid=(3,),
            in_specs=[row_spec, row_spec, full_spec(vec.shape)]
            + [full_spec(grad.shape) for grad in grads]
            + qkv_tiles(),
            out_specs=[row_spec, full_spec((8, D))],
            scratch_shapes=[pltpu.VMEM((rows, D), F32), pltpu.VMEM((D, D), LOW)],
        ),
        out_shape=[jax.ShapeDtypeStruct((rows, D), LOW), jax.ShapeDtypeStruct((8, D), F32)],
        compiler_params=params(60),
        name="qkv_bwd",
    )(own, slot, x, d_mid, vec, *grads, *([gathered] * 4))


def eliminate(blocks):
    count, size = len(blocks), blocks[0].shape[0]
    batch = min(count, 6)
    lane = lanes((1, 8, size))
    sub = lax.broadcasted_iota(jnp.int32, (1, 8, size), 1)
    wide_lane = lanes((size, size))
    shape = (batch, 8, size)

    def group(g, carry):
        base = pl.multiple_of(8 * g, 8)
        for at in range(0, count, batch):
            some = blocks[at : at + batch]
            slab = jnp.stack([y[pl.ds(base, 8), :] for y in some], axis=0)
            rolled = jnp.stack([pltpu.roll(slab[b], size - base, 1) for b in range(batch)], axis=0)
            columns = [jnp.broadcast_to(rolled[:, :, k : k + 1], shape) for k in range(8)]
            inside = (lane >= base) & (lane < base + 8)
            rows = jnp.where(inside, jnp.where(lane - base == sub, 1.0, 0.0), slab)
            scale = jnp.zeros(shape, F32)
            for j in range(8):
                inv_root = lax.rsqrt(jnp.broadcast_to(columns[j][:, j : j + 1, :], shape))
                scale = jnp.where(sub == j, inv_root, scale)
                factor = jnp.where(sub > j, columns[j] * (inv_root * inv_root), 0.0)
                rows = rows - factor * jnp.broadcast_to(rows[:, j : j + 1, :], shape)
                for k in range(j + 1, 8):
                    columns[k] = columns[k] - factor * jnp.broadcast_to(columns[k][:, j : j + 1, :], shape)
            rows = rows * scale
            passed = (wide_lane >= base) & (wide_lane < base + 8)
            for b, y in enumerate(some):
                high, mid, low = three_parts(rows[b])
                first = jnp.concatenate([high, high, mid, high, low, mid], axis=0)
                first = jnp.where(jnp.broadcast_to(lane[0, :1] >= base + 8, first.shape), first, 0.0)
                second = jnp.concatenate([high, mid, high, low, high, mid], axis=0)
                update = dot(first.astype(LOW), second.astype(LOW), 0, 0)
                y[...] = jnp.where(passed, 0.0, y[...]) - update
                y[pl.ds(base, 8), :] = rows[b]
        return carry

    lax.fori_loop(0, size // 8, group, 0)


def stats_kernel(ls_ref, rs_ref, lb_ref, rb_ref, left, right):
    for stats, basis, out in ((ls_ref, lb_ref, left), (rs_ref, rb_ref, right)):
        out[0] = BETA_STAT * dot_parts(low_parts(stats[0], 3), low_parts(basis[0], 3), 1, 0, 3)


def stats_product(left_stats, right_stats, left_basis, right_basis):
    count = left_stats.shape[0]
    block_spec = pl.BlockSpec((1, BLK, BLK), lambda i: (i, 0, 0))
    return pl.pallas_call(
        stats_kernel,
        grid=(count,),
        in_specs=[block_spec] * 4,
        out_specs=[block_spec] * 2,
        out_shape=[jax.ShapeDtypeStruct((count, BLK, BLK), F32)] * 2,
        compiler_params=params(32),
        name="stats",
    )(left_stats, right_stats, left_basis, right_basis)


def soap_kernel(
    seq_ref, g0, g1, g2, g3, w_ref, one_ref, two_ref, ls_ref, rs_ref, lb_ref, rb_ref, lp_ref, rp_ref,
    grad_ref, w_out, one_out, two_out, ls_out, rs_out, lb_out, rb_out,
    grad_s, gram, work, *inv,
):
    step = pl.program_id(0)
    slots = pl.num_programs(0)
    count = lb_out.shape[0]
    quarter = BLK // 4
    for piece, flip in ((g0, 0), (g1, 2), (g2, 1), (g3, 3)):
        start = pl.multiple_of((seq_ref[0] ^ flip) * quarter, quarter)
        grad_s[pl.ds(start, quarter), :] = piece[0]
    grad = grad_s[...]
    grad_ref[0] = grad.astype(F32)
    left, right = low_parts(lb_ref[0], 2), low_parts(rb_ref[0], 2)
    left_grad = dot_parts(left, [grad], 0, 0, 2)
    grad_right = dot_parts([grad], right, 1, 0, 2)
    rotated = dot(left_grad.astype(LOW), right[0], 1, 0)
    one = BETA_ONE * one_ref[0] + (1.0 - BETA_ONE) * rotated
    two = BETA_TWO * two_ref[0] + (1.0 - BETA_TWO) * rotated * rotated
    one_out[0] = one
    two_out[0] = two
    scaled = (one / (1.0 - BETA_ONE**STEP)) / (jnp.sqrt(two / (1.0 - BETA_TWO**STEP)) + ADAM_EPS)
    back = dot(dot(left[0], scaled.astype(LOW), 1, 0).astype(LOW), right[0], 1, 1)
    w_out[0] = w_ref[0] - RATE_MATRIX * (back + DECAY_RATE * w_ref[0])
    ls_out[0] = BETA_STAT * ls_ref[0] + (1.0 - BETA_STAT) * dot(grad, grad, 1, 1)
    rs_out[0] = BETA_STAT * rs_ref[0] + (1.0 - BETA_STAT) * dot(grad, grad, 0, 0)
    left_new = lp_ref[0] + (1.0 - BETA_STAT) * dot_parts([grad], low_parts(left_grad, 2), 1, 1, 2)
    right_new = rp_ref[0] + (1.0 - BETA_STAT) * dot_parts([grad], low_parts(grad_right, 2), 0, 0, 2)
    for side, product in enumerate((left_new, right_new)):
        at = side * count + step
        work[at] = product
        parts = low_parts(product, 3)
        for p in range(BLK // 128):
            c, on = slice(128 * p, 128 * p + 128), slice(128 * p, BLK)
            gram[at, c, on] = dot_parts([part[:, c] for part in parts], [part[:, on] for part in parts], 0, 0, 3)

    @pl.when(step == slots - 1)
    def _():
        for p in range(BLK // 128):
            c = slice(128 * p, 128 * p + 128)
            rest = slice(128 * p + 128, BLK)
            for b, block in enumerate(inv):
                block[...] = gram[b, c, c]
            eliminate(inv)
            for b, block in enumerate(inv):
                gram[b, c, c] = block[...]

            def solve(i, carry):
                wide = 2 if count % 2 == 0 else 1
                at = [side * count + wide * i + j for side in range(2) for j in range(wide)]
                factors = [low_parts(gram[b, c, c], 3) for b in at]
                solved = [
                    dot_parts(low_parts(work[b, :, c], 2), factor, 1, 1, 2)
                    for b, factor in zip(at, factors, strict=True)
                ]
                if p < BLK // 128 - 1:
                    uppers = [
                        low_parts(dot_parts(factor, low_parts(gram[b, c, rest], 3), 1, 0, 3), 3)
                        for b, factor in zip(at, factors, strict=True)
                    ]
                    works = [
                        work[b, :, rest] - dot_parts(low_parts(part, 2), upper, 1, 0, 2)
                        for b, part, upper in zip(at, solved, uppers, strict=True)
                    ]
                    grams = [
                        gram[b, rest, rest] - dot_parts(upper, upper, 0, 0, 3)
                        for b, upper in zip(at, uppers, strict=True)
                    ]
                    for b, new_work, new_gram in zip(at, works, grams, strict=True):
                        work[b, :, rest] = new_work
                        gram[b, rest, rest] = new_gram
                for j in range(wide):
                    lb_out[wide * i + j, :, c] = solved[j]
                    rb_out[wide * i + j, :, c] = solved[wide + j]
                return carry

            lax.fori_loop(0, count // (2 if count % 2 == 0 else 1), solve, 0)


def soap_update(seq, pieces, state, products):
    count = state[0].shape[0]
    piece_spec = pl.BlockSpec((1, BLK // 4, BLK), lambda i, s: (i, 0, 0))
    block_spec = pl.BlockSpec((1, BLK, BLK), lambda i, s: (i, 0, 0))
    whole_spec = pl.BlockSpec((count, BLK, BLK), lambda i, s: (0, 0, 0))
    shape = jax.ShapeDtypeStruct((count, BLK, BLK), F32)
    return pl.pallas_call(
        soap_kernel,
        grid_spec=pltpu.PrefetchScalarGridSpec(
            num_scalar_prefetch=1,
            grid=(count,),
            in_specs=[piece_spec] * 4 + [block_spec] * 9,
            out_specs=[block_spec] * 6 + [whole_spec] * 2,
            scratch_shapes=[
                pltpu.VMEM((BLK, BLK), LOW),
                pltpu.VMEM((2 * count, BLK, BLK), F32),
                pltpu.VMEM((2 * count, BLK, BLK), F32),
            ]
            + [pltpu.VMEM((128, 128), F32)] * (2 * count),
        ),
        out_shape=[shape] * 8,
        compiler_params=params(60),
        name="soap",
    )(seq, *pieces, *state, *products)


def split_kernel(dp, a_ref, b_ref, *outs):
    for k, out in enumerate(outs):
        out[...] = (a_ref[dp[0] ^ k].astype(F32) + b_ref[dp[0] ^ k].astype(F32)).astype(LOW)


def split_sum(dp, a, b):
    parts = a.shape[0]
    shape = a.shape[1:]
    return pl.pallas_call(
        split_kernel,
        grid_spec=pltpu.PrefetchScalarGridSpec(
            num_scalar_prefetch=1,
            grid=(1,),
            in_specs=[pl.BlockSpec(a.shape, lambda i, dp: (0,) * a.ndim)] * 2,
            out_specs=[pl.BlockSpec(shape, lambda i, dp: (0,) * len(shape))] * parts,
        ),
        out_shape=[jax.ShapeDtypeStruct(shape, LOW)] * parts,
        compiler_params=params(32),
        name="split_sum",
    )(dp, a, b)


def first_halves_kernel(keep, got, *outs, plans):
    per = keep.shape[4] // len(plans)
    names = ("x", 2, 1, 0)
    for g, plan in enumerate(plans):
        for out, side in zip(outs[2 * g : 2 * g + 2], (1, 0), strict=True):
            for n in range(4):
                where = {plan[0]: side, 2: 0}
                free = [name for name in plan[1:] if name != 2]
                where[free[0]], where[free[1]] = n // 2, n % 2
                at = tuple(where[name] for name in names) + (slice(per * g, per * g + per),)
                to = tuple(where[name] for name in plan[1:])
                out[to] = (keep[at].astype(F32) + got[at].astype(F32)).astype(LOW)


def first_halves(keep, got, plans):
    slots, rows, cols = keep.shape[4:]
    per, cut = slots // len(plans), rows // 3
    whole = pl.BlockSpec((2, 1, 2, 2, slots, cut, cols), lambda i, j: (0, i, 0, 0, 0, j, 0))
    outs = []
    for plan in plans:
        place = plan[1:].index(2)
        block = tuple(1 if n == place else 2 for n in range(3)) + (per, cut, cols)
        outs += [
            pl.BlockSpec(
                block,
                lambda i, j, place=place: tuple(i if n == place else 0 for n in range(3)) + (0, j, 0),
            )
        ] * 2
    shape = jax.ShapeDtypeStruct((2, 2, 2, per, rows, cols), LOW)
    return pl.pallas_call(
        functools.partial(first_halves_kernel, plans=plans),
        grid=(2, 3),
        in_specs=[whole, whole],
        out_specs=outs,
        out_shape=[shape] * len(outs),
        compiler_params=params(60),
        name="first_halves",
    )(keep, got)


def choose_kernel(dp, source, *refs, blocks):
    parts, early, out, held = refs[:-3], refs[-3], refs[-2], refs[-1]
    per, half = held.shape[1], held.shape[2]
    for k, part in enumerate(parts):
        held[k] = part[...]
    slots = out.shape[0]
    units = len(parts) * per

    def one(i, carry):
        block = source[i]

        @pl.when((2 * block >= units) & (block < blocks))
        def _():
            out[i] = early[i]

        @pl.when(block >= blocks)
        def _():
            out[i] = jnp.zeros(out.shape[1:], out.dtype)

        @pl.when(2 * block < units)
        def _():
            for h in range(2):
                unit = 2 * block + h
                out[i, h * half : h * half + half] = held[lax.div(unit, per) ^ dp[0], lax.rem(unit, per)]

        return carry

    lax.fori_loop(0, slots, one, 0)


def choose(dp, source, parts, early, blocks):
    return pl.pallas_call(
        functools.partial(choose_kernel, blocks=blocks),
        grid_spec=pltpu.PrefetchScalarGridSpec(
            num_scalar_prefetch=2,
            grid=(1,),
            in_specs=[pl.BlockSpec(parts[0].shape, lambda i, dp, src: (0, 0, 0))] * len(parts)
            + [pl.BlockSpec(early.shape, lambda i, dp, src: (0, 0, 0))],
            out_specs=pl.BlockSpec(early.shape, lambda i, dp, src: (0, 0, 0)),
            scratch_shapes=[pltpu.VMEM((len(parts),) + parts[0].shape, LOW)],
        ),
        out_shape=jax.ShapeDtypeStruct(early.shape, LOW),
        compiler_params=params(32),
        name="choose",
    )(dp, source, *parts, early)


def swap(x, axis, bit):
    size = lax.axis_size(axis)
    return lax.ppermute(x, axis, [(i, i ^ bit) for i in range(size)])


def add_low(a, b):
    return (a.astype(F32) + b.astype(F32)).astype(LOW)


class Halving:
    def __init__(self, kept, got, names, slots=None):
        self.kept, self.got, self.names, self.slots = kept, got, list(names), slots

    def take(self, name, index):
        axis = self.names.index(name)
        found = []
        for array in (self.kept, self.got):
            starts, limits = [0] * array.ndim, list(array.shape)
            starts[axis], limits[axis] = index, index + 1
            if self.slots is not None:
                starts[-3], limits[-3] = self.slots
            part = lax.slice(array, starts, limits)
            found.append(part.reshape(part.shape[:axis] + part.shape[axis + 1 :]))
        return add_low(*found)

    def send(self, name, ready=None):
        sent, kept = ready or (self.take(name, 1), self.take(name, 0))
        self.names.remove(name)
        self.kept, self.slots, self.name = kept, None, name
        return sent

    def receive(self, sent):
        axis, bit = ("seq", 2) if self.name == "x" else ("dp", 2**self.name)
        self.got = swap(sent, axis, bit)

    def total(self):
        return add_low(self.kept, self.got)


def quarters(piece):
    across = swap(piece, "seq", 2)
    return piece, across, swap(piece, "seq", 1), swap(across, "seq", 1)


def block_places(owners, owner_count, slot_count):
    block_count = owners.shape[0]
    ids = jnp.arange(block_count, dtype=jnp.int32)
    earlier = (owners[:, None] == owners[None, :]) & (ids[None, :] < ids[:, None])
    slots = jnp.sum(earlier.astype(jnp.int32), axis=1)
    places = owners * slot_count + slots
    matched = places[None, :] == jnp.arange(owner_count * slot_count, dtype=jnp.int32)[:, None]
    missing = 1 - jnp.any(matched, axis=1).astype(jnp.int32)
    sources = jnp.sum(jnp.where(matched, ids[None, :], 0), axis=1) + block_count * missing
    return slots, sources


def adam_vectors(gradient, vec, first_mom, second_mom):
    first_mom = BETA_ONE * first_mom + (1.0 - BETA_ONE) * gradient
    second_mom = BETA_TWO * second_mom + (1.0 - BETA_TWO) * gradient * gradient
    step_size = (first_mom / (1.0 - BETA_ONE**STEP)) / (
        jnp.sqrt(second_mom / (1.0 - BETA_TWO**STEP)) + ADAM_EPS
    )
    return first_mom, second_mom, vec - RATE_VECTOR * step_size


def on_device(
    tokens, cotangent, lengths, patch_mask, owners, master, moment_one, moment_two,
    left_stats, right_stats, left_basis, right_basis, vec, vec_one, vec_two,
):
    owner_count = lax.axis_size("dp")
    slot_count = master.shape[0]
    quarter = BLK // 4
    seq_id = lax.axis_index("seq").astype(jnp.int32)
    dp_id = lax.axis_index("dp").astype(jnp.int32)
    core, chip = seq_id % 2, seq_id // 2
    part_len = tokens.shape[1]
    slots, sources = block_places(owners, owner_count, slot_count)
    first_blocks = 3 * (D // BLK) ** 2

    mine = lax.dynamic_index_in_dim(
        master.reshape(slot_count, 4, quarter, BLK), seq_id, 1, keepdims=False
    ).astype(LOW)
    gathered = lax.all_gather(mine, AXES, axis=0, tiled=False).reshape(
        owner_count, 4, slot_count, quarter, BLK
    )

    products = stats_product(left_stats, right_stats, left_basis, right_basis)

    def halves_of(pair):
        kept = lax.dynamic_index_in_dim(pair, chip, 0, keepdims=False)
        return kept, lax.dynamic_index_in_dim(pair, 1 - chip, 0, keepdims=False)

    kept, sent = halves_of(tokens)
    x = jnp.concatenate([kept, swap(sent, "seq", 2)], axis=0)
    dy_kept, dy_sent = halves_of(cotangent)

    def to_positions(mine, other):
        return jnp.where(chip == 0, jnp.stack([mine, other]), jnp.stack([other, mine]))

    positions = jnp.arange(patch_mask.shape[-1], dtype=jnp.int32)
    live = (positions[None, :] < lengths[:, None]) & ((patch_mask == 1) | (positions[None, :] == 0))
    live = lax.dynamic_index_in_dim(live, chip, 0, keepdims=False).reshape(4, part_len)
    order = seq_id ^ jnp.array([0, 2, 1, 3], jnp.int32)
    fill = jnp.where(jnp.take(live, order, axis=0).reshape(-1), 0.0, NEG_FILL).astype(LOW)
    fill = jnp.broadcast_to(fill[:, None], (fill.shape[0], 128))

    bias = jnp.concatenate([vec[4], jnp.zeros_like(vec[4]), vec[5]])[None, :]
    gathered, products, dy_sent = lax.optimization_barrier((gathered, products, dy_sent))
    dy_got = swap(dy_sent, "seq", 2)
    q, kv, normed = qkv_forward(owners, slots, x, vec, bias, gathered)
    other = swap(kv, "seq", 1)
    attn, lse = attn_forward(q, kv, other, fill)
    attn, dy_got = lax.optimization_barrier((attn, dy_got))
    dy = jnp.concatenate([dy_kept, dy_got], axis=0)
    b1 = vec[8:].reshape(1, FF)
    seq_of, dp_of = seq_id.reshape(1), dp_id.reshape(1)
    result, d_mid, d_attn, keep, send, sums_two, bias_grad = mid_layer(
        owners, slots, owners ^ dp_id, seq_of, x, attn, dy, vec, b1, gathered
    )
    result_other = swap(result[part_len:], "seq", 2)

    bits = owner_count.bit_length() - 1
    if slot_count % 3 == 0 and bits == 3:
        plans = [["x", 0, 1, 2], [0, 1, "x", 2], [1, "x", 0, 2]]
    else:
        plans = [["x"] + list(range(bits))]
    per = slot_count // len(plans)
    names = ["x"] + list(range(bits))[::-1]
    shape = (2,) * (1 + bits) + keep.shape[2:]
    keep, got = keep.reshape(shape), swap(send, "seq", 1).reshape(shape)
    groups = [
        Halving(keep, got, names, (per * g, per * g + per)) for g in range(len(plans))
    ]
    guard = fill

    def advance(step, guard):
        if step == len(names) - 1 and len(groups) > 1:
            name = plans[0][step]
            sent = jnp.concatenate([group.take(name, 1) for group in groups], axis=0)
            kept = jnp.concatenate([group.take(name, 0) for group in groups], axis=0)
            groups[:] = [Halving(kept, None, [name])]
            sent, guard = lax.optimization_barrier((groups[0].send(name, (sent, kept)), guard))
            groups[0].receive(sent)
            return guard
        ready = [None] * len(plans)
        if step == 0 and len(plans) == 3:
            made = first_halves(keep, groups[0].got, plans)
            ready = [tuple(made[2 * g : 2 * g + 2]) for g in range(3)]
            for group, plan in zip(groups, plans, strict=True):
                group.names = list(plan)
        sent = [group.send(plan[step], own) for group, plan, own in zip(groups, plans, ready, strict=True)]
        *sent, guard = lax.optimization_barrier((*sent, guard))
        for group, array in zip(groups, sent, strict=True):
            group.receive(array)
        return guard

    grads = []
    taken = 0
    for first, count in ((0, 2), (2, 3), (5, 1)):
        if first:
            guard = advance(taken, guard)
            taken += 1
        parts = attn_backward(q, kv, other, guard, attn, lse, d_attn, first, count)
        got, parts, result_other = lax.optimization_barrier(
            ([group.got for group in groups], parts, result_other)
        )
        for group, array in zip(groups, got, strict=True):
            group.got = array
        dq, dk, dv, sent_kv = parts
        grads += [dq, dk, dv, swap(sent_kv, "seq", 1)]
    normed = advance(taken, normed)
    taken += 1
    late_keep, late_send, cols = qkv_grad(seq_of, normed, grads)
    late_shape = (2, -1, quarter, BLK)
    late = Halving(late_keep.reshape(late_shape), swap(late_send.reshape(late_shape), "seq", 1), ["x"])

    def after(value):
        got, value = lax.optimization_barrier(([group.got for group in groups], value))
        for group, array in zip(groups, got, strict=True):
            group.got = array
        return value

    sent_x = late.send("x")
    late.receive(sent_x)
    late.kept, d_mid = after(lax.optimization_barrier((late.kept, d_mid)))
    while taken < len(names):
        advance(taken, fill)
        taken += 1
    d_x, sums_one = qkv_backward(owners, slots, x, d_mid, vec, grads, gathered)
    late.got, d_x = lax.optimization_barrier((late.got, d_x))
    d_x = after(d_x)
    d_x_other = swap(d_x[part_len:], "seq", 2)
    early = groups[0].total()
    output = to_positions(result[:part_len], result_other)
    d_tokens = to_positions(d_x[:part_len], d_x_other)
    early, output, d_tokens = lax.optimization_barrier((early, output, d_tokens))

    mine_from = lax.dynamic_slice_in_dim(sources, dp_id * slot_count, slot_count)
    if 2 * first_blocks % owner_count == 0:
        unit = (owner_count, 2 * first_blocks // owner_count, quarter // 2, BLK)
        parts = split_sum(dp_of, late.kept.reshape(unit), late.got.reshape(unit))
        parts = [parts[0]] + [swap(part, "dp", k) for k, part in enumerate(parts) if k]
        total = sum(part.astype(F32) for part in parts).astype(LOW)
        parts = [total] + [swap(total, "dp", k) for k in range(1, owner_count)]
        piece = choose(dp_of, mine_from, parts, early, owners.shape[0])
    else:
        tiles = jnp.concatenate([late.total(), jnp.zeros((1, quarter, BLK), LOW)], axis=0)
        at = sources.reshape(owner_count, slot_count)[dp_id ^ jnp.arange(owner_count)]
        tiles = jnp.take(tiles, jnp.minimum(at, first_blocks).reshape(-1), axis=0)
        tiles = tiles.reshape((2,) * bits + (slot_count, quarter, BLK))
        owned = Halving(tiles, jnp.zeros_like(tiles), names[1:])
        for bit in range(bits):
            owned.receive(owned.send(bit))
        piece = jnp.where((mine_from < first_blocks)[:, None, None], owned.total(), early)
        piece = jnp.where((mine_from < owners.shape[0])[:, None, None], piece, jnp.zeros_like(piece))
    state = (master, moment_one, moment_two, left_stats, right_stats, left_basis, right_basis)
    piece, sums_one, sums_two, cols, bias_grad = lax.optimization_barrier(
        (piece, sums_one, sums_two, cols, bias_grad)
    )
    updates = soap_update(seq_of, quarters(piece), state, products)

    vec_grad = jnp.concatenate(
        [
            sums_one[0:2],
            sums_two[0:2],
            cols[:, :D],
            cols[:, 2 * D :],
            sums_two[2:4],
            bias_grad.reshape(-1, D),
        ],
        axis=0,
    )
    vec_parts = lax.all_gather(vec_grad, AXES, axis=0, tiled=False)
    updates, vec_parts = lax.optimization_barrier((updates, vec_parts))
    vec_total = jnp.sum(vec_parts, axis=0)
    vec_first, vec_second, vec_next = adam_vectors(vec_total, vec, vec_one, vec_two)
    grad_blocks, w_new, one_new, two_new, ls_new, rs_new, lb_new, rb_new = updates
    return (
        output, d_tokens, grad_blocks, w_new, one_new, two_new, ls_new, rs_new, lb_new, rb_new,
        vec_first, vec_second, vec_next,
    )


def solution(mesh):
    rows, blocks, whole = P("dp", "seq", None), P("dp", None, None), P()
    return jax.shard_map(
        on_device,
        mesh=mesh,
        in_specs=(rows, rows, P("dp"), P("dp", None), whole) + (blocks,) * 7 + (whole,) * 3,
        out_specs=(rows, rows) + (blocks,) * 8 + (whole,) * 3,
        check_vma=False,
    )
```
